32 devices in a mesh: seq: 4 (over x, core), head: 8 (over z, y).
Axes of the slice: x: 2, y: 2, z: 4, core: 2. Of those that a mesh axis runs over, the one named last changes fastest.
Arguments:
- tokens: bfloat16 [2048, 2048], P('seq', 'head'), may hold values from -6 to 6
- norm_gain: float32 [2048], replicated, may hold values from 0.25 to 1.75
- w_qkv: bfloat16 [3, 2048, 2048], P(None, None, 'head'), may hold values from -0.125 to 0.125
- head_scale: float32 [16], P('head'), may hold values from 4 to 24
- w_out: bfloat16 [2048, 2048], P('head'), may hold values from -0.25 to 0.25
- scale_ids: int32 [2048], replicated, may hold values from 0 to 9, as said below
Outputs:
- branch_out: bfloat16 [2048, 2048], P('seq', 'head')
The draws below stay inside these ranges and needn't reach their ends.
Inputs may be any that keep to these rules, and one draw needn't show every extreme that they name: scale_ids never falls from one token to the next, and every scale from 0 to 9 occurs.
All inputs are finite; a program needn't handle non-finite values.
Results may differ from the reference program's by a relative error of at most 0.014.
Values may be sent and summed in bfloat16 or wider, within the bound.
No kernel may reach another device: no remote copies, remote signals or barrier semaphores. Data moves between devices by JAX's collectives and lax.ppermute only.
A program may use at most 128 MiB of HBM per device.

```python
import math
import jax
import jax.numpy as jnp
from jax import lax

D = 2048
HEADS = 16
HEAD_DIM = 128
NSCALE = 10
TOKENS = 2048


def draw_scale_ids(key, part):
    sizes_table = jnp.array([1, 4, 9, 16, 36, 81, 169, 324, 576, 1024], jnp.int32)
    cumulative = jnp.cumsum(sizes_table)[:-1]
    base = cumulative * TOKENS // 2240
    spread = max(TOKENS // 512, 1)
    jitter = jax.random.randint(key, (NSCALE - 1,), -spread, spread + 1)
    bounds = jnp.clip(base + jitter, 1, TOKENS - NSCALE)
    offsets = jnp.arange(NSCALE - 1, dtype=jnp.int32)
    bounds = lax.cummax(bounds - offsets) + offsets
    position = jnp.arange(TOKENS, dtype=jnp.int32)
    return jnp.sum((position[:, None] >= bounds[None, :]).astype(jnp.int32), axis=1).astype(jnp.int32)


def block_scale(own_key, shape, split, low, top_value):
    factor_of = 1.0
    for dim, shards_of in split:
        steps = jax.random.uniform(jax.random.fold_in(jax.random.fold_in(own_key, 6), dim), (shards_of,), jnp.float32, low / len(split), top_value / len(split))
        factor_of = factor_of * jnp.repeat(jnp.exp(steps), shape[dim] // shards_of).reshape((-1,) + (1,) * (len(shape) - 1 - dim))
    return factor_of


def bell_draw(own_key, extent, scale, reach, pieces=(), kind=jnp.bfloat16):
    values = scale * jax.random.normal(own_key, extent, jnp.float32)
    if pieces:
        values = values * block_scale(own_key, extent, pieces, -0.22, 0.18)
    return jnp.clip(values, -reach, reach).astype(kind)


def setup_inputs(seed: int = 0) -> dict:
    splits = jax.random.split(jax.random.key(seed), 7)
    tokens = bell_draw(splits[0], (TOKENS, D), 1.0, 6.0, ((0, 4), (1, 8)))
    norm_gain = jnp.clip(1.0 + 0.15 * jax.random.normal(splits[1], (D,), jnp.float32), 0.25, 1.75)
    w_qkv = bell_draw(splits[2], (3, D, HEADS * HEAD_DIM), D ** -0.5, 0.125, ((2, 8),))
    head_scale = jnp.clip(jnp.exp(math.log(24.0) - 1.7917595 * jax.random.uniform(splits[3], (HEADS,), jnp.float32) ** block_scale(splits[3], (HEADS,), ((0, 8),), -0.2, 0.2)), 4.0, 24.0)
    w_out = bell_draw(splits[4], (HEADS * HEAD_DIM, D), (HEAD_DIM * 4) ** -0.5, 0.25, ((0, 8),))
    scale_ids = draw_scale_ids(jax.random.fold_in(splits[6], 71), 0)
    return dict(tokens=tokens, norm_gain=norm_gain, w_qkv=w_qkv, head_scale=head_scale, w_out=w_out, scale_ids=scale_ids)


def rms_normed(tokens, norm_gain):
    values = tokens.astype(jnp.float32)
    power = lax.optimization_barrier(jnp.mean(values * values, axis=-1, keepdims=True))
    return (values * lax.rsqrt(power + 1e-06) * norm_gain).astype(jnp.bfloat16)

def unit_rows(values, factor):
    power = lax.optimization_barrier(jnp.sum(values * values, axis=-1, keepdims=True))
    return (values * lax.rsqrt(power + 1e-06) * factor).astype(jnp.bfloat16)

def reference(tokens, norm_gain, w_qkv, head_scale, w_out, scale_ids):
    count = tokens.shape[0]
    normed = rms_normed(tokens, norm_gain)
    query = jnp.dot(normed, w_qkv[0], preferred_element_type=jnp.float32).reshape(count, HEADS, HEAD_DIM)
    keyset = jnp.dot(normed, w_qkv[1], preferred_element_type=jnp.float32).reshape(count, HEADS, HEAD_DIM)
    valset = jnp.dot(normed, w_qkv[2], preferred_element_type=jnp.float32).reshape(count, HEADS, HEAD_DIM)
    query_n = unit_rows(query, head_scale[None, :, None])
    key_n = unit_rows(keyset, 1.0).astype(jnp.float32)
    val_b = valset.astype(jnp.bfloat16).astype(jnp.float32)
    block = min(128, count)
    query_blocks = query_n.reshape(count // block, block, HEADS, HEAD_DIM)
    id_blocks = scale_ids.reshape(count // block, block)

    def one_block(args):
        qblk, qid = args
        score = jnp.einsum('qhd,khd->hqk', qblk.astype(jnp.float32), key_n)
        allowed = (scale_ids[None, :] <= qid[:, None])[None]
        score = jnp.where(allowed, score, -1e+30)
        top = lax.optimization_barrier(jnp.max(score, axis=-1, keepdims=True))
        expo = jnp.where(allowed, jnp.exp(score - top), 0.0)
        total = lax.optimization_barrier(jnp.sum(expo, axis=-1))
        weight = expo.astype(jnp.bfloat16).astype(jnp.float32)
        summed = jnp.einsum('hqk,khd->qhd', weight, val_b)
        return summed / jnp.transpose(total)[:, :, None]
    attended = lax.map(one_block, (query_blocks, id_blocks))
    attended = attended.reshape(count, HEADS * HEAD_DIM).astype(jnp.bfloat16)
    return jnp.dot(attended, w_out, preferred_element_type=jnp.float32).astype(jnp.bfloat16)
```

```python
import functools
import math

import jax
import jax.numpy as jnp
from jax import lax
from jax.experimental import pallas as pl
from jax.experimental.pallas import tpu as pltpu
from jax.sharding import PartitionSpec as P

CHUNKS = 1
LOG2E = math.log2(math.e)
VMEM = pl.BlockSpec(memory_space=pltpu.VMEM)
SMEM = pl.BlockSpec(memory_space=pltpu.SMEM)
F32 = jnp.float32
BF16 = jnp.bfloat16


def along(value, senders, step):
    return lax.ppermute(
        value, "head", [(2 * z + y, 2 * (z + step) + y) for z in senders for y in (0, 1)]
    )


def across(value, members):
    return lax.ppermute(value, "head", [(2 * z + y, 2 * z + 1 - y) for z in members for y in (0, 1)])


def gather_line(block, length):
    found = [((0, 1, 0), block)]
    ups, downs = [block], [block]
    swaps = [((0, 1, 1), across(block, range(length)))]
    for step in range(1, length):
        ups.append(along(ups[-1], range(step - 1, length - 1), 1))
        downs.append(along(downs[-1], range(1, length - step + 1), -1))
        found.append(((step, -1, 0), ups[-1]))
        found.append(((step, 1, 0), downs[-1]))
        swaps.append(((step, -1, 1), across(ups[-1], range(step, length))))
        swaps.append(((step, 1, 1), across(downs[-1], range(0, length - step))))
    return found + swaps


def project_kernel(rules, length, head_size, info, factor, *refs):
    blocks, (w_ref, q_ref, kv_ref, wide) = refs[: len(rules)], refs[len(rules) :]
    place, row = info[0], info[1]
    width = blocks[0].shape[1]
    for (step, side, other), block in zip(rules, blocks):
        source = place + side * step
        lane = (2 * source + (row if other == 0 else 1 - row)) * width

        @pl.when((source >= 0) & (source < length))
        def _():
            wide[:, pl.ds(pl.multiple_of(lane, width), width)] = block[...]

    rows, depth = wide.shape
    tile = math.gcd(rows, 128)
    out_width = q_ref.shape[1]

    @pl.loop(0, rows // tile)
    def _(index):
        here = pl.ds(pl.multiple_of(index * tile, tile), tile)
        x = wide[here, :]
        values = x.astype(F32)
        power = jnp.sum(values * values, axis=-1, keepdims=True) * (1.0 / depth)
        scale = lax.rsqrt(power + 1e-06)
        q = jnp.dot(x, w_ref[0], preferred_element_type=F32) * scale
        k = jnp.dot(x, w_ref[1], preferred_element_type=F32) * scale
        v = jnp.dot(x, w_ref[2], preferred_element_type=F32) * scale
        for head in range(out_width // head_size):
            lanes = slice(head * head_size, (head + 1) * head_size)
            qh, kh = q[:, lanes], k[:, lanes]
            q_size = lax.rsqrt(jnp.sum(qh * qh, axis=-1, keepdims=True) + 1e-06)
            k_size = lax.rsqrt(jnp.sum(kh * kh, axis=-1, keepdims=True) + 1e-06)
            q_ref[here, lanes] = (qh * (q_size * (factor[head] * LOG2E))).astype(BF16)
            kv_ref[here, lanes] = (kh * k_size).astype(BF16)
        kv_ref[here, out_width:] = v.astype(BF16)


def project(rules, blocks, weights, factor, info, length, head_size):
    rows, width = blocks[0].shape
    depth, out_width = weights.shape[1:]
    return pl.pallas_call(
        functools.partial(project_kernel, rules, length, head_size),
        out_shape=(
            jax.ShapeDtypeStruct((rows, out_width), BF16),
            jax.ShapeDtypeStruct((rows, 2 * out_width), BF16),
        ),
        in_specs=[SMEM, SMEM] + [VMEM] * (len(rules) + 1),
        out_specs=(VMEM, VMEM),
        scratch_shapes=[pltpu.VMEM((rows, depth), BF16)],
        compiler_params=pltpu.CompilerParams(vmem_limit_bytes=32 << 20),
        cost_estimate=pl.CostEstimate(
            flops=6 * rows * depth * out_width,
            bytes_accessed=2 * (rows * depth + 3 * depth * out_width),
            transcendentals=0,
        ),
        name="project",
    )(info, factor, *blocks, weights)


def attend_blocks(sources, ids, q_first, q_refs, id_col, id_row, kv_refs, v_ones, acc, head_size):
    heads = q_refs[0].shape[1] // head_size
    keys = kv_refs[0].shape[0]
    rows = q_refs[0].shape[0]
    for number, kv_ref in enumerate(kv_refs):
        for head in range(heads):
            start = (heads + head) * head_size
            v_ones[head, :, :head_size] = kv_ref[:, start : start + head_size]
            v_ones[head, :, head_size:] = jnp.ones((keys, head_size), BF16)
        first = sources[number]
        key_low, key_high = ids[first], ids[first + keys - 1]
        tile = math.gcd(rows, 256)
        for chunk, q_ref in enumerate(q_refs):

            @pl.loop(0, rows // tile)
            def _(index):
                here = pl.ds(pl.multiple_of(index * tile, tile), tile)
                base = chunk * rows + index * tile
                there = pl.ds(pl.multiple_of(base, tile), tile)
                q_low = ids[q_first + base]
                q_high = ids[q_first + base + tile - 1]

                def add(masked):
                    if masked:
                        allowed = id_row[first // keys] <= id_col[there, :]
                    for head in range(heads):
                        lanes = slice(head * head_size, (head + 1) * head_size)
                        score = lax.dot_general(
                            q_ref[here, lanes],
                            kv_ref[:, lanes],
                            (((1,), (1,)), ((), ())),
                            preferred_element_type=F32,
                        )
                        weight = jnp.exp2(score)
                        if masked:
                            weight = jnp.where(allowed, weight, 0.0)
                        wide = slice(2 * head * head_size, 2 * (head + 1) * head_size)
                        acc[there, wide] += jnp.dot(
                            weight.astype(BF16), v_ones[head], preferred_element_type=F32
                        )

                @pl.when(key_high <= q_low)
                def _():
                    add(False)

                @pl.when((key_high > q_low) & (key_low <= q_high))
                def _():
                    add(True)


def first_kernel(count_q, count_kv, head_size, info, ids, *refs):
    q_refs = refs[:count_q]
    id_col, id_row = refs[count_q : count_q + 2]
    kv_refs = refs[count_q + 2 : count_q + 2 + count_kv]
    acc, v_ones = refs[count_q + 2 + count_kv :]
    acc[...] = jnp.zeros_like(acc)
    sources = [info[3 + number] for number in range(count_kv)]
    attend_blocks(sources, ids, info[2], q_refs, id_col, id_row, kv_refs, v_ones, acc, head_size)


def last_kernel(count_q, count_kv, head_size, roles, length, info, ids, *refs):
    q_refs = refs[:count_q]
    id_col, id_row = refs[count_q : count_q + 2]
    kv_refs = refs[count_q + 2 : count_q + 2 + count_kv]
    rest = refs[count_q + 2 + count_kv :]
    acc_in, w_ref = rest[:2]
    outs, (v_ones, acc, attended) = rest[2:-3], rest[-3:]
    acc[...] = acc_in[...]
    sources = [info[3 + number] for number in range(count_kv)]
    attend_blocks(sources, ids, info[2], q_refs, id_col, id_row, kv_refs, v_ones, acc, head_size)
    heads = q_refs[0].shape[1] // head_size
    for head in range(heads):
        start = 2 * head * head_size
        attended[:, head * head_size : (head + 1) * head_size] = (
            acc[:, start : start + head_size]
            / acc[:, start + head_size : start + 2 * head_size]
        ).astype(BF16)
    place, row = info[0], info[1]
    width = outs[0].shape[1]
    for number, role in enumerate(roles):
        goal, valid = role(place)

        @pl.when(valid)
        def _():
            for other in (1, 0):
                lane = (2 * goal + (row if other == 0 else 1 - row)) * width
                outs[2 * number + 1 - other][...] = jnp.dot(
                    attended[...],
                    w_ref[:, pl.ds(pl.multiple_of(lane, width), width)],
                    preferred_element_type=F32,
                ).astype(BF16)


def attend_first(info, ids, queries, id_col, id_row, kvs, head_size):
    rows, width = queries[0].shape
    total = rows * len(queries)
    keys = kvs[0].shape[0]
    heads = width // head_size
    return pl.pallas_call(
        functools.partial(first_kernel, len(queries), len(kvs), head_size),
        out_shape=jax.ShapeDtypeStruct((total, 2 * width), F32),
        in_specs=[SMEM, SMEM] + [VMEM] * (len(queries) + 2 + len(kvs)),
        out_specs=VMEM,
        scratch_shapes=[pltpu.VMEM((heads, keys, 2 * head_size), BF16)],
        compiler_params=pltpu.CompilerParams(vmem_limit_bytes=48 << 20),
        cost_estimate=pl.CostEstimate(
            flops=6 * total * keys * len(kvs) * width,
            bytes_accessed=4 * keys * len(kvs) * width + 4 * total * width,
            transcendentals=total * keys * len(kvs) * heads,
        ),
        name="attend_first",
    )(info, ids, *queries, id_col, id_row, *kvs)


def attend_last(info, ids, queries, id_col, id_row, kvs, acc, w_out, roles, length, head_size):
    rows, width = queries[0].shape
    total = rows * len(queries)
    keys = kvs[0].shape[0]
    heads = width // head_size
    out_width = w_out.shape[1] // (2 * length)
    outs = 2 * len(roles)
    return pl.pallas_call(
        functools.partial(last_kernel, len(queries), len(kvs), head_size, roles, length),
        out_shape=(jax.ShapeDtypeStruct((total, out_width), BF16),) * outs,
        in_specs=[SMEM, SMEM] + [VMEM] * (len(queries) + 4 + len(kvs)),
        out_specs=(VMEM,) * outs,
        scratch_shapes=[
            pltpu.VMEM((heads, keys, 2 * head_size), BF16),
            pltpu.VMEM((total, 2 * width), F32),
            pltpu.VMEM((total, width), BF16),
        ],
        compiler_params=pltpu.CompilerParams(vmem_limit_bytes=48 << 20),
        cost_estimate=pl.CostEstimate(
            flops=6 * total * keys * len(kvs) * width + 2 * total * width * w_out.shape[1],
            bytes_accessed=4 * keys * len(kvs) * width + 4 * total * width * 4,
            transcendentals=total * keys * len(kvs) * heads,
        ),
        name="attend_last",
    )(info, ids, *queries, id_col, id_row, *kvs, acc, w_out)


def total_of(*parts):
    return sum(part.astype(F32) for part in parts).astype(BF16)


def line_roles(length):
    roles = []
    for step in range(length - 1, 0, -1):
        roles.append(lambda place, step=step: (place + step, place + step < length))
        roles.append(lambda place, step=step: (place - step, place - step >= 0))
    roles.append(lambda place: (place, place >= 0))
    return roles


def body(mesh_shape, tokens, norm_gain, w_qkv, head_scale, w_out, scale_ids):
    length = mesh_shape["head"] // 2
    outer = mesh_shape["seq"] // 2
    rows, width = tokens.shape
    head_size = w_qkv.shape[2] // head_scale.shape[0]
    chunk_rows = rows // CHUNKS
    head_at, seq_at = lax.axis_index("head"), lax.axis_index("seq")
    place, row = head_at // 2, head_at % 2
    chip, core = seq_at // 2, seq_at % 2

    weights = (w_qkv.astype(F32) * norm_gain[None, :, None]).astype(BF16)
    id_row = scale_ids.reshape(-1, 1, chunk_rows)
    id_col = lax.dynamic_slice_in_dim(scale_ids, seq_at * rows, rows)[:, None]

    info = jnp.stack([place, row]).astype(jnp.int32)
    queries, near, near_at, far, far_at = [], [], [], [], []
    for number in range(CHUNKS):
        part = tokens[number * chunk_rows : (number + 1) * chunk_rows]
        gathered = gather_line(part, length)
        query, kv = project(
            [rule for rule, data in gathered],
            [data for rule, data in gathered],
            weights, head_scale, info, length, head_size,
        )
        queries.append(query)
        swap = [(2 * a + b, 2 * a + 1 - b) for a in range(outer) for b in (0, 1)]
        start = number * chunk_rows
        for step in range(outer):
            if step:
                shift = [
                    (2 * a + b, 2 * ((a + step) % outer) + b) for a in range(outer) for b in (0, 1)
                ]
                held = lax.ppermute(kv, "seq", shift)
            else:
                held = kv
            source = 2 * ((chip + outer - step) % outer)
            group, group_at = (far, far_at) if step else (near, near_at)
            group.append(held)
            group_at.append((source + core) * rows + start)
            group.append(lax.ppermute(held, "seq", swap))
            group_at.append((source + 1 - core) * rows + start)

    near_info = jnp.stack([place, row, seq_at * rows] + near_at).astype(jnp.int32)
    far_info = jnp.stack([place, row, seq_at * rows] + far_at).astype(jnp.int32)
    acc = attend_first(near_info, scale_ids, queries, id_col, id_row, near, head_size)
    roles = line_roles(length)
    parts = attend_last(
        far_info, scale_ids, queries, id_col, id_row, far, acc, w_out, roles, length, head_size
    )
    up = down = None
    number = 0
    for step in range(length - 1, 0, -1):
        up_senders, down_senders = range(0, length - step), range(step, length)
        up_parts = [parts[number + 1], across(parts[number], up_senders)]
        down_parts = [parts[number + 3], across(parts[number + 2], down_senders)]
        if up is not None:
            up_parts.append(up)
            down_parts.append(down)
        up = along(total_of(*up_parts), up_senders, 1)
        down = along(total_of(*down_parts), down_senders, -1)
        number += 4
    return total_of(parts[number + 1], across(parts[number], range(length)), up, down)


def solution(mesh):
    placed = (P("seq", "head"), P(), P(None, None, "head"), P("head"), P("head", None), P())
    return jax.shard_map(
        functools.partial(body, dict(mesh.shape)),
        mesh=mesh,
        in_specs=placed,
        out_specs=P("seq", "head"),
        check_vma=False,
    )
```

```python
import functools
import math

import jax
import jax.numpy as jnp
from jax import lax
from jax.experimental import pallas as pl
from jax.experimental.pallas import tpu as pltpu
from jax.sharding import PartitionSpec as P

LOG2E = math.log2(math.e)
VMEM = pl.BlockSpec(memory_space=pltpu.VMEM)
SMEM = pl.BlockSpec(memory_space=pltpu.SMEM)
F32 = jnp.float32
BF16 = jnp.bfloat16


def ring_order(count):
    line = count // 2
    return [2 * z for z in range(line)] + [2 * z + 1 for z in reversed(range(line))]


def ring_place(index, count):
    return jnp.where(index % 2 == 0, index // 2, count - 1 - index // 2)


def ring_index(place, count):
    return jnp.where(place < count // 2, 2 * place, 2 * (count - 1 - place) + 1)


def along(value, step, count):
    order = ring_order(count)
    return lax.ppermute(
        value, "head", [(order[p], order[(p + step) % count]) for p in range(count)]
    )


def gather_kernel(count, has_acc, head_size, at, factor, *refs):
    blocks, gains, weights = refs[:count], refs[count : 2 * count], refs[2 * count : 3 * count]
    rest = refs[3 * count :]
    if has_acc:
        acc_in, power_in = rest[:2]
        rest = rest[2:]
    rows, width = blocks[0].shape
    groups, _, out_width = weights[0].shape
    tile = math.gcd(rows, 128)

    @pl.loop(0, rows // tile)
    def _(index):
        here = pl.ds(pl.multiple_of(index * tile, tile), tile)
        power = power_in[here, :] if has_acc else None
        scaled = []
        for block, gain in zip(blocks, gains):
            values = block[here, :].astype(F32)
            scaled.append((values * gain[0]).astype(BF16))
            square = values * values
            for lane in range(0, width, 128):
                piece = square[:, lane : lane + 128]
                power = piece if power is None else power + piece
        sums = []
        for group in range(groups):
            total = acc_in[here, group * out_width : (group + 1) * out_width] if has_acc else None
            for x, w_ref in zip(scaled, weights):
                product = jnp.dot(x, w_ref[group], preferred_element_type=F32)
                total = product if total is None else total + product
            sums.append(total)
        if head_size is None:
            acc, power_out = rest
            for group, total in enumerate(sums):
                acc[here, group * out_width : (group + 1) * out_width] = total
            power_out[here, :] = power
        else:
            q_ref, kv_ref = rest
            mean = jnp.sum(power, axis=-1, keepdims=True) * factor[out_width // head_size]
            scale = lax.rsqrt(mean + 1e-06)
            q, k, v = (total * scale for total in sums)
            for head in range(out_width // head_size):
                lanes = slice(head * head_size, (head + 1) * head_size)
                qh, kh = q[:, lanes], k[:, lanes]
                q_size = lax.rsqrt(jnp.sum(qh * qh, axis=-1, keepdims=True) + 1e-06)
                k_size = lax.rsqrt(jnp.sum(kh * kh, axis=-1, keepdims=True) + 1e-06)
                q_ref[here, lanes] = (qh * (q_size * (factor[head] * LOG2E))).astype(BF16)
                kv_ref[here, lanes] = (kh * k_size).astype(BF16)
            kv_ref[here, out_width:] = v.astype(BF16)


def gather_step(at, factor, blocks, gain, weights, state, head_size=None):
    rows, width = blocks[0].shape
    groups, depth, out_width = weights.shape
    count = len(blocks)
    whole = lambda shape: pl.BlockSpec(shape, lambda i, at, factor: (0, 0))
    in_specs = [whole((rows, width))] * count
    in_specs += [
        pl.BlockSpec((1, 1, width), lambda i, at, factor, n=n: (at[n], 0, 0)) for n in range(count)
    ]
    in_specs += [
        pl.BlockSpec((groups, width, out_width), lambda i, at, factor, n=n: (0, at[n], 0))
        for n in range(count)
    ]
    shapes = [(rows, groups * out_width), (rows, 128)]
    if state is not None:
        in_specs += [whole(shape) for shape in shapes]
    kinds = [F32, F32]
    if head_size is not None:
        shapes, kinds = [(rows, out_width), (rows, 2 * out_width)], [BF16, BF16]
    return pl.pallas_call(
        functools.partial(gather_kernel, count, state is not None, head_size),
        out_shape=tuple(jax.ShapeDtypeStruct(s, kind) for s, kind in zip(shapes, kinds)),
        grid_spec=pltpu.PrefetchScalarGridSpec(
            num_scalar_prefetch=2,
            grid=(1,),
            in_specs=in_specs,
            out_specs=tuple(whole(shape) for shape in shapes),
        ),
        compiler_params=pltpu.CompilerParams(vmem_limit_bytes=32 << 20),
        cost_estimate=pl.CostEstimate(
            flops=2 * rows * width * count * groups * out_width,
            bytes_accessed=2 * width * count * (rows + groups * out_width)
            + 8 * rows * groups * out_width,
            transcendentals=0,
        ),
        name="gather_step" if head_size is None else "gather_last",
    )(at, factor, *blocks, *[gain] * count, *[weights] * count, *(state or ()))


def attend_blocks(sources, ids, q_first, q_refs, id_col, id_row, kv_refs, v_ones, acc, head_size):
    heads = q_refs[0].shape[1] // head_size
    keys = kv_refs[0].shape[0]
    rows = q_refs[0].shape[0]
    for number, kv_ref in enumerate(kv_refs):
        for head in range(heads):
            start = (heads + head) * head_size
            v_ones[head, :, :head_size] = kv_ref[:, start : start + head_size]
            v_ones[head, :, head_size:] = jnp.ones((keys, head_size), BF16)
        first = sources[number]
        key_low, key_high = ids[first], ids[first + keys - 1]
        tile = math.gcd(rows, 256)
        for chunk, q_ref in enumerate(q_refs):

            @pl.loop(0, rows // tile)
            def _(index):
                here = pl.ds(pl.multiple_of(index * tile, tile), tile)
                base = chunk * rows + index * tile
                there = pl.ds(pl.multiple_of(base, tile), tile)
                q_low = ids[q_first + base]
                q_high = ids[q_first + base + tile - 1]

                def add(masked):
                    if masked:
                        allowed = id_row[first // keys] <= id_col[there, :]
                    for head in range(heads):
                        lanes = slice(head * head_size, (head + 1) * head_size)
                        score = lax.dot_general(
                            q_ref[here, lanes],
                            kv_ref[:, lanes],
                            (((1,), (1,)), ((), ())),
                            preferred_element_type=F32,
                        )
                        weight = jnp.exp2(score)
                        if masked:
                            weight = jnp.where(allowed, weight, 0.0)
                        wide = slice(2 * head * head_size, 2 * (head + 1) * head_size)
                        acc[there, wide] += jnp.dot(
                            weight.astype(BF16), v_ones[head], preferred_element_type=F32
                        )

                @pl.when(key_high <= q_low)
                def _():
                    add(False)

                @pl.when((key_high > q_low) & (key_low <= q_high))
                def _():
                    add(True)


def first_kernel(count_q, count_kv, head_size, info, ids, *refs):
    q_refs = refs[:count_q]
    id_col, id_row = refs[count_q : count_q + 2]
    kv_refs = refs[count_q + 2 : count_q + 2 + count_kv]
    acc, v_ones = refs[count_q + 2 + count_kv :]
    acc[...] = jnp.zeros_like(acc)
    sources = [info[1 + number] for number in range(count_kv)]
    attend_blocks(sources, ids, info[0], q_refs, id_col, id_row, kv_refs, v_ones, acc, head_size)


def last_kernel(count_q, count_kv, head_size, count_out, info, ids, *refs):
    q_refs = refs[:count_q]
    id_col, id_row = refs[count_q : count_q + 2]
    kv_refs = refs[count_q + 2 : count_q + 2 + count_kv]
    rest = refs[count_q + 2 + count_kv :]
    acc_in, w_ref = rest[:2]
    outs, (v_ones, acc, attended) = rest[2:-3], rest[-3:]
    acc[...] = acc_in[...]
    sources = [info[count_out + 1 + number] for number in range(count_kv)]
    attend_blocks(sources, ids, info[count_out], q_refs, id_col, id_row, kv_refs, v_ones, acc, head_size)
    heads = q_refs[0].shape[1] // head_size
    for head in range(heads):
        start = 2 * head * head_size
        attended[:, head * head_size : (head + 1) * head_size] = (
            acc[:, start : start + head_size]
            / acc[:, start + head_size : start + 2 * head_size]
        ).astype(BF16)
    width = outs[0].shape[1]
    for number, out in enumerate(outs):
        lane = info[number] * width
        out[...] = jnp.dot(
            attended[...],
            w_ref[:, pl.ds(pl.multiple_of(lane, width), width)],
            preferred_element_type=F32,
        ).astype(BF16)


def attend_first(info, ids, queries, id_col, id_row, kvs, head_size):
    rows, width = queries[0].shape
    total = rows * len(queries)
    keys = kvs[0].shape[0]
    heads = width // head_size
    return pl.pallas_call(
        functools.partial(first_kernel, len(queries), len(kvs), head_size),
        out_shape=jax.ShapeDtypeStruct((total, 2 * width), F32),
        in_specs=[SMEM, SMEM] + [VMEM] * (len(queries) + 2 + len(kvs)),
        out_specs=VMEM,
        scratch_shapes=[pltpu.VMEM((heads, keys, 2 * head_size), BF16)],
        compiler_params=pltpu.CompilerParams(vmem_limit_bytes=48 << 20),
        cost_estimate=pl.CostEstimate(
            flops=6 * total * keys * len(kvs) * width,
            bytes_accessed=4 * keys * len(kvs) * width + 4 * total * width,
            transcendentals=total * keys * len(kvs) * heads,
        ),
        name="attend_first",
    )(info, ids, *queries, id_col, id_row, *kvs)


def attend_last(info, ids, queries, id_col, id_row, kvs, acc, w_out, count_out, head_size):
    rows, width = queries[0].shape
    total = rows * len(queries)
    keys = kvs[0].shape[0]
    heads = width // head_size
    out_width = w_out.shape[1] // count_out
    return pl.pallas_call(
        functools.partial(last_kernel, len(queries), len(kvs), head_size, count_out),
        out_shape=(jax.ShapeDtypeStruct((total, out_width), BF16),) * count_out,
        in_specs=[SMEM, SMEM] + [VMEM] * (len(queries) + 4 + len(kvs)),
        out_specs=(VMEM,) * count_out,
        scratch_shapes=[
            pltpu.VMEM((heads, keys, 2 * head_size), BF16),
            pltpu.VMEM((total, 2 * width), F32),
            pltpu.VMEM((total, width), BF16),
        ],
        compiler_params=pltpu.CompilerParams(vmem_limit_bytes=48 << 20),
        cost_estimate=pl.CostEstimate(
            flops=6 * total * keys * len(kvs) * width + 2 * total * width * w_out.shape[1],
            bytes_accessed=4 * keys * len(kvs) * width + 4 * total * width * 4,
            transcendentals=total * keys * len(kvs) * heads,
        ),
        name="attend_last",
    )(info, ids, *queries, id_col, id_row, *kvs, acc, w_out)


def total_of(*parts):
    return sum(part.astype(F32) for part in parts).astype(BF16)


def body(mesh_shape, tokens, norm_gain, w_qkv, head_scale, w_out, scale_ids):
    ring = mesh_shape["head"]
    outer = mesh_shape["seq"] // 2
    rows, width = tokens.shape
    head_size = w_qkv.shape[2] // head_scale.shape[0]
    head_at, seq_at = lax.axis_index("head"), lax.axis_index("seq")
    place = ring_place(head_at, ring)
    chip, core = seq_at // 2, seq_at % 2
    index_at = lambda offset: ring_index((place + offset + ring) % ring, ring)

    id_row = scale_ids.reshape(-1, 1, rows)
    id_col = lax.dynamic_slice_in_dim(scale_ids, seq_at * rows, rows)[:, None]

    ahead, behind = ring // 2, ring - 1 - ring // 2
    gain = norm_gain.reshape(ring, 1, width)
    factor = jnp.concatenate([head_scale, jnp.full((1,), 1.0 / (ring * width), F32)])
    state, held_up, held_down = None, tokens, tokens
    blocks, offsets = [tokens], [0]
    for step in range(1, ahead + 1):
        held_up = along(held_up, 1, ring)
        blocks.append(held_up)
        offsets.append(-step)
        if step <= behind:
            held_down = along(held_down, -1, ring)
            blocks.append(held_down)
            offsets.append(step)
        if step in (1, ahead - 1, ahead):
            at = jnp.stack([index_at(offset) for offset in offsets]).astype(jnp.int32)
            state = gather_step(
                at, factor, blocks, gain, w_qkv, state, head_size if step == ahead else None
            )
            blocks, offsets = [], []
    query, kv = state

    swap = [(2 * a + b, 2 * a + 1 - b) for a in range(outer) for b in (0, 1)]
    near, near_at, far, far_at = [], [], [], []
    for step in range(outer):
        held = kv
        if step:
            shift = [(2 * a + b, 2 * ((a + step) % outer) + b) for a in range(outer) for b in (0, 1)]
            held = lax.ppermute(kv, "seq", shift)
        source = 2 * ((chip + outer - step) % outer)
        group, group_at = (far, far_at) if step else (near, near_at)
        group.append(held)
        group_at.append((source + core) * rows)
        group_at.append((source + 1 - core) * rows)
        if not step:
            group.append(lax.ppermute(held, "seq", swap))
    near_info = jnp.stack([seq_at * rows] + near_at).astype(jnp.int32)
    acc = attend_first(near_info, scale_ids, [query], id_col, id_row, near, head_size)
    acc, *far = lax.optimization_barrier((acc, *far))
    far = [data for held in far for data in (held, lax.ppermute(held, "seq", swap))]

    goals = list(range(ahead, 0, -1)) + list(range(-behind, 0)) + [0]
    far_info = jnp.stack([index_at(goal) for goal in goals] + [seq_at * rows] + far_at)
    parts = attend_last(
        far_info.astype(jnp.int32),
        scale_ids, [query], id_col, id_row, far, acc, w_out, ring, head_size,
    )
    up = along(parts[0], 1, ring)
    down = along(parts[ahead], -1, ring)
    for step in range(1, ahead):
        up = along(total_of(parts[step], up), 1, ring)
        if step < behind:
            down = along(total_of(parts[ahead + step], down), -1, ring)
    return total_of(parts[-1], up, down)


def solution(mesh):
    placed = (P("seq", "head"), P(), P(None, None, "head"), P("head"), P("head", None), P())
    return jax.shard_map(
        functools.partial(body, dict(mesh.shape)),
        mesh=mesh,
        in_specs=placed,
        out_specs=P("seq", "head"),
        check_vma=False,
    )
```

```python
import functools
import math

import jax
import jax.numpy as jnp
from jax import lax
from jax.experimental import pallas as pl
from jax.experimental.pallas import tpu as pltpu
from jax.sharding import PartitionSpec as P

LOG2E = math.log2(math.e)
VMEM = pl.BlockSpec(memory_space=pltpu.VMEM)
SMEM = pl.BlockSpec(memory_space=pltpu.SMEM)
F32 = jnp.float32
BF16 = jnp.bfloat16


def ring_order(count):
    line = count // 2
    return [2 * z for z in range(line)] + [2 * z + 1 for z in reversed(range(line))]


def ring_place(index, count):
    return jnp.where(index % 2 == 0, index // 2, count - 1 - index // 2)


def ring_index(place, count):
    return jnp.where(place < count // 2, 2 * place, 2 * (count - 1 - place) + 1)


def along(value, step, count):
    order = ring_order(count)
    return lax.ppermute(
        value, "head", [(order[p], order[(p + step) % count]) for p in range(count)]
    )


def gather_kernel(streams, count, has_state, head_size, at, factor, *refs):
    gain_ref, w_hbm = refs[:2]
    per_in = count + (2 if has_state else 0)
    ins = [refs[2 + s * per_in : 2 + (s + 1) * per_in] for s in range(streams)]
    outs = refs[2 + streams * per_in : -2]
    w_ref, sems = refs[-2:]
    width = ins[0][0].shape[1]
    rows = ins[0][0].shape[0]
    groups, out_width = w_hbm.shape[0], w_hbm.shape[2]

    def fetch(n):
        start = pl.multiple_of(at[n] * width, width)
        return pltpu.make_async_copy(w_hbm.at[:, pl.ds(start, width), :], w_ref.at[n], sems.at[n])

    for n in range(count):
        fetch(n).start()
    for n in range(count):
        fetch(n).wait()
    tile = math.gcd(rows, 128)
    for stream in range(streams):
        blocks = ins[stream][:count]
        state = ins[stream][count:]
        out = outs[2 * stream : 2 * stream + 2]

        @pl.loop(0, rows // tile)
        def _(index):
            here = pl.ds(pl.multiple_of(index * tile, tile), tile)
            power = state[1][here, :] if has_state else None
            scaled = []
            for n, block in enumerate(blocks):
                values = block[here, :].astype(F32)
                scaled.append((values * gain_ref[pl.ds(at[n], 1), :]).astype(BF16))
                square = values * values
                for lane in range(0, width, 128):
                    piece = square[:, lane : lane + 128]
                    power = piece if power is None else power + piece
            sums = []
            for group in range(groups):
                total = state[0][here, group * out_width : (group + 1) * out_width] if has_state else None
                for n, x in enumerate(scaled):
                    product = jnp.dot(x, w_ref[n, group], preferred_element_type=F32)
                    total = product if total is None else total + product
                sums.append(total)
            if head_size is None:
                for group, total in enumerate(sums):
                    out[0][here, group * out_width : (group + 1) * out_width] = total
                out[1][here, :] = power
            else:
                mean = jnp.sum(power, axis=-1, keepdims=True) * (1.0 / w_hbm.shape[1])
                scale = lax.rsqrt(mean + 1e-06)
                q, k, v = (total * scale for total in sums)
                for head in range(out_width // head_size):
                    lanes = slice(head * head_size, (head + 1) * head_size)
                    qh, kh = q[:, lanes], k[:, lanes]
                    q_size = lax.rsqrt(jnp.sum(qh * qh, axis=-1, keepdims=True) + 1e-06)
                    k_size = lax.rsqrt(jnp.sum(kh * kh, axis=-1, keepdims=True) + 1e-06)
                    out[0][here, lanes] = (qh * (q_size * (factor[head] * LOG2E))).astype(BF16)
                    out[1][here, lanes] = (kh * k_size).astype(BF16)
                out[1][here, out_width:] = v.astype(BF16)


def gather_step(at, factor, blocks, gain, weights, state, head_size=None):
    streams, count = len(blocks), len(blocks[0])
    rows, width = blocks[0][0].shape
    groups, depth, out_width = weights.shape
    if head_size is None:
        shapes, kinds = [(rows, groups * out_width), (rows, 128)], [F32, F32]
    else:
        shapes, kinds = [(rows, out_width), (rows, 2 * out_width)], [BF16, BF16]
    operands = []
    for stream in range(streams):
        operands += blocks[stream]
        operands += state[stream] if state else ()
    result = pl.pallas_call(
        functools.partial(gather_kernel, streams, count, bool(state), head_size),
        out_shape=tuple(jax.ShapeDtypeStruct(s, k) for s, k in zip(shapes, kinds)) * streams,
        in_specs=[SMEM, SMEM, VMEM, pl.BlockSpec(memory_space=pltpu.HBM)] + [VMEM] * len(operands),
        out_specs=(VMEM,) * (2 * streams),
        scratch_shapes=[
            pltpu.VMEM((count, groups, width, out_width), BF16),
            pltpu.SemaphoreType.DMA((count,)),
        ],
        compiler_params=pltpu.CompilerParams(vmem_limit_bytes=16 << 20),
        cost_estimate=pl.CostEstimate(
            flops=2 * streams * rows * width * count * groups * out_width,
            bytes_accessed=2 * width * count * (streams * rows + groups * out_width)
            + 8 * streams * rows * groups * out_width,
            transcendentals=0,
        ),
        name="gather_step" if head_size is None else "gather_last",
    )(at, factor, gain, weights, *operands)
    return [result[2 * s : 2 * s + 2] for s in range(streams)]


def attend_blocks(sources, ids, q_first, q_refs, id_col, id_row, kv_refs, v_ones, acc, head_size):
    heads = q_refs[0].shape[1] // head_size
    keys = kv_refs[0].shape[0]
    rows = q_refs[0].shape[0]
    for number, kv_ref in enumerate(kv_refs):
        for head in range(heads):
            start = (heads + head) * head_size
            v_ones[head, :, :head_size] = kv_ref[:, start : start + head_size]
            v_ones[head, :, head_size:] = jnp.ones((keys, head_size), BF16)
        first = sources[number]
        key_low, key_high = ids[first], ids[first + keys - 1]
        tile = math.gcd(rows, 256)
        for chunk, q_ref in enumerate(q_refs):

            @pl.loop(0, rows // tile)
            def _(index):
                here = pl.ds(pl.multiple_of(index * tile, tile), tile)
                base = chunk * rows + index * tile
                there = pl.ds(pl.multiple_of(base, tile), tile)
                q_low = ids[q_first + base]
                q_high = ids[q_first + base + tile - 1]

                def add(masked):
                    if masked:
                        allowed = id_row[first // keys] <= id_col[there, :]
                    for head in range(heads):
                        lanes = slice(head * head_size, (head + 1) * head_size)
                        score = lax.dot_general(
                            q_ref[here, lanes],
                            kv_ref[:, lanes],
                            (((1,), (1,)), ((), ())),
                            preferred_element_type=F32,
                        )
                        weight = jnp.exp2(score)
                        if masked:
                            weight = jnp.where(allowed, weight, 0.0)
                        wide = slice(2 * head * head_size, 2 * (head + 1) * head_size)
                        acc[there, wide] += jnp.dot(
                            weight.astype(BF16), v_ones[head], preferred_element_type=F32
                        )

                @pl.when(key_high <= q_low)
                def _():
                    add(False)

                @pl.when((key_high > q_low) & (key_low <= q_high))
                def _():
                    add(True)


def attend_kernel(count_q, count_kv, head_size, has_acc, count_out, info, ids, *refs):
    q_refs, rest = refs[:count_q], refs[count_q:]
    (id_col, id_row), rest = rest[:2], rest[2:]
    kv_refs, rest = rest[:count_kv], rest[count_kv:]
    rows, width = q_refs[0].shape
    if has_acc:
        acc_in, rest = rest[0], rest[1:]
    if count_out:
        w_ref, outs, (v_ones, acc, attended) = rest[0], rest[1:-3], rest[-3:]
    else:
        accs, (v_ones, acc) = rest[:-2], rest[-2:]
    acc[...] = acc_in[...] if has_acc else jnp.zeros_like(acc)
    sources = [info[number] for number in range(count_kv)]
    attend_blocks(
        sources, ids, info[count_kv], q_refs, id_col, id_row, kv_refs, v_ones, acc, head_size
    )
    if not count_out:
        for number, out in enumerate(accs):
            out[...] = acc[number * rows : (number + 1) * rows, :]
        return
    for head in range(width // head_size):
        start = 2 * head * head_size
        attended[:, head * head_size : (head + 1) * head_size] = (
            acc[:, start : start + head_size]
            / acc[:, start + head_size : start + 2 * head_size]
        ).astype(BF16)
    out_width = outs[0].shape[1]
    for number, out in enumerate(outs):
        lane = info[count_kv + 1 + number] * out_width
        out[...] = jnp.dot(
            attended[...],
            w_ref[:, pl.ds(pl.multiple_of(lane, out_width), out_width)],
            preferred_element_type=F32,
        ).astype(BF16)


def attend(info, ids, queries, id_col, id_row, kvs, head_size, acc=None, w_out=None, count_out=0):
    rows, width = queries[0].shape
    total = rows * len(queries)
    keys = kvs[0].shape[0]
    heads = width // head_size
    scratch = [
        pltpu.VMEM((heads, keys, 2 * head_size), BF16),
        pltpu.VMEM((total, 2 * width), F32),
    ]
    operands = [*queries, id_col, id_row, *kvs]
    if acc is not None:
        operands.append(acc)
    if count_out:
        operands.append(w_out)
        scratch.append(pltpu.VMEM((total, width), BF16))
        shape = jax.ShapeDtypeStruct((total, w_out.shape[1] // count_out), BF16)
    else:
        shape = jax.ShapeDtypeStruct((rows, 2 * width), F32)
    outs = count_out or len(queries)
    return pl.pallas_call(
        functools.partial(
            attend_kernel, len(queries), len(kvs), head_size, acc is not None, count_out
        ),
        out_shape=(shape,) * outs,
        in_specs=[SMEM, SMEM] + [VMEM] * len(operands),
        out_specs=(VMEM,) * outs,
        scratch_shapes=scratch,
        compiler_params=pltpu.CompilerParams(
            vmem_limit_bytes=(16 << 20) + 2 * kvs[0].size * 2 * len(kvs)
        ),
        cost_estimate=pl.CostEstimate(
            flops=6 * total * keys * len(kvs) * width + 2 * total * width * width * count_out,
            bytes_accessed=4 * keys * len(kvs) * width + 8 * total * width,
            transcendentals=total * keys * len(kvs) * heads,
        ),
        name="attend_last" if count_out else "attend",
    )(info, ids, *operands)


def total_of(*parts):
    return sum(part.astype(F32) for part in parts).astype(BF16)


def body(mesh_shape, tokens, norm_gain, w_qkv, head_scale, w_out, scale_ids):
    ring = mesh_shape["head"]
    outer = mesh_shape["seq"] // 2
    rows, width = tokens.shape
    half = rows // 2
    head_size = w_qkv.shape[2] // head_scale.shape[0]
    head_at, seq_at = lax.axis_index("head"), lax.axis_index("seq")
    place = ring_place(head_at, ring)
    chip, core = seq_at // 2, seq_at % 2
    index_at = lambda offset: ring_index((place + offset + ring) % ring, ring)
    numbers = lambda values: jnp.stack(values).astype(jnp.int32)

    streams = (0, 1)
    farthest = ring // 2
    reach = [(farthest, farthest - 1), (farthest - 1, farthest)]
    id_row = scale_ids.reshape(-1, 1, half)
    id_col = lax.dynamic_slice_in_dim(scale_ids, seq_at * rows, rows)[:, None]

    gain = norm_gain.reshape(ring, width)
    held = [[tokens[s * half : (s + 1) * half]] * 2 for s in streams]
    waiting, offsets, state = [[held[s][0]] for s in streams], [0], None
    for step in range(1, farthest + 1):
        for s in streams:
            for way, sign in enumerate((1, -1)):
                if step <= reach[s][way]:
                    held[s][way] = along(held[s][way], sign, ring)
        if 2 < step and state is not None:
            held, state = lax.optimization_barrier((held, state))
        for s in streams:
            waiting[s] += [held[s][way] for way in (0, 1) if step <= reach[s][way]]
        offsets += [-step, step] if step < farthest else [-step]
        if step < farthest - 1:
            at = numbers([index_at(offset) for offset in offsets])
            state = gather_step(at, head_scale, waiting, gain, w_qkv, state)
            waiting, offsets = [[] for s in streams], []
    at = numbers([index_at(offset) for offset in offsets])
    query, kv = [], []
    for s in streams:
        ((q, k_v),) = gather_step(
            at, head_scale, waiting[s : s + 1], gain, w_qkv, state[s : s + 1], head_size
        )
        query.append(q)
        kv.append(k_v)

    swap = [(2 * a + b, 2 * a + 1 - b) for a in range(outer) for b in (0, 1)]
    near, near_at, far, far_at = [], [], [], []
    for s in streams:
        for step in range(outer):
            source = 2 * ((chip + outer - step) % outer)
            places = [(source + core) * rows + s * half, (source + 1 - core) * rows + s * half]
            if step:
                shift = [
                    (2 * a + b, 2 * ((a + step) % outer) + b) for a in range(outer) for b in (0, 1)
                ]
                far.append(lax.ppermute(kv[s], "seq", shift))
                far_at += places
            else:
                near += [kv[s], lax.ppermute(kv[s], "seq", swap)]
                near_at += places
    near_info = numbers(near_at + [seq_at * rows])
    accs = attend(near_info, scale_ids, query, id_col, id_row, near, head_size)
    accs, far = lax.optimization_barrier((accs, far))
    far = [data for block in far for data in (block, lax.ppermute(block, "seq", swap))]

    parts, goals = [], []
    for s in streams:
        up, down = reach[s]
        goals = list(range(up, 0, -1)) + list(range(-down, 0)) + [0]
        info = numbers(far_at + [seq_at * rows + s * half] + [index_at(goal) for goal in goals])
        parts.append(
            attend(
                info, scale_ids, [query[s]], id_col[s * half : (s + 1) * half], id_row, far,
                head_size, accs[s], w_out, ring,
            )
        )
    sums = [[None, None] for s in streams]
    for step in range(farthest, 0, -1):
        for s in streams:
            for way, sign in enumerate((1, -1)):
                if step <= reach[s][way]:
                    first = 0 if way == 0 else reach[s][0]
                    part = parts[s][first + reach[s][way] - step]
                    if sums[s][way] is not None:
                        part = total_of(part, sums[s][way])
                    sums[s][way] = along(part, sign, ring)
    return jnp.concatenate([total_of(parts[s][-1], *sums[s]) for s in streams])


def solution(mesh):
    placed = (P("seq", "head"), P(), P(None, None, "head"), P("head"), P("head", None), P())
    return jax.shard_map(
        functools.partial(body, dict(mesh.shape)),
        mesh=mesh,
        in_specs=placed,
        out_specs=P("seq", "head"),
        check_vma=False,
    )
```

```python
import functools
import math

import jax
import jax.numpy as jnp
from jax import lax
from jax.experimental import pallas as pl
from jax.experimental.pallas import tpu as pltpu
from jax.sharding import PartitionSpec as P

LOG2E = math.log2(math.e)
VMEM = pl.BlockSpec(memory_space=pltpu.VMEM)
SMEM = pl.BlockSpec(memory_space=pltpu.SMEM)
F32 = jnp.float32
BF16 = jnp.bfloat16


def ring_order(count):
    line = count // 2
    return [2 * z for z in range(line)] + [2 * z + 1 for z in reversed(range(line))]


def ring_place(index, count):
    return jnp.where(index % 2 == 0, index // 2, count - 1 - index // 2)


def ring_index(place, count):
    return jnp.where(place < count // 2, 2 * place, 2 * (count - 1 - place) + 1)


def along(value, seq_count, count, start_lane=0, end_lane=0):
    order = ring_order(count)
    pairs = []
    for seq in range(seq_count):
        core = seq % 2
        lane = core if start_lane == 0 else 1 - core
        goal = seq - core + (lane if end_lane == 0 else 1 - lane)
        step = 1 - 2 * lane
        for p in range(count):
            pairs.append((seq * count + order[p], goal * count + order[(p + step) % count]))
    return lax.ppermute(value, ("seq", "head"), pairs)


def swapped(value, seq_count):
    return lax.ppermute(value, "seq", [(seq, seq + 1 - 2 * (seq % 2)) for seq in range(seq_count)])


def gather_kernel(count, has_state, head_size, at, factor, gain_ref, w_hbm, *refs):
    blocks, refs = refs[:count], refs[count:]
    if has_state:
        (acc_in, power_in), refs = refs[:2], refs[2:]
    outs, (w_ref, sems) = refs[:-2], refs[-2:]
    rows, width = blocks[0].shape
    groups, out_width = w_hbm.shape[0], w_hbm.shape[2]

    def fetch(n):
        start = pl.multiple_of(at[n] * width, width)
        return pltpu.make_async_copy(w_hbm.at[:, pl.ds(start, width), :], w_ref.at[n], sems.at[n])

    for n in range(count):
        fetch(n).start()
    for n in range(count):
        fetch(n).wait()
    tile = math.gcd(rows, 128)

    def step(index, out_at, store):
        here = pl.ds(pl.multiple_of(index * tile, tile), tile)
        power = power_in[here, :] if has_state else None
        scaled = []
        for n, block in enumerate(blocks):
            values = block[here, :].astype(F32)
            scaled.append((values * gain_ref[pl.ds(at[n], 1), :]).astype(BF16))
            square = values * values
            for lane in range(0, width, 128):
                piece = square[:, lane : lane + 128]
                power = piece if power is None else power + piece
        sums = []
        for group in range(groups):
            lanes = slice(group * out_width, (group + 1) * out_width)
            total = acc_in[here, lanes] if has_state else None
            for n, x in enumerate(scaled):
                product = jnp.dot(x, w_ref[n, group], preferred_element_type=F32)
                total = product if total is None else total + product
            sums.append(total)
        store(here, out_at, sums, power)

    if head_size is None:
        acc, power_out = outs

        def keep(here, out_at, sums, power):
            for group, total in enumerate(sums):
                acc[here, group * out_width : (group + 1) * out_width] = total
            power_out[here, :] = power

        pl.loop(0, rows // tile)(lambda index: step(index, None, keep))
        return

    q_ref, kv_refs = outs[0], outs[1:]
    per = kv_refs[0].shape[0] // tile
    for number, kv_ref in enumerate(kv_refs):

        def finish(here, there, sums, power):
            mean = jnp.sum(power, axis=-1, keepdims=True) * (1.0 / w_hbm.shape[1])
            scale = lax.rsqrt(mean + 1e-06)
            q, k, v = (total * scale for total in sums)
            for head in range(out_width // head_size):
                lanes = slice(head * head_size, (head + 1) * head_size)
                qh, kh = q[:, lanes], k[:, lanes]
                q_size = lax.rsqrt(jnp.sum(qh * qh, axis=-1, keepdims=True) + 1e-06)
                k_size = lax.rsqrt(jnp.sum(kh * kh, axis=-1, keepdims=True) + 1e-06)
                q_ref[here, lanes] = (qh * (q_size * (factor[head] * LOG2E))).astype(BF16)
                kv_ref[there, lanes] = (kh * k_size).astype(BF16)
            kv_ref[there, out_width:] = v.astype(BF16)

        @pl.loop(0, per)
        def _(index):
            there = pl.ds(pl.multiple_of(index * tile, tile), tile)
            step(number * per + index, there, finish)


def gather_step(at, factor, blocks, gain, weights, state, head_size=None):
    count = len(blocks)
    rows, width = blocks[0].shape
    groups, depth, out_width = weights.shape
    if head_size is None:
        shapes, kinds = [(rows, groups * out_width), (rows, 128)], [F32, F32]
    else:
        shapes = [(rows, out_width), (rows // 2, 2 * out_width), (rows // 2, 2 * out_width)]
        kinds = [BF16, BF16, BF16]
    operands = [*blocks, *(state or ())]
    return pl.pallas_call(
        functools.partial(gather_kernel, count, bool(state), head_size),
        out_shape=tuple(jax.ShapeDtypeStruct(s, k) for s, k in zip(shapes, kinds)),
        in_specs=[SMEM, SMEM, VMEM, pl.BlockSpec(memory_space=pltpu.HBM)] + [VMEM] * len(operands),
        out_specs=(VMEM,) * len(shapes),
        scratch_shapes=[
            pltpu.VMEM((count, groups, width, out_width), BF16),
            pltpu.SemaphoreType.DMA((count,)),
        ],
        compiler_params=pltpu.CompilerParams(vmem_limit_bytes=16 << 20),
        cost_estimate=pl.CostEstimate(
            flops=2 * rows * width * count * groups * out_width,
            bytes_accessed=2 * width * count * (rows + groups * out_width)
            + 8 * rows * groups * out_width,
            transcendentals=0,
        ),
        name="gather_step" if head_size is None else "gather_last",
    )(at, factor, gain, weights, *operands)


def attend_blocks(sources, ids, q_first, q_refs, id_col, id_row, kv_refs, v_ones, acc, head_size):
    heads = q_refs[0].shape[1] // head_size
    keys = kv_refs[0].shape[0]
    rows = q_refs[0].shape[0]
    for number, kv_ref in enumerate(kv_refs):
        for head in range(heads):
            start = (heads + head) * head_size
            v_ones[head, :, :head_size] = kv_ref[:, start : start + head_size]
            v_ones[head, :, head_size:] = jnp.ones((keys, head_size), BF16)
        first = sources[number]
        key_low, key_high = ids[first], ids[first + keys - 1]
        tile = math.gcd(rows, 256)
        for chunk, q_ref in enumerate(q_refs):

            @pl.loop(0, rows // tile)
            def _(index):
                here = pl.ds(pl.multiple_of(index * tile, tile), tile)
                base = chunk * rows + index * tile
                there = pl.ds(pl.multiple_of(base, tile), tile)
                q_low = ids[q_first + base]
                q_high = ids[q_first + base + tile - 1]

                def add(masked):
                    if masked:
                        allowed = id_row[first // keys] <= id_col[there, :]
                    for head in range(heads):
                        lanes = slice(head * head_size, (head + 1) * head_size)
                        score = lax.dot_general(
                            q_ref[here, lanes],
                            kv_ref[:, lanes],
                            (((1,), (1,)), ((), ())),
                            preferred_element_type=F32,
                        )
                        weight = jnp.exp2(score)
                        if masked:
                            weight = jnp.where(allowed, weight, 0.0)
                        wide = slice(2 * head * head_size, 2 * (head + 1) * head_size)
                        acc[there, wide] += jnp.dot(
                            weight.astype(BF16), v_ones[head], preferred_element_type=F32
                        )

                @pl.when(key_high <= q_low)
                def _():
                    add(False)

                @pl.when((key_high > q_low) & (key_low <= q_high))
                def _():
                    add(True)


def attend_kernel(count_q, count_kv, head_size, has_acc, count_out, info, ids, *refs):
    q_refs, rest = refs[:count_q], refs[count_q:]
    (id_col, id_row), rest = rest[:2], rest[2:]
    kv_refs, rest = rest[:count_kv], rest[count_kv:]
    rows, width = q_refs[0].shape
    if has_acc:
        acc_in, rest = rest[0], rest[1:]
    if count_out:
        w_ref, outs, (v_ones, acc, attended) = rest[0], rest[1:-3], rest[-3:]
    else:
        accs, (v_ones, acc) = rest[:-2], rest[-2:]
    acc[...] = acc_in[...] if has_acc else jnp.zeros_like(acc)
    sources = [info[number] for number in range(count_kv)]
    attend_blocks(
        sources, ids, info[count_kv], q_refs, id_col, id_row, kv_refs, v_ones, acc, head_size
    )
    if not count_out:
        for number, out in enumerate(accs):
            out[...] = acc[number * rows : (number + 1) * rows, :]
        return
    for head in range(width // head_size):
        start = 2 * head * head_size
        attended[:, head * head_size : (head + 1) * head_size] = (
            acc[:, start : start + head_size]
            / acc[:, start + head_size : start + 2 * head_size]
        ).astype(BF16)
    out_width = outs[0].shape[1]
    for number, out in enumerate(outs):
        lane = info[count_kv + 1 + number] * out_width
        out[...] = jnp.dot(
            attended[...],
            w_ref[:, pl.ds(pl.multiple_of(lane, out_width), out_width)],
            preferred_element_type=F32,
        ).astype(BF16)


def attend(info, ids, queries, id_col, id_row, kvs, head_size, acc=None, w_out=None, count_out=0):
    rows, width = queries[0].shape
    total = rows * len(queries)
    keys = kvs[0].shape[0]
    heads = width // head_size
    scratch = [
        pltpu.VMEM((heads, keys, 2 * head_size), BF16),
        pltpu.VMEM((total, 2 * width), F32),
    ]
    operands = [*queries, id_col, id_row, *kvs]
    if acc is not None:
        operands.append(acc)
    if count_out:
        operands.append(w_out)
        scratch.append(pltpu.VMEM((total, width), BF16))
        shape = jax.ShapeDtypeStruct((total, w_out.shape[1] // count_out), BF16)
    else:
        shape = jax.ShapeDtypeStruct((rows, 2 * width), F32)
    outs = count_out or len(queries)
    return pl.pallas_call(
        functools.partial(
            attend_kernel, len(queries), len(kvs), head_size, acc is not None, count_out
        ),
        out_shape=(shape,) * outs,
        in_specs=[SMEM, SMEM] + [VMEM] * len(operands),
        out_specs=(VMEM,) * outs,
        scratch_shapes=scratch,
        compiler_params=pltpu.CompilerParams(
            vmem_limit_bytes=(16 << 20) + 2 * kvs[0].size * 2 * len(kvs)
        ),
        cost_estimate=pl.CostEstimate(
            flops=6 * total * keys * len(kvs) * width + 2 * total * width * width * count_out,
            bytes_accessed=4 * keys * len(kvs) * width + 8 * total * width,
            transcendentals=total * keys * len(kvs) * heads,
        ),
        name="attend_last" if count_out else "attend",
    )(info, ids, *operands)


def total_of(*parts):
    return sum(part.astype(F32) for part in parts).astype(BF16)


def body(mesh_shape, tokens, norm_gain, w_qkv, head_scale, w_out, scale_ids):
    ring, seqs = mesh_shape["head"], mesh_shape["seq"]
    outer = seqs // 2
    rows, width = tokens.shape
    half = rows // 2
    head_size = w_qkv.shape[2] // head_scale.shape[0]
    head_at, seq_at = lax.axis_index("head"), lax.axis_index("seq")
    place = ring_place(head_at, ring)
    chip, core = seq_at // 2, seq_at % 2
    toward = 1 - 2 * core
    index_at = lambda offset: ring_index((place + toward * offset + ring) % ring, ring)
    numbers = lambda values: jnp.stack(values).astype(jnp.int32)
    id_row = scale_ids.reshape(-1, 1, half)
    id_col = lax.dynamic_slice_in_dim(scale_ids, seq_at * rows, rows)[:, None]

    farthest = ring // 2
    gain = norm_gain.reshape(ring, width)
    own = other = tokens
    waiting, offsets, state = [tokens], [0], None
    for step in range(1, farthest):
        own = along(own, seqs, ring)
        other = along(other, seqs, ring, start_lane=int(step == 1))
        if state is not None:
            own, other, state = lax.optimization_barrier((own, other, state))
        waiting += [own, swapped(other, seqs)]
        offsets += [-step, step]
        if step < farthest - 1:
            at = numbers([index_at(offset) for offset in offsets])
            state = gather_step(at, head_scale, waiting, gain, w_qkv, state)
            waiting, offsets = [], []
    waiting.append(along(own, seqs, ring))
    offsets.append(-farthest)
    at = numbers([index_at(offset) for offset in offsets])
    query, *kvs = gather_step(at, head_scale, waiting, gain, w_qkv, state, head_size)

    near, near_at = [], []
    far, far_at = [[] for kv in kvs], [[] for kv in kvs]
    for s, kv in enumerate(kvs):
        for step in range(outer):
            source = 2 * ((chip + outer - step) % outer)
            places = [(source + core) * rows + s * half, (source + 1 - core) * rows + s * half]
            if step:
                shift = [
                    (2 * a + b, 2 * ((a + step) % outer) + b) for a in range(outer) for b in (0, 1)
                ]
                far[s].append(lax.ppermute(kv, "seq", shift))
                far_at[s] += places
            else:
                near += [kv, swapped(kv, seqs)]
                near_at += places
    first = [seq_at * rows]
    (acc,) = attend(numbers(near_at + first), scale_ids, [query], id_col, id_row, near, head_size)
    goals = list(range(farthest, -farthest, -1))
    for s in range(len(kvs)):
        acc, far[s] = lax.optimization_barrier((acc, far[s]))
        blocks = [data for block in far[s] for data in (block, swapped(block, seqs))]
        if s + 1 < len(kvs):
            (acc,) = attend(
                numbers(far_at[s] + first), scale_ids, [query], id_col, id_row, blocks, head_size,
                acc,
            )
    info = numbers(far_at[-1] + first + [index_at(goal) for goal in goals])
    parts = attend(
        info, scale_ids, [query], id_col, id_row, blocks, head_size, acc, w_out, ring
    )
    parts = dict(zip(goals, parts))
    own = along(parts[farthest], seqs, ring)
    other = along(parts[1 - farthest], seqs, ring, start_lane=1)
    for step in range(farthest - 1, 0, -1):
        own = along(total_of(parts[step], own), seqs, ring)
        if step > 1:
            part = swapped(parts[1 - step], seqs)
            other = along(total_of(part, other), seqs, ring, end_lane=int(step == 2))
    return total_of(parts[0], own, other)


def solution(mesh):
    placed = (P("seq", "head"), P(), P(None, None, "head"), P("head"), P("head", None), P())
    return jax.shard_map(
        functools.partial(body, dict(mesh.shape)),
        mesh=mesh,
        in_specs=placed,
        out_specs=P("seq", "head"),
        check_vma=False,
    )
```

```python
import functools
import math

import jax
import jax.numpy as jnp
from jax import lax
from jax.experimental import pallas as pl
from jax.experimental.pallas import tpu as pltpu
from jax.sharding import PartitionSpec as P

LOG2E = math.log2(math.e)
VMEM = pl.BlockSpec(memory_space=pltpu.VMEM)
SMEM = pl.BlockSpec(memory_space=pltpu.SMEM)
F32 = jnp.float32
BF16 = jnp.bfloat16


def ring_order(count):
    line = count // 2
    return [2 * z for z in range(line)] + [2 * z + 1 for z in reversed(range(line))]


def ring_place(index, count):
    return jnp.where(index % 2 == 0, index // 2, count - 1 - index // 2)


def ring_index(place, count):
    return jnp.where(place < count // 2, 2 * place, 2 * (count - 1 - place) + 1)


def along(value, seq_count, count, start_lane=0, end_lane=0):
    order = ring_order(count)
    pairs = []
    for seq in range(seq_count):
        core = seq % 2
        lane = core if start_lane == 0 else 1 - core
        goal = seq - core + (lane if end_lane == 0 else 1 - lane)
        step = 1 - 2 * lane
        for p in range(count):
            pairs.append((seq * count + order[p], goal * count + order[(p + step) % count]))
    return lax.ppermute(value, ("seq", "head"), pairs)


def swapped(value, seq_count):
    return lax.ppermute(value, "seq", [(seq, seq + 1 - 2 * (seq % 2)) for seq in range(seq_count)])


def gather_kernel(count, has_state, head_size, at, factor, gain_ref, w_hbm, *refs):
    blocks, refs = refs[:count], refs[count:]
    if has_state:
        (acc_in, power_in), refs = refs[:2], refs[2:]
    outs, (w_ref, sems) = refs[:-2], refs[-2:]
    rows, width = blocks[0].shape
    groups, out_width = w_hbm.shape[0], w_hbm.shape[2]

    def fetch(n):
        start = pl.multiple_of(at[n] * width, width)
        return pltpu.make_async_copy(w_hbm.at[:, pl.ds(start, width), :], w_ref.at[n], sems.at[n])

    for n in range(count):
        fetch(n).start()
    for n in range(count):
        fetch(n).wait()
    tile = math.gcd(rows, 128)

    def step(index, store):
        here = pl.ds(pl.multiple_of(index * tile, tile), tile)
        power = power_in[here, :] if has_state else None
        scaled = []
        for n, block in enumerate(blocks):
            values = block[here, :].astype(F32)
            scaled.append((values * gain_ref[pl.ds(at[n], 1), :]).astype(BF16))
            square = values * values
            for lane in range(0, width, 128):
                piece = square[:, lane : lane + 128]
                power = piece if power is None else power + piece
        sums = []
        for group in range(groups):
            lanes = slice(group * out_width, (group + 1) * out_width)
            total = acc_in[here, lanes] if has_state else None
            for n, x in enumerate(scaled):
                product = jnp.dot(x, w_ref[n, group], preferred_element_type=F32)
                total = product if total is None else total + product
            sums.append(total)
        store(here, sums, power)

    if head_size is None:
        acc, power_out = outs

        def keep(here, sums, power):
            for group, total in enumerate(sums):
                acc[here, group * out_width : (group + 1) * out_width] = total
            power_out[here, :] = power

        pl.loop(0, rows // tile)(lambda index: step(index, keep))
        return

    q_ref, kv_ref = outs

    def finish(here, sums, power):
        mean = jnp.sum(power, axis=-1, keepdims=True) * (1.0 / w_hbm.shape[1])
        scale = lax.rsqrt(mean + 1e-06)
        q, k, v = (total * scale for total in sums)
        for head in range(out_width // head_size):
            lanes = slice(head * head_size, (head + 1) * head_size)
            qh, kh = q[:, lanes], k[:, lanes]
            q_size = lax.rsqrt(jnp.sum(qh * qh, axis=-1, keepdims=True) + 1e-06)
            k_size = lax.rsqrt(jnp.sum(kh * kh, axis=-1, keepdims=True) + 1e-06)
            q_ref[here, lanes] = (qh * (q_size * (factor[head] * LOG2E))).astype(BF16)
            kv_ref[here, lanes] = (kh * k_size).astype(BF16)
        kv_ref[here, out_width:] = v.astype(BF16)

    pl.loop(0, rows // tile)(lambda index: step(index, finish))


def in_hbm(value):
    return pltpu.with_memory_space_constraint(value, pltpu.HBM)


def in_vmem(value):
    return pltpu.with_memory_space_constraint(value, pltpu.VMEM)


def gather_step(at, factor, blocks, gain, weights, state, head_size=None):
    count = len(blocks)
    rows, width = blocks[0].shape
    groups, depth, out_width = weights.shape
    if head_size is None:
        shapes, kinds = [(rows, groups * out_width), (rows, 128)], [F32, F32]
    else:
        shapes, kinds = [(rows, out_width), (rows, 2 * out_width)], [BF16, BF16]
    operands = [*blocks, *map(in_vmem, state or ())]
    return pl.pallas_call(
        functools.partial(gather_kernel, count, bool(state), head_size),
        out_shape=tuple(pltpu.VMEM(s, k) for s, k in zip(shapes, kinds)),
        in_specs=[SMEM, SMEM, VMEM, pl.BlockSpec(memory_space=pltpu.HBM)] + [VMEM] * len(operands),
        out_specs=(VMEM,) * len(shapes),
        scratch_shapes=[
            pltpu.VMEM((count, groups, width, out_width), BF16),
            pltpu.SemaphoreType.DMA((count,)),
        ],
        compiler_params=pltpu.CompilerParams(vmem_limit_bytes=16 << 20),
        cost_estimate=pl.CostEstimate(
            flops=2 * rows * width * count * groups * out_width,
            bytes_accessed=2 * width * count * (rows + groups * out_width)
            + 8 * rows * groups * out_width,
            transcendentals=0,
        ),
        name="gather_step" if head_size is None else "gather_last",
    )(at, in_hbm(factor), in_hbm(gain), in_hbm(weights), *operands)


def attend_blocks(sources, ids, q_first, q_refs, id_col, id_row, kv_refs, v_ones, acc, head_size):
    heads = q_refs[0].shape[1] // head_size
    keys = kv_refs[0].shape[0]
    rows = q_refs[0].shape[0]
    for number, kv_ref in enumerate(kv_refs):
        for head in range(heads):
            start = (heads + head) * head_size
            v_ones[head, :, :head_size] = kv_ref[:, start : start + head_size]
            v_ones[head, :, head_size:] = jnp.ones((keys, head_size), BF16)
        first = sources[number]
        key_low, key_high = ids[first], ids[first + keys - 1]
        tile = math.gcd(rows, 256)
        for chunk, q_ref in enumerate(q_refs):

            @pl.loop(0, rows // tile)
            def _(index):
                here = pl.ds(pl.multiple_of(index * tile, tile), tile)
                base = chunk * rows + index * tile
                there = pl.ds(pl.multiple_of(base, tile), tile)
                q_low = ids[q_first + base]
                q_high = ids[q_first + base + tile - 1]

                def add(masked):
                    if masked:
                        allowed = id_row[first // keys] <= id_col[there, :]
                    for head in range(heads):
                        lanes = slice(head * head_size, (head + 1) * head_size)
                        score = lax.dot_general(
                            q_ref[here, lanes],
                            kv_ref[:, lanes],
                            (((1,), (1,)), ((), ())),
                            preferred_element_type=F32,
                        )
                        weight = jnp.exp2(score)
                        if masked:
                            weight = jnp.where(allowed, weight, 0.0)
                        wide = slice(2 * head * head_size, 2 * (head + 1) * head_size)
                        acc[there, wide] += jnp.dot(
                            weight.astype(BF16), v_ones[head], preferred_element_type=F32
                        )

                @pl.when(key_high <= q_low)
                def _():
                    add(False)

                @pl.when((key_high > q_low) & (key_low <= q_high))
                def _():
                    add(True)


def attend_kernel(count_q, count_kv, head_size, has_acc, count_out, info, ids, *refs):
    q_refs, rest = refs[:count_q], refs[count_q:]
    (id_col, id_row), rest = rest[:2], rest[2:]
    kv_refs, rest = rest[:count_kv], rest[count_kv:]
    rows, width = q_refs[0].shape
    if has_acc:
        acc_in, rest = rest[0], rest[1:]
    if count_out:
        w_ref, outs, (v_ones, acc, attended) = rest[0], rest[1:-3], rest[-3:]
    else:
        accs, (v_ones, acc) = rest[:-2], rest[-2:]
    acc[...] = acc_in[...] if has_acc else jnp.zeros_like(acc)
    sources = [info[number] for number in range(count_kv)]
    attend_blocks(
        sources, ids, info[count_kv], q_refs, id_col, id_row, kv_refs, v_ones, acc, head_size
    )
    if not count_out:
        for number, out in enumerate(accs):
            out[...] = acc[number * rows : (number + 1) * rows, :]
        return
    for head in range(width // head_size):
        start = 2 * head * head_size
        attended[:, head * head_size : (head + 1) * head_size] = (
            acc[:, start : start + head_size]
            / acc[:, start + head_size : start + 2 * head_size]
        ).astype(BF16)
    out_width = outs[0].shape[1]
    for number, out in enumerate(outs):
        lane = info[count_kv + 1 + number] * out_width
        out[...] = jnp.dot(
            attended[...],
            w_ref[:, pl.ds(pl.multiple_of(lane, out_width), out_width)],
            preferred_element_type=F32,
        ).astype(BF16)


def attend(info, ids, queries, id_col, id_row, kvs, head_size, acc=None, w_out=None, count_out=0):
    rows, width = queries[0].shape
    total = rows * len(queries)
    keys = kvs[0].shape[0]
    heads = width // head_size
    scratch = [
        pltpu.VMEM((heads, keys, 2 * head_size), BF16),
        pltpu.VMEM((total, 2 * width), F32),
    ]
    operands = [*map(in_vmem, queries), id_col, in_hbm(id_row), *map(in_vmem, kvs)]
    if acc is not None:
        operands.append(in_vmem(acc))
    if count_out:
        operands.append(in_hbm(w_out))
        scratch.append(pltpu.VMEM((total, width), BF16))
        shape = pltpu.VMEM((total, w_out.shape[1] // count_out), BF16)
    else:
        shape = pltpu.VMEM((rows, 2 * width), F32)
    outs = count_out or len(queries)
    return pl.pallas_call(
        functools.partial(
            attend_kernel, len(queries), len(kvs), head_size, acc is not None, count_out
        ),
        out_shape=(shape,) * outs,
        in_specs=[SMEM, SMEM] + [VMEM] * len(operands),
        out_specs=(VMEM,) * outs,
        scratch_shapes=scratch,
        compiler_params=pltpu.CompilerParams(
            vmem_limit_bytes=(16 << 20) + 2 * kvs[0].size * 2 * len(kvs)
        ),
        cost_estimate=pl.CostEstimate(
            flops=6 * total * keys * len(kvs) * width + 2 * total * width * width * count_out,
            bytes_accessed=4 * keys * len(kvs) * width + 8 * total * width,
            transcendentals=total * keys * len(kvs) * heads,
        ),
        name="attend_last" if count_out else "attend",
    )(info, in_hbm(ids), *operands)


def total_of(*parts):
    return sum(part.astype(F32) for part in parts).astype(BF16)


def body(mesh_shape, tokens, norm_gain, w_qkv, head_scale, w_out, scale_ids):
    ring, seqs = mesh_shape["head"], mesh_shape["seq"]
    outer = seqs // 2
    rows, width = tokens.shape
    head_size = w_qkv.shape[2] // head_scale.shape[0]
    head_at, seq_at = lax.axis_index("head"), lax.axis_index("seq")
    place = ring_place(head_at, ring)
    chip, core = seq_at // 2, seq_at % 2
    toward = 1 - 2 * core
    index_at = lambda offset: ring_index((place + toward * offset + ring) % ring, ring)
    numbers = lambda values: jnp.stack(values).astype(jnp.int32)
    id_row = scale_ids.reshape(-1, 1, rows)
    id_col = lax.dynamic_slice_in_dim(scale_ids, seq_at * rows, rows)[:, None]

    farthest = ring // 2
    gain = norm_gain.reshape(ring, width)
    own = other = tokens
    waiting, offsets, state = [in_hbm(tokens)], [0], None
    for step in range(1, farthest):
        own = along(own, seqs, ring)
        other = along(other, seqs, ring, start_lane=int(step == 1))
        if state is not None:
            own, other, state = lax.optimization_barrier((own, other, state))
        waiting += [in_vmem(own), in_vmem(swapped(other, seqs))]
        offsets += [-step, step]
        if step < farthest - 1:
            at = numbers([index_at(offset) for offset in offsets])
            state = gather_step(at, head_scale, waiting, gain, w_qkv, state)
            waiting, offsets = [], []
    waiting.append(in_vmem(along(own, seqs, ring)))
    offsets.append(-farthest)
    at = numbers([index_at(offset) for offset in offsets])
    query, kv = gather_step(at, head_scale, waiting, gain, w_qkv, state, head_size)

    far, straight, crossed = [], [], []
    for step in range(outer):
        source = 2 * ((chip + outer - step) % outer)
        straight.append((source + core) * rows)
        crossed.append((source + 1 - core) * rows)
        if step:
            far.append(lax.ppermute(kv, "seq", [
                (2 * a + b, 2 * ((a + step) % outer) + b) for a in range(outer) for b in (0, 1)
            ]))
    first = [seq_at * rows]
    info = numbers(straight[:1] + crossed[:1] + first)
    keys = [kv, swapped(kv, seqs)]
    (acc,) = attend(info, scale_ids, [query], id_col, id_row, keys, head_size)
    acc, far = lax.optimization_barrier((acc, far))
    far_crossed = [swapped(block, seqs) for block in far]
    info = numbers(straight[1:] + first)
    (acc,) = attend(info, scale_ids, [query], id_col, id_row, far, head_size, acc)

    goals = list(range(farthest, -farthest, -1))
    info = numbers(crossed[1:] + first + [index_at(goal) for goal in goals])
    parts = attend(
        info, scale_ids, [query], id_col, id_row, far_crossed, head_size, acc, w_out, ring
    )
    parts = dict(zip(goals, parts))
    own = along(parts[farthest], seqs, ring)
    other = along(parts[1 - farthest], seqs, ring, start_lane=1)
    for step in range(farthest - 1, 0, -1):
        own = along(total_of(parts[step], own), seqs, ring)
        if step > 1:
            part = swapped(parts[1 - step], seqs)
            other = along(total_of(part, other), seqs, ring, end_lane=int(step == 2))
    return total_of(parts[0], own, other)


def solution(mesh):
    placed = (P("seq", "head"), P(), P(None, None, "head"), P("head"), P("head", None), P())
    return jax.shard_map(
        functools.partial(body, dict(mesh.shape)),
        mesh=mesh,
        in_specs=placed,
        out_specs=P("seq", "head"),
        check_vma=False,
    )
```

```python
import functools
import math

import jax
import jax.numpy as jnp
from jax import lax
from jax.experimental import pallas as pl
from jax.experimental.pallas import tpu as pltpu
from jax.sharding import PartitionSpec as P

LOG2E = math.log2(math.e)
VMEM = pl.BlockSpec(memory_space=pltpu.VMEM)
SMEM = pl.BlockSpec(memory_space=pltpu.SMEM)
F32 = jnp.float32
BF16 = jnp.bfloat16


def ring_order(count):
    line = count // 2
    return [2 * z for z in range(line)] + [2 * z + 1 for z in reversed(range(line))]


def ring_place(index, count):
    return jnp.where(index % 2 == 0, index // 2, count - 1 - index // 2)


def ring_index(place, count):
    return jnp.where(place < count // 2, 2 * place, 2 * (count - 1 - place) + 1)


def along(value, step, count):
    order = ring_order(count)
    return lax.ppermute(
        value, "head", [(order[p], order[(p + step) % count]) for p in range(count)]
    )


def swapped(value, seq_count):
    return lax.ppermute(value, "seq", [(seq, seq + 1 - 2 * (seq % 2)) for seq in range(seq_count)])


def in_hbm(value):
    return pltpu.with_memory_space_constraint(value, pltpu.HBM)


def in_vmem(value):
    return pltpu.with_memory_space_constraint(value, pltpu.VMEM)


def fold_kernel(gain_ref, w_hbm, out_ref, sems):
    lanes = gain_ref.shape[1]
    chunks = sems.shape[0]
    size = w_hbm.shape[1] // chunks

    def fetch(n):
        here = (slice(None), pl.ds(n * size, size), slice(None))
        return pltpu.make_async_copy(w_hbm.at[here], out_ref.at[here], sems.at[n])

    for n in range(chunks):
        fetch(n).start()
    columns = jnp.transpose(gain_ref[...])
    for n in range(chunks):
        fetch(n).wait()
        for first in range(n * size, (n + 1) * size, lanes):
            column = columns[:, first // lanes : first // lanes + 1]
            for group in range(w_hbm.shape[0]):
                here = (group, slice(first, first + lanes), slice(None))
                out_ref[here] = (out_ref[here].astype(F32) * column).astype(BF16)


def fold_gain(gain, weights):
    groups, depth, width = weights.shape
    lanes = math.gcd(depth, 128)
    return pl.pallas_call(
        fold_kernel,
        out_shape=pltpu.VMEM(weights.shape, BF16),
        in_specs=[VMEM, pl.BlockSpec(memory_space=pltpu.HBM)],
        out_specs=VMEM,
        scratch_shapes=[pltpu.SemaphoreType.DMA((math.gcd(depth // lanes, 8),))],
        compiler_params=pltpu.CompilerParams(vmem_limit_bytes=16 << 20),
        cost_estimate=pl.CostEstimate(
            flops=weights.size, bytes_accessed=4 * weights.size, transcendentals=0
        ),
        name="fold_gain",
    )(in_hbm(gain.reshape(depth // lanes, lanes)), in_hbm(weights))


def project_kernel(head_size, base, at, factor, tokens_hbm, w_ref, *refs):
    blocks, (q_ref, kv_ref, wide, sem) = refs[:-4], refs[-4:]
    rows, width = blocks[0].shape
    out_width = w_ref.shape[2]

    def lanes_of(n):
        return pl.ds(pl.multiple_of(at[n] * width, width), width)

    own = pltpu.make_async_copy(
        tokens_hbm.at[pl.ds(base, rows), :], wide.at[:, lanes_of(0)], sem
    )
    own.start()
    for n, block in enumerate(blocks):
        wide[:, lanes_of(n + 1)] = block[...]
    own.wait()
    depth = wide.shape[1]
    q = jnp.dot(wide[...], w_ref[0], preferred_element_type=F32)
    k = jnp.dot(wide[...], w_ref[1], preferred_element_type=F32)
    v = jnp.dot(wide[...], w_ref[2], preferred_element_type=F32)
    power = None
    for lane in range(0, depth, 128):
        values = wide[:, lane : lane + 128].astype(F32)
        power = values * values if power is None else power + values * values
    scale = lax.rsqrt(jnp.sum(power, axis=-1, keepdims=True) * (1.0 / depth) + 1e-06)
    q, k, v = q * scale, k * scale, v * scale
    for head in range(out_width // head_size):
        lanes = slice(head * head_size, (head + 1) * head_size)
        qh, kh = q[:, lanes], k[:, lanes]
        q_size = lax.rsqrt(jnp.sum(qh * qh, axis=-1, keepdims=True) + 1e-06)
        k_size = lax.rsqrt(jnp.sum(kh * kh, axis=-1, keepdims=True) + 1e-06)
        q_ref[:, lanes] = (qh * (q_size * (factor[head] * LOG2E))).astype(BF16)
        kv_ref[:, lanes] = (kh * k_size).astype(BF16)
    kv_ref[:, out_width:] = v.astype(BF16)


def project(at, factor, tokens, weights, blocks, base, head_size):
    rows, width = blocks[0].shape
    groups, depth, out_width = weights.shape
    return pl.pallas_call(
        functools.partial(project_kernel, head_size, base),
        out_shape=(pltpu.VMEM((rows, out_width), BF16), pltpu.VMEM((rows, 2 * out_width), BF16)),
        in_specs=[SMEM, SMEM, pl.BlockSpec(memory_space=pltpu.HBM)] + [VMEM] * (1 + len(blocks)),
        out_specs=(VMEM, VMEM),
        scratch_shapes=[pltpu.VMEM((rows, depth), BF16), pltpu.SemaphoreType.DMA(())],
        compiler_params=pltpu.CompilerParams(vmem_limit_bytes=16 << 20),
        cost_estimate=pl.CostEstimate(
            flops=2 * rows * depth * groups * out_width,
            bytes_accessed=2 * depth * (rows + groups * out_width),
            transcendentals=0,
        ),
        name="project",
    )(at, in_hbm(factor), in_hbm(tokens), in_vmem(weights), *map(in_vmem, blocks))


def attend_blocks(sources, ids, q_first, q_refs, id_col, id_row, kv_refs, v_ones, acc, head_size):
    heads = q_refs[0].shape[1] // head_size
    keys = kv_refs[0].shape[0]
    rows = q_refs[0].shape[0]
    for number, kv_ref in enumerate(kv_refs):
        for head in range(heads):
            start = (heads + head) * head_size
            v_ones[head, :, :head_size] = kv_ref[:, start : start + head_size]
            v_ones[head, :, head_size:] = jnp.ones((keys, head_size), BF16)
        first = sources[number]
        key_low, key_high = ids[first], ids[first + keys - 1]
        tile = math.gcd(rows, 256)
        for chunk, q_ref in enumerate(q_refs):

            @pl.loop(0, rows // tile)
            def _(index):
                here = pl.ds(pl.multiple_of(index * tile, tile), tile)
                base = chunk * rows + index * tile
                there = pl.ds(pl.multiple_of(base, tile), tile)
                q_low = ids[q_first + base]
                q_high = ids[q_first + base + tile - 1]

                def add(masked):
                    if masked:
                        allowed = id_row[first // keys] <= id_col[there, :]
                    for head in range(heads):
                        lanes = slice(head * head_size, (head + 1) * head_size)
                        score = lax.dot_general(
                            q_ref[here, lanes],
                            kv_ref[:, lanes],
                            (((1,), (1,)), ((), ())),
                            preferred_element_type=F32,
                        )
                        weight = jnp.exp2(score)
                        if masked:
                            weight = jnp.where(allowed, weight, 0.0)
                        wide = slice(2 * head * head_size, 2 * (head + 1) * head_size)
                        acc[there, wide] += jnp.dot(
                            weight.astype(BF16), v_ones[head], preferred_element_type=F32
                        )

                @pl.when(key_high <= q_low)
                def _():
                    add(False)

                @pl.when((key_high > q_low) & (key_low <= q_high))
                def _():
                    add(True)


def attend_kernel(count_q, count_kv, head_size, has_acc, count_out, info, ids, *refs):
    q_refs, rest = refs[:count_q], refs[count_q:]
    (id_col, id_row), rest = rest[:2], rest[2:]
    kv_refs, rest = rest[:count_kv], rest[count_kv:]
    rows, width = q_refs[0].shape
    if has_acc:
        acc_in, rest = rest[0], rest[1:]
    if count_out:
        w_ref, outs, (v_ones, acc, attended) = rest[0], rest[1:-3], rest[-3:]
    else:
        acc_out, v_ones, acc = rest
    acc[...] = acc_in[...] if has_acc else jnp.zeros_like(acc)
    sources = [info[number] for number in range(count_kv)]
    attend_blocks(
        sources, ids, info[count_kv], q_refs, id_col, id_row, kv_refs, v_ones, acc, head_size
    )
    if not count_out:
        acc_out[...] = acc[...]
        return
    for head in range(width // head_size):
        start = 2 * head * head_size
        attended[:, head * head_size : (head + 1) * head_size] = (
            acc[:, start : start + head_size]
            / acc[:, start + head_size : start + 2 * head_size]
        ).astype(BF16)
    out_width = outs[0].shape[1]
    for number, out in enumerate(outs):
        lane = info[count_kv + 1 + number] * out_width
        stream = number * count_q // count_out
        out[...] = jnp.dot(
            attended[stream * rows : (stream + 1) * rows, :],
            w_ref[:, pl.ds(pl.multiple_of(lane, out_width), out_width)],
            preferred_element_type=F32,
        ).astype(BF16)


def attend(info, ids, queries, id_col, id_row, kvs, head_size, acc=None, w_out=None, count_out=0):
    rows, width = queries[0].shape
    total = rows * len(queries)
    keys = kvs[0].shape[0]
    heads = width // head_size
    scratch = [
        pltpu.VMEM((heads, keys, 2 * head_size), BF16),
        pltpu.VMEM((total, 2 * width), F32),
    ]
    operands = [*map(in_vmem, queries), id_col, in_hbm(id_row), *map(in_vmem, kvs)]
    if acc is not None:
        operands.append(in_vmem(acc))
    if count_out:
        operands.append(in_hbm(w_out))
        scratch.append(pltpu.VMEM((total, width), BF16))
        shape = pltpu.VMEM((rows, w_out.shape[1] * len(queries) // count_out), BF16)
    else:
        shape = pltpu.VMEM((total, 2 * width), F32)
    outs = count_out or 1
    return pl.pallas_call(
        functools.partial(
            attend_kernel, len(queries), len(kvs), head_size, acc is not None, count_out
        ),
        out_shape=(shape,) * outs,
        in_specs=[SMEM, SMEM] + [VMEM] * len(operands),
        out_specs=(VMEM,) * outs,
        scratch_shapes=scratch,
        compiler_params=pltpu.CompilerParams(
            vmem_limit_bytes=(16 << 20) + 2 * kvs[0].size * 2 * len(kvs)
        ),
        cost_estimate=pl.CostEstimate(
            flops=6 * total * keys * len(kvs) * width + 2 * rows * width * width * count_out,
            bytes_accessed=4 * keys * len(kvs) * width + 8 * total * width,
            transcendentals=total * keys * len(kvs) * heads,
        ),
        name="attend_last" if count_out else "attend",
    )(info, in_hbm(ids), *operands)


def total_of(*parts):
    return sum(part.astype(F32) for part in parts).astype(BF16)


def body(mesh_shape, tokens, norm_gain, w_qkv, head_scale, w_out, scale_ids):
    ring, seqs = mesh_shape["head"], mesh_shape["seq"]
    outer = seqs // 2
    rows, width = tokens.shape
    half = rows // 2
    head_size = w_qkv.shape[2] // head_scale.shape[0]
    head_at, seq_at = lax.axis_index("head"), lax.axis_index("seq")
    place = ring_place(head_at, ring)
    chip, core = seq_at // 2, seq_at % 2
    index_at = lambda offset: ring_index((place + offset + ring) % ring, ring)
    numbers = lambda values: jnp.stack(values).astype(jnp.int32)
    id_row = scale_ids.reshape(-1, 1, half)
    id_col = lax.dynamic_slice_in_dim(scale_ids, seq_at * rows, rows)[:, None]

    streams, ways = (0, 1), ((0, 1), (1, -1))
    farthest = ring // 2
    reach = [(farthest, farthest - 1), (farthest - 1, farthest)]

    held = [[tokens[s * half : (s + 1) * half]] * 2 for s in streams]
    blocks, offsets = [[] for s in streams], [[0] for s in streams]
    for step in range(1, farthest + 1):
        for s in streams:
            for way, sign in ways:
                if step <= reach[s][way]:
                    held[s][way] = along(held[s][way], sign, ring)
        if step == 1:
            held[1][1], weights = lax.optimization_barrier(
                (held[1][1], fold_gain(norm_gain, w_qkv))
            )
        for s in streams:
            for way, sign in ways:
                if step <= reach[s][way]:
                    blocks[s].append(held[s][way])
                    offsets[s].append(-sign * step)
    queries, kvs = [], []
    for s in streams:
        at = numbers([index_at(offset) for offset in offsets[s]])
        query, kv = project(at, head_scale, tokens, weights, blocks[s], s * half, head_size)
        queries.append(query)
        kvs.append(kv)

    far, straight, crossed = [], [], []
    for step in range(outer):
        source = 2 * ((chip + outer - step) % outer)
        for s in streams:
            straight.append((source + core) * rows + s * half)
            crossed.append((source + 1 - core) * rows + s * half)
            if step:
                far.append(lax.ppermute(kvs[s], "seq", [
                    (2 * a + b, 2 * ((a + step) % outer) + b) for a in range(outer) for b in (0, 1)
                ]))
    first = [seq_at * rows]
    info = numbers(straight[:2] + crossed[:2] + first)
    keys = kvs + [swapped(kv, seqs) for kv in kvs]
    (acc,) = attend(info, scale_ids, queries, id_col, id_row, keys, head_size)
    acc, far = lax.optimization_barrier((acc, far))
    far_crossed = [swapped(block, seqs) for block in far]
    info = numbers(straight[2:] + first)
    (acc,) = attend(info, scale_ids, queries, id_col, id_row, far, head_size, acc)

    goals = [[*range(up, 0, -1), *range(-down, 0), 0] for up, down in reach]
    info = numbers(crossed[2:] + first + [index_at(goal) for goal in goals[0] + goals[1]])
    parts = attend(
        info, scale_ids, queries, id_col, id_row, far_crossed, head_size, acc, w_out, 2 * ring
    )
    parts = [dict(zip(goals[s], parts[s * ring : (s + 1) * ring])) for s in streams]
    sums = [[None, None] for s in streams]
    for step in range(farthest, 0, -1):
        for s in streams:
            for way, sign in ways:
                if step <= reach[s][way]:
                    part = parts[s][sign * step]
                    if sums[s][way] is not None:
                        part = total_of(part, sums[s][way])
                    sums[s][way] = along(part, sign, ring)
    return jnp.concatenate([total_of(parts[s][0], *sums[s]) for s in streams])


def solution(mesh):
    placed = (P("seq", "head"), P(), P(None, None, "head"), P("head"), P("head", None), P())
    return jax.shard_map(
        functools.partial(body, dict(mesh.shape)),
        mesh=mesh,
        in_specs=placed,
        out_specs=P("seq", "head"),
        check_vma=False,
    )
```

```python
import functools
import math

import jax
import jax.numpy as jnp
from jax import lax
from jax.experimental import pallas as pl
from jax.experimental.pallas import tpu as pltpu
from jax.sharding import PartitionSpec as P

LOG2E = math.log2(math.e)
VMEM = pl.BlockSpec(memory_space=pltpu.VMEM)
SMEM = pl.BlockSpec(memory_space=pltpu.SMEM)
F32 = jnp.float32
BF16 = jnp.bfloat16


def ring_order(count):
    line = count // 2
    return [2 * z for z in range(line)] + [2 * z + 1 for z in reversed(range(line))]


def ring_place(index, count):
    return jnp.where(index % 2 == 0, index // 2, count - 1 - index // 2)


def ring_index(place, count):
    return jnp.where(place < count // 2, 2 * place, 2 * (count - 1 - place) + 1)


def along(value, step, count):
    order = ring_order(count)
    return lax.ppermute(
        value, "head", [(order[p], order[(p + step) % count]) for p in range(count)]
    )


def swapped(value, seq_count):
    return lax.ppermute(value, "seq", [(seq, seq + 1 - 2 * (seq % 2)) for seq in range(seq_count)])


def in_hbm(value):
    return pltpu.with_memory_space_constraint(value, pltpu.HBM)


def in_vmem(value):
    return pltpu.with_memory_space_constraint(value, pltpu.VMEM)


def fold_kernel(order, at, gain_ref, w_hbm, out_ref, sems):
    lanes = gain_ref.shape[1]
    size = w_hbm.shape[1] // len(order)
    per = size // lanes

    def fetch(n):
        start = pl.multiple_of(at[order[n]] * size, size)
        return pltpu.make_async_copy(
            w_hbm.at[:, pl.ds(start, size), :], out_ref.at[:, n * size : (n + 1) * size, :], sems.at[n]
        )

    for n in range(len(order)):
        fetch(n).start()
    for n in range(len(order)):
        columns = jnp.transpose(gain_ref[pl.ds(at[order[n]] * per, per), :])
        fetch(n).wait()
        for piece in range(per):
            first = n * size + piece * lanes
            for group in range(w_hbm.shape[0]):
                here = (group, slice(first, first + lanes), slice(None))
                scaled = out_ref[here].astype(F32) * columns[:, piece : piece + 1]
                out_ref[here] = scaled.astype(BF16)


def fold_gain(order, at, gain, weights):
    depth = weights.shape[1]
    lanes = math.gcd(depth // len(order), 128)
    return pl.pallas_call(
        functools.partial(fold_kernel, order),
        out_shape=pltpu.VMEM(weights.shape, BF16),
        in_specs=[SMEM, VMEM, pl.BlockSpec(memory_space=pltpu.HBM)],
        out_specs=VMEM,
        scratch_shapes=[pltpu.SemaphoreType.DMA((len(order),))],
        compiler_params=pltpu.CompilerParams(vmem_limit_bytes=16 << 20),
        cost_estimate=pl.CostEstimate(
            flops=weights.size, bytes_accessed=4 * weights.size, transcendentals=0
        ),
        name="fold_gain",
    )(at, in_hbm(gain.reshape(depth // lanes, lanes)), in_hbm(weights))


def place_kernel(targets, *refs):
    blocks, wide, sems = refs[: len(targets)], refs[-2], refs[-1]
    copies = []
    for n, (block, (row, lane)) in enumerate(zip(blocks, targets)):
        rows, width = block.shape
        here = wide.at[row : row + rows, lane : lane + width]
        copies.append(pltpu.make_async_copy(block, here, sems.at[n]))
    for copy in copies:
        copy.start()
    for copy in copies:
        copy.wait()


def placed(targets, blocks, wide, shape):
    operands = [*blocks] + ([] if wide is None else [in_vmem(wide)])
    return pl.pallas_call(
        functools.partial(place_kernel, targets),
        out_shape=pltpu.VMEM(shape, BF16),
        in_specs=[pl.BlockSpec(memory_space=pl.ANY)] * len(operands),
        out_specs=pl.BlockSpec(memory_space=pl.ANY),
        scratch_shapes=[pltpu.SemaphoreType.DMA((len(targets),))],
        input_output_aliases={} if wide is None else {len(blocks): 0},
        cost_estimate=pl.CostEstimate(flops=0, bytes_accessed=1 << 20, transcendentals=0),
        name="place",
    )(*operands)


def project_kernel(head_size, factor, wide, w_ref, *refs):
    lasts, (q_ref, kv_ref) = refs[:-2], refs[-2:]
    rows, width = lasts[0].shape
    depth, out_width = w_ref.shape[1:]
    done = depth - width
    for stream, last in enumerate(lasts):
        here = slice(stream * rows, (stream + 1) * rows)
        q, k, v = (
            jnp.dot(wide[here, :done], w_ref[group, :done, :], preferred_element_type=F32)
            + jnp.dot(last[...], w_ref[group, done:, :], preferred_element_type=F32)
            for group in range(3)
        )
        power = None
        for lane in range(0, depth, 128):
            if lane < done:
                values = wide[here, lane : lane + 128].astype(F32)
            else:
                values = last[:, lane - done : lane - done + 128].astype(F32)
            power = values * values if power is None else power + values * values
        scale = lax.rsqrt(jnp.sum(power, axis=-1, keepdims=True) * (1.0 / depth) + 1e-06)
        q, k, v = q * scale, k * scale, v * scale
        for head in range(out_width // head_size):
            lanes = slice(head * head_size, (head + 1) * head_size)
            qh, kh = q[:, lanes], k[:, lanes]
            q_size = lax.rsqrt(jnp.sum(qh * qh, axis=-1, keepdims=True) + 1e-06)
            k_size = lax.rsqrt(jnp.sum(kh * kh, axis=-1, keepdims=True) + 1e-06)
            q_ref[here, lanes] = (qh * (q_size * (factor[head] * LOG2E))).astype(BF16)
            kv_ref[here, lanes] = (kh * k_size).astype(BF16)
        kv_ref[here, out_width:] = v.astype(BF16)


def project(factor, wide, weights, lasts, head_size):
    rows = wide.shape[0]
    groups, depth, out_width = weights.shape
    return pl.pallas_call(
        functools.partial(project_kernel, head_size),
        out_shape=(pltpu.VMEM((rows, out_width), BF16), pltpu.VMEM((rows, 2 * out_width), BF16)),
        in_specs=[SMEM] + [VMEM] * (2 + len(lasts)),
        out_specs=(VMEM, VMEM),
        compiler_params=pltpu.CompilerParams(vmem_limit_bytes=16 << 20),
        cost_estimate=pl.CostEstimate(
            flops=2 * rows * depth * groups * out_width,
            bytes_accessed=2 * depth * (rows + groups * out_width),
            transcendentals=0,
        ),
        name="project",
    )(in_hbm(factor), in_vmem(wide), in_vmem(weights), *map(in_vmem, lasts))


def attend_blocks(sources, ids, q_first, q_refs, id_col, id_row, kv_refs, v_ones, acc, head_size):
    heads = q_refs[0].shape[1] // head_size
    keys = kv_refs[0].shape[0]
    rows = q_refs[0].shape[0]
    for number, kv_ref in enumerate(kv_refs):
        for head in range(heads):
            start = (heads + head) * head_size
            v_ones[head, :, :head_size] = kv_ref[:, start : start + head_size]
            v_ones[head, :, head_size:] = jnp.ones((keys, head_size), BF16)
        first = sources[number]
        key_low, key_high = ids[first], ids[first + keys - 1]
        tile = math.gcd(rows, 256)
        for chunk, q_ref in enumerate(q_refs):

            @pl.loop(0, rows // tile)
            def _(index):
                here = pl.ds(pl.multiple_of(index * tile, tile), tile)
                base = chunk * rows + index * tile
                there = pl.ds(pl.multiple_of(base, tile), tile)
                q_low = ids[q_first + base]
                q_high = ids[q_first + base + tile - 1]

                def add(masked):
                    if masked:
                        allowed = id_row[first // keys] <= id_col[there, :]
                    for head in range(heads):
                        lanes = slice(head * head_size, (head + 1) * head_size)
                        score = lax.dot_general(
                            q_ref[here, lanes],
                            kv_ref[:, lanes],
                            (((1,), (1,)), ((), ())),
                            preferred_element_type=F32,
                        )
                        weight = jnp.exp2(score)
                        if masked:
                            weight = jnp.where(allowed, weight, 0.0)
                        wide = slice(2 * head * head_size, 2 * (head + 1) * head_size)
                        acc[there, wide] += jnp.dot(
                            weight.astype(BF16), v_ones[head], preferred_element_type=F32
                        )

                @pl.when(key_high <= q_low)
                def _():
                    add(False)

                @pl.when((key_high > q_low) & (key_low <= q_high))
                def _():
                    add(True)


def attend_kernel(
    count_q, count_kv, head_size, has_acc, count_out, count_streams, info, ids, *refs
):
    q_refs, rest = refs[:count_q], refs[count_q:]
    (id_col, id_row), rest = rest[:2], rest[2:]
    kv_refs, rest = rest[:count_kv], rest[count_kv:]
    rows, width = q_refs[0].shape
    if has_acc:
        acc_in, rest = rest[0], rest[1:]
    if count_out:
        w_ref, outs, (v_ones, acc, attended) = rest[0], rest[1:-3], rest[-3:]
    else:
        acc_out, v_ones, acc = rest
    acc[...] = acc_in[...] if has_acc else jnp.zeros_like(acc)
    sources = [info[number] for number in range(count_kv)]
    attend_blocks(
        sources, ids, info[count_kv], q_refs, id_col, id_row, kv_refs, v_ones, acc, head_size
    )
    if not count_out:
        acc_out[...] = acc[...]
        return
    for head in range(width // head_size):
        start = 2 * head * head_size
        attended[:, head * head_size : (head + 1) * head_size] = (
            acc[:, start : start + head_size]
            / acc[:, start + head_size : start + 2 * head_size]
        ).astype(BF16)
    out_width = outs[0].shape[1]
    for number, out in enumerate(outs):
        lane = info[count_kv + 1 + number] * out_width
        first = number * count_streams // count_out * out.shape[0]
        out[...] = jnp.dot(
            attended[first : first + out.shape[0], :],
            w_ref[:, pl.ds(pl.multiple_of(lane, out_width), out_width)],
            preferred_element_type=F32,
        ).astype(BF16)


def attend(info, ids, queries, id_col, id_row, kvs, head_size, acc=None, w_out=None, streams=0):
    rows, width = queries[0].shape
    total = rows * len(queries)
    keys = kvs[0].shape[0]
    heads = width // head_size
    count_out = streams * w_out.shape[1] // width if streams else 0
    scratch = [
        pltpu.VMEM((heads, keys, 2 * head_size), BF16),
        pltpu.VMEM((total, 2 * width), F32),
    ]
    operands = [*map(in_vmem, queries), id_col, in_hbm(id_row), *map(in_vmem, kvs)]
    if acc is not None:
        operands.append(in_vmem(acc))
    if count_out:
        operands.append(in_hbm(w_out))
        scratch.append(pltpu.VMEM((total, width), BF16))
        shape = pltpu.VMEM((total // streams, w_out.shape[1] * streams // count_out), BF16)
    else:
        shape = pltpu.VMEM((total, 2 * width), F32)
    outs = count_out or 1
    return pl.pallas_call(
        functools.partial(
            attend_kernel, len(queries), len(kvs), head_size, acc is not None, count_out, streams
        ),
        out_shape=(shape,) * outs,
        in_specs=[SMEM, SMEM] + [VMEM] * len(operands),
        out_specs=(VMEM,) * outs,
        scratch_shapes=scratch,
        compiler_params=pltpu.CompilerParams(
            vmem_limit_bytes=(16 << 20) + 2 * kvs[0].size * 2 * len(kvs)
        ),
        cost_estimate=pl.CostEstimate(
            flops=6 * total * keys * len(kvs) * width + 2 * total * width * width * count_out,
            bytes_accessed=4 * keys * len(kvs) * width + 8 * total * width,
            transcendentals=total * keys * len(kvs) * heads,
        ),
        name="attend_last" if count_out else "attend",
    )(info, in_hbm(ids), *operands)


def total_of(*parts):
    return sum(part.astype(F32) for part in parts).astype(BF16)


def body(mesh_shape, tokens, norm_gain, w_qkv, head_scale, w_out, scale_ids):
    ring, seqs = mesh_shape["head"], mesh_shape["seq"]
    outer = seqs // 2
    rows, width = tokens.shape
    half = rows // 2
    head_size = w_qkv.shape[2] // head_scale.shape[0]
    head_at, seq_at = lax.axis_index("head"), lax.axis_index("seq")
    place = ring_place(head_at, ring)
    chip, core = seq_at // 2, seq_at % 2
    index_at = lambda offset: ring_index((place + offset + ring) % ring, ring)
    numbers = lambda values: jnp.stack(values).astype(jnp.int32)
    id_row = scale_ids.reshape(-1, 1, rows)
    id_col = lax.dynamic_slice_in_dim(scale_ids, seq_at * rows, rows)[:, None]
    at = [index_at(offset) for offset in range(ring)]

    streams, ways = (0, 1), ((0, 1), (1, -1))
    farthest = ring // 2
    reach = [(farthest, farthest - 1), (farthest - 1, farthest)]

    order = [0] + [sign * step % ring for step in range(1, farthest) for sign in (-1, 1)] + [farthest]
    held = [[tokens[s * half : (s + 1) * half]] * 2 for s in streams]
    wide, blocks, targets = None, [in_hbm(tokens)], [(0, 0)]
    for step in range(1, farthest + 1):
        for s in streams:
            for way, sign in ways:
                if step <= reach[s][way]:
                    held[s][way] = along(held[s][way], sign, ring)
        if step == 1:
            held[1][1], weights = lax.optimization_barrier(
                (held[1][1], fold_gain(order, numbers(at), norm_gain, w_qkv))
            )
        elif step == 2:
            wide = placed(targets, blocks, wide, (rows, ring * width))
            blocks, targets = [], []
        elif step == 3:
            held[1][1], wide = lax.optimization_barrier(
                (held[1][1], placed(targets, blocks, wide, (rows, ring * width)))
            )
            blocks, targets = [], []
        if step < farthest:
            for s in streams:
                for way, sign in ways:
                    blocks.append(in_vmem(held[s][way]))
                    targets.append((s * half, (2 * step - 1 + way) * width))
    wide = placed(targets, blocks, wide, (rows, ring * width))
    lasts = [held[0][0], held[1][1]]
    query, kv = project(head_scale, wide, weights, lasts, head_size)

    far, straight, crossed = [], [], []
    for step in range(outer):
        source = 2 * ((chip + outer - step) % outer)
        straight.append((source + core) * rows)
        crossed.append((source + 1 - core) * rows)
        if step:
            far.append(lax.ppermute(kv, "seq", [
                (2 * a + b, 2 * ((a + step) % outer) + b) for a in range(outer) for b in (0, 1)
            ]))
    first = [seq_at * rows]
    info = numbers(straight[:1] + crossed[:1] + first)
    keys = [kv, swapped(kv, seqs)]
    (acc,) = attend(info, scale_ids, [query], id_col, id_row, keys, head_size)
    acc, far = lax.optimization_barrier((acc, far))
    far_crossed = [swapped(block, seqs) for block in far]
    info = numbers(straight[1:] + first)
    (acc,) = attend(info, scale_ids, [query], id_col, id_row, far, head_size, acc)

    goals = [[*range(up, 0, -1), *range(-down, 0), 0] for up, down in reach]
    info = numbers(crossed[1:] + first + [at[goal % ring] for goal in goals[0] + goals[1]])
    parts = attend(
        info, scale_ids, [query], id_col, id_row, far_crossed, head_size, acc, w_out, len(streams)
    )
    parts = [dict(zip(goals[s], parts[s * ring : (s + 1) * ring])) for s in streams]
    sums = [[None, None] for s in streams]
    for step in range(farthest, 0, -1):
        for s in streams:
            for way, sign in ways:
                if step <= reach[s][way]:
                    part = parts[s][sign * step]
                    if sums[s][way] is not None:
                        part = total_of(part, sums[s][way])
                    sums[s][way] = along(part, sign, ring)
    return jnp.concatenate([total_of(parts[s][0], *sums[s]) for s in streams])


def solution(mesh):
    placed = (P("seq", "head"), P(), P(None, None, "head"), P("head"), P("head", None), P())
    return jax.shard_map(
        functools.partial(body, dict(mesh.shape)),
        mesh=mesh,
        in_specs=placed,
        out_specs=P("seq", "head"),
        check_vma=False,
    )
```

```python
import functools
import math

import jax
import jax.numpy as jnp
from jax import lax
from jax.experimental import pallas as pl
from jax.experimental.pallas import tpu as pltpu
from jax.sharding import PartitionSpec as P

LOG2E = math.log2(math.e)
VMEM = pl.BlockSpec(memory_space=pltpu.VMEM)
SMEM = pl.BlockSpec(memory_space=pltpu.SMEM)
F32 = jnp.float32
BF16 = jnp.bfloat16


def ring_order(count):
    line = count // 2
    return [2 * z for z in range(line)] + [2 * z + 1 for z in reversed(range(line))]


def ring_place(index, count):
    return jnp.where(index % 2 == 0, index // 2, count - 1 - index // 2)


def ring_index(place, count):
    return jnp.where(place < count // 2, 2 * place, 2 * (count - 1 - place) + 1)


def along(value, step, count):
    order = ring_order(count)
    return lax.ppermute(
        value, "head", [(order[p], order[(p + step) % count]) for p in range(count)]
    )


def swapped(value, seq_count):
    return lax.ppermute(value, "seq", [(seq, seq + 1 - 2 * (seq % 2)) for seq in range(seq_count)])


def in_hbm(value):
    return pltpu.with_memory_space_constraint(value, pltpu.HBM)


def in_vmem(value):
    return pltpu.with_memory_space_constraint(value, pltpu.VMEM)


def fold_kernel(order, at, gain_ref, w_hbm, out_ref, sems):
    lanes = gain_ref.shape[1]
    size = w_hbm.shape[1] // len(order)
    per = size // lanes

    def fetch(n):
        start = pl.multiple_of(at[order[n]] * size, size)
        return pltpu.make_async_copy(
            w_hbm.at[:, pl.ds(start, size), :], out_ref.at[:, n * size : (n + 1) * size, :], sems.at[n]
        )

    for n in range(len(order)):
        fetch(n).start()
    for n in range(len(order)):
        columns = jnp.transpose(gain_ref[pl.ds(at[order[n]] * per, per), :])
        fetch(n).wait()
        for piece in range(per):
            first = n * size + piece * lanes
            for group in range(w_hbm.shape[0]):
                here = (group, slice(first, first + lanes), slice(None))
                scaled = out_ref[here].astype(F32) * columns[:, piece : piece + 1]
                out_ref[here] = scaled.astype(BF16)


def fold_gain(order, at, gain, weights):
    depth = weights.shape[1]
    lanes = math.gcd(depth // len(order), 128)
    return pl.pallas_call(
        functools.partial(fold_kernel, order),
        out_shape=pltpu.VMEM(weights.shape, BF16),
        in_specs=[SMEM, VMEM, pl.BlockSpec(memory_space=pltpu.HBM)],
        out_specs=VMEM,
        scratch_shapes=[pltpu.SemaphoreType.DMA((len(order),))],
        compiler_params=pltpu.CompilerParams(vmem_limit_bytes=16 << 20),
        cost_estimate=pl.CostEstimate(
            flops=weights.size, bytes_accessed=4 * weights.size, transcendentals=0
        ),
        name="fold_gain",
    )(at, in_hbm(gain.reshape(depth // lanes, lanes)), in_hbm(weights))


def place_kernel(targets, *refs):
    blocks, wide, sems = refs[: len(targets)], refs[-2], refs[-1]
    copies = []
    for n, (block, (row, lane)) in enumerate(zip(blocks, targets)):
        rows, width = block.shape
        here = wide.at[row : row + rows, lane : lane + width]
        copies.append(pltpu.make_async_copy(block, here, sems.at[n]))
    for copy in copies:
        copy.start()
    for copy in copies:
        copy.wait()


def placed(targets, blocks, wide, shape):
    operands = [*blocks] + ([] if wide is None else [in_vmem(wide)])
    return pl.pallas_call(
        functools.partial(place_kernel, targets),
        out_shape=pltpu.VMEM(shape, BF16),
        in_specs=[pl.BlockSpec(memory_space=pl.ANY)] * len(operands),
        out_specs=pl.BlockSpec(memory_space=pl.ANY),
        scratch_shapes=[pltpu.SemaphoreType.DMA((len(targets),))],
        input_output_aliases={} if wide is None else {len(blocks): 0},
        compiler_params=pltpu.CompilerParams(vmem_limit_bytes=1 << 20),
        cost_estimate=pl.CostEstimate(flops=0, bytes_accessed=1 << 20, transcendentals=0),
        name="place",
    )(*operands)


def project_kernel(head_size, factor, wide, w_ref, *refs):
    lasts, (q_ref, kv_ref) = refs[:-2], refs[-2:]
    rows, width = lasts[0].shape
    depth, out_width = w_ref.shape[1:]
    done = depth - width
    for stream, last in enumerate(lasts):
        here = slice(stream * rows, (stream + 1) * rows)
        q, k, v = (
            jnp.dot(wide[here, :done], w_ref[group, :done, :], preferred_element_type=F32)
            + jnp.dot(last[...], w_ref[group, done:, :], preferred_element_type=F32)
            for group in range(3)
        )
        power = None
        for lane in range(0, depth, 128):
            if lane < done:
                values = wide[here, lane : lane + 128].astype(F32)
            else:
                values = last[:, lane - done : lane - done + 128].astype(F32)
            power = values * values if power is None else power + values * values
        scale = lax.rsqrt(jnp.sum(power, axis=-1, keepdims=True) * (1.0 / depth) + 1e-06)
        q, k, v = q * scale, k * scale, v * scale
        for head in range(out_width // head_size):
            lanes = slice(head * head_size, (head + 1) * head_size)
            qh, kh = q[:, lanes], k[:, lanes]
            q_size = lax.rsqrt(jnp.sum(qh * qh, axis=-1, keepdims=True) + 1e-06)
            k_size = lax.rsqrt(jnp.sum(kh * kh, axis=-1, keepdims=True) + 1e-06)
            q_ref[here, lanes] = (qh * (q_size * (factor[head] * LOG2E))).astype(BF16)
            kv_ref[here, lanes] = (kh * k_size).astype(BF16)
        kv_ref[here, out_width:] = v.astype(BF16)


def project(factor, wide, weights, lasts, head_size):
    rows = wide.shape[0]
    groups, depth, out_width = weights.shape
    return pl.pallas_call(
        functools.partial(project_kernel, head_size),
        out_shape=(pltpu.VMEM((rows, out_width), BF16), pltpu.VMEM((rows, 2 * out_width), BF16)),
        in_specs=[SMEM] + [VMEM] * (2 + len(lasts)),
        out_specs=(VMEM, VMEM),
        compiler_params=pltpu.CompilerParams(vmem_limit_bytes=16 << 20),
        cost_estimate=pl.CostEstimate(
            flops=2 * rows * depth * groups * out_width,
            bytes_accessed=2 * depth * (rows + groups * out_width),
            transcendentals=0,
        ),
        name="project",
    )(in_hbm(factor), in_vmem(wide), in_vmem(weights), *map(in_vmem, lasts))


def attend_blocks(sources, ids, q_first, q_refs, id_col, id_row, kv_refs, v_ones, acc, head_size):
    heads = q_refs[0].shape[1] // head_size
    keys = kv_refs[0].shape[0]
    rows = q_refs[0].shape[0]
    for number, kv_ref in enumerate(kv_refs):
        for head in range(heads):
            start = (heads + head) * head_size
            v_ones[head, :, :head_size] = kv_ref[:, start : start + head_size]
            v_ones[head, :, head_size:] = jnp.ones((keys, head_size), BF16)
        first = sources[number]
        key_low, key_high = ids[first], ids[first + keys - 1]
        tile = math.gcd(rows, 256)
        for chunk, q_ref in enumerate(q_refs):

            @pl.loop(0, rows // tile)
            def _(index):
                here = pl.ds(pl.multiple_of(index * tile, tile), tile)
                base = chunk * rows + index * tile
                there = pl.ds(pl.multiple_of(base, tile), tile)
                q_low = ids[q_first + base]
                q_high = ids[q_first + base + tile - 1]

                def add(masked):
                    if masked:
                        allowed = id_row[first // keys] <= id_col[there, :]
                    for head in range(heads):
                        lanes = slice(head * head_size, (head + 1) * head_size)
                        score = lax.dot_general(
                            q_ref[here, lanes],
                            kv_ref[:, lanes],
                            (((1,), (1,)), ((), ())),
                            preferred_element_type=F32,
                        )
                        weight = jnp.exp2(score)
                        if masked:
                            weight = jnp.where(allowed, weight, 0.0)
                        wide = slice(2 * head * head_size, 2 * (head + 1) * head_size)
                        acc[there, wide] += jnp.dot(
                            weight.astype(BF16), v_ones[head], preferred_element_type=F32
                        )

                @pl.when(key_high <= q_low)
                def _():
                    add(False)

                @pl.when((key_high > q_low) & (key_low <= q_high))
                def _():
                    add(True)


def attend_kernel(
    count_q, count_kv, head_size, has_acc, count_out, count_streams, info, ids, *refs
):
    q_refs, rest = refs[:count_q], refs[count_q:]
    (id_col, id_row), rest = rest[:2], rest[2:]
    kv_refs, rest = rest[:count_kv], rest[count_kv:]
    rows, width = q_refs[0].shape
    if has_acc:
        acc_in, rest = rest[0], rest[1:]
    if count_out:
        w_ref, outs, (v_ones, acc, attended) = rest[0], rest[1:-3], rest[-3:]
    else:
        acc_out, v_ones, acc = rest
    acc[...] = acc_in[...] if has_acc else jnp.zeros_like(acc)
    sources = [info[number] for number in range(count_kv)]
    attend_blocks(
        sources, ids, info[count_kv], q_refs, id_col, id_row, kv_refs, v_ones, acc, head_size
    )
    if not count_out:
        acc_out[...] = acc[...]
        return
    for head in range(width // head_size):
        start = 2 * head * head_size
        attended[:, head * head_size : (head + 1) * head_size] = (
            acc[:, start : start + head_size]
            / acc[:, start + head_size : start + 2 * head_size]
        ).astype(BF16)
    out_width = outs[0].shape[1]
    for number, out in enumerate(outs):
        lane = info[count_kv + 1 + number] * out_width
        first = number * count_streams // count_out * out.shape[0]
        out[...] = jnp.dot(
            attended[first : first + out.shape[0], :],
            w_ref[:, pl.ds(pl.multiple_of(lane, out_width), out_width)],
            preferred_element_type=F32,
        ).astype(BF16)


def attend(info, ids, queries, id_col, id_row, kvs, head_size, acc=None, w_out=None, streams=0):
    rows, width = queries[0].shape
    total = rows * len(queries)
    keys = kvs[0].shape[0]
    heads = width // head_size
    count_out = streams * w_out.shape[1] // width if streams else 0
    scratch = [
        pltpu.VMEM((heads, keys, 2 * head_size), BF16),
        pltpu.VMEM((total, 2 * width), F32),
    ]
    operands = [*map(in_vmem, queries), id_col, in_hbm(id_row), *map(in_vmem, kvs)]
    if acc is not None:
        operands.append(in_vmem(acc))
    if count_out:
        operands.append(in_hbm(w_out))
        scratch.append(pltpu.VMEM((total, width), BF16))
        shape = pltpu.VMEM((total // streams, w_out.shape[1] * streams // count_out), BF16)
    else:
        shape = pltpu.VMEM((total, 2 * width), F32)
    outs = count_out or 1
    return pl.pallas_call(
        functools.partial(
            attend_kernel, len(queries), len(kvs), head_size, acc is not None, count_out, streams
        ),
        out_shape=(shape,) * outs,
        in_specs=[SMEM, SMEM] + [VMEM] * len(operands),
        out_specs=(VMEM,) * outs,
        scratch_shapes=scratch,
        compiler_params=pltpu.CompilerParams(
            vmem_limit_bytes=(16 << 20) + 2 * kvs[0].size * 2 * len(kvs)
        ),
        cost_estimate=pl.CostEstimate(
            flops=6 * total * keys * len(kvs) * width + 2 * total * width * width * count_out,
            bytes_accessed=4 * keys * len(kvs) * width + 8 * total * width,
            transcendentals=total * keys * len(kvs) * heads,
        ),
        name="attend_last" if count_out else "attend",
    )(info, in_hbm(ids), *operands)


def total_of(*parts):
    return sum(part.astype(F32) for part in parts).astype(BF16)


def body(mesh_shape, tokens, norm_gain, w_qkv, head_scale, w_out, scale_ids):
    ring, seqs = mesh_shape["head"], mesh_shape["seq"]
    outer = seqs // 2
    rows, width = tokens.shape
    half = rows // 2
    head_size = w_qkv.shape[2] // head_scale.shape[0]
    head_at, seq_at = lax.axis_index("head"), lax.axis_index("seq")
    place = ring_place(head_at, ring)
    chip, core = seq_at // 2, seq_at % 2
    index_at = lambda offset: ring_index((place + offset + ring) % ring, ring)
    numbers = lambda values: jnp.stack(values).astype(jnp.int32)
    id_row = scale_ids.reshape(-1, 1, rows)
    id_col = lax.dynamic_slice_in_dim(scale_ids, seq_at * rows, rows)[:, None]
    at = [index_at(offset) for offset in range(ring)]

    streams, ways = (0, 1), ((0, 1), (1, -1))
    farthest = ring // 2
    reach = [(farthest, farthest - 1), (farthest - 1, farthest)]

    order = [0] + [sign * step % ring for step in range(1, farthest) for sign in (-1, 1)] + [farthest]
    held = [[tokens[s * half : (s + 1) * half]] * 2 for s in streams]
    wide, blocks, targets = None, [in_hbm(tokens)], [(0, 0)]
    for step in range(1, farthest + 1):
        for s in streams:
            for way, sign in ways:
                if step <= reach[s][way]:
                    held[s][way] = along(held[s][way], sign, ring)
        if step == 1:
            held[1][1], weights = lax.optimization_barrier(
                (held[1][1], fold_gain(order, numbers(at), norm_gain, w_qkv))
            )
        elif step == 2:
            wide = placed(targets, blocks, wide, (rows, ring * width))
            blocks, targets = [], []
        elif step == 3:
            held[1][1], wide = lax.optimization_barrier(
                (held[1][1], placed(targets, blocks, wide, (rows, ring * width)))
            )
            blocks, targets = [], []
        if step < farthest:
            for s in streams:
                for way, sign in ways:
                    blocks.append(in_vmem(held[s][way]))
                    targets.append((s * half, (2 * step - 1 + way) * width))
    wide = placed(targets, blocks, wide, (rows, ring * width))
    lasts = [held[0][0], held[1][1]]
    query, kv = project(head_scale, wide, weights, lasts, head_size)

    far, straight, crossed = [], [], []
    for step in range(outer):
        source = 2 * ((chip + outer - step) % outer)
        straight.append((source + core) * rows)
        crossed.append((source + 1 - core) * rows)
        if step:
            far.append(lax.ppermute(kv, "seq", [
                (2 * a + b, 2 * ((a + step) % outer) + b) for a in range(outer) for b in (0, 1)
            ]))
    first = [seq_at * rows]
    info = numbers(straight[:1] + crossed[:1] + first)
    keys = [kv, swapped(kv, seqs)]
    (acc,) = attend(info, scale_ids, [query], id_col, id_row, keys, head_size)
    acc, far = lax.optimization_barrier((acc, far))
    far_crossed = [swapped(block, seqs) for block in far]
    info = numbers(straight[1:] + first)
    (acc,) = attend(info, scale_ids, [query], id_col, id_row, far, head_size, acc)

    goals = [[*range(up, 0, -1), *range(-down, 0), 0] for up, down in reach]
    info = numbers(crossed[1:] + first + [at[goal % ring] for goal in goals[0] + goals[1]])
    parts = attend(
        info, scale_ids, [query], id_col, id_row, far_crossed, head_size, acc, w_out, len(streams)
    )
    parts = [dict(zip(goals[s], parts[s * ring : (s + 1) * ring])) for s in streams]
    sums = [[None, None] for s in streams]
    for step in range(farthest, 0, -1):
        for s in streams:
            for way, sign in ways:
                if step <= reach[s][way]:
                    part = parts[s][sign * step]
                    if sums[s][way] is not None:
                        part = total_of(part, sums[s][way])
                    sums[s][way] = along(part, sign, ring)
    return jnp.concatenate([total_of(parts[s][0], *sums[s]) for s in streams])


def solution(mesh):
    placed = (P("seq", "head"), P(), P(None, None, "head"), P("head"), P("head", None), P())
    return jax.shard_map(
        functools.partial(body, dict(mesh.shape)),
        mesh=mesh,
        in_specs=placed,
        out_specs=P("seq", "head"),
        check_vma=False,
    )
```

```python
import functools
import math

import jax
import jax.numpy as jnp
from jax import lax
from jax.experimental import pallas as pl
from jax.experimental.pallas import tpu as pltpu
from jax.sharding import PartitionSpec as P

LOG2E = math.log2(math.e)
VMEM = pl.BlockSpec(memory_space=pltpu.VMEM)
SMEM = pl.BlockSpec(memory_space=pltpu.SMEM)
F32 = jnp.float32
BF16 = jnp.bfloat16


def ring_order(count):
    line = count // 2
    return [2 * z for z in range(line)] + [2 * z + 1 for z in reversed(range(line))]


def ring_place(index, count):
    return jnp.where(index % 2 == 0, index // 2, count - 1 - index // 2)


def ring_index(place, count):
    return jnp.where(place < count // 2, 2 * place, 2 * (count - 1 - place) + 1)


def along(value, step, count):
    order = ring_order(count)
    return lax.ppermute(
        value, "head", [(order[p], order[(p + step) % count]) for p in range(count)]
    )


def swapped(value, seq_count):
    return lax.ppermute(value, "seq", [(seq, seq + 1 - 2 * (seq % 2)) for seq in range(seq_count)])


def in_hbm(value):
    return pltpu.with_memory_space_constraint(value, pltpu.HBM)


def in_vmem(value):
    return pltpu.with_memory_space_constraint(value, pltpu.VMEM)


def fold_kernel(order, at, gain_ref, w_hbm, out_ref, sems):
    lanes = gain_ref.shape[1]
    size = w_hbm.shape[1] // len(order)
    per = size // lanes

    def fetch(n):
        start = pl.multiple_of(at[order[n]] * size, size)
        return pltpu.make_async_copy(
            w_hbm.at[:, pl.ds(start, size), :], out_ref.at[:, n * size : (n + 1) * size, :], sems.at[n]
        )

    for n in range(len(order)):
        fetch(n).start()
    for n in range(len(order)):
        columns = jnp.transpose(gain_ref[pl.ds(at[order[n]] * per, per), :])
        fetch(n).wait()
        for piece in range(per):
            first = n * size + piece * lanes
            for group in range(w_hbm.shape[0]):
                here = (group, slice(first, first + lanes), slice(None))
                scaled = out_ref[here].astype(F32) * columns[:, piece : piece + 1]
                out_ref[here] = scaled.astype(BF16)


def fold_gain(order, at, gain, weights):
    depth = weights.shape[1]
    lanes = math.gcd(depth // len(order), 128)
    return pl.pallas_call(
        functools.partial(fold_kernel, order),
        out_shape=pltpu.VMEM(weights.shape, BF16),
        in_specs=[SMEM, VMEM, pl.BlockSpec(memory_space=pltpu.HBM)],
        out_specs=VMEM,
        scratch_shapes=[pltpu.SemaphoreType.DMA((len(order),))],
        compiler_params=pltpu.CompilerParams(vmem_limit_bytes=16 << 20),
        cost_estimate=pl.CostEstimate(
            flops=weights.size, bytes_accessed=4 * weights.size, transcendentals=0
        ),
        name="fold_gain",
    )(at, in_hbm(gain.reshape(depth // lanes, lanes)), in_hbm(weights))


def place_kernel(targets, *refs):
    blocks, wide, sems = refs[: len(targets)], refs[-2], refs[-1]
    copies = []
    for n, (block, (row, lane)) in enumerate(zip(blocks, targets)):
        rows, width = block.shape
        here = wide.at[row : row + rows, lane : lane + width]
        copies.append(pltpu.make_async_copy(block, here, sems.at[n]))
    for copy in copies:
        copy.start()
    for copy in copies:
        copy.wait()


def placed(targets, blocks, wide, shape):
    operands = [*blocks] + ([] if wide is None else [in_vmem(wide)])
    return pl.pallas_call(
        functools.partial(place_kernel, targets),
        out_shape=pltpu.VMEM(shape, BF16),
        in_specs=[pl.BlockSpec(memory_space=pl.ANY)] * len(operands),
        out_specs=pl.BlockSpec(memory_space=pl.ANY),
        scratch_shapes=[pltpu.SemaphoreType.DMA((len(targets),))],
        input_output_aliases={} if wide is None else {len(blocks): 0},
        compiler_params=pltpu.CompilerParams(vmem_limit_bytes=1 << 20),
        cost_estimate=pl.CostEstimate(flops=0, bytes_accessed=1 << 20, transcendentals=0),
        name="place",
    )(*operands)


def unit_rows(values, factor):
    power = jnp.sum(values * values, axis=-1, keepdims=True)
    return (values * (lax.rsqrt(power + 1e-06) * factor)).astype(BF16)


def project_kernel(head_size, base, groups, factor, wide, w_ref, out_ref):
    rows = out_ref.shape[0]
    depth, out_width = w_ref.shape[1:]
    tile = math.gcd(rows, 256)
    for first in range(0, rows, tile):
        here = slice(first, first + tile)
        there = slice(base + first, base + first + tile)
        power = None
        for lane in range(0, depth, 128):
            values = wide[there, lane : lane + 128].astype(F32)
            power = values * values if power is None else power + values * values
        scale = lax.rsqrt(jnp.sum(power, axis=-1, keepdims=True) * (1.0 / depth) + 1e-06)
        for number, group in enumerate(groups):
            start = number * out_width
            product = jnp.dot(wide[there, :], w_ref[group], preferred_element_type=F32) * scale
            if group == 2:
                out_ref[here, start : start + out_width] = product.astype(BF16)
                continue
            for head in range(out_width // head_size):
                lanes = slice(head * head_size, (head + 1) * head_size)
                amount = factor[head] * LOG2E if group == 0 else 1.0
                out_ref[here, start + head * head_size : start + (head + 1) * head_size] = unit_rows(
                    product[:, lanes], amount
                )


def project(factor, wide, weights, base, rows, groups, head_size):
    depth, out_width = weights.shape[1:]
    return pl.pallas_call(
        functools.partial(project_kernel, head_size, base, groups),
        out_shape=pltpu.VMEM((rows, len(groups) * out_width), BF16),
        in_specs=[SMEM] + [VMEM] * 2,
        out_specs=VMEM,
        compiler_params=pltpu.CompilerParams(vmem_limit_bytes=16 << 20),
        cost_estimate=pl.CostEstimate(
            flops=2 * rows * depth * len(groups) * out_width,
            bytes_accessed=2 * depth * (rows + len(groups) * out_width),
            transcendentals=0,
        ),
        name="project_q" if groups == (0,) else "project_kv",
    )(in_hbm(factor), in_vmem(wide), in_vmem(weights))


def attend_blocks(sources, ids, q_first, q_refs, id_col, id_row, kv_refs, v_ones, acc, head_size):
    heads = q_refs[0].shape[1] // head_size
    keys = kv_refs[0].shape[0]
    rows = q_refs[0].shape[0]
    for number, kv_ref in enumerate(kv_refs):
        for head in range(heads):
            start = (heads + head) * head_size
            v_ones[head, :, :head_size] = kv_ref[:, start : start + head_size]
            v_ones[head, :, head_size:] = jnp.ones((keys, head_size), BF16)
        first = sources[number]
        key_low, key_high = ids[first], ids[first + keys - 1]
        tile = math.gcd(rows, 256)
        for chunk, q_ref in enumerate(q_refs):

            @pl.loop(0, rows // tile)
            def _(index):
                here = pl.ds(pl.multiple_of(index * tile, tile), tile)
                base = chunk * rows + index * tile
                there = pl.ds(pl.multiple_of(base, tile), tile)
                q_low = ids[q_first + base]
                q_high = ids[q_first + base + tile - 1]

                def add(masked):
                    if masked:
                        allowed = id_row[first // keys] <= id_col[there, :]
                    for head in range(heads):
                        lanes = slice(head * head_size, (head + 1) * head_size)
                        score = lax.dot_general(
                            q_ref[here, lanes],
                            kv_ref[:, lanes],
                            (((1,), (1,)), ((), ())),
                            preferred_element_type=F32,
                        )
                        weight = jnp.exp2(score)
                        if masked:
                            weight = jnp.where(allowed, weight, 0.0)
                        wide = slice(2 * head * head_size, 2 * (head + 1) * head_size)
                        acc[there, wide] += jnp.dot(
                            weight.astype(BF16), v_ones[head], preferred_element_type=F32
                        )

                @pl.when(key_high <= q_low)
                def _():
                    add(False)

                @pl.when((key_high > q_low) & (key_low <= q_high))
                def _():
                    add(True)


def attend_kernel(
    count_q, count_kv, head_size, has_acc, count_out, count_streams, info, ids, *refs
):
    q_refs, rest = refs[:count_q], refs[count_q:]
    (id_col, id_row), rest = rest[:2], rest[2:]
    kv_refs, rest = rest[:count_kv], rest[count_kv:]
    rows, width = q_refs[0].shape
    if has_acc:
        acc_in, rest = rest[0], rest[1:]
    if count_out:
        w_ref, outs, (v_ones, acc, attended) = rest[0], rest[1:-3], rest[-3:]
    else:
        acc_out, v_ones, acc = rest
    acc[...] = acc_in[...] if has_acc else jnp.zeros_like(acc)
    sources = [info[number] for number in range(count_kv)]
    attend_blocks(
        sources, ids, info[count_kv], q_refs, id_col, id_row, kv_refs, v_ones, acc, head_size
    )
    if not count_out:
        acc_out[...] = acc[...]
        return
    for head in range(width // head_size):
        start = 2 * head * head_size
        attended[:, head * head_size : (head + 1) * head_size] = (
            acc[:, start : start + head_size]
            / acc[:, start + head_size : start + 2 * head_size]
        ).astype(BF16)
    out_width = outs[0].shape[1]
    for number, out in enumerate(outs):
        lane = info[count_kv + 1 + number] * out_width
        first = number * count_streams // count_out * out.shape[0]
        out[...] = jnp.dot(
            attended[first : first + out.shape[0], :],
            w_ref[:, pl.ds(pl.multiple_of(lane, out_width), out_width)],
            preferred_element_type=F32,
        ).astype(BF16)


def attend(info, ids, queries, id_col, id_row, kvs, head_size, acc=None, w_out=None, streams=0):
    rows, width = queries[0].shape
    total = rows * len(queries)
    keys = kvs[0].shape[0]
    heads = width // head_size
    count_out = streams * w_out.shape[1] // width if streams else 0
    scratch = [
        pltpu.VMEM((heads, keys, 2 * head_size), BF16),
        pltpu.VMEM((total, 2 * width), F32),
    ]
    operands = [*map(in_vmem, queries), id_col, in_hbm(id_row), *map(in_vmem, kvs)]
    if acc is not None:
        operands.append(in_vmem(acc))
    if count_out:
        operands.append(in_hbm(w_out))
        scratch.append(pltpu.VMEM((total, width), BF16))
        shape = pltpu.VMEM((total // streams, w_out.shape[1] * streams // count_out), BF16)
    else:
        shape = pltpu.VMEM((total, 2 * width), F32)
    outs = count_out or 1
    return pl.pallas_call(
        functools.partial(
            attend_kernel, len(queries), len(kvs), head_size, acc is not None, count_out, streams
        ),
        out_shape=(shape,) * outs,
        in_specs=[SMEM, SMEM] + [VMEM] * len(operands),
        out_specs=(VMEM,) * outs,
        scratch_shapes=scratch,
        compiler_params=pltpu.CompilerParams(
            vmem_limit_bytes=(16 << 20) + 2 * kvs[0].size * 2 * len(kvs)
        ),
        cost_estimate=pl.CostEstimate(flops=1 << 20, bytes_accessed=1 << 10, transcendentals=0),
        name="attend_last" if count_out else "attend",
    )(info, in_hbm(ids), *operands)


def total_of(*parts):
    return sum(part.astype(F32) for part in parts).astype(BF16)


def body(mesh_shape, tokens, norm_gain, w_qkv, head_scale, w_out, scale_ids):
    ring, seqs = mesh_shape["head"], mesh_shape["seq"]
    outer = seqs // 2
    rows, width = tokens.shape
    half = rows // 2
    head_size = w_qkv.shape[2] // head_scale.shape[0]
    head_at, seq_at = lax.axis_index("head"), lax.axis_index("seq")
    place = ring_place(head_at, ring)
    chip, core = seq_at // 2, seq_at % 2
    index_at = lambda offset: ring_index((place + offset + ring) % ring, ring)
    numbers = lambda values: jnp.stack(values).astype(jnp.int32)
    id_row = scale_ids.reshape(-1, 1, half)
    id_col = lax.dynamic_slice_in_dim(scale_ids, seq_at * rows, rows)[:, None]
    at = [index_at(offset) for offset in range(ring)]

    streams, ways = (0, 1), ((0, 1), (1, -1))
    farthest = ring // 2
    reach = [(farthest, farthest - 1), (farthest - 1, farthest)]

    order = [0] + [sign * step % ring for step in range(1, farthest) for sign in (-1, 1)] + [farthest]
    held = [[tokens[s * half : (s + 1) * half]] * 2 for s in streams]
    wide, blocks, targets = None, [in_hbm(tokens)], [(0, 0)]
    for step in range(1, farthest + 1):
        for s in streams:
            for way, sign in ways:
                if step <= reach[s][way]:
                    held[s][way] = along(held[s][way], sign, ring)
        if step == 1:
            held[1][1], weights = lax.optimization_barrier(
                (held[1][1], fold_gain(order, numbers(at), norm_gain, w_qkv))
            )
        elif step == 2:
            wide = placed(targets, blocks, wide, (rows, ring * width))
            blocks, targets = [], []
        elif step == 3:
            held[1][1], wide = lax.optimization_barrier(
                (held[1][1], placed(targets, blocks, wide, (rows, ring * width)))
            )
            blocks, targets = [], []
        if step < farthest:
            for s in streams:
                for way, sign in ways:
                    blocks.append(in_vmem(held[s][way]))
                    targets.append((s * half, (2 * step - 1 + way) * width))
    wide = placed(targets, blocks, wide, (rows, ring * width))
    kvs = []
    for s, last in enumerate((held[0][0], held[1][1])):
        wide = placed([(s * half, (ring - 1) * width)], [in_vmem(last)], wide, (rows, ring * width))
        kv = project(head_scale, wide, weights, s * half, half, (1, 2), head_size)
        wide, kv = lax.optimization_barrier((wide, kv))
        kvs.append(kv)
    query = project(head_scale, wide, weights, 0, rows, (0,), head_size)

    far, straight, crossed = [[], []], [[], []], [[], []]
    for step in range(outer):
        source = 2 * ((chip + outer - step) % outer)
        for s in streams:
            straight[s].append((source + core) * rows + s * half)
            crossed[s].append((source + 1 - core) * rows + s * half)
            if step:
                far[s].append(lax.ppermute(kvs[s], "seq", [
                    (2 * a + b, 2 * ((a + step) % outer) + b) for a in range(outer) for b in (0, 1)
                ]))
    first = [seq_at * rows]
    groups = [[(kvs[0], straight[0][0]), (swapped(kvs[0], seqs), crossed[0][0]), (kvs[1], straight[1][0])]]
    groups.append(list(zip(far[0], straight[0][1:])))
    groups.append([*zip(far[1], straight[1][1:]), (swapped(kvs[1], seqs), crossed[1][0])])
    acc = None
    for number, group in enumerate(groups):
        keys, places = [key for key, place in group], [place for key, place in group]
        if number:
            acc, keys = lax.optimization_barrier((acc, keys))
        if number == 2:
            far[1] = keys[:-1]
            far_crossed = [swapped(block, seqs) for s in streams for block in far[s]]
        info = numbers(places + first)
        (acc,) = attend(info, scale_ids, [query], id_col, id_row, keys, head_size, acc)

    goals = [[*range(up, 0, -1), *range(-down, 0), 0] for up, down in reach]
    info = numbers(crossed[0][1:] + crossed[1][1:] + first + [at[goal % ring] for goal in goals[0] + goals[1]])
    parts = attend(
        info, scale_ids, [query], id_col, id_row, far_crossed, head_size, acc, w_out, len(streams)
    )
    parts = [dict(zip(goals[s], parts[s * ring : (s + 1) * ring])) for s in streams]
    sums = [[None, None] for s in streams]
    for step in range(farthest, 0, -1):
        for s in streams:
            for way, sign in ways:
                if step <= reach[s][way]:
                    part = parts[s][sign * step]
                    if sums[s][way] is not None:
                        part = total_of(part, sums[s][way])
                    sums[s][way] = along(part, sign, ring)
    return jnp.concatenate([total_of(parts[s][0], *sums[s]) for s in streams])


def solution(mesh):
    placed = (P("seq", "head"), P(), P(None, None, "head"), P("head"), P("head", None), P())
    return jax.shard_map(
        functools.partial(body, dict(mesh.shape)),
        mesh=mesh,
        in_specs=placed,
        out_specs=P("seq", "head"),
        check_vma=False,
    )
```

```python
import functools
import math

import jax
import jax.numpy as jnp
from jax import lax
from jax.experimental import pallas as pl
from jax.experimental.pallas import tpu as pltpu
from jax.sharding import PartitionSpec as P

LOG2E = math.log2(math.e)
VMEM = pl.BlockSpec(memory_space=pltpu.VMEM)
SMEM = pl.BlockSpec(memory_space=pltpu.SMEM)
F32 = jnp.float32
BF16 = jnp.bfloat16


def ring_order(count):
    line = count // 2
    return [2 * z for z in range(line)] + [2 * z + 1 for z in reversed(range(line))]


def ring_place(index, count):
    return jnp.where(index % 2 == 0, index // 2, count - 1 - index // 2)


def ring_index(place, count):
    return jnp.where(place < count // 2, 2 * place, 2 * (count - 1 - place) + 1)


def along(value, step, count):
    order = ring_order(count)
    return lax.ppermute(
        value, "head", [(order[p], order[(p + step) % count]) for p in range(count)]
    )


def swapped(value, seq_count):
    return lax.ppermute(value, "seq", [(seq, seq + 1 - 2 * (seq % 2)) for seq in range(seq_count)])


def in_hbm(value):
    return pltpu.with_memory_space_constraint(value, pltpu.HBM)


def in_vmem(value):
    return pltpu.with_memory_space_constraint(value, pltpu.VMEM)


def fold_kernel(order, groups, has_tokens, at, gain_ref, w_hbm, *refs):
    sems = refs[-1]
    out_ref = refs[1] if has_tokens else refs[0]
    lanes = gain_ref.shape[1]
    size = w_hbm.shape[1] // len(order)
    per = size // lanes

    def fetch(n):
        start = pl.multiple_of(at[order[n]] * size, size)
        return pltpu.make_async_copy(
            w_hbm.at[groups[0] : groups[0] + len(groups), pl.ds(start, size), :],
            out_ref.at[:, n * size : (n + 1) * size, :],
            sems.at[n],
        )

    for n in range(len(order)):
        fetch(n).start()
    if has_tokens:
        tokens, wide = refs[0], refs[2]
        own = pltpu.make_async_copy(tokens, wide.at[:, : tokens.shape[1]], sems.at[len(order)])
        own.start()
    for n in range(len(order)):
        columns = jnp.transpose(gain_ref[pl.ds(at[order[n]] * per, per), :])
        fetch(n).wait()
        for piece in range(per):
            first = n * size + piece * lanes
            for group in range(len(groups)):
                here = (group, slice(first, first + lanes), slice(None))
                scaled = out_ref[here].astype(F32) * columns[:, piece : piece + 1]
                out_ref[here] = scaled.astype(BF16)
    if has_tokens:
        own.wait()


def fold_gain(order, groups, at, gain, weights, tokens=None):
    depth, width = weights.shape[1:]
    lanes = math.gcd(depth // len(order), 128)
    hbm = pl.BlockSpec(memory_space=pltpu.HBM)
    operands = [at, in_hbm(gain.reshape(depth // lanes, lanes)), in_hbm(weights)]
    shapes, specs = [pltpu.VMEM((len(groups), depth, width), BF16)], [VMEM]
    if tokens is not None:
        operands.append(in_hbm(tokens))
        shapes.append(pltpu.VMEM((tokens.shape[0], depth), BF16))
        specs.append(pl.BlockSpec(memory_space=pl.ANY))
    size = len(groups) * depth * width
    return pl.pallas_call(
        functools.partial(fold_kernel, order, groups, tokens is not None),
        out_shape=tuple(shapes),
        in_specs=[SMEM, VMEM, hbm] + [hbm] * (len(operands) - 3),
        out_specs=tuple(specs),
        scratch_shapes=[pltpu.SemaphoreType.DMA((len(order) + 1,))],
        compiler_params=pltpu.CompilerParams(vmem_limit_bytes=16 << 20),
        cost_estimate=pl.CostEstimate(flops=size, bytes_accessed=4 * size, transcendentals=0),
        name="fold_gain",
    )(*operands)


def place_kernel(targets, *refs):
    blocks, wide, sems = refs[: len(targets)], refs[-2], refs[-1]
    copies = []
    for n, (block, (row, lane)) in enumerate(zip(blocks, targets)):
        rows, width = block.shape
        here = wide.at[row : row + rows, lane : lane + width]
        copies.append(pltpu.make_async_copy(block, here, sems.at[n]))
    for copy in copies:
        copy.start()
    for copy in copies:
        copy.wait()


def placed(targets, blocks, wide):
    operands = [*map(in_vmem, blocks), in_vmem(wide)]
    return pl.pallas_call(
        functools.partial(place_kernel, targets),
        out_shape=pltpu.VMEM(wide.shape, BF16),
        in_specs=[pl.BlockSpec(memory_space=pl.ANY)] * len(operands),
        out_specs=pl.BlockSpec(memory_space=pl.ANY),
        scratch_shapes=[pltpu.SemaphoreType.DMA((len(targets),))],
        input_output_aliases={len(blocks): 0},
        compiler_params=pltpu.CompilerParams(vmem_limit_bytes=1 << 20),
        cost_estimate=pl.CostEstimate(flops=0, bytes_accessed=1 << 20, transcendentals=0),
        name="place",
    )(*operands)


def unit_rows(values, factor):
    power = jnp.sum(values * values, axis=-1, keepdims=True)
    return (values * (lax.rsqrt(power + 1e-06) * factor)).astype(BF16)


def project_kernel(head_size, base, groups, factor, wide, w_ref, out_ref):
    rows = out_ref.shape[0]
    depth, out_width = w_ref.shape[1:]
    tile = math.gcd(rows, 256)
    for first in range(0, rows, tile):
        here = slice(first, first + tile)
        there = slice(base + first, base + first + tile)
        power = None
        for lane in range(0, depth, 128):
            values = wide[there, lane : lane + 128].astype(F32)
            power = values * values if power is None else power + values * values
        scale = lax.rsqrt(jnp.sum(power, axis=-1, keepdims=True) * (1.0 / depth) + 1e-06)
        for number, group in enumerate(groups):
            start = number * out_width
            product = jnp.dot(wide[there, :], w_ref[number], preferred_element_type=F32) * scale
            if group == 2:
                out_ref[here, start : start + out_width] = product.astype(BF16)
                continue
            for head in range(out_width // head_size):
                lanes = slice(head * head_size, (head + 1) * head_size)
                amount = factor[head] * LOG2E if group == 0 else 1.0
                out_ref[here, start + head * head_size : start + (head + 1) * head_size] = unit_rows(
                    product[:, lanes], amount
                )


def project(factor, wide, weights, base, rows, groups, head_size):
    depth, out_width = weights.shape[1:]
    return pl.pallas_call(
        functools.partial(project_kernel, head_size, base, groups),
        out_shape=pltpu.VMEM((rows, len(groups) * out_width), BF16),
        in_specs=[SMEM] + [VMEM] * 2,
        out_specs=VMEM,
        compiler_params=pltpu.CompilerParams(vmem_limit_bytes=16 << 20),
        cost_estimate=pl.CostEstimate(
            flops=2 * rows * depth * len(groups) * out_width,
            bytes_accessed=2 * depth * (rows + len(groups) * out_width),
            transcendentals=0,
        ),
        name="project_q" if groups == (0,) else "project_kv",
    )(in_hbm(factor), in_vmem(wide), in_vmem(weights))


def attend_blocks(sources, ids, q_first, q_ref, id_col, id_row, kv_refs, v_ones, acc, head_size):
    rows, width = q_ref.shape
    heads = width // head_size
    keys = kv_refs[0].shape[0]
    piece = id_row.shape[2]
    tile = math.gcd(rows, 256)
    for number, kv_ref in enumerate(kv_refs):
        for head in range(heads):
            start = (heads + head) * head_size
            v_ones[head, :, :head_size] = kv_ref[:, start : start + head_size]
            v_ones[head, :, head_size:] = jnp.ones((keys, head_size), BF16)
        first = sources[number]
        key_low, key_high = ids[first], ids[first + keys - 1]

        @pl.loop(0, rows // tile)
        def _(index):
            base = pl.multiple_of(index * tile, tile)
            here = pl.ds(base, tile)
            q_low, q_high = ids[q_first + base], ids[q_first + base + tile - 1]

            def add(low, high, masked):
                if masked:
                    allowed = id_row[first // piece + low // piece] <= id_col[here, :]
                for head in range(heads):
                    lanes = slice(head * head_size, (head + 1) * head_size)
                    score = lax.dot_general(
                        q_ref[here, lanes],
                        kv_ref[low:high, lanes],
                        (((1,), (1,)), ((), ())),
                        preferred_element_type=F32,
                    )
                    weight = jnp.exp2(score)
                    if masked:
                        weight = jnp.where(allowed, weight, 0.0)
                    spread = slice(2 * head * head_size, 2 * (head + 1) * head_size)
                    acc[here, spread] += jnp.dot(
                        weight.astype(BF16), v_ones[head, low:high, :], preferred_element_type=F32
                    )

            @pl.when(key_high <= q_low)
            def _():
                add(0, keys, False)

            @pl.when((key_high > q_low) & (key_low <= q_high))
            def _():
                for low in range(0, keys, piece):
                    piece_low, piece_high = ids[first + low], ids[first + low + piece - 1]

                    @pl.when(piece_high <= q_low)
                    def _():
                        add(low, low + piece, False)

                    @pl.when((piece_high > q_low) & (piece_low <= q_high))
                    def _():
                        add(low, low + piece, True)


def attend_kernel(
    count_kv, head_size, has_acc, count_out, count_streams, info, ids, q_ref, id_col, id_row, *refs
):
    kv_refs, rest = refs[:count_kv], refs[count_kv:]
    width = q_ref.shape[1]
    if has_acc:
        acc_in, rest = rest[0], rest[1:]
    if count_out:
        w_ref, outs, (v_ones, acc, attended) = rest[0], rest[1:-3], rest[-3:]
    else:
        acc_out, v_ones, acc = rest
    acc[...] = acc_in[...] if has_acc else jnp.zeros_like(acc)
    sources = [info[number] for number in range(count_kv)]
    attend_blocks(
        sources, ids, info[count_kv], q_ref, id_col, id_row, kv_refs, v_ones, acc, head_size
    )
    if not count_out:
        acc_out[...] = acc[...]
        return
    for head in range(width // head_size):
        start = 2 * head * head_size
        attended[:, head * head_size : (head + 1) * head_size] = (
            acc[:, start : start + head_size]
            / acc[:, start + head_size : start + 2 * head_size]
        ).astype(BF16)
    out_width = outs[0].shape[1]
    for number, out in enumerate(outs):
        lane = info[count_kv + 1 + number] * out_width
        first = number * count_streams // count_out * out.shape[0]
        out[...] = jnp.dot(
            attended[first : first + out.shape[0], :],
            w_ref[:, pl.ds(pl.multiple_of(lane, out_width), out_width)],
            preferred_element_type=F32,
        ).astype(BF16)


def attend(info, ids, query, id_col, id_row, kvs, head_size, acc=None, w_out=None, streams=0):
    total, width = query.shape
    keys = kvs[0].shape[0]
    heads = width // head_size
    count_out = streams * w_out.shape[1] // width if streams else 0
    scratch = [
        pltpu.VMEM((heads, keys, 2 * head_size), BF16),
        pltpu.VMEM((total, 2 * width), F32),
    ]
    operands = [in_vmem(query), id_col, in_hbm(id_row), *map(in_vmem, kvs)]
    if acc is not None:
        operands.append(in_vmem(acc))
    if count_out:
        operands.append(in_hbm(w_out))
        scratch.append(pltpu.VMEM((total, width), BF16))
        shape = pltpu.VMEM((total // streams, w_out.shape[1] * streams // count_out), BF16)
    else:
        shape = pltpu.VMEM((total, 2 * width), F32)
    outs = count_out or 1
    return pl.pallas_call(
        functools.partial(
            attend_kernel, len(kvs), head_size, acc is not None, count_out, streams
        ),
        out_shape=(shape,) * outs,
        in_specs=[SMEM, SMEM] + [VMEM] * len(operands),
        out_specs=(VMEM,) * outs,
        scratch_shapes=scratch,
        compiler_params=pltpu.CompilerParams(
            vmem_limit_bytes=(16 << 20) + 2 * kvs[0].size * 2 * len(kvs)
        ),
        cost_estimate=pl.CostEstimate(flops=1 << 20, bytes_accessed=1 << 10, transcendentals=0),
        name="attend_last" if count_out else "attend",
    )(info, in_hbm(ids), *operands)


def total_of(*parts):
    return sum(part.astype(F32) for part in parts).astype(BF16)


def body(mesh_shape, tokens, norm_gain, w_qkv, head_scale, w_out, scale_ids):
    ring, seqs = mesh_shape["head"], mesh_shape["seq"]
    outer = seqs // 2
    rows, width = tokens.shape
    half = rows // 2
    head_size = w_qkv.shape[2] // head_scale.shape[0]
    head_at, seq_at = lax.axis_index("head"), lax.axis_index("seq")
    place = ring_place(head_at, ring)
    chip, core = seq_at // 2, seq_at % 2
    index_at = lambda offset: ring_index((place + offset + ring) % ring, ring)
    numbers = lambda values: jnp.stack(values).astype(jnp.int32)
    id_row = scale_ids.reshape(-1, 1, half)
    id_col = lax.dynamic_slice_in_dim(scale_ids, seq_at * rows, rows)[:, None]
    at = [index_at(offset) for offset in range(ring)]

    streams = (0, 1)
    farthest = ring // 2
    reach = [(farthest, farthest - 1), (farthest - 1, farthest)]
    lanes = ((0, 0, 1), (1, 1, -1), (0, 1, -1), (1, 0, 1))

    order = [0] + [sign * step % ring for step in range(1, farthest) for sign in (-1, 1)] + [farthest]
    held = [[tokens[s * half : (s + 1) * half]] * 2 for s in streams]
    wide, blocks, targets = None, [], []
    for step in range(1, farthest + 1):
        for s, way, sign in lanes:
            if step <= reach[s][way]:
                held[s][way] = along(held[s][way], sign, ring)
        if step == 1:
            held[0][0], (w_kv, wide) = lax.optimization_barrier(
                (held[0][0], fold_gain(order, (1, 2), numbers(at), norm_gain, w_qkv, tokens))
            )
        elif step == 2:
            held[0][0], (w_q,) = lax.optimization_barrier(
                (held[0][0], fold_gain(order, (0,), numbers(at), norm_gain, w_qkv))
            )
        if blocks:
            wide = placed(targets, blocks, wide)
        columns = [(2 * step - 1 + way) * width for way in (0, 1)]
        if step == farthest:
            columns = [(ring - 1) * width] * 2
        blocks = [held[s][way] for s, way, sign in lanes if step <= reach[s][way]]
        targets = [(s * half, columns[way]) for s, way, sign in lanes if step <= reach[s][way]]
    wide = placed(targets, blocks, wide)
    kv = project(head_scale, wide, w_kv, 0, rows, (1, 2), head_size)
    query = project(head_scale, wide, w_q, 0, rows, (0,), head_size)

    far, straight, crossed = [], [], []
    for step in range(outer):
        source = 2 * ((chip + outer - step) % outer)
        straight.append((source + core) * rows)
        crossed.append((source + 1 - core) * rows)
        if step:
            far.append(lax.ppermute(kv, "seq", [
                (2 * a + b, 2 * ((a + step) % outer) + b) for a in range(outer) for b in (0, 1)
            ]))
    first = [seq_at * rows]
    info = numbers(straight[:1] + crossed[:1] + first)
    keys = [kv, swapped(kv, seqs)]
    (acc,) = attend(info, scale_ids, query, id_col, id_row, keys, head_size)
    acc, far = lax.optimization_barrier((acc, far))
    far_crossed = [swapped(block, seqs) for block in far]
    info = numbers(straight[1:] + first)
    (acc,) = attend(info, scale_ids, query, id_col, id_row, far, head_size, acc)

    goals = [[*range(up, 0, -1), *range(-down, 0), 0] for up, down in reach]
    info = numbers(crossed[1:] + first + [at[goal % ring] for goal in goals[0] + goals[1]])
    parts = attend(
        info, scale_ids, query, id_col, id_row, far_crossed, head_size, acc, w_out, len(streams)
    )
    parts = [dict(zip(goals[s], parts[s * ring : (s + 1) * ring])) for s in streams]
    sums = [[None, None] for s in streams]
    for step in range(farthest, 0, -1):
        for s, way, sign in lanes:
            if step <= reach[s][way]:
                part = parts[s][sign * step]
                if sums[s][way] is not None:
                    part = total_of(part, sums[s][way])
                sums[s][way] = along(part, sign, ring)
    ends = lax.optimization_barrier([sums[s][way] for s, way, sign in lanes[::-1]])
    for (s, way, sign), end in zip(lanes[::-1], ends):
        sums[s][way] = end
    return jnp.concatenate([total_of(parts[s][0], *sums[s]) for s in streams])


def solution(mesh):
    placed = (P("seq", "head"), P(), P(None, None, "head"), P("head"), P("head", None), P())
    return jax.shard_map(
        functools.partial(body, dict(mesh.shape)),
        mesh=mesh,
        in_specs=placed,
        out_specs=P("seq", "head"),
        check_vma=False,
    )
```

```python
import functools
import math

import jax
import jax.numpy as jnp
from jax import lax
from jax.experimental import pallas as pl
from jax.experimental.pallas import tpu as pltpu
from jax.sharding import PartitionSpec as P

LOG2E = math.log2(math.e)
VMEM = pl.BlockSpec(memory_space=pltpu.VMEM)
SMEM = pl.BlockSpec(memory_space=pltpu.SMEM)
F32 = jnp.float32
BF16 = jnp.bfloat16


def ring_order(count):
    line = count // 2
    return [2 * z for z in range(line)] + [2 * z + 1 for z in reversed(range(line))]


def ring_place(index, count):
    return jnp.where(index % 2 == 0, index // 2, count - 1 - index // 2)


def ring_index(place, count):
    return jnp.where(place < count // 2, 2 * place, 2 * (count - 1 - place) + 1)


def along(value, step, count):
    order = ring_order(count)
    return lax.ppermute(
        value, "head", [(order[p], order[(p + step) % count]) for p in range(count)]
    )


def swapped(value, seq_count):
    return lax.ppermute(value, "seq", [(seq, seq + 1 - 2 * (seq % 2)) for seq in range(seq_count)])


def in_hbm(value):
    return pltpu.with_memory_space_constraint(value, pltpu.HBM)


def in_vmem(value):
    return pltpu.with_memory_space_constraint(value, pltpu.VMEM)


def fold_kernel(order, at, gain_ref, w_hbm, out_ref, sems):
    lanes = gain_ref.shape[1]
    size = w_hbm.shape[1] // len(order)
    per = size // lanes

    def fetch(n):
        start = pl.multiple_of(at[order[n]] * size, size)
        return pltpu.make_async_copy(
            w_hbm.at[:, pl.ds(start, size), :], out_ref.at[:, n * size : (n + 1) * size, :], sems.at[n]
        )

    for n in range(len(order)):
        fetch(n).start()
    for n in range(len(order)):
        columns = jnp.transpose(gain_ref[pl.ds(at[order[n]] * per, per), :])
        fetch(n).wait()
        for piece in range(per):
            first = n * size + piece * lanes
            for group in range(w_hbm.shape[0]):
                here = (group, slice(first, first + lanes), slice(None))
                scaled = out_ref[here].astype(F32) * columns[:, piece : piece + 1]
                out_ref[here] = scaled.astype(BF16)


def fold_gain(order, at, gain, weights):
    depth = weights.shape[1]
    lanes = math.gcd(depth // len(order), 128)
    return pl.pallas_call(
        functools.partial(fold_kernel, order),
        out_shape=pltpu.VMEM(weights.shape, BF16),
        in_specs=[SMEM, VMEM, pl.BlockSpec(memory_space=pltpu.HBM)],
        out_specs=VMEM,
        scratch_shapes=[pltpu.SemaphoreType.DMA((len(order),))],
        compiler_params=pltpu.CompilerParams(vmem_limit_bytes=16 << 20),
        cost_estimate=pl.CostEstimate(
            flops=weights.size, bytes_accessed=4 * weights.size, transcendentals=0
        ),
        name="fold_gain",
    )(at, in_hbm(gain.reshape(depth // lanes, lanes)), in_hbm(weights))


def place_kernel(targets, *refs):
    blocks, wide, sems = refs[: len(targets)], refs[-2], refs[-1]
    copies = []
    for n, (block, (row, lane)) in enumerate(zip(blocks, targets)):
        rows, width = block.shape
        here = wide.at[row : row + rows, lane : lane + width]
        copies.append(pltpu.make_async_copy(block, here, sems.at[n]))
    for copy in copies:
        copy.start()
    for copy in copies:
        copy.wait()


def placed(targets, blocks, wide, shape):
    operands = [*blocks] + ([] if wide is None else [in_vmem(wide)])
    return pl.pallas_call(
        functools.partial(place_kernel, targets),
        out_shape=pltpu.VMEM(shape, BF16),
        in_specs=[pl.BlockSpec(memory_space=pl.ANY)] * len(operands),
        out_specs=pl.BlockSpec(memory_space=pl.ANY),
        scratch_shapes=[pltpu.SemaphoreType.DMA((len(targets),))],
        input_output_aliases={} if wide is None else {len(blocks): 0},
        compiler_params=pltpu.CompilerParams(vmem_limit_bytes=1 << 20),
        cost_estimate=pl.CostEstimate(flops=0, bytes_accessed=1 << 20, transcendentals=0),
        name="place",
    )(*operands)


def project_kernel(head_size, factor, wide, w_ref, *refs):
    count = len(refs) // 2 - 1
    lasts, (q_ref, kv_ref), pieces = refs[:count], refs[count : count + 2], refs[count + 2 :]
    rows, width = lasts[0].shape
    depth, out_width = w_ref.shape[1:]
    done = depth - width
    for stream, last in enumerate(lasts):
        here = slice(stream * rows, (stream + 1) * rows)
        q, k, v = (
            jnp.dot(wide[here, :done], w_ref[group, :done, :], preferred_element_type=F32)
            + jnp.dot(last[...], w_ref[group, done:, :], preferred_element_type=F32)
            for group in range(3)
        )
        power = None
        for lane in range(0, depth, 128):
            if lane < done:
                values = wide[here, lane : lane + 128].astype(F32)
            else:
                values = last[:, lane - done : lane - done + 128].astype(F32)
            power = values * values if power is None else power + values * values
        scale = lax.rsqrt(jnp.sum(power, axis=-1, keepdims=True) * (1.0 / depth) + 1e-06)
        q, k, v = q * scale, k * scale, v * scale
        for head in range(out_width // head_size):
            lanes = slice(head * head_size, (head + 1) * head_size)
            qh, kh = q[:, lanes], k[:, lanes]
            q_size = lax.rsqrt(jnp.sum(qh * qh, axis=-1, keepdims=True) + 1e-06)
            k_size = lax.rsqrt(jnp.sum(kh * kh, axis=-1, keepdims=True) + 1e-06)
            q_ref[here, lanes] = (qh * (q_size * (factor[head] * LOG2E))).astype(BF16)
            kv_ref[here, lanes] = (kh * k_size).astype(BF16)
        kv_ref[here, out_width:] = v.astype(BF16)
        pieces[stream][...] = kv_ref[here, :]


def project(factor, wide, weights, lasts, head_size):
    rows = wide.shape[0]
    groups, depth, out_width = weights.shape
    return pl.pallas_call(
        functools.partial(project_kernel, head_size),
        out_shape=(
            pltpu.VMEM((rows, out_width), BF16),
            pltpu.VMEM((rows, 2 * out_width), BF16),
            *[pltpu.VMEM((rows // len(lasts), 2 * out_width), BF16)] * len(lasts),
        ),
        in_specs=[SMEM] + [VMEM] * (2 + len(lasts)),
        out_specs=(VMEM,) * (2 + len(lasts)),
        compiler_params=pltpu.CompilerParams(vmem_limit_bytes=16 << 20),
        cost_estimate=pl.CostEstimate(
            flops=2 * rows * depth * groups * out_width,
            bytes_accessed=2 * depth * (rows + groups * out_width),
            transcendentals=0,
        ),
        name="project",
    )(in_hbm(factor), in_vmem(wide), in_vmem(weights), *map(in_vmem, lasts))


def attend_blocks(sources, ids, q_first, q_refs, id_col, id_row, kv_refs, v_ones, acc, head_size):
    heads = q_refs[0].shape[1] // head_size
    keys = kv_refs[0].shape[0]
    rows = q_refs[0].shape[0]
    for number, kv_ref in enumerate(kv_refs):
        for head in range(heads):
            start = (heads + head) * head_size
            v_ones[head, :, :head_size] = kv_ref[:, start : start + head_size]
            v_ones[head, :, head_size:] = jnp.ones((keys, head_size), BF16)
        first = sources[number]
        key_low, key_high = ids[first], ids[first + keys - 1]
        tile = math.gcd(rows, 256)
        for chunk, q_ref in enumerate(q_refs):

            @pl.loop(0, rows // tile)
            def _(index):
                here = pl.ds(pl.multiple_of(index * tile, tile), tile)
                base = chunk * rows + index * tile
                there = pl.ds(pl.multiple_of(base, tile), tile)
                q_low = ids[q_first + base]
                q_high = ids[q_first + base + tile - 1]

                def add(masked):
                    if masked:
                        allowed = id_row[first // keys] <= id_col[there, :]
                    for head in range(heads):
                        lanes = slice(head * head_size, (head + 1) * head_size)
                        score = lax.dot_general(
                            q_ref[here, lanes],
                            kv_ref[:, lanes],
                            (((1,), (1,)), ((), ())),
                            preferred_element_type=F32,
                        )
                        weight = jnp.exp2(score)
                        if masked:
                            weight = jnp.where(allowed, weight, 0.0)
                        wide = slice(2 * head * head_size, 2 * (head + 1) * head_size)
                        acc[there, wide] += jnp.dot(
                            weight.astype(BF16), v_ones[head], preferred_element_type=F32
                        )

                @pl.when(key_high <= q_low)
                def _():
                    add(False)

                @pl.when((key_high > q_low) & (key_low <= q_high))
                def _():
                    add(True)


def attend_kernel(
    count_q, count_kv, head_size, has_acc, count_out, count_streams, info, ids, *refs
):
    q_refs, rest = refs[:count_q], refs[count_q:]
    (id_col, id_row), rest = rest[:2], rest[2:]
    kv_refs, rest = rest[:count_kv], rest[count_kv:]
    rows, width = q_refs[0].shape
    if has_acc:
        acc_in, rest = rest[0], rest[1:]
    if count_out:
        w_ref, outs, (v_ones, acc, attended) = rest[0], rest[1:-3], rest[-3:]
    else:
        acc_out, v_ones, acc = rest
    acc[...] = acc_in[...] if has_acc else jnp.zeros_like(acc)
    sources = [info[number] for number in range(count_kv)]
    attend_blocks(
        sources, ids, info[count_kv], q_refs, id_col, id_row, kv_refs, v_ones, acc, head_size
    )
    if not count_out:
        acc_out[...] = acc[...]
        return
    for head in range(width // head_size):
        start = 2 * head * head_size
        attended[:, head * head_size : (head + 1) * head_size] = (
            acc[:, start : start + head_size]
            / acc[:, start + head_size : start + 2 * head_size]
        ).astype(BF16)
    out_width = outs[0].shape[1]
    for number, out in enumerate(outs):
        lane = info[count_kv + 1 + number] * out_width
        first = number * count_streams // count_out * out.shape[0]
        out[...] = jnp.dot(
            attended[first : first + out.shape[0], :],
            w_ref[:, pl.ds(pl.multiple_of(lane, out_width), out_width)],
            preferred_element_type=F32,
        ).astype(BF16)


def attend(info, ids, queries, id_col, kvs, head_size, acc=None, w_out=None, streams=0):
    rows, width = queries[0].shape
    total = rows * len(queries)
    keys = kvs[0].shape[0]
    heads = width // head_size
    count_out = streams * w_out.shape[1] // width if streams else 0
    scratch = [
        pltpu.VMEM((heads, keys, 2 * head_size), BF16),
        pltpu.VMEM((total, 2 * width), F32),
    ]
    operands = [*map(in_vmem, queries), id_col, in_hbm(ids.reshape(-1, 1, keys)), *map(in_vmem, kvs)]
    if acc is not None:
        operands.append(in_vmem(acc))
    if count_out:
        operands.append(in_hbm(w_out))
        scratch.append(pltpu.VMEM((total, width), BF16))
        shape = pltpu.VMEM((total // streams, w_out.shape[1] * streams // count_out), BF16)
    else:
        shape = pltpu.VMEM((total, 2 * width), F32)
    outs = count_out or 1
    return pl.pallas_call(
        functools.partial(
            attend_kernel, len(queries), len(kvs), head_size, acc is not None, count_out, streams
        ),
        out_shape=(shape,) * outs,
        in_specs=[SMEM, SMEM] + [VMEM] * len(operands),
        out_specs=(VMEM,) * outs,
        scratch_shapes=scratch,
        compiler_params=pltpu.CompilerParams(
            vmem_limit_bytes=(16 << 20) + 2 * kvs[0].size * 2 * len(kvs)
        ),
        cost_estimate=pl.CostEstimate(flops=1 << 20, bytes_accessed=1 << 10, transcendentals=0),
        name="attend_last" if count_out else "attend",
    )(info, in_hbm(ids), *operands)


def total_of(*parts):
    return sum(part.astype(F32) for part in parts).astype(BF16)


def body(mesh_shape, tokens, norm_gain, w_qkv, head_scale, w_out, scale_ids):
    ring, seqs = mesh_shape["head"], mesh_shape["seq"]
    outer = seqs // 2
    rows, width = tokens.shape
    half = rows // 2
    head_size = w_qkv.shape[2] // head_scale.shape[0]
    head_at, seq_at = lax.axis_index("head"), lax.axis_index("seq")
    place = ring_place(head_at, ring)
    chip, core = seq_at // 2, seq_at % 2
    index_at = lambda offset: ring_index((place + offset + ring) % ring, ring)
    numbers = lambda values: jnp.stack(values).astype(jnp.int32)
    id_col = lax.dynamic_slice_in_dim(scale_ids, seq_at * rows, rows)[:, None]
    at = [index_at(offset) for offset in range(ring)]

    streams, ways = (0, 1), ((0, 1), (1, -1))
    farthest = ring // 2
    reach = [(farthest, farthest - 1), (farthest - 1, farthest)]

    order = [0] + [sign * step % ring for step in range(1, farthest) for sign in (-1, 1)] + [farthest]
    held = [[tokens[s * half : (s + 1) * half]] * 2 for s in streams]
    wide, blocks, targets = None, [in_hbm(tokens)], [(0, 0)]
    for step in range(1, farthest + 1):
        for s in streams:
            for way, sign in ways:
                if step <= reach[s][way]:
                    held[s][way] = along(held[s][way], sign, ring)
        if step == 1:
            held[1][1], weights = lax.optimization_barrier(
                (held[1][1], fold_gain(order, numbers(at), norm_gain, w_qkv))
            )
        elif step == 2:
            wide = placed(targets, blocks, wide, (rows, ring * width))
            blocks, targets = [], []
        elif step == 3:
            held[1][1], wide = lax.optimization_barrier(
                (held[1][1], placed(targets, blocks, wide, (rows, ring * width)))
            )
            blocks, targets = [], []
        if step < farthest:
            for s in streams:
                for way, sign in ways:
                    blocks.append(in_vmem(held[s][way]))
                    targets.append((s * half, (2 * step - 1 + way) * width))
    wide = placed(targets, blocks, wide, (rows, ring * width))
    lasts = [held[0][0], held[1][1]]
    query, kv, *pieces = project(head_scale, wide, weights, lasts, head_size)

    far, straight, crossed = [], [], []
    for step in range(outer):
        source = 2 * ((chip + outer - step) % outer)
        straight.append((source + core) * rows)
        crossed.append((source + 1 - core) * rows)
        if step:
            far.append(lax.ppermute(kv, "seq", [
                (2 * a + b, 2 * ((a + step) % outer) + b) for a in range(outer) for b in (0, 1)
            ]))
    first = [seq_at * rows]
    places = crossed[0] + jnp.arange(len(pieces)) * half
    near = [(kv, straight[0])], [(swapped(piece, seqs), places[s]) for s, piece in enumerate(pieces)]
    acc = None
    for group in (*near, list(zip(far, straight[1:]))):
        keys = [key for key, place in group]
        if acc is not None:
            acc, keys = lax.optimization_barrier((acc, keys))
        info = numbers([place for key, place in group] + first)
        far_crossed = [swapped(block, seqs) for block in keys]
        (acc,) = attend(info, scale_ids, [query], id_col, keys, head_size, acc)

    goals = [[*range(up, 0, -1), *range(-down, 0), 0] for up, down in reach]
    info = numbers(crossed[1:] + first + [at[goal % ring] for goal in goals[0] + goals[1]])
    parts = attend(
        info, scale_ids, [query], id_col, far_crossed, head_size, acc, w_out, len(streams)
    )
    parts = [dict(zip(goals[s], parts[s * ring : (s + 1) * ring])) for s in streams]
    sums = [[None, None] for s in streams]
    for step in range(farthest, 0, -1):
        for s in streams:
            for way, sign in ways:
                if step <= reach[s][way]:
                    part = parts[s][sign * step]
                    if sums[s][way] is not None:
                        part = total_of(part, sums[s][way])
                    sums[s][way] = along(part, sign, ring)
    return jnp.concatenate([total_of(parts[s][0], *sums[s]) for s in streams])


def solution(mesh):
    placed = (P("seq", "head"), P(), P(None, None, "head"), P("head"), P("head", None), P())
    return jax.shard_map(
        functools.partial(body, dict(mesh.shape)),
        mesh=mesh,
        in_specs=placed,
        out_specs=P("seq", "head"),
        check_vma=False,
    )
```

```python
import functools
import math

import jax
import jax.numpy as jnp
from jax import lax
from jax.experimental import pallas as pl
from jax.experimental.pallas import tpu as pltpu
from jax.sharding import PartitionSpec as P

LOG2E = math.log2(math.e)
VMEM = pl.BlockSpec(memory_space=pltpu.VMEM)
SMEM = pl.BlockSpec(memory_space=pltpu.SMEM)
F32 = jnp.float32
BF16 = jnp.bfloat16


def ring_order(count):
    line = count // 2
    return [2 * z for z in range(line)] + [2 * z + 1 for z in reversed(range(line))]


def ring_place(index, count):
    return jnp.where(index % 2 == 0, index // 2, count - 1 - index // 2)


def ring_index(place, count):
    return jnp.where(place < count // 2, 2 * place, 2 * (count - 1 - place) + 1)


def along(value, step, count):
    order = ring_order(count)
    return lax.ppermute(
        value, "head", [(order[p], order[(p + step) % count]) for p in range(count)]
    )


def swapped(value, seq_count):
    return lax.ppermute(value, "seq", [(seq, seq + 1 - 2 * (seq % 2)) for seq in range(seq_count)])


def in_hbm(value):
    return pltpu.with_memory_space_constraint(value, pltpu.HBM)


def in_vmem(value):
    return pltpu.with_memory_space_constraint(value, pltpu.VMEM)


def fold_kernel(order, at, gain_ref, w_hbm, out_ref, sems):
    lanes = gain_ref.shape[1]
    size = w_hbm.shape[1] // len(order)
    per = size // lanes

    def fetch(n):
        start = pl.multiple_of(at[order[n]] * size, size)
        return pltpu.make_async_copy(
            w_hbm.at[:, pl.ds(start, size), :], out_ref.at[:, n * size : (n + 1) * size, :], sems.at[n]
        )

    for n in range(len(order)):
        fetch(n).start()
    for n in range(len(order)):
        columns = jnp.transpose(gain_ref[pl.ds(at[order[n]] * per, per), :])
        fetch(n).wait()
        for piece in range(per):
            first = n * size + piece * lanes
            for group in range(w_hbm.shape[0]):
                here = (group, slice(first, first + lanes), slice(None))
                scaled = out_ref[here].astype(F32) * columns[:, piece : piece + 1]
                out_ref[here] = scaled.astype(BF16)


def fold_gain(order, at, gain, weights):
    depth = weights.shape[1]
    lanes = math.gcd(depth // len(order), 128)
    return pl.pallas_call(
        functools.partial(fold_kernel, order),
        out_shape=pltpu.VMEM(weights.shape, BF16),
        in_specs=[SMEM, VMEM, pl.BlockSpec(memory_space=pltpu.HBM)],
        out_specs=VMEM,
        scratch_shapes=[pltpu.SemaphoreType.DMA((len(order),))],
        compiler_params=pltpu.CompilerParams(vmem_limit_bytes=16 << 20),
        cost_estimate=pl.CostEstimate(
            flops=weights.size, bytes_accessed=4 * weights.size, transcendentals=0
        ),
        name="fold_gain",
    )(at, in_hbm(gain.reshape(depth // lanes, lanes)), in_hbm(weights))


def place_kernel(targets, *refs):
    blocks, wide, sems = refs[: len(targets)], refs[-2], refs[-1]
    copies = []
    for n, (block, (row, lane)) in enumerate(zip(blocks, targets)):
        rows, width = block.shape
        here = wide.at[row : row + rows, lane : lane + width]
        copies.append(pltpu.make_async_copy(block, here, sems.at[n]))
    for copy in copies:
        copy.start()
    for copy in copies:
        copy.wait()


def placed(targets, blocks, wide, shape):
    operands = [*blocks] + ([] if wide is None else [in_vmem(wide)])
    return pl.pallas_call(
        functools.partial(place_kernel, targets),
        out_shape=pltpu.VMEM(shape, BF16),
        in_specs=[pl.BlockSpec(memory_space=pl.ANY)] * len(operands),
        out_specs=pl.BlockSpec(memory_space=pl.ANY),
        scratch_shapes=[pltpu.SemaphoreType.DMA((len(targets),))],
        input_output_aliases={} if wide is None else {len(blocks): 0},
        compiler_params=pltpu.CompilerParams(vmem_limit_bytes=1 << 20),
        cost_estimate=pl.CostEstimate(flops=0, bytes_accessed=1 << 20, transcendentals=0),
        name="place",
    )(*operands)


def project_kernel(head_size, groups, count, factor, wide, w_ref, out_ref, *pieces):
    rows = wide.shape[0] // count
    depth, out_width = w_ref.shape[1:]
    for part in range(count):
        here = slice(part * rows, (part + 1) * rows)
        products = [
            jnp.dot(wide[here, :], w_ref[group], preferred_element_type=F32) for group in groups
        ]
        power = None
        for lane in range(0, depth, 128):
            values = wide[here, lane : lane + 128].astype(F32)
            power = values * values if power is None else power + values * values
        scale = lax.rsqrt(jnp.sum(power, axis=-1, keepdims=True) * (1.0 / depth) + 1e-06)
        for number, (group, product) in enumerate(zip(groups, products)):
            start = number * out_width
            product = product * scale
            for head in range(out_width // head_size):
                value = product[:, head * head_size : (head + 1) * head_size]
                if group < 2:
                    size = lax.rsqrt(jnp.sum(value * value, axis=-1, keepdims=True) + 1e-06)
                    value = value * (size * (factor[head] * LOG2E) if group == 0 else size)
                lanes = slice(start + head * head_size, start + (head + 1) * head_size)
                out_ref[here, lanes] = value.astype(BF16)
        if pieces:
            pieces[part][...] = out_ref[here, :]


def project(factor, wide, weights, groups, count, apart, head_size):
    rows = wide.shape[0]
    depth, out_width = weights.shape[1:]
    width = len(groups) * out_width
    shapes = [(rows, width)] + [(rows // count, width)] * (count if apart else 0)
    return pl.pallas_call(
        functools.partial(project_kernel, head_size, groups, count),
        out_shape=tuple(pltpu.VMEM(shape, BF16) for shape in shapes),
        in_specs=[SMEM] + [VMEM] * 2,
        out_specs=(VMEM,) * len(shapes),
        compiler_params=pltpu.CompilerParams(vmem_limit_bytes=16 << 20),
        cost_estimate=pl.CostEstimate(
            flops=2 * rows * depth * width,
            bytes_accessed=2 * depth * (rows + width),
            transcendentals=0,
        ),
        name="project_q" if groups == (0,) else "project_kv",
    )(in_hbm(factor), in_vmem(wide), in_vmem(weights))


def attend_blocks(sources, ids, q_first, q_refs, id_col, id_row, kv_refs, v_ones, acc, head_size):
    heads = q_refs[0].shape[1] // head_size
    keys = kv_refs[0].shape[0]
    rows = q_refs[0].shape[0]
    for number, kv_ref in enumerate(kv_refs):
        for head in range(heads):
            start = (heads + head) * head_size
            v_ones[head, :, :head_size] = kv_ref[:, start : start + head_size]
            v_ones[head, :, head_size:] = jnp.ones((keys, head_size), BF16)
        first = sources[number]
        key_low, key_high = ids[first], ids[first + keys - 1]
        tile = math.gcd(rows, 256)
        for chunk, q_ref in enumerate(q_refs):

            @pl.loop(0, rows // tile)
            def _(index):
                here = pl.ds(pl.multiple_of(index * tile, tile), tile)
                base = chunk * rows + index * tile
                there = pl.ds(pl.multiple_of(base, tile), tile)
                q_low = ids[q_first + base]
                q_high = ids[q_first + base + tile - 1]

                def add(masked):
                    if masked:
                        allowed = id_row[first // keys] <= id_col[there, :]
                    for head in range(heads):
                        lanes = slice(head * head_size, (head + 1) * head_size)
                        score = lax.dot_general(
                            q_ref[here, lanes],
                            kv_ref[:, lanes],
                            (((1,), (1,)), ((), ())),
                            preferred_element_type=F32,
                        )
                        weight = jnp.exp2(score)
                        if masked:
                            weight = jnp.where(allowed, weight, 0.0)
                        wide = slice(2 * head * head_size, 2 * (head + 1) * head_size)
                        acc[there, wide] += jnp.dot(
                            weight.astype(BF16), v_ones[head], preferred_element_type=F32
                        )

                @pl.when(key_high <= q_low)
                def _():
                    add(False)

                @pl.when((key_high > q_low) & (key_low <= q_high))
                def _():
                    add(True)


def attend_kernel(
    count_q, count_kv, head_size, has_acc, count_out, count_streams, info, ids, *refs
):
    q_refs, rest = refs[:count_q], refs[count_q:]
    (id_col, id_row), rest = rest[:2], rest[2:]
    kv_refs, rest = rest[:count_kv], rest[count_kv:]
    rows, width = q_refs[0].shape
    if has_acc:
        acc_in, rest = rest[0], rest[1:]
    if count_out:
        w_ref, outs, (v_ones, acc, attended) = rest[0], rest[1:-3], rest[-3:]
    else:
        acc_out, v_ones, acc = rest
    acc[...] = acc_in[...] if has_acc else jnp.zeros_like(acc)
    sources = [info[number] for number in range(count_kv)]
    attend_blocks(
        sources, ids, info[count_kv], q_refs, id_col, id_row, kv_refs, v_ones, acc, head_size
    )
    if not count_out:
        acc_out[...] = acc[...]
        return
    for head in range(width // head_size):
        start = 2 * head * head_size
        attended[:, head * head_size : (head + 1) * head_size] = (
            acc[:, start : start + head_size]
            / acc[:, start + head_size : start + 2 * head_size]
        ).astype(BF16)
    out_width = outs[0].shape[1]
    for number, out in enumerate(outs):
        lane = info[count_kv + 1 + number] * out_width
        first = number * count_streams // count_out * out.shape[0]
        out[...] = jnp.dot(
            attended[first : first + out.shape[0], :],
            w_ref[:, pl.ds(pl.multiple_of(lane, out_width), out_width)],
            preferred_element_type=F32,
        ).astype(BF16)


def attend(info, ids, queries, id_col, kvs, head_size, acc=None, w_out=None, streams=0):
    rows, width = queries[0].shape
    total = rows * len(queries)
    keys = kvs[0].shape[0]
    heads = width // head_size
    count_out = streams * w_out.shape[1] // width if streams else 0
    scratch = [
        pltpu.VMEM((heads, keys, 2 * head_size), BF16),
        pltpu.VMEM((total, 2 * width), F32),
    ]
    operands = [*map(in_vmem, queries), id_col, in_hbm(ids.reshape(-1, 1, keys)), *map(in_vmem, kvs)]
    if acc is not None:
        operands.append(in_vmem(acc))
    if count_out:
        operands.append(in_vmem(w_out))
        scratch.append(pltpu.VMEM((total, width), BF16))
        shape = pltpu.VMEM((total // streams, w_out.shape[1] * streams // count_out), BF16)
    else:
        shape = pltpu.VMEM((total, 2 * width), F32)
    outs = count_out or 1
    return pl.pallas_call(
        functools.partial(
            attend_kernel, len(queries), len(kvs), head_size, acc is not None, count_out, streams
        ),
        out_shape=(shape,) * outs,
        in_specs=[SMEM, SMEM] + [VMEM] * len(operands),
        out_specs=(VMEM,) * outs,
        scratch_shapes=scratch,
        compiler_params=pltpu.CompilerParams(
            vmem_limit_bytes=(16 << 20) + 2 * kvs[0].size * 2 * len(kvs)
        ),
        cost_estimate=pl.CostEstimate(flops=1 << 20, bytes_accessed=1 << 10, transcendentals=0),
        name="attend_last" if count_out else "attend",
    )(info, in_hbm(ids), *operands)


def total_of(*parts):
    return sum(part.astype(F32) for part in parts).astype(BF16)


def body(mesh_shape, tokens, norm_gain, w_qkv, head_scale, w_out, scale_ids):
    ring, seqs = mesh_shape["head"], mesh_shape["seq"]
    outer = seqs // 2
    rows, width = tokens.shape
    half = rows // 2
    head_size = w_qkv.shape[2] // head_scale.shape[0]
    head_at, seq_at = lax.axis_index("head"), lax.axis_index("seq")
    place = ring_place(head_at, ring)
    chip, core = seq_at // 2, seq_at % 2
    index_at = lambda offset: ring_index((place + offset + ring) % ring, ring)
    numbers = lambda values: jnp.stack(values).astype(jnp.int32)
    id_col = lax.dynamic_slice_in_dim(scale_ids, seq_at * rows, rows)[:, None]
    at = [index_at(offset) for offset in range(ring)]

    streams, ways = (0, 1), ((0, 1), (1, -1))
    farthest = ring // 2
    reach = [(farthest, farthest - 1), (farthest - 1, farthest)]

    order = [0] + [sign * step % ring for step in range(1, farthest) for sign in (-1, 1)] + [farthest]
    held = [[tokens[s * half : (s + 1) * half]] * 2 for s in streams]
    wide, blocks, targets = None, [in_hbm(tokens)], [(0, 0)]
    for step in range(1, farthest + 1):
        for s in streams:
            for way, sign in ways:
                if step <= reach[s][way]:
                    held[s][way] = along(held[s][way], sign, ring)
        if step == 1:
            held[1][1], weights = lax.optimization_barrier(
                (held[1][1], fold_gain(order, numbers(at), norm_gain, w_qkv))
            )
        elif step == 2:
            wide = placed(targets, blocks, wide, (rows, ring * width))
            blocks, targets = [], []
        elif step == 3:
            held[1][1], wide = lax.optimization_barrier(
                (held[1][1], placed(targets, blocks, wide, (rows, ring * width)))
            )
            blocks, targets = [], []
        if step < farthest:
            for s in streams:
                for way, sign in ways:
                    blocks.append(in_vmem(held[s][way]))
                    targets.append((s * half, (2 * step - 1 + way) * width))
    wide = placed(targets, blocks, wide, (rows, ring * width))
    lasts, column = [held[0][0], held[1][1]], (ring - 1) * width
    targets = [(s * half, column) for s in streams]
    wide = placed(targets, [*map(in_vmem, lasts)], wide, (rows, ring * width))
    kv, *pieces = project(head_scale, wide, weights, (1, 2), len(streams), True, head_size)
    (query,) = project(head_scale, wide, weights, (0,), len(streams), False, head_size)

    far, straight, crossed = [], [], []
    for step in range(outer):
        source = 2 * ((chip + outer - step) % outer)
        straight.append((source + core) * rows)
        crossed.append((source + 1 - core) * rows)
        if step:
            far.append(lax.ppermute(kv, "seq", [
                (2 * a + b, 2 * ((a + step) % outer) + b) for a in range(outer) for b in (0, 1)
            ]))
    first = [seq_at * rows]
    places = crossed[0] + jnp.arange(len(pieces)) * half
    near = [(kv, straight[0])], [(swapped(piece, seqs), places[s]) for s, piece in enumerate(pieces)]
    acc = None
    for group in (*near, list(zip(far, straight[1:]))):
        keys = [key for key, place in group]
        if acc is not None:
            acc, keys = lax.optimization_barrier((acc, keys))
        info = numbers([place for key, place in group] + first)
        far_crossed = [swapped(block, seqs) for block in keys]
        (acc,) = attend(info, scale_ids, [query], id_col, keys, head_size, acc)

    goals = [[*range(up, 0, -1), *range(-down, 0), 0] for up, down in reach]
    info = numbers(crossed[1:] + first + [at[goal % ring] for goal in goals[0] + goals[1]])
    parts = attend(
        info, scale_ids, [query], id_col, far_crossed, head_size, acc, w_out, len(streams)
    )
    parts = [dict(zip(goals[s], parts[s * ring : (s + 1) * ring])) for s in streams]
    sums = [[None, None] for s in streams]
    for step in range(farthest, 0, -1):
        for s in streams:
            for way, sign in ways:
                if step <= reach[s][way]:
                    part = parts[s][sign * step]
                    if sums[s][way] is not None:
                        part = total_of(part, sums[s][way])
                    sums[s][way] = along(part, sign, ring)
    return jnp.concatenate([total_of(parts[s][0], *sums[s]) for s in streams])


def solution(mesh):
    placed = (P("seq", "head"), P(), P(None, None, "head"), P("head"), P("head", None), P())
    return jax.shard_map(
        functools.partial(body, dict(mesh.shape)),
        mesh=mesh,
        in_specs=placed,
        out_specs=P("seq", "head"),
        check_vma=False,
    )
```

```python
import functools
import math

import jax
import jax.numpy as jnp
from jax import lax
from jax.experimental import pallas as pl
from jax.experimental.pallas import tpu as pltpu
from jax.sharding import PartitionSpec as P

LOG2E = math.log2(math.e)
VMEM = pl.BlockSpec(memory_space=pltpu.VMEM)
SMEM = pl.BlockSpec(memory_space=pltpu.SMEM)
F32 = jnp.float32
BF16 = jnp.bfloat16


def ring_order(count):
    line = count // 2
    return [2 * z for z in range(line)] + [2 * z + 1 for z in reversed(range(line))]


def ring_place(index, count):
    return jnp.where(index % 2 == 0, index // 2, count - 1 - index // 2)


def ring_index(place, count):
    return jnp.where(place < count // 2, 2 * place, 2 * (count - 1 - place) + 1)


def along(value, step, count):
    order = ring_order(count)
    return lax.ppermute(
        value, "head", [(order[p], order[(p + step) % count]) for p in range(count)]
    )


def swapped(value, seq_count):
    return lax.ppermute(value, "seq", [(seq, seq + 1 - 2 * (seq % 2)) for seq in range(seq_count)])


def in_hbm(value):
    return pltpu.with_memory_space_constraint(value, pltpu.HBM)


def in_vmem(value):
    return pltpu.with_memory_space_constraint(value, pltpu.VMEM)


def fold_kernel(order, at, gain_ref, w_hbm, out_ref, sems):
    lanes = gain_ref.shape[1]
    size = w_hbm.shape[1] // len(order)
    per = size // lanes

    def fetch(n):
        start = pl.multiple_of(at[order[n]] * size, size)
        return pltpu.make_async_copy(
            w_hbm.at[:, pl.ds(start, size), :], out_ref.at[:, n * size : (n + 1) * size, :], sems.at[n]
        )

    for n in range(len(order)):
        fetch(n).start()
    for n in range(len(order)):
        columns = jnp.transpose(gain_ref[pl.ds(at[order[n]] * per, per), :])
        fetch(n).wait()
        for piece in range(per):
            first = n * size + piece * lanes
            for group in range(w_hbm.shape[0]):
                here = (group, slice(first, first + lanes), slice(None))
                scaled = out_ref[here].astype(F32) * columns[:, piece : piece + 1]
                out_ref[here] = scaled.astype(BF16)


def fold_gain(order, at, gain, weights):
    depth = weights.shape[1]
    lanes = math.gcd(depth // len(order), 128)
    return pl.pallas_call(
        functools.partial(fold_kernel, order),
        out_shape=pltpu.VMEM(weights.shape, BF16),
        in_specs=[SMEM, VMEM, pl.BlockSpec(memory_space=pltpu.HBM)],
        out_specs=VMEM,
        scratch_shapes=[pltpu.SemaphoreType.DMA((len(order),))],
        compiler_params=pltpu.CompilerParams(vmem_limit_bytes=16 << 20),
        cost_estimate=pl.CostEstimate(
            flops=weights.size, bytes_accessed=4 * weights.size, transcendentals=0
        ),
        name="fold_gain",
    )(at, in_hbm(gain.reshape(depth // lanes, lanes)), in_hbm(weights))


def place_kernel(targets, *refs):
    blocks, wide, sems = refs[: len(targets)], refs[-2], refs[-1]
    copies = []
    for n, (block, (row, lane)) in enumerate(zip(blocks, targets)):
        rows, width = block.shape
        here = wide.at[row : row + rows, lane : lane + width]
        copies.append(pltpu.make_async_copy(block, here, sems.at[n]))
    for copy in copies:
        copy.start()
    for copy in copies:
        copy.wait()


def placed(targets, blocks, wide, shape):
    operands = [*blocks] + ([] if wide is None else [in_vmem(wide)])
    return pl.pallas_call(
        functools.partial(place_kernel, targets),
        out_shape=pltpu.VMEM(shape, BF16),
        in_specs=[pl.BlockSpec(memory_space=pl.ANY)] * len(operands),
        out_specs=pl.BlockSpec(memory_space=pl.ANY),
        scratch_shapes=[pltpu.SemaphoreType.DMA((len(targets),))],
        input_output_aliases={} if wide is None else {len(blocks): 0},
        compiler_params=pltpu.CompilerParams(vmem_limit_bytes=1 << 20),
        cost_estimate=pl.CostEstimate(flops=0, bytes_accessed=1 << 20, transcendentals=0),
        name="place",
    )(*operands)


def project_kernel(head_size, count, factor, wide, w_ref, *refs):
    lasts, q_ref = refs[:count], refs[count]
    halves, pieces = refs[count + 1 : 2 * count + 1], refs[2 * count + 1 :]
    rows, width = lasts[0].shape
    depth, out_width = w_ref.shape[1:]
    done = depth - width
    for stream, last in enumerate(lasts):
        here = slice(stream * rows, (stream + 1) * rows)
        kv_ref = halves[stream]
        q, k, v = (
            jnp.dot(wide[here, :done], w_ref[group, :done, :], preferred_element_type=F32)
            + jnp.dot(last[...], w_ref[group, done:, :], preferred_element_type=F32)
            for group in range(3)
        )
        power = None
        for lane in range(0, depth, 128):
            if lane < done:
                values = wide[here, lane : lane + 128].astype(F32)
            else:
                values = last[:, lane - done : lane - done + 128].astype(F32)
            power = values * values if power is None else power + values * values
        scale = lax.rsqrt(jnp.sum(power, axis=-1, keepdims=True) * (1.0 / depth) + 1e-06)
        q, k, v = q * scale, k * scale, v * scale
        for head in range(out_width // head_size):
            lanes = slice(head * head_size, (head + 1) * head_size)
            qh, kh = q[:, lanes], k[:, lanes]
            q_size = lax.rsqrt(jnp.sum(qh * qh, axis=-1, keepdims=True) + 1e-06)
            k_size = lax.rsqrt(jnp.sum(kh * kh, axis=-1, keepdims=True) + 1e-06)
            q_ref[here, lanes] = (qh * (q_size * (factor[head] * LOG2E))).astype(BF16)
            kv_ref[:, lanes] = (kh * k_size).astype(BF16)
        kv_ref[:, out_width:] = v.astype(BF16)
    start = 0
    for piece in pieces:
        size = piece.shape[0]
        for stream, half in enumerate(halves):
            low, high = max(start, stream * rows), min(start + size, (stream + 1) * rows)
            if low < high:
                piece[low - start : high - start, :] = half[low - stream * rows : high - stream * rows, :]
        start += size


def project(factor, wide, weights, lasts, count_pieces, head_size):
    rows = wide.shape[0]
    units = rows // 16
    sizes = [16 * ((units + n) // count_pieces) for n in range(count_pieces)]
    groups, depth, out_width = weights.shape
    return pl.pallas_call(
        functools.partial(project_kernel, head_size, len(lasts)),
        out_shape=(
            pltpu.VMEM((rows, out_width), BF16),
            *[pltpu.VMEM((rows // len(lasts), 2 * out_width), BF16)] * len(lasts),
            *[pltpu.VMEM((size, 2 * out_width), BF16) for size in sizes],
        ),
        in_specs=[SMEM] + [VMEM] * (2 + len(lasts)),
        out_specs=(VMEM,) * (1 + len(lasts) + count_pieces),
        compiler_params=pltpu.CompilerParams(vmem_limit_bytes=16 << 20),
        cost_estimate=pl.CostEstimate(
            flops=2 * rows * depth * groups * out_width,
            bytes_accessed=2 * depth * (rows + groups * out_width),
            transcendentals=0,
        ),
        name="project",
    )(in_hbm(factor), in_vmem(wide), in_vmem(weights), *map(in_vmem, lasts))


def attend_kernel(
    head_size, counts, has_acc, count_out, count_streams, info, ids, q_ref, id_row, *refs
):
    count_blocks, count_parts = counts
    kv_refs, rest = refs[: count_blocks * count_parts], refs[count_blocks * count_parts :]
    if has_acc:
        acc_in, rest = rest[0], rest[1:]
    if count_out:
        w_ref, outs, (k_all, v_ones, acc, attended) = rest[0], rest[1:-4], rest[-4:]
    else:
        acc_out, k_all, v_ones, acc = rest
    acc[...] = acc_in[...] if has_acc else jnp.zeros_like(acc)
    rows, width = q_ref.shape
    heads = width // head_size
    keys = k_all.shape[0]
    tile = id_row.shape[2]
    q_first = info[count_blocks]
    v_ones[:, :, head_size:] = jnp.ones((heads, keys, head_size), BF16)
    for number in range(count_blocks):
        begin = 0
        for kv_ref in kv_refs[number * count_parts : (number + 1) * count_parts]:
            here = slice(begin, begin + kv_ref.shape[0])
            begin += kv_ref.shape[0]
            k_all[here, :] = kv_ref[:, :width]
            for head in range(heads):
                start = width + head * head_size
                v_ones[head, here, :head_size] = kv_ref[:, start : start + head_size]
        first = info[number]
        key_low, key_high = ids[first], ids[first + keys - 1]

        @pl.loop(0, rows // tile)
        def _(index):
            base = pl.multiple_of(index * tile, tile)
            here = pl.ds(base, tile)
            q_low, q_high = ids[q_first + base], ids[q_first + base + tile - 1]

            def add(masked):
                if masked:
                    key_ids = [id_row[first // tile + n] for n in range(keys // tile)]
                    own = jnp.broadcast_to(id_row[q_first // tile + index], (8, tile))
                    allowed = jnp.concatenate(key_ids, axis=1) <= jnp.transpose(own)[:, :1]
                for head in range(heads):
                    lanes = slice(head * head_size, (head + 1) * head_size)
                    score = lax.dot_general(
                        q_ref[here, lanes],
                        k_all[:, lanes],
                        (((1,), (1,)), ((), ())),
                        preferred_element_type=F32,
                    )
                    weight = jnp.exp2(score)
                    if masked:
                        weight = jnp.where(allowed, weight, 0.0)
                    spread = slice(2 * head * head_size, 2 * (head + 1) * head_size)
                    acc[here, spread] += jnp.dot(
                        weight.astype(BF16), v_ones[head], preferred_element_type=F32
                    )

            @pl.when(key_high <= q_low)
            def _():
                add(False)

            @pl.when((key_high > q_low) & (key_low <= q_high))
            def _():
                add(True)

    if not count_out:
        acc_out[...] = acc[...]
        return
    for head in range(heads):
        start = 2 * head * head_size
        attended[:, head * head_size : (head + 1) * head_size] = (
            acc[:, start : start + head_size]
            / acc[:, start + head_size : start + 2 * head_size]
        ).astype(BF16)
    out_rows, out_width = outs[0].shape
    for number, out in enumerate(outs):
        lane = info[count_blocks + 1 + number] * out_width
        first = number * count_streams // count_out * out_rows
        out[...] = jnp.dot(
            attended[first : first + out_rows, :],
            w_ref[:, pl.ds(pl.multiple_of(lane, out_width), out_width)],
            preferred_element_type=F32,
        ).astype(BF16)


def attend(info, ids, query, blocks, head_size, acc=None, w_out=None, streams=0):
    total, width = query.shape
    parts = [part for block in blocks for part in block]
    keys = sum(part.shape[0] for part in blocks[0])
    heads = width // head_size
    count_out = streams * w_out.shape[1] // width if streams else 0
    scratch = [
        pltpu.VMEM((keys, width), BF16),
        pltpu.VMEM((heads, keys, 2 * head_size), BF16),
        pltpu.VMEM((total, 2 * width), F32),
    ]
    operands = [in_vmem(query), in_hbm(ids.reshape(-1, 1, math.gcd(total, 256)))]
    operands += map(in_vmem, parts)
    if acc is not None:
        operands.append(in_vmem(acc))
    if count_out:
        operands.append(in_vmem(w_out))
        scratch.append(pltpu.VMEM((total, width), BF16))
        shape = pltpu.VMEM((total // streams, w_out.shape[1] * streams // count_out), BF16)
    else:
        shape = pltpu.VMEM((total, 2 * width), F32)
    outs = count_out or 1
    return pl.pallas_call(
        functools.partial(
            attend_kernel, head_size, (len(blocks), len(blocks[0])), acc is not None, count_out, streams
        ),
        out_shape=(shape,) * outs,
        in_specs=[SMEM, SMEM] + [VMEM] * len(operands),
        out_specs=(VMEM,) * outs,
        scratch_shapes=scratch,
        compiler_params=pltpu.CompilerParams(
            vmem_limit_bytes=(16 << 20) + 4 * sum(part.size for part in parts)
        ),
        cost_estimate=pl.CostEstimate(flops=1 << 20, bytes_accessed=1 << 10, transcendentals=0),
        name="attend_last" if count_out else "attend",
    )(info, in_hbm(ids), *operands)


def load_kernel(source, target, sem):
    copy = pltpu.make_async_copy(source, target, sem)
    copy.start()
    copy.wait()


def loaded(value):
    return pl.pallas_call(
        load_kernel,
        out_shape=pltpu.VMEM(value.shape, value.dtype),
        in_specs=[pl.BlockSpec(memory_space=pltpu.HBM)],
        out_specs=pl.BlockSpec(memory_space=pl.ANY),
        scratch_shapes=[pltpu.SemaphoreType.DMA(())],
        compiler_params=pltpu.CompilerParams(vmem_limit_bytes=1 << 20),
        cost_estimate=pl.CostEstimate(flops=0, bytes_accessed=1 << 20, transcendentals=0),
        name="load",
    )(in_hbm(value))


def total_of(*parts):
    return sum(part.astype(F32) for part in parts).astype(BF16)


def body(mesh_shape, tokens, norm_gain, w_qkv, head_scale, w_out, scale_ids):
    ring, seqs = mesh_shape["head"], mesh_shape["seq"]
    outer = seqs // 2
    rows, width = tokens.shape
    half = rows // 2
    head_size = w_qkv.shape[2] // head_scale.shape[0]
    head_at, seq_at = lax.axis_index("head"), lax.axis_index("seq")
    place = ring_place(head_at, ring)
    chip, core = seq_at // 2, seq_at % 2
    index_at = lambda offset: ring_index((place + offset + ring) % ring, ring)
    numbers = lambda values: jnp.stack(values).astype(jnp.int32)
    at = [index_at(offset) for offset in range(ring)]

    streams, ways = (0, 1), ((0, 1), (1, -1))
    farthest = ring // 2
    reach = [(farthest, farthest - 1), (farthest - 1, farthest)]

    order = [0] + [sign * step % ring for step in range(1, farthest) for sign in (-1, 1)] + [farthest]
    held = [[tokens[s * half : (s + 1) * half]] * 2 for s in streams]
    wide, blocks, targets = None, [in_hbm(tokens)], [(0, 0)]
    for step in range(1, farthest + 1):
        for s in streams:
            for way, sign in ways:
                if step <= reach[s][way]:
                    held[s][way] = along(held[s][way], sign, ring)
        if step == 1:
            held[1][1], weights = lax.optimization_barrier(
                (held[1][1], fold_gain(order, numbers(at), norm_gain, w_qkv))
            )
        elif step == 2:
            wide = placed(targets, blocks, wide, (rows, ring * width))
            blocks, targets = [], []
        elif step == 3:
            held[1][1], wide = lax.optimization_barrier(
                (held[1][1], placed(targets, blocks, wide, (rows, ring * width)))
            )
            blocks, targets = [], []
        if step < farthest:
            for s in streams:
                for way, sign in ways:
                    blocks.append(in_vmem(held[s][way]))
                    targets.append((s * half, (2 * step - 1 + way) * width))
    wide = placed(targets, blocks, wide, (rows, ring * width))
    lasts = [held[0][0], held[1][1]]
    query, *kvs = project(head_scale, wide, weights, lasts, 3, head_size)
    halves, pieces = kvs[:2], kvs[2:]

    far, straight, crossed = [], [], []
    for step in range(outer):
        source = 2 * ((chip + outer - step) % outer)
        straight.append((source + core) * rows)
        crossed.append((source + 1 - core) * rows)
        if step:
            shift = [(2 * a + b, 2 * ((a + step) % outer) + b) for a in range(outer) for b in (0, 1)]
            far.append([lax.ppermute(kv, "seq", shift) for kv in halves])
    first = [seq_at * rows]
    (acc,) = attend(numbers(straight[:1] + first), scale_ids, query, [halves], head_size)
    near = [[swapped(piece, seqs) for piece in pieces]]
    acc, near = lax.optimization_barrier((acc, near))
    (acc,) = attend(numbers(crossed[:1] + first), scale_ids, query, near, head_size, acc)
    acc, far, w_near = lax.optimization_barrier((acc, far, loaded(w_out)))
    far_crossed = [[swapped(part, seqs) for part in block] for block in far]
    (acc,) = attend(numbers(straight[1:] + first), scale_ids, query, far, head_size, acc)

    goals = [[*range(up, 0, -1), *range(-down, 0), 0] for up, down in reach]
    info = numbers(crossed[1:] + first + [at[goal % ring] for goal in goals[0] + goals[1]])
    parts = attend(
        info, scale_ids, query, far_crossed, head_size, acc, w_near, len(streams)
    )
    parts = [dict(zip(goals[s], parts[s * ring : (s + 1) * ring])) for s in streams]
    sums = [[None, None] for s in streams]
    for step in range(farthest, 0, -1):
        for s in streams:
            for way, sign in ways:
                if step <= reach[s][way]:
                    part = parts[s][sign * step]
                    if sums[s][way] is not None:
                        part = total_of(part, sums[s][way])
                    sums[s][way] = along(part, sign, ring)
    return jnp.concatenate([total_of(parts[s][0], *sums[s]) for s in streams])


def solution(mesh):
    placed = (P("seq", "head"), P(), P(None, None, "head"), P("head"), P("head", None), P())
    return jax.shard_map(
        functools.partial(body, dict(mesh.shape)),
        mesh=mesh,
        in_specs=placed,
        out_specs=P("seq", "head"),
        check_vma=False,
    )
```

```python
import functools
import math

import jax
import jax.numpy as jnp
from jax import lax
from jax.experimental import pallas as pl
from jax.experimental.pallas import tpu as pltpu
from jax.sharding import PartitionSpec as P

LOG2E = math.log2(math.e)
VMEM = pl.BlockSpec(memory_space=pltpu.VMEM)
SMEM = pl.BlockSpec(memory_space=pltpu.SMEM)
F32 = jnp.float32
BF16 = jnp.bfloat16


def ring_order(count):
    line = count // 2
    return [2 * z for z in range(line)] + [2 * z + 1 for z in reversed(range(line))]


def ring_place(index, count):
    return jnp.where(index % 2 == 0, index // 2, count - 1 - index // 2)


def ring_index(place, count):
    return jnp.where(place < count // 2, 2 * place, 2 * (count - 1 - place) + 1)


def along(value, step, count):
    order = ring_order(count)
    return lax.ppermute(
        value, "head", [(order[p], order[(p + step) % count]) for p in range(count)]
    )


def swapped(value, seq_count):
    return lax.ppermute(value, "seq", [(seq, seq + 1 - 2 * (seq % 2)) for seq in range(seq_count)])


def in_hbm(value):
    return pltpu.with_memory_space_constraint(value, pltpu.HBM)


def in_vmem(value):
    return pltpu.with_memory_space_constraint(value, pltpu.VMEM)


def fold_kernel(order, at, gain_ref, w_hbm, out_ref, sems):
    lanes = gain_ref.shape[1]
    size = w_hbm.shape[1] // len(order)
    per = size // lanes

    def fetch(n):
        start = pl.multiple_of(at[order[n]] * size, size)
        return pltpu.make_async_copy(
            w_hbm.at[:, pl.ds(start, size), :], out_ref.at[:, n * size : (n + 1) * size, :], sems.at[n]
        )

    for n in range(len(order)):
        fetch(n).start()
    for n in range(len(order)):
        columns = jnp.transpose(gain_ref[pl.ds(at[order[n]] * per, per), :])
        fetch(n).wait()
        for piece in range(per):
            first = n * size + piece * lanes
            for group in range(w_hbm.shape[0]):
                here = (group, slice(first, first + lanes), slice(None))
                scaled = out_ref[here].astype(F32) * columns[:, piece : piece + 1]
                out_ref[here] = scaled.astype(BF16)


def fold_gain(order, at, gain, weights):
    depth = weights.shape[1]
    lanes = math.gcd(depth // len(order), 128)
    return pl.pallas_call(
        functools.partial(fold_kernel, order),
        out_shape=pltpu.VMEM(weights.shape, BF16),
        in_specs=[SMEM, VMEM, pl.BlockSpec(memory_space=pltpu.HBM)],
        out_specs=VMEM,
        scratch_shapes=[pltpu.SemaphoreType.DMA((len(order),))],
        compiler_params=pltpu.CompilerParams(vmem_limit_bytes=16 << 20),
        cost_estimate=pl.CostEstimate(
            flops=weights.size, bytes_accessed=4 * weights.size, transcendentals=0
        ),
        name="fold_gain",
    )(at, in_hbm(gain.reshape(depth // lanes, lanes)), in_hbm(weights))


def place_kernel(targets, *refs):
    blocks, wide, sems = refs[: len(targets)], refs[-2], refs[-1]
    copies = []
    for n, (block, (row, lane)) in enumerate(zip(blocks, targets)):
        rows, width = block.shape
        here = wide.at[row : row + rows, lane : lane + width]
        copies.append(pltpu.make_async_copy(block, here, sems.at[n]))
    for copy in copies:
        copy.start()
    for copy in copies:
        copy.wait()


def placed(targets, blocks, wide, shape):
    operands = [*blocks] + ([] if wide is None else [in_vmem(wide)])
    return pl.pallas_call(
        functools.partial(place_kernel, targets),
        out_shape=pltpu.VMEM(shape, BF16),
        in_specs=[pl.BlockSpec(memory_space=pl.ANY)] * len(operands),
        out_specs=pl.BlockSpec(memory_space=pl.ANY),
        scratch_shapes=[pltpu.SemaphoreType.DMA((len(targets),))],
        input_output_aliases={} if wide is None else {len(blocks): 0},
        compiler_params=pltpu.CompilerParams(vmem_limit_bytes=1 << 20),
        cost_estimate=pl.CostEstimate(flops=0, bytes_accessed=1 << 20, transcendentals=0),
        name="place",
    )(*operands)


def begin_kernel(blocks, wide, w_ref, state):
    rows, depth = wide.shape
    out_width = w_ref.shape[2]
    done = depth - depth // blocks
    tile = math.gcd(rows, 256)
    for first in range(0, rows, tile):
        here = slice(first, first + tile)
        for group in range(3):
            state[here, group * out_width : (group + 1) * out_width] = jnp.dot(
                wide[here, :done], w_ref[group, :done, :], preferred_element_type=F32
            )
        power = None
        for lane in range(0, done, 128):
            values = wide[here, lane : lane + 128].astype(F32)
            power = values * values if power is None else power + values * values
        state[here, 3 * out_width :] = power


def finish_kernel(head_size, factor, state, w_ref, *refs):
    count = (len(refs) - 2) // 2
    lasts, (q_ref, kv_ref), pieces = refs[:count], refs[count : count + 2], refs[count + 2 :]
    rows, width = lasts[0].shape
    depth, out_width = w_ref.shape[1:]
    for stream, last in enumerate(lasts):
        here = slice(stream * rows, (stream + 1) * rows)
        q, k, v = (
            state[here, group * out_width : (group + 1) * out_width]
            + jnp.dot(last[...], w_ref[group, depth - width :, :], preferred_element_type=F32)
            for group in range(3)
        )
        power = state[here, 3 * out_width :]
        for lane in range(0, width, 128):
            values = last[:, lane : lane + 128].astype(F32)
            power += values * values
        scale = lax.rsqrt(jnp.sum(power, axis=-1, keepdims=True) * (1.0 / depth) + 1e-06)
        q, k, v = q * scale, k * scale, v * scale
        for head in range(out_width // head_size):
            lanes = slice(head * head_size, (head + 1) * head_size)
            qh, kh = q[:, lanes], k[:, lanes]
            q_size = lax.rsqrt(jnp.sum(qh * qh, axis=-1, keepdims=True) + 1e-06)
            k_size = lax.rsqrt(jnp.sum(kh * kh, axis=-1, keepdims=True) + 1e-06)
            q_ref[here, lanes] = (qh * (q_size * (factor[head] * LOG2E))).astype(BF16)
            kv_ref[here, lanes] = (kh * k_size).astype(BF16)
        kv_ref[here, out_width:] = v.astype(BF16)
        pieces[stream][...] = kv_ref[here, :]


def project_begin(wide, weights, blocks):
    rows, depth = wide.shape
    groups, _, out_width = weights.shape
    return pl.pallas_call(
        functools.partial(begin_kernel, blocks),
        out_shape=pltpu.VMEM((rows, groups * out_width + 128), F32),
        in_specs=[VMEM] * 2,
        out_specs=VMEM,
        compiler_params=pltpu.CompilerParams(vmem_limit_bytes=16 << 20),
        cost_estimate=pl.CostEstimate(
            flops=2 * rows * depth * groups * out_width,
            bytes_accessed=2 * depth * (rows + groups * out_width),
            transcendentals=0,
        ),
        name="project_begin",
    )(in_vmem(wide), in_vmem(weights))


def project_finish(factor, state, weights, lasts, head_size):
    rows, width = lasts[0].shape
    out_width = weights.shape[2]
    total = rows * len(lasts)
    return pl.pallas_call(
        functools.partial(finish_kernel, head_size),
        out_shape=(
            pltpu.VMEM((total, out_width), BF16),
            pltpu.VMEM((total, 2 * out_width), BF16),
            *[pltpu.VMEM((rows, 2 * out_width), BF16)] * len(lasts),
        ),
        in_specs=[SMEM] + [VMEM] * (2 + len(lasts)),
        out_specs=(VMEM,) * (2 + len(lasts)),
        compiler_params=pltpu.CompilerParams(vmem_limit_bytes=16 << 20),
        cost_estimate=pl.CostEstimate(
            flops=6 * total * width * out_width, bytes_accessed=8 * total * out_width, transcendentals=0
        ),
        name="project_finish",
    )(in_hbm(factor), in_vmem(state), in_vmem(weights), *map(in_vmem, lasts))


def attend_kernel(
    head_size, counts, has_acc, count_out, count_streams, info, ids, q_ref, id_row, *refs
):
    count_blocks, count_parts = counts
    kv_refs, rest = refs[: count_blocks * count_parts], refs[count_blocks * count_parts :]
    if has_acc:
        acc_in, rest = rest[0], rest[1:]
    if count_out:
        w_ref, outs, (k_all, v_ones, acc, attended) = rest[0], rest[1:-4], rest[-4:]
    else:
        acc_out, k_all, v_ones, acc = rest
    acc[...] = acc_in[...] if has_acc else jnp.zeros_like(acc)
    rows, width = q_ref.shape
    heads = width // head_size
    keys = k_all.shape[0]
    tile = id_row.shape[2]
    q_first = info[count_blocks]
    v_ones[:, :, head_size:] = jnp.ones((heads, keys, head_size), BF16)
    for number in range(count_blocks):
        begin = 0
        for kv_ref in kv_refs[number * count_parts : (number + 1) * count_parts]:
            here = slice(begin, begin + kv_ref.shape[0])
            begin += kv_ref.shape[0]
            k_all[here, :] = kv_ref[:, :width]
            for head in range(heads):
                start = width + head * head_size
                v_ones[head, here, :head_size] = kv_ref[:, start : start + head_size]
        first = info[number]
        key_low, key_high = ids[first], ids[first + keys - 1]

        @pl.loop(0, rows // tile)
        def _(index):
            base = pl.multiple_of(index * tile, tile)
            here = pl.ds(base, tile)
            q_low, q_high = ids[q_first + base], ids[q_first + base + tile - 1]

            def add(masked):
                if masked:
                    key_ids = [id_row[first // tile + n] for n in range(keys // tile)]
                    own = jnp.broadcast_to(id_row[q_first // tile + index], (8, tile))
                    allowed = jnp.concatenate(key_ids, axis=1) <= jnp.transpose(own)[:, :1]
                for head in range(heads):
                    lanes = slice(head * head_size, (head + 1) * head_size)
                    score = lax.dot_general(
                        q_ref[here, lanes],
                        k_all[:, lanes],
                        (((1,), (1,)), ((), ())),
                        preferred_element_type=F32,
                    )
                    weight = jnp.exp2(score)
                    if masked:
                        weight = jnp.where(allowed, weight, 0.0)
                    spread = slice(2 * head * head_size, 2 * (head + 1) * head_size)
                    acc[here, spread] += jnp.dot(
                        weight.astype(BF16), v_ones[head], preferred_element_type=F32
                    )

            @pl.when(key_high <= q_low)
            def _():
                add(False)

            @pl.when((key_high > q_low) & (key_low <= q_high))
            def _():
                add(True)

    if not count_out:
        acc_out[...] = acc[...]
        return
    for head in range(heads):
        start = 2 * head * head_size
        attended[:, head * head_size : (head + 1) * head_size] = (
            acc[:, start : start + head_size]
            / acc[:, start + head_size : start + 2 * head_size]
        ).astype(BF16)
    out_rows, out_width = outs[0].shape
    for number, out in enumerate(outs):
        lane = info[count_blocks + 1 + number] * out_width
        first = number * count_streams // count_out * out_rows
        out[...] = jnp.dot(
            attended[first : first + out_rows, :],
            w_ref[:, pl.ds(pl.multiple_of(lane, out_width), out_width)],
            preferred_element_type=F32,
        ).astype(BF16)


def attend(info, ids, query, blocks, head_size, acc=None, w_out=None, streams=0):
    total, width = query.shape
    parts = [part for block in blocks for part in block]
    keys = sum(part.shape[0] for part in blocks[0])
    heads = width // head_size
    count_out = streams * w_out.shape[1] // width if streams else 0
    scratch = [
        pltpu.VMEM((keys, width), BF16),
        pltpu.VMEM((heads, keys, 2 * head_size), BF16),
        pltpu.VMEM((total, 2 * width), F32),
    ]
    operands = [in_vmem(query), in_hbm(ids.reshape(-1, 1, math.gcd(total, 256)))]
    operands += map(in_vmem, parts)
    if acc is not None:
        operands.append(in_vmem(acc))
    if count_out:
        operands.append(in_vmem(w_out))
        scratch.append(pltpu.VMEM((total, width), BF16))
        shape = pltpu.VMEM((total // streams, w_out.shape[1] * streams // count_out), BF16)
    else:
        shape = pltpu.VMEM((total, 2 * width), F32)
    outs = count_out or 1
    return pl.pallas_call(
        functools.partial(
            attend_kernel, head_size, (len(blocks), len(blocks[0])), acc is not None, count_out, streams
        ),
        out_shape=(shape,) * outs,
        in_specs=[SMEM, SMEM] + [VMEM] * len(operands),
        out_specs=(VMEM,) * outs,
        scratch_shapes=scratch,
        compiler_params=pltpu.CompilerParams(
            vmem_limit_bytes=(16 << 20) + 4 * sum(part.size for part in parts)
        ),
        cost_estimate=pl.CostEstimate(flops=1 << 20, bytes_accessed=1 << 10, transcendentals=0),
        name="attend_last" if count_out else "attend",
    )(info, in_hbm(ids), *operands)


def load_kernel(source, target, sem):
    copy = pltpu.make_async_copy(source, target, sem)
    copy.start()
    copy.wait()


def loaded(value):
    return pl.pallas_call(
        load_kernel,
        out_shape=pltpu.VMEM(value.shape, value.dtype),
        in_specs=[pl.BlockSpec(memory_space=pltpu.HBM)],
        out_specs=pl.BlockSpec(memory_space=pl.ANY),
        scratch_shapes=[pltpu.SemaphoreType.DMA(())],
        compiler_params=pltpu.CompilerParams(vmem_limit_bytes=1 << 20),
        cost_estimate=pl.CostEstimate(flops=0, bytes_accessed=1 << 20, transcendentals=0),
        name="load",
    )(in_hbm(value))


def total_of(*parts):
    return sum(part.astype(F32) for part in parts).astype(BF16)


def body(mesh_shape, tokens, norm_gain, w_qkv, head_scale, w_out, scale_ids):
    ring, seqs = mesh_shape["head"], mesh_shape["seq"]
    outer = seqs // 2
    rows, width = tokens.shape
    half = rows // 2
    head_size = w_qkv.shape[2] // head_scale.shape[0]
    head_at, seq_at = lax.axis_index("head"), lax.axis_index("seq")
    place = ring_place(head_at, ring)
    chip, core = seq_at // 2, seq_at % 2
    index_at = lambda offset: ring_index((place + offset + ring) % ring, ring)
    numbers = lambda values: jnp.stack(values).astype(jnp.int32)
    at = [index_at(offset) for offset in range(ring)]

    streams, ways = (0, 1), ((0, 1), (1, -1))
    farthest = ring // 2
    reach = [(farthest, farthest - 1), (farthest - 1, farthest)]

    order = [0] + [sign * step % ring for step in range(1, farthest) for sign in (-1, 1)] + [farthest]
    held = [[tokens[s * half : (s + 1) * half]] * 2 for s in streams]
    wide, blocks, targets = None, [in_hbm(tokens)], [(0, 0)]
    for step in range(1, farthest + 1):
        for s in streams:
            for way, sign in ways:
                if step <= reach[s][way]:
                    held[s][way] = along(held[s][way], sign, ring)
        if step == 1:
            held[1][1], weights = lax.optimization_barrier(
                (held[1][1], fold_gain(order, numbers(at), norm_gain, w_qkv))
            )
        elif step == 2:
            wide = placed(targets, blocks, wide, (rows, ring * width))
            blocks, targets = [], []
        elif step == 3:
            held[1][1], wide = lax.optimization_barrier(
                (held[1][1], placed(targets, blocks, wide, (rows, ring * width)))
            )
            blocks, targets = [], []
        if step < farthest:
            for s in streams:
                for way, sign in ways:
                    blocks.append(in_vmem(held[s][way]))
                    targets.append((s * half, (2 * step - 1 + way) * width))
    wide = placed(targets, blocks, wide, (rows, ring * width))
    lasts = [held[0][0], held[1][1]]
    state = project_begin(wide, weights, ring)
    query, kv, *pieces = project_finish(head_scale, state, weights, lasts, head_size)

    far, straight, crossed = [], [], []
    for step in range(outer):
        source = 2 * ((chip + outer - step) % outer)
        straight.append((source + core) * rows)
        crossed.append((source + 1 - core) * rows)
        if step:
            shift = [(2 * a + b, 2 * ((a + step) % outer) + b) for a in range(outer) for b in (0, 1)]
            far.append([lax.ppermute(kv, "seq", shift)])
    first = [seq_at * rows]
    (acc,) = attend(numbers(straight[:1] + first), scale_ids, query, [[kv]], head_size)
    near = [[swapped(piece, seqs) for piece in pieces]]
    acc, near = lax.optimization_barrier((acc, near))
    (acc,) = attend(numbers(crossed[:1] + first), scale_ids, query, near, head_size, acc)
    acc, far, w_near = lax.optimization_barrier((acc, far, loaded(w_out)))
    far_crossed = [[swapped(part, seqs) for part in block] for block in far]
    (acc,) = attend(numbers(straight[1:] + first), scale_ids, query, far, head_size, acc)

    goals = [[*range(up, 0, -1), *range(-down, 0), 0] for up, down in reach]
    info = numbers(crossed[1:] + first + [at[goal % ring] for goal in goals[0] + goals[1]])
    parts = attend(
        info, scale_ids, query, far_crossed, head_size, acc, w_near, len(streams)
    )
    parts = [dict(zip(goals[s], parts[s * ring : (s + 1) * ring])) for s in streams]
    sums = [[None, None] for s in streams]
    for step in range(farthest, 0, -1):
        for s in streams:
            for way, sign in ways:
                if step <= reach[s][way]:
                    part = parts[s][sign * step]
                    if sums[s][way] is not None:
                        part = total_of(part, sums[s][way])
                    sums[s][way] = along(part, sign, ring)
    return jnp.concatenate([total_of(parts[s][0], *sums[s]) for s in streams])


def solution(mesh):
    placed = (P("seq", "head"), P(), P(None, None, "head"), P("head"), P("head", None), P())
    return jax.shard_map(
        functools.partial(body, dict(mesh.shape)),
        mesh=mesh,
        in_specs=placed,
        out_specs=P("seq", "head"),
        check_vma=False,
    )
```

```python
import functools
import math

import jax
import jax.numpy as jnp
from jax import lax
from jax.experimental import pallas as pl
from jax.experimental.pallas import tpu as pltpu
from jax.sharding import PartitionSpec as P

LOG2E = math.log2(math.e)
VMEM = pl.BlockSpec(memory_space=pltpu.VMEM)
SMEM = pl.BlockSpec(memory_space=pltpu.SMEM)
F32 = jnp.float32
BF16 = jnp.bfloat16


def ring_order(count):
    line = count // 2
    return [2 * z for z in range(line)] + [2 * z + 1 for z in reversed(range(line))]


def ring_place(index, count):
    return jnp.where(index % 2 == 0, index // 2, count - 1 - index // 2)


def ring_index(place, count):
    return jnp.where(place < count // 2, 2 * place, 2 * (count - 1 - place) + 1)


def along(value, step, count):
    order = ring_order(count)
    return lax.ppermute(
        value, "head", [(order[p], order[(p + step) % count]) for p in range(count)]
    )


def swapped(value, seq_count):
    return lax.ppermute(value, "seq", [(seq, seq + 1 - 2 * (seq % 2)) for seq in range(seq_count)])


def in_hbm(value):
    return pltpu.with_memory_space_constraint(value, pltpu.HBM)


def in_vmem(value):
    return pltpu.with_memory_space_constraint(value, pltpu.VMEM)


def fold_kernel(order, at, gain_ref, w_hbm, out_ref, sems):
    lanes = gain_ref.shape[1]
    size = w_hbm.shape[1] // len(order)
    per = size // lanes

    def fetch(n):
        start = pl.multiple_of(at[order[n]] * size, size)
        return pltpu.make_async_copy(
            w_hbm.at[:, pl.ds(start, size), :], out_ref.at[:, n * size : (n + 1) * size, :], sems.at[n]
        )

    for n in range(len(order)):
        fetch(n).start()
    for n in range(len(order)):
        columns = jnp.transpose(gain_ref[pl.ds(at[order[n]] * per, per), :])
        fetch(n).wait()
        for piece in range(per):
            first = n * size + piece * lanes
            for group in range(w_hbm.shape[0]):
                here = (group, slice(first, first + lanes), slice(None))
                scaled = out_ref[here].astype(F32) * columns[:, piece : piece + 1]
                out_ref[here] = scaled.astype(BF16)


def fold_gain(order, at, gain, weights):
    depth = weights.shape[1]
    lanes = math.gcd(depth // len(order), 128)
    return pl.pallas_call(
        functools.partial(fold_kernel, order),
        out_shape=pltpu.VMEM(weights.shape, BF16),
        in_specs=[SMEM, VMEM, pl.BlockSpec(memory_space=pltpu.HBM)],
        out_specs=VMEM,
        scratch_shapes=[pltpu.SemaphoreType.DMA((len(order),))],
        compiler_params=pltpu.CompilerParams(vmem_limit_bytes=16 << 20),
        cost_estimate=pl.CostEstimate(
            flops=weights.size, bytes_accessed=4 * weights.size, transcendentals=0
        ),
        name="fold_gain",
    )(at, in_hbm(gain.reshape(depth // lanes, lanes)), in_hbm(weights))


def place_kernel(targets, *refs):
    blocks, wide, sems = refs[: len(targets)], refs[-2], refs[-1]
    copies = []
    for n, (block, (row, lane)) in enumerate(zip(blocks, targets)):
        rows, width = block.shape
        here = wide.at[row : row + rows, lane : lane + width]
        copies.append(pltpu.make_async_copy(block, here, sems.at[n]))
    for copy in copies:
        copy.start()
    for copy in copies:
        copy.wait()


def placed(targets, blocks, wide, shape):
    operands = [*blocks] + ([] if wide is None else [in_vmem(wide)])
    return pl.pallas_call(
        functools.partial(place_kernel, targets),
        out_shape=pltpu.VMEM(shape, BF16),
        in_specs=[pl.BlockSpec(memory_space=pl.ANY)] * len(operands),
        out_specs=pl.BlockSpec(memory_space=pl.ANY),
        scratch_shapes=[pltpu.SemaphoreType.DMA((len(targets),))],
        input_output_aliases={} if wide is None else {len(blocks): 0},
        compiler_params=pltpu.CompilerParams(vmem_limit_bytes=1 << 20),
        cost_estimate=pl.CostEstimate(flops=0, bytes_accessed=1 << 20, transcendentals=0),
        name="place",
    )(*operands)


def begin_kernel(blocks, wide, w_ref, state):
    rows, depth = wide.shape
    out_width = w_ref.shape[2]
    done = depth - depth // blocks
    tile = math.gcd(rows, 256)
    for first in range(0, rows, tile):
        here = slice(first, first + tile)
        for group in range(3):
            state[here, group * out_width : (group + 1) * out_width] = jnp.dot(
                wide[here, :done], w_ref[group, :done, :], preferred_element_type=F32
            )
        power = None
        for lane in range(0, done, 128):
            values = wide[here, lane : lane + 128].astype(F32)
            power = values * values if power is None else power + values * values
        state[here, 3 * out_width :] = power


def finish_kernel(head_size, factor, state, w_ref, *refs):
    count = 2
    lasts, (q_ref, kv_ref), rest = refs[:count], refs[count : count + 2], refs[count + 2 :]
    halves, pieces = rest[:count], rest[count:]
    rows, width = lasts[0].shape
    depth, out_width = w_ref.shape[1:]
    for stream, last in enumerate(lasts):
        here = slice(stream * rows, (stream + 1) * rows)
        q, k, v = (
            state[here, group * out_width : (group + 1) * out_width]
            + jnp.dot(last[...], w_ref[group, depth - width :, :], preferred_element_type=F32)
            for group in range(3)
        )
        power = state[here, 3 * out_width :]
        for lane in range(0, width, 128):
            values = last[:, lane : lane + 128].astype(F32)
            power += values * values
        scale = lax.rsqrt(jnp.sum(power, axis=-1, keepdims=True) * (1.0 / depth) + 1e-06)
        q, k, v = q * scale, k * scale, v * scale
        for head in range(out_width // head_size):
            lanes = slice(head * head_size, (head + 1) * head_size)
            qh, kh = q[:, lanes], k[:, lanes]
            q_size = lax.rsqrt(jnp.sum(qh * qh, axis=-1, keepdims=True) + 1e-06)
            k_size = lax.rsqrt(jnp.sum(kh * kh, axis=-1, keepdims=True) + 1e-06)
            q_ref[here, lanes] = (qh * (q_size * (factor[head] * LOG2E))).astype(BF16)
            kv_ref[here, lanes] = (kh * k_size).astype(BF16)
        kv_ref[here, out_width:] = v.astype(BF16)
        halves[stream][...] = kv_ref[here, :]
    start = 0
    for piece in pieces:
        piece[...] = kv_ref[start : start + piece.shape[0], :]
        start += piece.shape[0]


def project_begin(wide, weights, blocks):
    rows, depth = wide.shape
    groups, _, out_width = weights.shape
    return pl.pallas_call(
        functools.partial(begin_kernel, blocks),
        out_shape=pltpu.VMEM((rows, groups * out_width + 128), F32),
        in_specs=[VMEM] * 2,
        out_specs=VMEM,
        compiler_params=pltpu.CompilerParams(vmem_limit_bytes=16 << 20),
        cost_estimate=pl.CostEstimate(
            flops=2 * rows * depth * groups * out_width,
            bytes_accessed=2 * depth * (rows + groups * out_width),
            transcendentals=0,
        ),
        name="project_begin",
    )(in_vmem(wide), in_vmem(weights))


def project_finish(factor, state, weights, lasts, count_pieces, head_size):
    rows, width = lasts[0].shape
    out_width = weights.shape[2]
    total = rows * len(lasts)
    units = total // 16
    sizes = [rows] * len(lasts)
    sizes += [16 * ((units + n) // count_pieces) for n in range(count_pieces)]
    return pl.pallas_call(
        functools.partial(finish_kernel, head_size),
        out_shape=(
            pltpu.VMEM((total, out_width), BF16),
            pltpu.VMEM((total, 2 * out_width), BF16),
            *[pltpu.VMEM((size, 2 * out_width), BF16) for size in sizes],
        ),
        in_specs=[SMEM] + [VMEM] * (2 + len(lasts)),
        out_specs=(VMEM,) * (2 + len(sizes)),
        compiler_params=pltpu.CompilerParams(vmem_limit_bytes=16 << 20),
        cost_estimate=pl.CostEstimate(
            flops=6 * total * width * out_width, bytes_accessed=8 * total * out_width, transcendentals=0
        ),
        name="project_finish",
    )(in_hbm(factor), in_vmem(state), in_vmem(weights), *map(in_vmem, lasts))


def attend_kernel(
    head_size, counts, has_acc, count_out, count_streams, info, ids, q_ref, id_row, *refs
):
    count_blocks, count_parts = counts
    kv_refs, rest = refs[: count_blocks * count_parts], refs[count_blocks * count_parts :]
    if has_acc:
        acc_in, rest = rest[0], rest[1:]
    if count_out:
        w_ref, outs, (k_all, v_ones, acc, attended) = rest[0], rest[1:-4], rest[-4:]
    else:
        acc_out, k_all, v_ones, acc = rest
    acc[...] = acc_in[...] if has_acc else jnp.zeros_like(acc)
    rows, width = q_ref.shape
    heads = width // head_size
    keys = k_all.shape[0]
    tile = id_row.shape[2]
    q_first = info[count_blocks]
    v_ones[:, :, head_size:] = jnp.ones((heads, keys, head_size), BF16)
    for number in range(count_blocks):
        begin = 0
        for kv_ref in kv_refs[number * count_parts : (number + 1) * count_parts]:
            here = slice(begin, begin + kv_ref.shape[0])
            begin += kv_ref.shape[0]
            k_all[here, :] = kv_ref[:, :width]
            for head in range(heads):
                start = width + head * head_size
                v_ones[head, here, :head_size] = kv_ref[:, start : start + head_size]
        first = info[number]
        key_low, key_high = ids[first], ids[first + keys - 1]

        @pl.loop(0, rows // tile)
        def _(index):
            base = pl.multiple_of(index * tile, tile)
            here = pl.ds(base, tile)
            q_low, q_high = ids[q_first + base], ids[q_first + base + tile - 1]

            def add(masked):
                if masked:
                    key_ids = [id_row[first // tile + n] for n in range(keys // tile)]
                    own = jnp.broadcast_to(id_row[q_first // tile + index], (8, tile))
                    allowed = jnp.concatenate(key_ids, axis=1) <= jnp.transpose(own)[:, :1]
                for head in range(heads):
                    lanes = slice(head * head_size, (head + 1) * head_size)
                    score = lax.dot_general(
                        q_ref[here, lanes],
                        k_all[:, lanes],
                        (((1,), (1,)), ((), ())),
                        preferred_element_type=F32,
                    )
                    weight = jnp.exp2(score)
                    if masked:
                        weight = jnp.where(allowed, weight, 0.0)
                    spread = slice(2 * head * head_size, 2 * (head + 1) * head_size)
                    acc[here, spread] += jnp.dot(
                        weight.astype(BF16), v_ones[head], preferred_element_type=F32
                    )

            @pl.when(key_high <= q_low)
            def _():
                add(False)

            @pl.when((key_high > q_low) & (key_low <= q_high))
            def _():
                add(True)

    if not count_out:
        acc_out[...] = acc[...]
        return
    for head in range(heads):
        start = 2 * head * head_size
        attended[:, head * head_size : (head + 1) * head_size] = (
            acc[:, start : start + head_size]
            / acc[:, start + head_size : start + 2 * head_size]
        ).astype(BF16)
    out_rows, out_width = outs[0].shape
    for number, out in enumerate(outs):
        lane = info[count_blocks + 1 + number] * out_width
        first = number * count_streams // count_out * out_rows
        out[...] = jnp.dot(
            attended[first : first + out_rows, :],
            w_ref[:, pl.ds(pl.multiple_of(lane, out_width), out_width)],
            preferred_element_type=F32,
        ).astype(BF16)


def attend(info, ids, query, blocks, head_size, acc=None, w_out=None, streams=0):
    total, width = query.shape
    parts = [part for block in blocks for part in block]
    keys = sum(part.shape[0] for part in blocks[0])
    heads = width // head_size
    count_out = streams * w_out.shape[1] // width if streams else 0
    scratch = [
        pltpu.VMEM((keys, width), BF16),
        pltpu.VMEM((heads, keys, 2 * head_size), BF16),
        pltpu.VMEM((total, 2 * width), F32),
    ]
    operands = [in_vmem(query), in_hbm(ids.reshape(-1, 1, math.gcd(total, 256)))]
    operands += map(in_vmem, parts)
    if acc is not None:
        operands.append(in_vmem(acc))
    if count_out:
        operands.append(in_hbm(w_out))
        scratch.append(pltpu.VMEM((total, width), BF16))
        shape = pltpu.VMEM((total // streams, w_out.shape[1] * streams // count_out), BF16)
    else:
        shape = pltpu.VMEM((total, 2 * width), F32)
    outs = count_out or 1
    return pl.pallas_call(
        functools.partial(
            attend_kernel, head_size, (len(blocks), len(blocks[0])), acc is not None, count_out, streams
        ),
        out_shape=(shape,) * outs,
        in_specs=[SMEM, SMEM] + [VMEM] * len(operands),
        out_specs=(VMEM,) * outs,
        scratch_shapes=scratch,
        compiler_params=pltpu.CompilerParams(
            vmem_limit_bytes=(16 << 20) + 4 * sum(part.size for part in parts)
        ),
        cost_estimate=pl.CostEstimate(flops=1 << 20, bytes_accessed=1 << 10, transcendentals=0),
        name="attend_last" if count_out else "attend",
    )(info, in_hbm(ids), *operands)


def total_of(*parts):
    return sum(part.astype(F32) for part in parts).astype(BF16)


def body(mesh_shape, tokens, norm_gain, w_qkv, head_scale, w_out, scale_ids):
    ring, seqs = mesh_shape["head"], mesh_shape["seq"]
    outer = seqs // 2
    rows, width = tokens.shape
    half = rows // 2
    head_size = w_qkv.shape[2] // head_scale.shape[0]
    head_at, seq_at = lax.axis_index("head"), lax.axis_index("seq")
    place = ring_place(head_at, ring)
    chip, core = seq_at // 2, seq_at % 2
    index_at = lambda offset: ring_index((place + offset + ring) % ring, ring)
    numbers = lambda values: jnp.stack(values).astype(jnp.int32)
    at = [index_at(offset) for offset in range(ring)]

    streams, ways = (0, 1), ((0, 1), (1, -1))
    farthest = ring // 2
    reach = [(farthest, farthest - 1), (farthest - 1, farthest)]

    order = [0] + [sign * step % ring for step in range(1, farthest) for sign in (-1, 1)] + [farthest]
    held = [[tokens[s * half : (s + 1) * half]] * 2 for s in streams]
    wide, blocks, targets = None, [in_hbm(tokens)], [(0, 0)]
    for step in range(1, farthest + 1):
        for s in streams:
            for way, sign in ways:
                if step <= reach[s][way]:
                    held[s][way] = along(held[s][way], sign, ring)
        if step == 1:
            held[1][1], weights = lax.optimization_barrier(
                (held[1][1], fold_gain(order, numbers(at), norm_gain, w_qkv))
            )
        elif step == 2:
            wide = placed(targets, blocks, wide, (rows, ring * width))
            blocks, targets = [], []
        elif step == 3:
            held[1][1], wide = lax.optimization_barrier(
                (held[1][1], placed(targets, blocks, wide, (rows, ring * width)))
            )
            blocks, targets = [], []
        if step < farthest:
            for s in streams:
                for way, sign in ways:
                    blocks.append(in_vmem(held[s][way]))
                    targets.append((s * half, (2 * step - 1 + way) * width))
    wide = placed(targets, blocks, wide, (rows, ring * width))
    lasts = [held[0][0], held[1][1]]
    state = project_begin(wide, weights, ring)
    query, kv, *parts = project_finish(head_scale, state, weights, lasts, 3, head_size)
    halves, pieces = parts[:2], parts[2:]

    far, straight, crossed = [], [], []
    for step in range(outer):
        source = 2 * ((chip + outer - step) % outer)
        straight.append((source + core) * rows)
        crossed.append((source + 1 - core) * rows)
        if step:
            shift = [(2 * a + b, 2 * ((a + step) % outer) + b) for a in range(outer) for b in (0, 1)]
            far.append([lax.ppermute(part, "seq", shift) for part in halves])
    first = [seq_at * rows]
    (acc,) = attend(numbers(straight[:1] + first), scale_ids, query, [[kv]], head_size)
    near = [[swapped(piece, seqs) for piece in pieces]]
    acc, near = lax.optimization_barrier((acc, near))
    (acc,) = attend(numbers(crossed[:1] + first), scale_ids, query, near, head_size, acc)
    acc, far = lax.optimization_barrier((acc, far))
    far_crossed = [[swapped(part, seqs) for part in block] for block in far]
    (acc,) = attend(numbers(straight[1:] + first), scale_ids, query, far, head_size, acc)

    goals = [[*range(up, 0, -1), *range(-down, 0), 0] for up, down in reach]
    info = numbers(crossed[1:] + first + [at[goal % ring] for goal in goals[0] + goals[1]])
    parts = attend(
        info, scale_ids, query, far_crossed, head_size, acc, w_out, len(streams)
    )
    parts = [dict(zip(goals[s], parts[s * ring : (s + 1) * ring])) for s in streams]
    sums = [[None, None] for s in streams]
    for step in range(farthest, 0, -1):
        for s in streams:
            for way, sign in ways:
                if step <= reach[s][way]:
                    part = parts[s][sign * step]
                    if sums[s][way] is not None:
                        part = total_of(part, sums[s][way])
                    sums[s][way] = along(part, sign, ring)
    return jnp.concatenate([total_of(parts[s][0], *sums[s]) for s in streams])


def solution(mesh):
    placed = (P("seq", "head"), P(), P(None, None, "head"), P("head"), P("head", None), P())
    return jax.shard_map(
        functools.partial(body, dict(mesh.shape)),
        mesh=mesh,
        in_specs=placed,
        out_specs=P("seq", "head"),
        check_vma=False,
    )
```

```python
import functools
import math

import jax
import jax.numpy as jnp
from jax import lax
from jax.experimental import pallas as pl
from jax.experimental.pallas import tpu as pltpu
from jax.sharding import PartitionSpec as P

LOG2E = math.log2(math.e)
VMEM = pl.BlockSpec(memory_space=pltpu.VMEM)
SMEM = pl.BlockSpec(memory_space=pltpu.SMEM)
F32 = jnp.float32
BF16 = jnp.bfloat16


def ring_order(count):
    line = count // 2
    return [2 * z for z in range(line)] + [2 * z + 1 for z in reversed(range(line))]


def ring_place(index, count):
    return jnp.where(index % 2 == 0, index // 2, count - 1 - index // 2)


def ring_index(place, count):
    return jnp.where(place < count // 2, 2 * place, 2 * (count - 1 - place) + 1)


def along(value, step, count):
    order = ring_order(count)
    return lax.ppermute(
        value, "head", [(order[p], order[(p + step) % count]) for p in range(count)]
    )


def swapped(value, seq_count):
    return lax.ppermute(value, "seq", [(seq, seq + 1 - 2 * (seq % 2)) for seq in range(seq_count)])


def in_hbm(value):
    return pltpu.with_memory_space_constraint(value, pltpu.HBM)


def in_vmem(value):
    return pltpu.with_memory_space_constraint(value, pltpu.VMEM)


def fold_kernel(order, at, gain_ref, w_hbm, tokens, out_ref, wide, sems):
    lanes = gain_ref.shape[1]
    size = w_hbm.shape[1] // len(order)
    per = size // lanes

    def fetch(n):
        start = pl.multiple_of(at[order[n]] * size, size)
        return pltpu.make_async_copy(
            w_hbm.at[:, pl.ds(start, size), :],
            out_ref.at[:, n * size : (n + 1) * size, :],
            sems.at[n],
        )

    for n in range(len(order)):
        fetch(n).start()
    own = pltpu.make_async_copy(tokens, wide.at[:, : tokens.shape[1]], sems.at[len(order)])
    own.start()
    for n in range(len(order)):
        columns = jnp.transpose(gain_ref[pl.ds(at[order[n]] * per, per), :])
        fetch(n).wait()
        for piece in range(per):
            first = n * size + piece * lanes
            for group in range(w_hbm.shape[0]):
                here = (group, slice(first, first + lanes), slice(None))
                scaled = out_ref[here].astype(F32) * columns[:, piece : piece + 1]
                out_ref[here] = scaled.astype(BF16)
    own.wait()


def fold_gain(order, at, gain, weights, tokens):
    depth = weights.shape[1]
    lanes = math.gcd(depth // len(order), 128)
    hbm = pl.BlockSpec(memory_space=pltpu.HBM)
    return pl.pallas_call(
        functools.partial(fold_kernel, order),
        out_shape=(pltpu.VMEM(weights.shape, BF16), pltpu.VMEM((tokens.shape[0], depth), BF16)),
        in_specs=[SMEM, VMEM, hbm, hbm],
        out_specs=(VMEM, pl.BlockSpec(memory_space=pl.ANY)),
        scratch_shapes=[pltpu.SemaphoreType.DMA((len(order) + 1,))],
        compiler_params=pltpu.CompilerParams(vmem_limit_bytes=16 << 20),
        cost_estimate=pl.CostEstimate(
            flops=weights.size, bytes_accessed=4 * weights.size, transcendentals=0
        ),
        name="fold_gain",
    )(at, in_hbm(gain.reshape(depth // lanes, lanes)), in_hbm(weights), in_hbm(tokens))


def place_kernel(targets, *refs):
    blocks, wide, sems = refs[: len(targets)], refs[-2], refs[-1]
    copies = []
    for n, (block, (row, lane)) in enumerate(zip(blocks, targets)):
        rows, width = block.shape
        here = wide.at[row : row + rows, lane : lane + width]
        copies.append(pltpu.make_async_copy(block, here, sems.at[n]))
    for copy in copies:
        copy.start()
    for copy in copies:
        copy.wait()


def placed(targets, blocks, wide):
    operands = [*map(in_vmem, blocks), in_vmem(wide)]
    return pl.pallas_call(
        functools.partial(place_kernel, targets),
        out_shape=pltpu.VMEM(wide.shape, BF16),
        in_specs=[pl.BlockSpec(memory_space=pl.ANY)] * len(operands),
        out_specs=pl.BlockSpec(memory_space=pl.ANY),
        scratch_shapes=[pltpu.SemaphoreType.DMA((len(targets),))],
        input_output_aliases={len(blocks): 0},
        compiler_params=pltpu.CompilerParams(vmem_limit_bytes=1 << 20),
        cost_estimate=pl.CostEstimate(flops=0, bytes_accessed=1 << 20, transcendentals=0),
        name="place",
    )(*operands)


def begin_kernel(blocks, wide, w_ref, state):
    rows, depth = wide.shape
    out_width = w_ref.shape[2]
    done = depth - depth // blocks
    tile = math.gcd(rows, 256)
    for first in range(0, rows, tile):
        here = slice(first, first + tile)
        for group in range(3):
            state[here, group * out_width : (group + 1) * out_width] = jnp.dot(
                wide[here, :done], w_ref[group, :done, :], preferred_element_type=F32
            )
        power = None
        for lane in range(0, done, 128):
            values = wide[here, lane : lane + 128].astype(F32)
            power = values * values if power is None else power + values * values
        state[here, 3 * out_width :] = power


def finish_kernel(head_size, factor, state, w_ref, *refs):
    count = 2
    lasts, (q_ref, kv_ref), rest = refs[:count], refs[count : count + 2], refs[count + 2 :]
    halves, pieces = rest[:count], rest[count:]
    rows, width = lasts[0].shape
    depth, out_width = w_ref.shape[1:]
    for stream, last in enumerate(lasts):
        here = slice(stream * rows, (stream + 1) * rows)
        q, k, v = (
            state[here, group * out_width : (group + 1) * out_width]
            + jnp.dot(last[...], w_ref[group, depth - width :, :], preferred_element_type=F32)
            for group in range(3)
        )
        power = state[here, 3 * out_width :]
        for lane in range(0, width, 128):
            values = last[:, lane : lane + 128].astype(F32)
            power += values * values
        scale = lax.rsqrt(jnp.sum(power, axis=-1, keepdims=True) * (1.0 / depth) + 1e-06)
        q, k, v = q * scale, k * scale, v * scale
        for head in range(out_width // head_size):
            lanes = slice(head * head_size, (head + 1) * head_size)
            qh, kh = q[:, lanes], k[:, lanes]
            q_size = lax.rsqrt(jnp.sum(qh * qh, axis=-1, keepdims=True) + 1e-06)
            k_size = lax.rsqrt(jnp.sum(kh * kh, axis=-1, keepdims=True) + 1e-06)
            q_ref[here, lanes] = (qh * (q_size * (factor[head] * LOG2E))).astype(BF16)
            kv_ref[here, lanes] = (kh * k_size).astype(BF16)
        kv_ref[here, out_width:] = v.astype(BF16)
        halves[stream][...] = kv_ref[here, :]
    start = 0
    for piece in pieces:
        piece[...] = kv_ref[start : start + piece.shape[0], :]
        start += piece.shape[0]


def project_begin(wide, weights, blocks):
    rows, depth = wide.shape
    groups, _, out_width = weights.shape
    return pl.pallas_call(
        functools.partial(begin_kernel, blocks),
        out_shape=pltpu.VMEM((rows, groups * out_width + 128), F32),
        in_specs=[VMEM] * 2,
        out_specs=VMEM,
        compiler_params=pltpu.CompilerParams(vmem_limit_bytes=16 << 20),
        cost_estimate=pl.CostEstimate(
            flops=2 * rows * depth * groups * out_width,
            bytes_accessed=2 * depth * (rows + groups * out_width),
            transcendentals=0,
        ),
        name="project_begin",
    )(in_vmem(wide), in_vmem(weights))


def project_finish(factor, state, weights, lasts, count_pieces, head_size):
    rows, width = lasts[0].shape
    out_width = weights.shape[2]
    total = rows * len(lasts)
    units = total // 16
    sizes = [rows] * len(lasts)
    sizes += [16 * ((units + n) // count_pieces) for n in range(count_pieces)]
    return pl.pallas_call(
        functools.partial(finish_kernel, head_size),
        out_shape=(
            pltpu.VMEM((total, out_width), BF16),
            pltpu.VMEM((total, 2 * out_width), BF16),
            *[pltpu.VMEM((size, 2 * out_width), BF16) for size in sizes],
        ),
        in_specs=[SMEM] + [VMEM] * (2 + len(lasts)),
        out_specs=(VMEM,) * (2 + len(sizes)),
        compiler_params=pltpu.CompilerParams(vmem_limit_bytes=16 << 20),
        cost_estimate=pl.CostEstimate(
            flops=6 * total * width * out_width, bytes_accessed=8 * total * out_width, transcendentals=0
        ),
        name="project_finish",
    )(in_hbm(factor), in_vmem(state), in_vmem(weights), *map(in_vmem, lasts))


def attend_kernel(
    head_size, counts, has_acc, count_out, count_streams, info, ids, q_ref, id_row, *refs
):
    count_blocks, count_parts = counts
    kv_refs, rest = refs[: count_blocks * count_parts], refs[count_blocks * count_parts :]
    if has_acc:
        acc_in, rest = rest[0], rest[1:]
    if count_out:
        w_ref, outs, (k_all, v_ones, acc, attended) = rest[0], rest[1:-4], rest[-4:]
    else:
        acc_out, k_all, v_ones, acc = rest
    acc[...] = acc_in[...] if has_acc else jnp.zeros_like(acc)
    rows, width = q_ref.shape
    heads = width // head_size
    keys = k_all.shape[0]
    tile = id_row.shape[2]
    q_first = info[count_blocks]
    v_ones[:, :, head_size:] = jnp.ones((heads, keys, head_size), BF16)
    for number in range(count_blocks):
        begin = 0
        for kv_ref in kv_refs[number * count_parts : (number + 1) * count_parts]:
            here = slice(begin, begin + kv_ref.shape[0])
            begin += kv_ref.shape[0]
            k_all[here, :] = kv_ref[:, :width]
            for head in range(heads):
                start = width + head * head_size
                v_ones[head, here, :head_size] = kv_ref[:, start : start + head_size]
        first = info[number]
        key_low, key_high = ids[first], ids[first + keys - 1]

        @pl.loop(0, rows // tile)
        def _(index):
            base = pl.multiple_of(index * tile, tile)
            here = pl.ds(base, tile)
            q_low, q_high = ids[q_first + base], ids[q_first + base + tile - 1]

            def add(masked):
                if masked:
                    own = jnp.broadcast_to(id_row[q_first // tile + index], (8, tile))
                    own = jnp.transpose(own)[:, :1]
                    allowed = [id_row[first // tile + n] <= own for n in range(keys // tile)]
                for head in range(heads):
                    lanes = slice(head * head_size, (head + 1) * head_size)
                    spread = slice(2 * head * head_size, 2 * (head + 1) * head_size)
                    total = acc[here, spread]
                    for low in range(0, keys, tile):
                        score = lax.dot_general(
                            q_ref[here, lanes],
                            k_all[low : low + tile, lanes],
                            (((1,), (1,)), ((), ())),
                            preferred_element_type=F32,
                        )
                        weight = jnp.exp2(score)
                        if masked:
                            weight = jnp.where(allowed[low // tile], weight, 0.0)
                        total += jnp.dot(
                            weight.astype(BF16),
                            v_ones[head, low : low + tile, :],
                            preferred_element_type=F32,
                        )
                    acc[here, spread] = total

            @pl.when(key_high <= q_low)
            def _():
                add(False)

            @pl.when((key_high > q_low) & (key_low <= q_high))
            def _():
                add(True)

    if not count_out:
        acc_out[...] = acc[...]
        return
    for head in range(heads):
        start = 2 * head * head_size
        attended[:, head * head_size : (head + 1) * head_size] = (
            acc[:, start : start + head_size]
            / acc[:, start + head_size : start + 2 * head_size]
        ).astype(BF16)
    out_rows, out_width = outs[0].shape
    for number, out in enumerate(outs):
        lane = info[count_blocks + 1 + number] * out_width
        first = number * count_streams // count_out * out_rows
        out[...] = jnp.dot(
            attended[first : first + out_rows, :],
            w_ref[:, pl.ds(pl.multiple_of(lane, out_width), out_width)],
            preferred_element_type=F32,
        ).astype(BF16)


def attend(info, ids, query, blocks, head_size, acc=None, w_out=None, streams=0):
    total, width = query.shape
    parts = [part for block in blocks for part in block]
    keys = sum(part.shape[0] for part in blocks[0])
    heads = width // head_size
    count_out = streams * w_out.shape[1] // width if streams else 0
    scratch = [
        pltpu.VMEM((keys, width), BF16),
        pltpu.VMEM((heads, keys, 2 * head_size), BF16),
        pltpu.VMEM((total, 2 * width), F32),
    ]
    operands = [in_vmem(query), in_hbm(ids.reshape(-1, 1, math.gcd(total, 256)))]
    operands += map(in_vmem, parts)
    if acc is not None:
        operands.append(in_vmem(acc))
    if count_out:
        operands.append(in_hbm(w_out))
        scratch.append(pltpu.VMEM((total, width), BF16))
        shape = pltpu.VMEM((total // streams, w_out.shape[1] * streams // count_out), BF16)
    else:
        shape = pltpu.VMEM((total, 2 * width), F32)
    outs = count_out or 1
    return pl.pallas_call(
        functools.partial(
            attend_kernel, head_size, (len(blocks), len(blocks[0])), acc is not None, count_out, streams
        ),
        out_shape=(shape,) * outs,
        in_specs=[SMEM, SMEM] + [VMEM] * len(operands),
        out_specs=(VMEM,) * outs,
        scratch_shapes=scratch,
        compiler_params=pltpu.CompilerParams(
            vmem_limit_bytes=(16 << 20) + 4 * sum(part.size for part in parts)
        ),
        cost_estimate=pl.CostEstimate(flops=1 << 20, bytes_accessed=1 << 10, transcendentals=0),
        name="attend_last" if count_out else "attend",
    )(info, in_hbm(ids), *operands)


def total_of(*parts):
    return sum(part.astype(F32) for part in parts).astype(BF16)


def body(mesh_shape, tokens, norm_gain, w_qkv, head_scale, w_out, scale_ids):
    ring, seqs = mesh_shape["head"], mesh_shape["seq"]
    outer = seqs // 2
    rows, width = tokens.shape
    half = rows // 2
    head_size = w_qkv.shape[2] // head_scale.shape[0]
    head_at, seq_at = lax.axis_index("head"), lax.axis_index("seq")
    place = ring_place(head_at, ring)
    chip, core = seq_at // 2, seq_at % 2
    index_at = lambda offset: ring_index((place + offset + ring) % ring, ring)
    numbers = lambda values: jnp.stack(values).astype(jnp.int32)
    at = [index_at(offset) for offset in range(ring)]

    streams, ways = (0, 1), ((0, 1), (1, -1))
    farthest = ring // 2
    reach = [(farthest, farthest - 1), (farthest - 1, farthest)]

    order = [0] + [sign * step % ring for step in range(1, farthest) for sign in (-1, 1)] + [farthest]
    held = [[tokens[s * half : (s + 1) * half]] * 2 for s in streams]
    blocks, targets = [], []
    for step in range(1, farthest + 1):
        for s in streams:
            for way, sign in ways:
                if step <= reach[s][way]:
                    held[s][way] = along(held[s][way], sign, ring)
        if step == 1:
            held[1][1], (weights, wide) = lax.optimization_barrier(
                (held[1][1], fold_gain(order, numbers(at), norm_gain, w_qkv, tokens))
            )
        elif step == 2:
            wide = placed(targets, blocks, wide)
            blocks, targets = [], []
        elif step == 3:
            held[1][1], wide = lax.optimization_barrier(
                (held[1][1], placed(targets, blocks, wide))
            )
            blocks, targets = [], []
        if step < farthest:
            for s in streams:
                for way, sign in ways:
                    blocks.append(held[s][way])
                    targets.append((s * half, (2 * step - 1 + way) * width))
    wide = placed(targets, blocks, wide)
    lasts = [held[0][0], held[1][1]]
    state = project_begin(wide, weights, ring)
    query, kv, *parts = project_finish(head_scale, state, weights, lasts, 3, head_size)
    halves, pieces = parts[:2], parts[2:]

    far, straight, crossed = [], [], []
    for step in range(outer):
        source = 2 * ((chip + outer - step) % outer)
        straight.append((source + core) * rows)
        crossed.append((source + 1 - core) * rows)
        if step:
            shift = [(2 * a + b, 2 * ((a + step) % outer) + b) for a in range(outer) for b in (0, 1)]
            far.append([lax.ppermute(part, "seq", shift) for part in halves])
    first = [seq_at * rows]
    (acc,) = attend(numbers(straight[:1] + first), scale_ids, query, [[kv]], head_size)
    near = [[swapped(piece, seqs) for piece in pieces]]
    acc, near = lax.optimization_barrier((acc, near))
    (acc,) = attend(numbers(crossed[:1] + first), scale_ids, query, near, head_size, acc)
    acc, far = lax.optimization_barrier((acc, far))
    far_crossed = [[swapped(part, seqs) for part in block] for block in far]
    (acc,) = attend(numbers(straight[1:] + first), scale_ids, query, far, head_size, acc)

    goals = [[*range(up, 0, -1), *range(-down, 0), 0] for up, down in reach]
    info = numbers(crossed[1:] + first + [at[goal % ring] for goal in goals[0] + goals[1]])
    parts = attend(
        info, scale_ids, query, far_crossed, head_size, acc, w_out, len(streams)
    )
    parts = [dict(zip(goals[s], parts[s * ring : (s + 1) * ring])) for s in streams]
    sums = [[None, None] for s in streams]
    for step in range(farthest, 0, -1):
        for s in streams:
            for way, sign in ways:
                if step <= reach[s][way]:
                    part = parts[s][sign * step]
                    if sums[s][way] is not None:
                        part = total_of(part, sums[s][way])
                    sums[s][way] = along(part, sign, ring)
    return jnp.concatenate([total_of(parts[s][0], *sums[s]) for s in streams])


def solution(mesh):
    placed = (P("seq", "head"), P(), P(None, None, "head"), P("head"), P("head", None), P())
    return jax.shard_map(
        functools.partial(body, dict(mesh.shape)),
        mesh=mesh,
        in_specs=placed,
        out_specs=P("seq", "head"),
        check_vma=False,
    )
```

```python
import functools
import math

import jax
import jax.numpy as jnp
from jax import lax
from jax.experimental import pallas as pl
from jax.experimental.pallas import tpu as pltpu
from jax.sharding import PartitionSpec as P

LOG2E = math.log2(math.e)
VMEM = pl.BlockSpec(memory_space=pltpu.VMEM)
SMEM = pl.BlockSpec(memory_space=pltpu.SMEM)
F32 = jnp.float32
BF16 = jnp.bfloat16


def ring_order(count):
    line = count // 2
    return [2 * z for z in range(line)] + [2 * z + 1 for z in reversed(range(line))]


def ring_place(index, count):
    return jnp.where(index % 2 == 0, index // 2, count - 1 - index // 2)


def ring_index(place, count):
    return jnp.where(place < count // 2, 2 * place, 2 * (count - 1 - place) + 1)


def along(value, step, count):
    order = ring_order(count)
    return lax.ppermute(
        value, "head", [(order[p], order[(p + step) % count]) for p in range(count)]
    )


def swapped(value, seq_count):
    return lax.ppermute(value, "seq", [(seq, seq + 1 - 2 * (seq % 2)) for seq in range(seq_count)])


def in_hbm(value):
    return pltpu.with_memory_space_constraint(value, pltpu.HBM)


def in_vmem(value):
    return pltpu.with_memory_space_constraint(value, pltpu.VMEM)


def fold_kernel(order, at, gain_ref, w_hbm, tokens, out_ref, wide, sems):
    lanes = gain_ref.shape[1]
    size = w_hbm.shape[1] // len(order)
    per = size // lanes

    def fetch(n):
        start = pl.multiple_of(at[order[n]] * size, size)
        return pltpu.make_async_copy(
            w_hbm.at[:, pl.ds(start, size), :],
            out_ref.at[:, n * size : (n + 1) * size, :],
            sems.at[n],
        )

    for n in range(len(order)):
        fetch(n).start()
    own = pltpu.make_async_copy(tokens, wide.at[:, : tokens.shape[1]], sems.at[len(order)])
    own.start()
    for n in range(len(order)):
        columns = jnp.transpose(gain_ref[pl.ds(at[order[n]] * per, per), :])
        fetch(n).wait()
        for piece in range(per):
            first = n * size + piece * lanes
            for group in range(w_hbm.shape[0]):
                here = (group, slice(first, first + lanes), slice(None))
                scaled = out_ref[here].astype(F32) * columns[:, piece : piece + 1]
                out_ref[here] = scaled.astype(BF16)
    own.wait()


def fold_gain(order, at, gain, weights, tokens):
    depth = weights.shape[1]
    lanes = math.gcd(depth // len(order), 128)
    hbm = pl.BlockSpec(memory_space=pltpu.HBM)
    return pl.pallas_call(
        functools.partial(fold_kernel, order),
        out_shape=(pltpu.VMEM(weights.shape, BF16), pltpu.VMEM((tokens.shape[0], depth), BF16)),
        in_specs=[SMEM, VMEM, hbm, hbm],
        out_specs=(VMEM, pl.BlockSpec(memory_space=pl.ANY)),
        scratch_shapes=[pltpu.SemaphoreType.DMA((len(order) + 1,))],
        compiler_params=pltpu.CompilerParams(vmem_limit_bytes=16 << 20),
        cost_estimate=pl.CostEstimate(
            flops=weights.size, bytes_accessed=4 * weights.size, transcendentals=0
        ),
        name="fold_gain",
    )(at, in_hbm(gain.reshape(depth // lanes, lanes)), in_hbm(weights), in_hbm(tokens))


def place_kernel(targets, *refs):
    blocks, wide, sems = refs[: len(targets)], refs[-2], refs[-1]
    copies = []
    for n, (block, (row, lane)) in enumerate(zip(blocks, targets)):
        rows, width = block.shape
        here = wide.at[row : row + rows, lane : lane + width]
        copies.append(pltpu.make_async_copy(block, here, sems.at[n]))
    for copy in copies:
        copy.start()
    for copy in copies:
        copy.wait()


def placed(targets, blocks, wide):
    operands = [*map(in_vmem, blocks), in_vmem(wide)]
    return pl.pallas_call(
        functools.partial(place_kernel, targets),
        out_shape=pltpu.VMEM(wide.shape, BF16),
        in_specs=[pl.BlockSpec(memory_space=pl.ANY)] * len(operands),
        out_specs=pl.BlockSpec(memory_space=pl.ANY),
        scratch_shapes=[pltpu.SemaphoreType.DMA((len(targets),))],
        input_output_aliases={len(blocks): 0},
        compiler_params=pltpu.CompilerParams(vmem_limit_bytes=1 << 20),
        cost_estimate=pl.CostEstimate(flops=0, bytes_accessed=1 << 20, transcendentals=0),
        name="place",
    )(*operands)


def begin_kernel(blocks, wide, w_ref, state):
    rows, depth = wide.shape
    out_width = w_ref.shape[2]
    done = depth - depth // blocks
    tile = math.gcd(rows, 256)
    for first in range(0, rows, tile):
        here = slice(first, first + tile)
        for group in range(3):
            state[here, group * out_width : (group + 1) * out_width] = jnp.dot(
                wide[here, :done], w_ref[group, :done, :], preferred_element_type=F32
            )
        power = None
        for lane in range(0, done, 128):
            values = wide[here, lane : lane + 128].astype(F32)
            power = values * values if power is None else power + values * values
        state[here, 3 * out_width :] = power


def finish_kernel(head_size, factor, state, w_ref, *refs):
    count = 2
    lasts, (q_ref, kv_ref), rest = refs[:count], refs[count : count + 2], refs[count + 2 :]
    halves, pieces = rest[:count], rest[count:]
    rows, width = lasts[0].shape
    depth, out_width = w_ref.shape[1:]
    for stream, last in enumerate(lasts):
        here = slice(stream * rows, (stream + 1) * rows)
        q, k, v = (
            state[here, group * out_width : (group + 1) * out_width]
            + jnp.dot(last[...], w_ref[group, depth - width :, :], preferred_element_type=F32)
            for group in range(3)
        )
        power = state[here, 3 * out_width :]
        for lane in range(0, width, 128):
            values = last[:, lane : lane + 128].astype(F32)
            power += values * values
        scale = lax.rsqrt(jnp.sum(power, axis=-1, keepdims=True) * (1.0 / depth) + 1e-06)
        q, k, v = q * scale, k * scale, v * scale
        for head in range(out_width // head_size):
            lanes = slice(head * head_size, (head + 1) * head_size)
            qh, kh = q[:, lanes], k[:, lanes]
            q_size = lax.rsqrt(jnp.sum(qh * qh, axis=-1, keepdims=True) + 1e-06)
            k_size = lax.rsqrt(jnp.sum(kh * kh, axis=-1, keepdims=True) + 1e-06)
            q_ref[here, lanes] = (qh * (q_size * (factor[head] * LOG2E))).astype(BF16)
            kv_ref[here, lanes] = (kh * k_size).astype(BF16)
        kv_ref[here, out_width:] = v.astype(BF16)
        halves[stream][...] = kv_ref[here, :]
    start = 0
    for piece in pieces:
        piece[...] = kv_ref[start : start + piece.shape[0], :]
        start += piece.shape[0]


def project_begin(wide, weights, blocks):
    rows, depth = wide.shape
    groups, _, out_width = weights.shape
    return pl.pallas_call(
        functools.partial(begin_kernel, blocks),
        out_shape=pltpu.VMEM((rows, groups * out_width + 128), F32),
        in_specs=[VMEM] * 2,
        out_specs=VMEM,
        compiler_params=pltpu.CompilerParams(vmem_limit_bytes=16 << 20),
        cost_estimate=pl.CostEstimate(
            flops=2 * rows * depth * groups * out_width,
            bytes_accessed=2 * depth * (rows + groups * out_width),
            transcendentals=0,
        ),
        name="project_begin",
    )(in_vmem(wide), in_vmem(weights))


def project_finish(factor, state, weights, lasts, count_pieces, head_size):
    rows, width = lasts[0].shape
    out_width = weights.shape[2]
    total = rows * len(lasts)
    units = total // 16
    sizes = [rows] * len(lasts)
    sizes += [16 * ((units + n) // count_pieces) for n in range(count_pieces)]
    return pl.pallas_call(
        functools.partial(finish_kernel, head_size),
        out_shape=(
            pltpu.VMEM((total, out_width), BF16),
            pltpu.VMEM((total, 2 * out_width), BF16),
            *[pltpu.HBM((size, 2 * out_width), BF16) for size in sizes[: len(lasts)]],
            *[pltpu.VMEM((size, 2 * out_width), BF16) for size in sizes[len(lasts) :]],
        ),
        in_specs=[SMEM] + [VMEM] * (2 + len(lasts)),
        out_specs=(VMEM,) * (2 + len(sizes)),
        compiler_params=pltpu.CompilerParams(vmem_limit_bytes=16 << 20),
        cost_estimate=pl.CostEstimate(
            flops=6 * total * width * out_width, bytes_accessed=8 * total * out_width, transcendentals=0
        ),
        name="project_finish",
    )(in_hbm(factor), in_vmem(state), in_vmem(weights), *map(in_vmem, lasts))


def attend_kernel(
    head_size, counts, has_acc, count_out, count_streams, info, ids, q_ref, id_row, *refs
):
    count_blocks, count_parts = counts
    kv_refs, rest = refs[: count_blocks * count_parts], refs[count_blocks * count_parts :]
    if has_acc:
        acc_in, rest = rest[0], rest[1:]
    if count_out:
        w_ref, outs, (k_all, v_ones, acc, attended) = rest[0], rest[1:-4], rest[-4:]
    else:
        acc_out, k_all, v_ones, acc = rest
    acc[...] = acc_in[...] if has_acc else jnp.zeros_like(acc)
    rows, width = q_ref.shape
    heads = width // head_size
    keys = k_all.shape[0]
    tile = id_row.shape[2]
    q_first = info[count_blocks]
    v_ones[:, :, head_size:] = jnp.ones((heads, keys, head_size), BF16)
    for number in range(count_blocks):
        begin = 0
        for kv_ref in kv_refs[number * count_parts : (number + 1) * count_parts]:
            here = slice(begin, begin + kv_ref.shape[0])
            begin += kv_ref.shape[0]
            k_all[here, :] = kv_ref[:, :width]
            for head in range(heads):
                start = width + head * head_size
                v_ones[head, here, :head_size] = kv_ref[:, start : start + head_size]
        first = info[number]
        key_low, key_high = ids[first], ids[first + keys - 1]

        @pl.loop(0, rows // tile)
        def _(index):
            base = pl.multiple_of(index * tile, tile)
            here = pl.ds(base, tile)
            q_low, q_high = ids[q_first + base], ids[q_first + base + tile - 1]

            def add(masked):
                if masked:
                    own = jnp.broadcast_to(id_row[q_first // tile + index], (8, tile))
                    own = jnp.transpose(own)[:, :1]
                    allowed = [id_row[first // tile + n] <= own for n in range(keys // tile)]
                for head in range(heads):
                    lanes = slice(head * head_size, (head + 1) * head_size)
                    spread = slice(2 * head * head_size, 2 * (head + 1) * head_size)
                    total = acc[here, spread]
                    for low in range(0, keys, tile):
                        score = lax.dot_general(
                            q_ref[here, lanes],
                            k_all[low : low + tile, lanes],
                            (((1,), (1,)), ((), ())),
                            preferred_element_type=F32,
                        )
                        weight = jnp.exp2(score)
                        if masked:
                            weight = jnp.where(allowed[low // tile], weight, 0.0)
                        total += jnp.dot(
                            weight.astype(BF16),
                            v_ones[head, low : low + tile, :],
                            preferred_element_type=F32,
                        )
                    acc[here, spread] = total

            @pl.when(key_high <= q_low)
            def _():
                add(False)

            @pl.when((key_high > q_low) & (key_low <= q_high))
            def _():
                add(True)

    if not count_out:
        acc_out[...] = acc[...]
        return
    for head in range(heads):
        start = 2 * head * head_size
        attended[:, head * head_size : (head + 1) * head_size] = (
            acc[:, start : start + head_size]
            / acc[:, start + head_size : start + 2 * head_size]
        ).astype(BF16)
    out_rows, out_width = outs[0].shape
    for number, out in enumerate(outs):
        lane = info[count_blocks + 1 + number] * out_width
        first = number * count_streams // count_out * out_rows
        out[...] = jnp.dot(
            attended[first : first + out_rows, :],
            w_ref[:, pl.ds(pl.multiple_of(lane, out_width), out_width)],
            preferred_element_type=F32,
        ).astype(BF16)


def attend(info, ids, query, blocks, head_size, acc=None, w_out=None, streams=0):
    total, width = query.shape
    parts = [part for block in blocks for part in block]
    keys = sum(part.shape[0] for part in blocks[0])
    heads = width // head_size
    count_out = streams * w_out.shape[1] // width if streams else 0
    scratch = [
        pltpu.VMEM((keys, width), BF16),
        pltpu.VMEM((heads, keys, 2 * head_size), BF16),
        pltpu.VMEM((total, 2 * width), F32),
    ]
    operands = [in_vmem(query), in_hbm(ids.reshape(-1, 1, math.gcd(total, 256)))]
    operands += map(in_vmem, parts)
    if acc is not None:
        operands.append(in_vmem(acc))
    if count_out:
        operands.append(in_hbm(w_out))
        scratch.append(pltpu.VMEM((total, width), BF16))
        shape = pltpu.VMEM((total // streams, w_out.shape[1] * streams // count_out), BF16)
    else:
        shape = pltpu.VMEM((total, 2 * width), F32)
    outs = count_out or 1
    return pl.pallas_call(
        functools.partial(
            attend_kernel, head_size, (len(blocks), len(blocks[0])), acc is not None, count_out, streams
        ),
        out_shape=(shape,) * outs,
        in_specs=[SMEM, SMEM] + [VMEM] * len(operands),
        out_specs=(VMEM,) * outs,
        scratch_shapes=scratch,
        compiler_params=pltpu.CompilerParams(
            vmem_limit_bytes=(16 << 20) + 4 * sum(part.size for part in parts)
        ),
        cost_estimate=pl.CostEstimate(flops=1 << 20, bytes_accessed=1 << 10, transcendentals=0),
        name="attend_last" if count_out else "attend",
    )(info, in_hbm(ids), *operands)


def total_of(*parts):
    return sum(part.astype(F32) for part in parts).astype(BF16)


def body(mesh_shape, tokens, norm_gain, w_qkv, head_scale, w_out, scale_ids):
    ring, seqs = mesh_shape["head"], mesh_shape["seq"]
    outer = seqs // 2
    rows, width = tokens.shape
    half = rows // 2
    head_size = w_qkv.shape[2] // head_scale.shape[0]
    head_at, seq_at = lax.axis_index("head"), lax.axis_index("seq")
    place = ring_place(head_at, ring)
    chip, core = seq_at // 2, seq_at % 2
    index_at = lambda offset: ring_index((place + offset + ring) % ring, ring)
    numbers = lambda values: jnp.stack(values).astype(jnp.int32)
    at = [index_at(offset) for offset in range(ring)]

    streams = (0, 1)
    lanes = ((0, 0, 1), (1, 1, -1), (0, 1, -1), (1, 0, 1))
    farthest = ring // 2
    reach = [(farthest, farthest - 1), (farthest - 1, farthest)]

    order = [0] + [sign * step % ring for step in range(1, farthest) for sign in (-1, 1)] + [farthest]
    held = [[tokens[s * half : (s + 1) * half]] * 2 for s in streams]
    blocks, targets = [], []
    for step in range(1, farthest + 1):
        for s, way, sign in lanes:
            if step <= reach[s][way]:
                held[s][way] = along(held[s][way], sign, ring)
        if step == 1:
            held[0][0], (weights, wide) = lax.optimization_barrier(
                (held[0][0], fold_gain(order, numbers(at), norm_gain, w_qkv, tokens))
            )
        elif step == 2:
            wide = placed(targets, blocks, wide)
            blocks, targets = [], []
        elif step == 3:
            held[1][1], wide = lax.optimization_barrier(
                (held[1][1], placed(targets, blocks, wide))
            )
            blocks, targets = [], []
        if step < farthest:
            for s, way, sign in lanes:
                blocks.append(held[s][way])
                targets.append((s * half, (2 * step - 1 + way) * width))
    wide = placed(targets, blocks, wide)
    lasts = [held[0][0], held[1][1]]
    state = project_begin(wide, weights, ring)
    query, kv, *parts = project_finish(head_scale, state, weights, lasts, 3, head_size)
    halves, pieces = parts[:2], parts[2:]

    far, straight, crossed = [], [], []
    for step in range(outer):
        source = 2 * ((chip + outer - step) % outer)
        straight.append((source + core) * rows)
        crossed.append((source + 1 - core) * rows)
        if step:
            shift = [(2 * a + b, 2 * ((a + step) % outer) + b) for a in range(outer) for b in (0, 1)]
            far.append([lax.ppermute(part, "seq", shift) for part in halves])
    first = [seq_at * rows]
    (acc,) = attend(numbers(straight[:1] + first), scale_ids, query, [[kv]], head_size)
    near = [[swapped(piece, seqs) for piece in pieces]]
    acc, near = lax.optimization_barrier((acc, near))
    (acc,) = attend(numbers(crossed[:1] + first), scale_ids, query, near, head_size, acc)
    acc, far = lax.optimization_barrier((acc, far))
    far_crossed = [[swapped(part, seqs) for part in block] for block in far]
    (acc,) = attend(numbers(straight[1:] + first), scale_ids, query, far, head_size, acc)

    goals = [[*range(up, 0, -1), *range(-down, 0), 0] for up, down in reach]
    info = numbers(crossed[1:] + first + [at[goal % ring] for goal in goals[0] + goals[1]])
    parts = attend(
        info, scale_ids, query, far_crossed, head_size, acc, w_out, len(streams)
    )
    parts = [dict(zip(goals[s], parts[s * ring : (s + 1) * ring])) for s in streams]
    sums = [[None, None] for s in streams]
    for step in range(farthest, 0, -1):
        for s, way, sign in lanes:
            if step <= reach[s][way]:
                part = parts[s][sign * step]
                if sums[s][way] is not None:
                    part = total_of(part, sums[s][way])
                sums[s][way] = along(part, sign, ring)
    ends = lax.optimization_barrier([sums[s][way] for s, way, sign in lanes[::-1]])
    for (s, way, sign), end in zip(lanes[::-1], ends):
        sums[s][way] = end
    return jnp.concatenate([total_of(parts[s][0], *sums[s]) for s in streams])


def solution(mesh):
    placed = (P("seq", "head"), P(), P(None, None, "head"), P("head"), P("head", None), P())
    return jax.shard_map(
        functools.partial(body, dict(mesh.shape)),
        mesh=mesh,
        in_specs=placed,
        out_specs=P("seq", "head"),
        check_vma=False,
    )
```

```python
import functools
import math

import jax
import jax.numpy as jnp
from jax import lax
from jax.experimental import pallas as pl
from jax.experimental.pallas import tpu as pltpu
from jax.sharding import PartitionSpec as P

LOG2E = math.log2(math.e)
VMEM = pl.BlockSpec(memory_space=pltpu.VMEM)
SMEM = pl.BlockSpec(memory_space=pltpu.SMEM)
F32 = jnp.float32
BF16 = jnp.bfloat16


def ring_order(count):
    line = count // 2
    return [2 * z for z in range(line)] + [2 * z + 1 for z in reversed(range(line))]


def ring_place(index, count):
    return jnp.where(index % 2 == 0, index // 2, count - 1 - index // 2)


def ring_index(place, count):
    return jnp.where(place < count // 2, 2 * place, 2 * (count - 1 - place) + 1)


def along(value, step, count):
    order = ring_order(count)
    return lax.ppermute(
        value, "head", [(order[p], order[(p + step) % count]) for p in range(count)]
    )


def swapped(value, seq_count):
    return lax.ppermute(value, "seq", [(seq, seq + 1 - 2 * (seq % 2)) for seq in range(seq_count)])


def in_hbm(value):
    return pltpu.with_memory_space_constraint(value, pltpu.HBM)


def in_vmem(value):
    return pltpu.with_memory_space_constraint(value, pltpu.VMEM)


def fold_kernel(order, at, gain_hbm, w_hbm, tokens, out_ref, wide, gain_ref, sems):
    lanes = gain_ref.shape[1]
    size = w_hbm.shape[1] // len(order)
    per = size // lanes

    def fetch(n):
        start = pl.multiple_of(at[order[n]] * size, size)
        return pltpu.make_async_copy(
            w_hbm.at[:, pl.ds(start, size), :],
            out_ref.at[:, n * size : (n + 1) * size, :],
            sems.at[n],
        )

    gains = pltpu.make_async_copy(gain_hbm, gain_ref, sems.at[len(order) + 1])
    gains.start()
    for n in range(len(order)):
        fetch(n).start()
    own = pltpu.make_async_copy(tokens, wide.at[:, : tokens.shape[1]], sems.at[len(order)])
    own.start()
    gains.wait()
    for n in range(len(order)):
        columns = jnp.transpose(gain_ref[pl.ds(at[order[n]] * per, per), :])
        fetch(n).wait()
        for piece in range(per):
            first = n * size + piece * lanes
            for group in range(w_hbm.shape[0]):
                here = (group, slice(first, first + lanes), slice(None))
                scaled = out_ref[here].astype(F32) * columns[:, piece : piece + 1]
                out_ref[here] = scaled.astype(BF16)
    own.wait()


def fold_gain(order, at, gain, weights, tokens):
    depth = weights.shape[1]
    lanes = math.gcd(depth // len(order), 128)
    hbm = pl.BlockSpec(memory_space=pltpu.HBM)
    return pl.pallas_call(
        functools.partial(fold_kernel, order),
        out_shape=(pltpu.VMEM(weights.shape, BF16), pltpu.VMEM((tokens.shape[0], depth), BF16)),
        in_specs=[SMEM, hbm, hbm, hbm],
        out_specs=(VMEM, pl.BlockSpec(memory_space=pl.ANY)),
        scratch_shapes=[
            pltpu.VMEM((depth // lanes, lanes), F32),
            pltpu.SemaphoreType.DMA((len(order) + 2,)),
        ],
        compiler_params=pltpu.CompilerParams(vmem_limit_bytes=16 << 20),
        cost_estimate=pl.CostEstimate(
            flops=weights.size, bytes_accessed=4 * weights.size, transcendentals=0
        ),
        name="fold_gain",
    )(at, in_hbm(gain.reshape(depth // lanes, lanes)), in_hbm(weights), in_hbm(tokens))


def place_kernel(targets, *refs):
    blocks, wide, sems = refs[: len(targets)], refs[-2], refs[-1]
    copies = []
    for n, (block, (row, lane)) in enumerate(zip(blocks, targets)):
        rows, width = block.shape
        here = wide.at[row : row + rows, lane : lane + width]
        copies.append(pltpu.make_async_copy(block, here, sems.at[n]))
    for copy in copies:
        copy.start()
    for copy in copies:
        copy.wait()


def placed(targets, blocks, wide):
    operands = [*map(in_vmem, blocks), in_vmem(wide)]
    return pl.pallas_call(
        functools.partial(place_kernel, targets),
        out_shape=pltpu.VMEM(wide.shape, BF16),
        in_specs=[pl.BlockSpec(memory_space=pl.ANY)] * len(operands),
        out_specs=pl.BlockSpec(memory_space=pl.ANY),
        scratch_shapes=[pltpu.SemaphoreType.DMA((len(targets),))],
        input_output_aliases={len(blocks): 0},
        compiler_params=pltpu.CompilerParams(vmem_limit_bytes=1 << 20),
        cost_estimate=pl.CostEstimate(flops=0, bytes_accessed=1 << 20, transcendentals=0),
        name="place",
    )(*operands)


def begin_kernel(blocks, wide, w_ref, state):
    rows, depth = wide.shape
    out_width = w_ref.shape[2]
    done = depth - depth // blocks
    tile = math.gcd(rows, 256)
    for first in range(0, rows, tile):
        here = slice(first, first + tile)
        for group in range(3):
            state[here, group * out_width : (group + 1) * out_width] = jnp.dot(
                wide[here, :done], w_ref[group, :done, :], preferred_element_type=F32
            )
        power = None
        for lane in range(0, done, 128):
            values = wide[here, lane : lane + 128].astype(F32)
            power = values * values if power is None else power + values * values
        state[here, 3 * out_width :] = power


def finish_kernel(head_size, factor, state, w_ref, *refs):
    count = 2
    lasts, (q_ref, kv_ref), rest = refs[:count], refs[count : count + 2], refs[count + 2 :]
    halves, pieces = rest[:count], rest[count:]
    rows, width = lasts[0].shape
    depth, out_width = w_ref.shape[1:]
    for stream, last in enumerate(lasts):
        here = slice(stream * rows, (stream + 1) * rows)
        q, k, v = (
            state[here, group * out_width : (group + 1) * out_width]
            + jnp.dot(last[...], w_ref[group, depth - width :, :], preferred_element_type=F32)
            for group in range(3)
        )
        power = state[here, 3 * out_width :]
        for lane in range(0, width, 128):
            values = last[:, lane : lane + 128].astype(F32)
            power += values * values
        scale = lax.rsqrt(jnp.sum(power, axis=-1, keepdims=True) * (1.0 / depth) + 1e-06)
        q, k, v = q * scale, k * scale, v * scale
        for head in range(out_width // head_size):
            lanes = slice(head * head_size, (head + 1) * head_size)
            qh, kh = q[:, lanes], k[:, lanes]
            q_size = lax.rsqrt(jnp.sum(qh * qh, axis=-1, keepdims=True) + 1e-06)
            k_size = lax.rsqrt(jnp.sum(kh * kh, axis=-1, keepdims=True) + 1e-06)
            q_ref[here, lanes] = (qh * (q_size * factor[head])).astype(BF16)
            kv_ref[here, lanes] = (kh * k_size).astype(BF16)
        kv_ref[here, out_width:] = v.astype(BF16)
        halves[stream][...] = kv_ref[here, :]
    start = 0
    for piece in pieces:
        piece[...] = kv_ref[start : start + piece.shape[0], :]
        start += piece.shape[0]


def project_begin(wide, weights, blocks):
    rows, depth = wide.shape
    groups, _, out_width = weights.shape
    return pl.pallas_call(
        functools.partial(begin_kernel, blocks),
        out_shape=pltpu.VMEM((rows, groups * out_width + 128), F32),
        in_specs=[VMEM] * 2,
        out_specs=VMEM,
        compiler_params=pltpu.CompilerParams(vmem_limit_bytes=16 << 20),
        cost_estimate=pl.CostEstimate(
            flops=2 * rows * depth * groups * out_width,
            bytes_accessed=2 * depth * (rows + groups * out_width),
            transcendentals=0,
        ),
        name="project_begin",
    )(in_vmem(wide), in_vmem(weights))


def project_finish(factor, state, weights, lasts, count_pieces, head_size):
    rows, width = lasts[0].shape
    out_width = weights.shape[2]
    total = rows * len(lasts)
    units = total // 16
    sizes = [rows] * len(lasts)
    sizes += [16 * ((units + n) // count_pieces) for n in range(count_pieces)]
    return pl.pallas_call(
        functools.partial(finish_kernel, head_size),
        out_shape=(
            pltpu.VMEM((total, out_width), BF16),
            pltpu.VMEM((total, 2 * out_width), BF16),
            *[pltpu.VMEM((size, 2 * out_width), BF16) for size in sizes],
        ),
        in_specs=[SMEM] + [VMEM] * (2 + len(lasts)),
        out_specs=(VMEM,) * (2 + len(sizes)),
        compiler_params=pltpu.CompilerParams(vmem_limit_bytes=16 << 20),
        cost_estimate=pl.CostEstimate(
            flops=6 * total * width * out_width, bytes_accessed=8 * total * out_width, transcendentals=0
        ),
        name="project_finish",
    )(factor, in_vmem(state), in_vmem(weights), *map(in_vmem, lasts))


def attend_kernel(
    head_size, counts, has_acc, count_out, count_streams, info, ids_hbm, rows_hbm, q_ref, *refs
):
    refs, (ids, id_row, sems) = refs[:-3], refs[-3:]
    fetch_ids = pltpu.make_async_copy(ids_hbm, ids, sems.at[0])
    fetch_ids.start()
    count_blocks, count_parts = counts
    kv_refs, rest = refs[: count_blocks * count_parts], refs[count_blocks * count_parts :]
    if has_acc:
        acc_in, rest = rest[0], rest[1:]
    if count_out:
        w_hbm, outs, (k_all, v_ones, acc, attended, w_ref) = rest[0], rest[1:-5], rest[-5:]
        fetch_w = pltpu.make_async_copy(w_hbm, w_ref, sems.at[1])
        fetch_w.start()
    else:
        acc_out, k_all, v_ones, acc = rest
    acc[...] = acc_in[...] if has_acc else jnp.zeros_like(acc)
    rows, width = q_ref.shape
    heads = width // head_size
    keys = k_all.shape[0]
    tile = id_row.shape[2]
    q_first = info[count_blocks]
    v_ones[:, :, head_size:] = jnp.ones((heads, keys, head_size), BF16)
    for number in range(count_blocks):
        begin = 0
        for kv_ref in kv_refs[number * count_parts : (number + 1) * count_parts]:
            here = slice(begin, begin + kv_ref.shape[0])
            begin += kv_ref.shape[0]
            k_all[here, :] = kv_ref[:, :width]
            for head in range(heads):
                start = width + head * head_size
                v_ones[head, here, :head_size] = kv_ref[:, start : start + head_size]
        if number == 0:
            fetch_ids.wait()
        first = info[number]
        key_low, key_high = ids[first], ids[first + keys - 1]

        @pl.loop(0, rows // tile)
        def _(index):
            base = pl.multiple_of(index * tile, tile)
            here = pl.ds(base, tile)
            q_low, q_high = ids[q_first + base], ids[q_first + base + tile - 1]

            def add(masked):
                if masked:
                    fetch_rows = pltpu.make_async_copy(rows_hbm, id_row, sems.at[2])
                    fetch_rows.start()
                    fetch_rows.wait()
                    own = jnp.broadcast_to(id_row[q_first // tile + index], (8, tile))
                    own = jnp.transpose(own)[:, :1]
                    allowed = [id_row[first // tile + n] <= own for n in range(keys // tile)]
                for head in range(heads):
                    lanes = slice(head * head_size, (head + 1) * head_size)
                    spread = slice(2 * head * head_size, 2 * (head + 1) * head_size)
                    total = acc[here, spread]
                    for low in range(0, keys, tile):
                        score = lax.dot_general(
                            q_ref[here, lanes],
                            k_all[low : low + tile, lanes],
                            (((1,), (1,)), ((), ())),
                            preferred_element_type=F32,
                        )
                        weight = jnp.exp2(score)
                        if masked:
                            weight = jnp.where(allowed[low // tile], weight, 0.0)
                        total += jnp.dot(
                            weight.astype(BF16),
                            v_ones[head, low : low + tile, :],
                            preferred_element_type=F32,
                        )
                    acc[here, spread] = total

            @pl.when(key_high <= q_low)
            def _():
                add(False)

            @pl.when((key_high > q_low) & (key_low <= q_high))
            def _():
                add(True)

    if not count_out:
        acc_out[...] = acc[...]
        return
    for head in range(heads):
        start = 2 * head * head_size
        attended[:, head * head_size : (head + 1) * head_size] = (
            acc[:, start : start + head_size]
            / acc[:, start + head_size : start + 2 * head_size]
        ).astype(BF16)
    out_rows, out_width = outs[0].shape
    fetch_w.wait()
    for number, out in enumerate(outs):
        lane = info[count_blocks + 1 + number] * out_width
        first = number * count_streams // count_out * out_rows
        out[...] = jnp.dot(
            attended[first : first + out_rows, :],
            w_ref[:, pl.ds(pl.multiple_of(lane, out_width), out_width)],
            preferred_element_type=F32,
        ).astype(BF16)


def attend(info, ids, query, blocks, head_size, acc=None, w_out=None, streams=0):
    total, width = query.shape
    parts = [part for block in blocks for part in block]
    keys = sum(part.shape[0] for part in blocks[0])
    heads = width // head_size
    count_out = streams * w_out.shape[1] // width if streams else 0
    scratch = [
        pltpu.VMEM((keys, width), BF16),
        pltpu.VMEM((heads, keys, 2 * head_size), BF16),
        pltpu.VMEM((total, 2 * width), F32),
    ]
    id_rows = ids.reshape(-1, 1, math.gcd(total, 256))
    operands = [in_vmem(query), *map(in_vmem, parts)]
    if acc is not None:
        operands.append(in_vmem(acc))
    if count_out:
        operands.append(in_hbm(w_out))
        scratch += [pltpu.VMEM((total, width), BF16), pltpu.VMEM(w_out.shape, BF16)]
        shape = pltpu.VMEM((total // streams, w_out.shape[1] * streams // count_out), BF16)
    else:
        shape = pltpu.VMEM((total, 2 * width), F32)
    outs = count_out or 1
    scratch += [
        pltpu.SMEM(ids.shape, jnp.int32),
        pltpu.VMEM(id_rows.shape, jnp.int32),
        pltpu.SemaphoreType.DMA((3,)),
    ]
    hbm = pl.BlockSpec(memory_space=pltpu.HBM)
    in_specs = [SMEM, hbm, hbm] + [VMEM] * len(operands)
    if count_out:
        in_specs[-1] = hbm
    return pl.pallas_call(
        functools.partial(
            attend_kernel, head_size, (len(blocks), len(blocks[0])), acc is not None, count_out, streams
        ),
        out_shape=(shape,) * outs,
        in_specs=in_specs,
        out_specs=(VMEM,) * outs,
        scratch_shapes=scratch,
        compiler_params=pltpu.CompilerParams(
            vmem_limit_bytes=(16 << 20) + 4 * sum(part.size for part in parts)
        ),
        cost_estimate=pl.CostEstimate(flops=1 << 20, bytes_accessed=1 << 10, transcendentals=0),
        name="attend_last" if count_out else "attend",
    )(info, in_hbm(ids), in_hbm(id_rows), *operands)


def total_of(*parts):
    return sum(part.astype(F32) for part in parts).astype(BF16)


def body(mesh_shape, tokens, norm_gain, w_qkv, head_scale, w_out, scale_ids):
    ring, seqs = mesh_shape["head"], mesh_shape["seq"]
    outer = seqs // 2
    rows, width = tokens.shape
    half = rows // 2
    head_size = w_qkv.shape[2] // head_scale.shape[0]
    head_at, seq_at = lax.axis_index("head"), lax.axis_index("seq")
    place = ring_place(head_at, ring)
    chip, core = seq_at // 2, seq_at % 2
    index_at = lambda offset: ring_index((place + offset + ring) % ring, ring)
    numbers = lambda values: jnp.stack(values).astype(jnp.int32)
    at = [index_at(offset) for offset in range(ring)]

    streams = (0, 1)
    lanes = ((0, 0, 1), (1, 1, -1), (0, 1, -1), (1, 0, 1))
    farthest = ring // 2
    reach = [(farthest, farthest - 1), (farthest - 1, farthest)]

    order = [0] + [sign * step % ring for step in range(1, farthest) for sign in (-1, 1)] + [farthest]
    held = [[tokens[s * half : (s + 1) * half]] * 2 for s in streams]
    blocks, targets = [], []
    for step in range(1, farthest + 1):
        for s, way, sign in lanes:
            if step <= reach[s][way]:
                held[s][way] = along(held[s][way], sign, ring)
        if step == 1:
            held[0][0], (weights, wide) = lax.optimization_barrier(
                (held[0][0], fold_gain(order, numbers(at), norm_gain, w_qkv, tokens))
            )
        elif step == 2:
            wide = placed(targets, blocks, wide)
            blocks, targets = [], []
        elif step == 3:
            held[1][1], wide = lax.optimization_barrier(
                (held[1][1], placed(targets, blocks, wide))
            )
            blocks, targets = [], []
        if step < farthest:
            for s, way, sign in lanes:
                blocks.append(held[s][way])
                targets.append((s * half, (2 * step - 1 + way) * width))
    wide = placed(targets, blocks, wide)
    lasts = [held[0][0], held[1][1]]
    state, factor = lax.optimization_barrier((project_begin(wide, weights, ring), head_scale * LOG2E))
    query, kv, *parts = project_finish(factor, state, weights, lasts, 3, head_size)
    halves, pieces = parts[:2], parts[2:]

    far, straight, crossed = [], [], []
    for step in range(outer):
        source = 2 * ((chip + outer - step) % outer)
        straight.append((source + core) * rows)
        crossed.append((source + 1 - core) * rows)
        if step:
            shift = [(2 * a + b, 2 * ((a + step) % outer) + b) for a in range(outer) for b in (0, 1)]
            far.append([lax.ppermute(part, "seq", shift) for part in halves])
    first = [seq_at * rows]
    (acc,) = attend(numbers(straight[:1] + first), scale_ids, query, [[kv]], head_size)
    near = [[swapped(piece, seqs) for piece in pieces]]
    acc, near = lax.optimization_barrier((acc, near))
    (acc,) = attend(numbers(crossed[:1] + first), scale_ids, query, near, head_size, acc)
    acc, far = lax.optimization_barrier((acc, far))
    far_crossed = [[swapped(part, seqs) for part in block] for block in far]
    (acc,) = attend(numbers(straight[1:] + first), scale_ids, query, far, head_size, acc)

    goals = [[*range(up, 0, -1), *range(-down, 0), 0] for up, down in reach]
    info = numbers(crossed[1:] + first + [at[goal % ring] for goal in goals[0] + goals[1]])
    parts = attend(
        info, scale_ids, query, far_crossed, head_size, acc, w_out, len(streams)
    )
    parts = [dict(zip(goals[s], parts[s * ring : (s + 1) * ring])) for s in streams]
    sums = [[None, None] for s in streams]
    for step in range(farthest, 0, -1):
        for s, way, sign in lanes:
            if step <= reach[s][way]:
                part = parts[s][sign * step]
                if sums[s][way] is not None:
                    part = total_of(part, sums[s][way])
                sums[s][way] = along(part, sign, ring)
    ends = lax.optimization_barrier([sums[s][way] for s, way, sign in lanes[::-1]])
    for (s, way, sign), end in zip(lanes[::-1], ends):
        sums[s][way] = end
    return jnp.concatenate([total_of(parts[s][0], *sums[s]) for s in streams])


def solution(mesh):
    placed = (P("seq", "head"), P(), P(None, None, "head"), P("head"), P("head", None), P())
    return jax.shard_map(
        functools.partial(body, dict(mesh.shape)),
        mesh=mesh,
        in_specs=placed,
        out_specs=P("seq", "head"),
        check_vma=False,
    )
```

```python
import functools
import math

import jax
import jax.numpy as jnp
from jax import lax
from jax.experimental import pallas as pl
from jax.experimental.pallas import tpu as pltpu
from jax.sharding import PartitionSpec as P

LOG2E = math.log2(math.e)
VMEM = pl.BlockSpec(memory_space=pltpu.VMEM)
SMEM = pl.BlockSpec(memory_space=pltpu.SMEM)
F32 = jnp.float32
BF16 = jnp.bfloat16


def ring_order(count):
    line = count // 2
    return [2 * z for z in range(line)] + [2 * z + 1 for z in reversed(range(line))]


def ring_place(index, count):
    return jnp.where(index % 2 == 0, index // 2, count - 1 - index // 2)


def ring_index(place, count):
    return jnp.where(place < count // 2, 2 * place, 2 * (count - 1 - place) + 1)


def along(value, step, count):
    order = ring_order(count)
    return lax.ppermute(
        value, "head", [(order[p], order[(p + step) % count]) for p in range(count)]
    )


def swapped(value, seq_count):
    return lax.ppermute(value, "seq", [(seq, seq + 1 - 2 * (seq % 2)) for seq in range(seq_count)])


def in_hbm(value):
    return pltpu.with_memory_space_constraint(value, pltpu.HBM)


def in_vmem(value):
    return pltpu.with_memory_space_constraint(value, pltpu.VMEM)


def fold_kernel(order, at, gain_hbm, w_hbm, tokens, out_ref, wide, gain_ref, sems):
    lanes = gain_ref.shape[1]
    size = w_hbm.shape[1] // len(order)
    per = size // lanes

    def fetch(n):
        start = pl.multiple_of(at[order[n]] * size, size)
        return pltpu.make_async_copy(
            w_hbm.at[:, pl.ds(start, size), :],
            out_ref.at[:, n * size : (n + 1) * size, :],
            sems.at[n],
        )

    gains = pltpu.make_async_copy(gain_hbm, gain_ref, sems.at[len(order) + 1])
    gains.start()
    for n in range(len(order)):
        fetch(n).start()
    own = pltpu.make_async_copy(tokens, wide.at[:, : tokens.shape[1]], sems.at[len(order)])
    own.start()
    gains.wait()
    for n in range(len(order)):
        columns = jnp.transpose(gain_ref[pl.ds(at[order[n]] * per, per), :])
        fetch(n).wait()
        for piece in range(per):
            first = n * size + piece * lanes
            for group in range(w_hbm.shape[0]):
                here = (group, slice(first, first + lanes), slice(None))
                scaled = out_ref[here].astype(F32) * columns[:, piece : piece + 1]
                out_ref[here] = scaled.astype(BF16)
    own.wait()


def fold_gain(order, at, gain, weights, tokens):
    depth = weights.shape[1]
    lanes = math.gcd(depth // len(order), 128)
    hbm = pl.BlockSpec(memory_space=pltpu.HBM)
    return pl.pallas_call(
        functools.partial(fold_kernel, order),
        out_shape=(pltpu.VMEM(weights.shape, BF16), pltpu.VMEM((tokens.shape[0], depth), BF16)),
        in_specs=[SMEM, hbm, hbm, hbm],
        out_specs=(VMEM, pl.BlockSpec(memory_space=pl.ANY)),
        scratch_shapes=[
            pltpu.VMEM((depth // lanes, lanes), F32),
            pltpu.SemaphoreType.DMA((len(order) + 2,)),
        ],
        compiler_params=pltpu.CompilerParams(vmem_limit_bytes=16 << 20),
        cost_estimate=pl.CostEstimate(
            flops=weights.size, bytes_accessed=4 * weights.size, transcendentals=0
        ),
        name="fold_gain",
    )(at, in_hbm(gain.reshape(depth // lanes, lanes)), in_hbm(weights), in_hbm(tokens))


def place_kernel(targets, *refs):
    blocks, wide, sems = refs[: len(targets)], refs[-2], refs[-1]
    copies = []
    for n, (block, (row, lane)) in enumerate(zip(blocks, targets)):
        rows, width = block.shape
        here = wide.at[row : row + rows, lane : lane + width]
        copies.append(pltpu.make_async_copy(block, here, sems.at[n]))
    for copy in copies:
        copy.start()
    for copy in copies:
        copy.wait()


def placed(targets, blocks, wide):
    operands = [*map(in_vmem, blocks), in_vmem(wide)]
    return pl.pallas_call(
        functools.partial(place_kernel, targets),
        out_shape=pltpu.VMEM(wide.shape, BF16),
        in_specs=[pl.BlockSpec(memory_space=pl.ANY)] * len(operands),
        out_specs=pl.BlockSpec(memory_space=pl.ANY),
        scratch_shapes=[pltpu.SemaphoreType.DMA((len(targets),))],
        input_output_aliases={len(blocks): 0},
        compiler_params=pltpu.CompilerParams(vmem_limit_bytes=1 << 20),
        cost_estimate=pl.CostEstimate(flops=0, bytes_accessed=1 << 20, transcendentals=0),
        name="place",
    )(*operands)


def begin_kernel(blocks, wide, w_ref, state):
    rows, depth = wide.shape
    out_width = w_ref.shape[2]
    done = depth - depth // blocks
    tile = math.gcd(rows, 256)
    for first in range(0, rows, tile):
        here = slice(first, first + tile)
        for group in range(3):
            state[here, group * out_width : (group + 1) * out_width] = jnp.dot(
                wide[here, :done], w_ref[group, :done, :], preferred_element_type=F32
            )
        power = None
        for lane in range(0, done, 128):
            values = wide[here, lane : lane + 128].astype(F32)
            power = values * values if power is None else power + values * values
        state[here, 3 * out_width :] = power


def finish_kernel(head_size, factor, state, w_ref, *refs):
    count = 2
    lasts, (q_ref, kv_ref), rest = refs[:count], refs[count : count + 2], refs[count + 2 :]
    halves, pieces = rest[:count], rest[count:]
    rows, width = lasts[0].shape
    depth, out_width = w_ref.shape[1:]
    for stream, last in enumerate(lasts):
        here = slice(stream * rows, (stream + 1) * rows)
        q, k, v = (
            state[here, group * out_width : (group + 1) * out_width]
            + jnp.dot(last[...], w_ref[group, depth - width :, :], preferred_element_type=F32)
            for group in range(3)
        )
        power = state[here, 3 * out_width :]
        for lane in range(0, width, 128):
            values = last[:, lane : lane + 128].astype(F32)
            power += values * values
        scale = lax.rsqrt(jnp.sum(power, axis=-1, keepdims=True) * (1.0 / depth) + 1e-06)
        q, k, v = q * scale, k * scale, v * scale
        for head in range(out_width // head_size):
            lanes = slice(head * head_size, (head + 1) * head_size)
            qh, kh = q[:, lanes], k[:, lanes]
            q_size = lax.rsqrt(jnp.sum(qh * qh, axis=-1, keepdims=True) + 1e-06)
            k_size = lax.rsqrt(jnp.sum(kh * kh, axis=-1, keepdims=True) + 1e-06)
            q_ref[here, lanes] = (qh * (q_size * factor[head])).astype(BF16)
            kv_ref[here, lanes] = (kh * k_size).astype(BF16)
        kv_ref[here, out_width:] = v.astype(BF16)
        halves[stream][...] = kv_ref[here, :]
    start = 0
    for piece in pieces:
        piece[...] = kv_ref[start : start + piece.shape[0], :]
        start += piece.shape[0]


def project_begin(wide, weights, blocks):
    rows, depth = wide.shape
    groups, _, out_width = weights.shape
    return pl.pallas_call(
        functools.partial(begin_kernel, blocks),
        out_shape=pltpu.VMEM((rows, groups * out_width + 128), F32),
        in_specs=[VMEM] * 2,
        out_specs=VMEM,
        compiler_params=pltpu.CompilerParams(vmem_limit_bytes=16 << 20),
        cost_estimate=pl.CostEstimate(
            flops=2 * rows * depth * groups * out_width,
            bytes_accessed=2 * depth * (rows + groups * out_width),
            transcendentals=0,
        ),
        name="project_begin",
    )(in_vmem(wide), in_vmem(weights))


def project_finish(factor, state, weights, lasts, count_pieces, head_size):
    rows, width = lasts[0].shape
    out_width = weights.shape[2]
    total = rows * len(lasts)
    units = total // 16
    sizes = [rows] * len(lasts)
    sizes += [16 * ((units + n) // count_pieces) for n in range(count_pieces)]
    return pl.pallas_call(
        functools.partial(finish_kernel, head_size),
        out_shape=(
            pltpu.VMEM((total, out_width), BF16),
            pltpu.VMEM((total, 2 * out_width), BF16),
            *[pltpu.VMEM((size, 2 * out_width), BF16) for size in sizes],
        ),
        in_specs=[SMEM] + [VMEM] * (2 + len(lasts)),
        out_specs=(VMEM,) * (2 + len(sizes)),
        compiler_params=pltpu.CompilerParams(vmem_limit_bytes=16 << 20),
        cost_estimate=pl.CostEstimate(
            flops=6 * total * width * out_width, bytes_accessed=8 * total * out_width, transcendentals=0
        ),
        name="project_finish",
    )(factor, in_vmem(state), in_vmem(weights), *map(in_vmem, lasts))


def attend_kernel(
    head_size, counts, has_acc, count_out, count_streams, info, ids, id_row, q_ref, *refs
):
    count_blocks, count_parts = counts
    kv_refs, rest = refs[: count_blocks * count_parts], refs[count_blocks * count_parts :]
    if has_acc:
        acc_in, rest = rest[0], rest[1:]
    if count_out:
        w_hbm, outs, (k_all, v_ones, acc, attended, w_ref, sem) = rest[0], rest[1:-6], rest[-6:]
        fetch_w = pltpu.make_async_copy(w_hbm, w_ref, sem)
        fetch_w.start()
    else:
        acc_out, k_all, v_ones, acc = rest
    acc[...] = acc_in[...] if has_acc else jnp.zeros_like(acc)
    rows, width = q_ref.shape
    heads = width // head_size
    keys = k_all.shape[0]
    tile = id_row.shape[2]
    q_first = info[count_blocks]
    v_ones[:, :, head_size:] = jnp.ones((heads, keys, head_size), BF16)
    for number in range(count_blocks):
        begin = 0
        for kv_ref in kv_refs[number * count_parts : (number + 1) * count_parts]:
            here = slice(begin, begin + kv_ref.shape[0])
            begin += kv_ref.shape[0]
            k_all[here, :] = kv_ref[:, :width]
            for head in range(heads):
                start = width + head * head_size
                v_ones[head, here, :head_size] = kv_ref[:, start : start + head_size]
        first = info[number]
        key_low, key_high = ids[first], ids[first + keys - 1]

        @pl.loop(0, rows // tile)
        def _(index):
            base = pl.multiple_of(index * tile, tile)
            here = pl.ds(base, tile)
            q_low, q_high = ids[q_first + base], ids[q_first + base + tile - 1]

            def add(masked):
                if masked:
                    own = jnp.broadcast_to(id_row[q_first // tile + index], (8, tile))
                    own = jnp.transpose(own)[:, :1]
                    allowed = [id_row[first // tile + n] <= own for n in range(keys // tile)]
                for head in range(heads):
                    lanes = slice(head * head_size, (head + 1) * head_size)
                    spread = slice(2 * head * head_size, 2 * (head + 1) * head_size)
                    total = acc[here, spread]
                    for low in range(0, keys, tile):
                        score = lax.dot_general(
                            q_ref[here, lanes],
                            k_all[low : low + tile, lanes],
                            (((1,), (1,)), ((), ())),
                            preferred_element_type=F32,
                        )
                        weight = jnp.exp2(score)
                        if masked:
                            weight = jnp.where(allowed[low // tile], weight, 0.0)
                        total += jnp.dot(
                            weight.astype(BF16),
                            v_ones[head, low : low + tile, :],
                            preferred_element_type=F32,
                        )
                    acc[here, spread] = total

            @pl.when(key_high <= q_low)
            def _():
                add(False)

            @pl.when((key_high > q_low) & (key_low <= q_high))
            def _():
                add(True)

    if not count_out:
        acc_out[...] = acc[...]
        return
    for head in range(heads):
        start = 2 * head * head_size
        attended[:, head * head_size : (head + 1) * head_size] = (
            acc[:, start : start + head_size]
            / acc[:, start + head_size : start + 2 * head_size]
        ).astype(BF16)
    out_rows, out_width = outs[0].shape
    fetch_w.wait()
    for number, out in enumerate(outs):
        lane = info[count_blocks + 1 + number] * out_width
        first = number * count_streams // count_out * out_rows
        out[...] = jnp.dot(
            attended[first : first + out_rows, :],
            w_ref[:, pl.ds(pl.multiple_of(lane, out_width), out_width)],
            preferred_element_type=F32,
        ).astype(BF16)


def attend(info, ids, query, blocks, head_size, acc=None, w_out=None, streams=0):
    total, width = query.shape
    parts = [part for block in blocks for part in block]
    keys = sum(part.shape[0] for part in blocks[0])
    heads = width // head_size
    count_out = streams * w_out.shape[1] // width if streams else 0
    scratch = [
        pltpu.VMEM((keys, width), BF16),
        pltpu.VMEM((heads, keys, 2 * head_size), BF16),
        pltpu.VMEM((total, 2 * width), F32),
    ]
    id_rows = ids.reshape(-1, 1, math.gcd(total, 256))
    operands = [in_vmem(query), *map(in_vmem, parts)]
    if acc is not None:
        operands.append(in_vmem(acc))
    if count_out:
        operands.append(in_hbm(w_out))
        scratch += [
            pltpu.VMEM((total, width), BF16),
            pltpu.VMEM(w_out.shape, BF16),
            pltpu.SemaphoreType.DMA(()),
        ]
        shape = pltpu.VMEM((total // streams, w_out.shape[1] * streams // count_out), BF16)
    else:
        shape = pltpu.VMEM((total, 2 * width), F32)
    outs = count_out or 1
    in_specs = [SMEM, SMEM, VMEM] + [VMEM] * len(operands)
    if count_out:
        in_specs[-1] = pl.BlockSpec(memory_space=pltpu.HBM)
    return pl.pallas_call(
        functools.partial(
            attend_kernel, head_size, (len(blocks), len(blocks[0])), acc is not None, count_out, streams
        ),
        out_shape=(shape,) * outs,
        in_specs=in_specs,
        out_specs=(VMEM,) * outs,
        scratch_shapes=scratch,
        compiler_params=pltpu.CompilerParams(
            vmem_limit_bytes=(16 << 20) + 4 * sum(part.size for part in parts)
        ),
        cost_estimate=pl.CostEstimate(flops=1 << 20, bytes_accessed=1 << 10, transcendentals=0),
        name="attend_last" if count_out else "attend",
    )(info, in_hbm(ids), in_hbm(id_rows), *operands)


def total_of(*parts):
    return sum(part.astype(F32) for part in parts).astype(BF16)


def body(mesh_shape, tokens, norm_gain, w_qkv, head_scale, w_out, scale_ids):
    ring, seqs = mesh_shape["head"], mesh_shape["seq"]
    outer = seqs // 2
    rows, width = tokens.shape
    half = rows // 2
    head_size = w_qkv.shape[2] // head_scale.shape[0]
    head_at, seq_at = lax.axis_index("head"), lax.axis_index("seq")
    place = ring_place(head_at, ring)
    chip, core = seq_at // 2, seq_at % 2
    index_at = lambda offset: ring_index((place + offset + ring) % ring, ring)
    numbers = lambda values: jnp.stack(values).astype(jnp.int32)
    at = [index_at(offset) for offset in range(ring)]

    streams = (0, 1)
    lanes = ((0, 0, 1), (1, 1, -1), (0, 1, -1), (1, 0, 1))
    farthest = ring // 2
    reach = [(farthest, farthest - 1), (farthest - 1, farthest)]

    order = [0] + [sign * step % ring for step in range(1, farthest) for sign in (-1, 1)] + [farthest]
    held = [[tokens[s * half : (s + 1) * half]] * 2 for s in streams]
    blocks, targets = [], []
    for step in range(1, farthest + 1):
        for s, way, sign in lanes:
            if step <= reach[s][way]:
                held[s][way] = along(held[s][way], sign, ring)
        if step == 1:
            held[0][0], (weights, wide) = lax.optimization_barrier(
                (held[0][0], fold_gain(order, numbers(at), norm_gain, w_qkv, tokens))
            )
        elif step == 2:
            wide = placed(targets, blocks, wide)
            blocks, targets = [], []
        elif step == 3:
            held[1][1], wide = lax.optimization_barrier(
                (held[1][1], placed(targets, blocks, wide))
            )
            blocks, targets = [], []
        if step < farthest:
            for s, way, sign in lanes:
                blocks.append(held[s][way])
                targets.append((s * half, (2 * step - 1 + way) * width))
    wide = placed(targets, blocks, wide)
    lasts = [held[0][0], held[1][1]]
    state, factor = lax.optimization_barrier((project_begin(wide, weights, ring), head_scale * LOG2E))
    query, kv, *parts = project_finish(factor, state, weights, lasts, 3, head_size)
    halves, pieces = parts[:2], parts[2:]

    far, straight, crossed = [], [], []
    for step in range(outer):
        source = 2 * ((chip + outer - step) % outer)
        straight.append((source + core) * rows)
        crossed.append((source + 1 - core) * rows)
        if step:
            shift = [(2 * a + b, 2 * ((a + step) % outer) + b) for a in range(outer) for b in (0, 1)]
            far.append([lax.ppermute(part, "seq", shift) for part in halves])
    first = [seq_at * rows]
    (acc,) = attend(numbers(straight[:1] + first), scale_ids, query, [[kv]], head_size)
    near = [[swapped(piece, seqs) for piece in pieces]]
    acc, near = lax.optimization_barrier((acc, near))
    (acc,) = attend(numbers(crossed[:1] + first), scale_ids, query, near, head_size, acc)
    acc, far = lax.optimization_barrier((acc, far))
    far_crossed = [[swapped(part, seqs) for part in block] for block in far]
    (acc,) = attend(numbers(straight[1:] + first), scale_ids, query, far, head_size, acc)

    goals = [[*range(up, 0, -1), *range(-down, 0), 0] for up, down in reach]
    info = numbers(crossed[1:] + first + [at[goal % ring] for goal in goals[0] + goals[1]])
    parts = attend(
        info, scale_ids, query, far_crossed, head_size, acc, w_out, len(streams)
    )
    parts = [dict(zip(goals[s], parts[s * ring : (s + 1) * ring])) for s in streams]
    sums = [[None, None] for s in streams]
    for step in range(farthest, 0, -1):
        for s, way, sign in lanes:
            if step <= reach[s][way]:
                part = parts[s][sign * step]
                if sums[s][way] is not None:
                    part = total_of(part, sums[s][way])
                sums[s][way] = along(part, sign, ring)
    ends = lax.optimization_barrier([sums[s][way] for s, way, sign in lanes[::-1]])
    for (s, way, sign), end in zip(lanes[::-1], ends):
        sums[s][way] = end
    return jnp.concatenate([total_of(parts[s][0], *sums[s]) for s in streams])


def solution(mesh):
    placed = (P("seq", "head"), P(), P(None, None, "head"), P("head"), P("head", None), P())
    return jax.shard_map(
        functools.partial(body, dict(mesh.shape)),
        mesh=mesh,
        in_specs=placed,
        out_specs=P("seq", "head"),
        check_vma=False,
    )
```

```python
import functools
import math

import jax
import jax.numpy as jnp
from jax import lax
from jax.experimental import pallas as pl
from jax.experimental.pallas import tpu as pltpu
from jax.sharding import PartitionSpec as P

LOG2E = math.log2(math.e)
VMEM = pl.BlockSpec(memory_space=pltpu.VMEM)
SMEM = pl.BlockSpec(memory_space=pltpu.SMEM)
F32 = jnp.float32
BF16 = jnp.bfloat16


def ring_order(count):
    line = count // 2
    return [2 * z for z in range(line)] + [2 * z + 1 for z in reversed(range(line))]


def ring_place(index, count):
    return jnp.where(index % 2 == 0, index // 2, count - 1 - index // 2)


def ring_index(place, count):
    return jnp.where(place < count // 2, 2 * place, 2 * (count - 1 - place) + 1)


def along(value, step, count):
    order = ring_order(count)
    return lax.ppermute(
        value, "head", [(order[p], order[(p + step) % count]) for p in range(count)]
    )


def swapped(value, seq_count):
    return lax.ppermute(value, "seq", [(seq, seq + 1 - 2 * (seq % 2)) for seq in range(seq_count)])


def in_hbm(value):
    return pltpu.with_memory_space_constraint(value, pltpu.HBM)


def in_vmem(value):
    return pltpu.with_memory_space_constraint(value, pltpu.VMEM)


def fold_kernel(order, at, gain_hbm, w_hbm, tokens, out_ref, wide, gain_ref, sems):
    lanes = gain_ref.shape[1]
    size = w_hbm.shape[1] // len(order)
    per = size // lanes

    def fetch(n):
        start = pl.multiple_of(at[order[n]] * size, size)
        return pltpu.make_async_copy(
            w_hbm.at[:, pl.ds(start, size), :],
            out_ref.at[:, n * size : (n + 1) * size, :],
            sems.at[n],
        )

    gains = pltpu.make_async_copy(gain_hbm, gain_ref, sems.at[len(order) + 1])
    gains.start()
    for n in range(len(order)):
        fetch(n).start()
    own = pltpu.make_async_copy(tokens, wide.at[:, : tokens.shape[1]], sems.at[len(order)])
    own.start()
    gains.wait()
    for n in range(len(order)):
        columns = jnp.transpose(gain_ref[pl.ds(at[order[n]] * per, per), :])
        fetch(n).wait()
        for piece in range(per):
            first = n * size + piece * lanes
            for group in range(w_hbm.shape[0]):
                here = (group, slice(first, first + lanes), slice(None))
                scaled = out_ref[here].astype(F32) * columns[:, piece : piece + 1]
                out_ref[here] = scaled.astype(BF16)
    own.wait()


def fold_gain(order, at, gain, weights, tokens):
    depth = weights.shape[1]
    lanes = math.gcd(depth // len(order), 128)
    hbm = pl.BlockSpec(memory_space=pltpu.HBM)
    return pl.pallas_call(
        functools.partial(fold_kernel, order),
        out_shape=(pltpu.VMEM(weights.shape, BF16), pltpu.VMEM((tokens.shape[0], depth), BF16)),
        in_specs=[SMEM, hbm, hbm, hbm],
        out_specs=(VMEM, pl.BlockSpec(memory_space=pl.ANY)),
        scratch_shapes=[
            pltpu.VMEM((depth // lanes, lanes), F32),
            pltpu.SemaphoreType.DMA((len(order) + 2,)),
        ],
        compiler_params=pltpu.CompilerParams(vmem_limit_bytes=16 << 20),
        cost_estimate=pl.CostEstimate(
            flops=weights.size, bytes_accessed=4 * weights.size, transcendentals=0
        ),
        name="fold_gain",
    )(at, in_hbm(gain.reshape(depth // lanes, lanes)), in_hbm(weights), in_hbm(tokens))


def place_kernel(targets, *refs):
    blocks, wide, sems = refs[: len(targets)], refs[-2], refs[-1]
    copies = []
    for n, (block, (row, lane)) in enumerate(zip(blocks, targets)):
        rows, width = block.shape
        here = wide.at[row : row + rows, lane : lane + width]
        copies.append(pltpu.make_async_copy(block, here, sems.at[n]))
    for copy in copies:
        copy.start()
    for copy in copies:
        copy.wait()


def placed(targets, blocks, wide):
    operands = [*map(in_vmem, blocks), in_vmem(wide)]
    return pl.pallas_call(
        functools.partial(place_kernel, targets),
        out_shape=pltpu.VMEM(wide.shape, BF16),
        in_specs=[pl.BlockSpec(memory_space=pl.ANY)] * len(operands),
        out_specs=pl.BlockSpec(memory_space=pl.ANY),
        scratch_shapes=[pltpu.SemaphoreType.DMA((len(targets),))],
        input_output_aliases={len(blocks): 0},
        compiler_params=pltpu.CompilerParams(vmem_limit_bytes=1 << 20),
        cost_estimate=pl.CostEstimate(flops=0, bytes_accessed=1 << 20, transcendentals=0),
        name="place",
    )(*operands)


def begin_kernel(blocks, wide, w_ref, state):
    rows, depth = wide.shape
    out_width = w_ref.shape[2]
    done = depth - depth // blocks
    tile = math.gcd(rows, 256)
    for first in range(0, rows, tile):
        here = slice(first, first + tile)
        for group in range(3):
            state[here, group * out_width : (group + 1) * out_width] = jnp.dot(
                wide[here, :done], w_ref[group, :done, :], preferred_element_type=F32
            )
        power = None
        for lane in range(0, done, 128):
            values = wide[here, lane : lane + 128].astype(F32)
            power = values * values if power is None else power + values * values
        state[here, 3 * out_width :] = power


def finish_kernel(head_size, factor, state, w_ref, *refs):
    count = 2
    lasts, q_ref = refs[:count], refs[count]
    halves, pieces = refs[count + 1 : 2 * count + 1], refs[2 * count + 1 :]
    rows, width = lasts[0].shape
    depth, out_width = w_ref.shape[1:]
    for stream, last in enumerate(lasts):
        here = slice(stream * rows, (stream + 1) * rows)
        kv_ref = halves[stream]
        q, k, v = (
            state[here, group * out_width : (group + 1) * out_width]
            + jnp.dot(last[...], w_ref[group, depth - width :, :], preferred_element_type=F32)
            for group in range(3)
        )
        power = state[here, 3 * out_width :]
        for lane in range(0, width, 128):
            values = last[:, lane : lane + 128].astype(F32)
            power += values * values
        scale = lax.rsqrt(jnp.sum(power, axis=-1, keepdims=True) * (1.0 / depth) + 1e-06)
        q, k, v = q * scale, k * scale, v * scale
        for head in range(out_width // head_size):
            lanes = slice(head * head_size, (head + 1) * head_size)
            qh, kh = q[:, lanes], k[:, lanes]
            q_size = lax.rsqrt(jnp.sum(qh * qh, axis=-1, keepdims=True) + 1e-06)
            k_size = lax.rsqrt(jnp.sum(kh * kh, axis=-1, keepdims=True) + 1e-06)
            q_ref[here, lanes] = (qh * (q_size * (factor[head] * LOG2E))).astype(BF16)
            kv_ref[:, lanes] = (kh * k_size).astype(BF16)
        kv_ref[:, out_width:] = v.astype(BF16)
    start = 0
    for piece in pieces:
        end = start + piece.shape[0]
        for stream, half in enumerate(halves):
            base = stream * rows
            low, high = max(start, base), min(end, base + rows)
            if low < high:
                piece[low - start : high - start, :] = half[low - base : high - base, :]
        start = end


def project_begin(wide, weights, blocks):
    rows, depth = wide.shape
    groups, _, out_width = weights.shape
    return pl.pallas_call(
        functools.partial(begin_kernel, blocks),
        out_shape=pltpu.VMEM((rows, groups * out_width + 128), F32),
        in_specs=[VMEM] * 2,
        out_specs=VMEM,
        compiler_params=pltpu.CompilerParams(vmem_limit_bytes=16 << 20),
        cost_estimate=pl.CostEstimate(
            flops=2 * rows * depth * groups * out_width,
            bytes_accessed=2 * depth * (rows + groups * out_width),
            transcendentals=0,
        ),
        name="project_begin",
    )(in_vmem(wide), in_vmem(weights))


def project_finish(factor, state, weights, lasts, count_pieces, head_size):
    rows, width = lasts[0].shape
    out_width = weights.shape[2]
    total = rows * len(lasts)
    units = total // 16
    sizes = [rows] * len(lasts)
    sizes += [16 * ((units + n) // count_pieces) for n in range(count_pieces)]
    return pl.pallas_call(
        functools.partial(finish_kernel, head_size),
        out_shape=(
            pltpu.VMEM((total, out_width), BF16),
            *[pltpu.VMEM((size, 2 * out_width), BF16) for size in sizes],
        ),
        in_specs=[SMEM] + [VMEM] * (2 + len(lasts)),
        out_specs=(VMEM,) * (1 + len(sizes)),
        compiler_params=pltpu.CompilerParams(vmem_limit_bytes=16 << 20),
        cost_estimate=pl.CostEstimate(
            flops=6 * total * width * out_width, bytes_accessed=8 * total * out_width, transcendentals=0
        ),
        name="project_finish",
    )(in_hbm(factor), in_vmem(state), in_vmem(weights), *map(in_vmem, lasts))


def attend_kernel(
    head_size, counts, has_acc, count_out, count_streams, info, ids, id_row, q_ref, *refs
):
    count_blocks, count_parts = counts
    kv_refs, rest = refs[: count_blocks * count_parts], refs[count_blocks * count_parts :]
    if has_acc:
        acc_in, rest = rest[0], rest[1:]
    if count_out:
        w_hbm, outs, (k_all, v_ones, acc, attended, w_ref, sem) = rest[0], rest[1:-6], rest[-6:]
        fetch_w = pltpu.make_async_copy(w_hbm, w_ref, sem)
        fetch_w.start()
    else:
        acc_out, k_all, v_ones, acc = rest
    acc[...] = acc_in[...] if has_acc else jnp.zeros_like(acc)
    rows, width = q_ref.shape
    heads = width // head_size
    keys = k_all.shape[0]
    tile = id_row.shape[2]
    q_first = info[count_blocks]
    v_ones[:, :, head_size:] = jnp.ones((heads, keys, head_size), BF16)
    for number in range(count_blocks):
        begin = 0
        for kv_ref in kv_refs[number * count_parts : (number + 1) * count_parts]:
            here = slice(begin, begin + kv_ref.shape[0])
            begin += kv_ref.shape[0]
            k_all[here, :] = kv_ref[:, :width]
            for head in range(heads):
                start = width + head * head_size
                v_ones[head, here, :head_size] = kv_ref[:, start : start + head_size]
        first = info[number]
        key_low, key_high = ids[first], ids[first + keys - 1]

        @pl.loop(0, rows // tile)
        def _(index):
            base = pl.multiple_of(index * tile, tile)
            here = pl.ds(base, tile)
            q_low, q_high = ids[q_first + base], ids[q_first + base + tile - 1]

            def add(masked):
                if masked:
                    own = jnp.broadcast_to(id_row[q_first // tile + index], (8, tile))
                    own = jnp.transpose(own)[:, :1]
                    allowed = [id_row[first // tile + n] <= own for n in range(keys // tile)]
                for head in range(heads):
                    lanes = slice(head * head_size, (head + 1) * head_size)
                    spread = slice(2 * head * head_size, 2 * (head + 1) * head_size)
                    total = acc[here, spread]
                    for low in range(0, keys, tile):
                        score = lax.dot_general(
                            q_ref[here, lanes],
                            k_all[low : low + tile, lanes],
                            (((1,), (1,)), ((), ())),
                            preferred_element_type=F32,
                        )
                        weight = jnp.exp2(score)
                        if masked:
                            weight = jnp.where(allowed[low // tile], weight, 0.0)
                        total += jnp.dot(
                            weight.astype(BF16),
                            v_ones[head, low : low + tile, :],
                            preferred_element_type=F32,
                        )
                    acc[here, spread] = total

            @pl.when(key_high <= q_low)
            def _():
                add(False)

            @pl.when((key_high > q_low) & (key_low <= q_high))
            def _():
                add(True)

    if not count_out:
        acc_out[...] = acc[...]
        return
    for head in range(heads):
        start = 2 * head * head_size
        attended[:, head * head_size : (head + 1) * head_size] = (
            acc[:, start : start + head_size]
            / acc[:, start + head_size : start + 2 * head_size]
        ).astype(BF16)
    out_rows, out_width = outs[0].shape
    fetch_w.wait()
    for number, out in enumerate(outs):
        lane = info[count_blocks + 1 + number] * out_width
        first = number * count_streams // count_out * out_rows
        out[...] = jnp.dot(
            attended[first : first + out_rows, :],
            w_ref[:, pl.ds(pl.multiple_of(lane, out_width), out_width)],
            preferred_element_type=F32,
        ).astype(BF16)


def attend(info, ids, query, blocks, head_size, acc=None, w_out=None, streams=0):
    total, width = query.shape
    parts = [part for block in blocks for part in block]
    keys = sum(part.shape[0] for part in blocks[0])
    heads = width // head_size
    count_out = streams * w_out.shape[1] // width if streams else 0
    scratch = [
        pltpu.VMEM((keys, width), BF16),
        pltpu.VMEM((heads, keys, 2 * head_size), BF16),
        pltpu.VMEM((total, 2 * width), F32),
    ]
    id_rows = ids.reshape(-1, 1, math.gcd(total, 256))
    operands = [in_vmem(query), *map(in_vmem, parts)]
    if acc is not None:
        operands.append(in_vmem(acc))
    if count_out:
        operands.append(in_hbm(w_out))
        scratch += [
            pltpu.VMEM((total, width), BF16),
            pltpu.VMEM(w_out.shape, BF16),
            pltpu.SemaphoreType.DMA(()),
        ]
        shape = pltpu.VMEM((total // streams, w_out.shape[1] * streams // count_out), BF16)
    else:
        shape = pltpu.VMEM((total, 2 * width), F32)
    outs = count_out or 1
    in_specs = [SMEM, SMEM, VMEM] + [VMEM] * len(operands)
    if count_out:
        in_specs[-1] = pl.BlockSpec(memory_space=pltpu.HBM)
    return pl.pallas_call(
        functools.partial(
            attend_kernel, head_size, (len(blocks), len(blocks[0])), acc is not None, count_out, streams
        ),
        out_shape=(shape,) * outs,
        in_specs=in_specs,
        out_specs=(VMEM,) * outs,
        scratch_shapes=scratch,
        compiler_params=pltpu.CompilerParams(
            vmem_limit_bytes=(16 << 20) + 4 * sum(part.size for part in parts)
        ),
        cost_estimate=pl.CostEstimate(flops=1 << 20, bytes_accessed=1 << 10, transcendentals=0),
        name="attend_last" if count_out else "attend",
    )(info, in_hbm(ids), in_hbm(id_rows), *operands)


def total_of(*parts):
    return sum(part.astype(F32) for part in parts).astype(BF16)


def body(mesh_shape, tokens, norm_gain, w_qkv, head_scale, w_out, scale_ids):
    ring, seqs = mesh_shape["head"], mesh_shape["seq"]
    outer = seqs // 2
    rows, width = tokens.shape
    half = rows // 2
    head_size = w_qkv.shape[2] // head_scale.shape[0]
    head_at, seq_at = lax.axis_index("head"), lax.axis_index("seq")
    place = ring_place(head_at, ring)
    chip, core = seq_at // 2, seq_at % 2
    index_at = lambda offset: ring_index((place + offset + ring) % ring, ring)
    numbers = lambda values: jnp.stack(values).astype(jnp.int32)
    at = [index_at(offset) for offset in range(ring)]

    streams = (0, 1)
    lanes = ((0, 0, 1), (1, 1, -1), (0, 1, -1), (1, 0, 1))
    farthest = ring // 2
    reach = [(farthest, farthest - 1), (farthest - 1, farthest)]

    order = [0] + [sign * step % ring for step in range(1, farthest) for sign in (-1, 1)] + [farthest]
    held = [[tokens[s * half : (s + 1) * half]] * 2 for s in streams]
    blocks, targets = [], []
    for step in range(1, farthest + 1):
        for s, way, sign in lanes:
            if step <= reach[s][way]:
                held[s][way] = along(held[s][way], sign, ring)
        if step == 1:
            held[0][0], (weights, wide) = lax.optimization_barrier(
                (held[0][0], fold_gain(order, numbers(at), norm_gain, w_qkv, tokens))
            )
        elif step == 2:
            wide = placed(targets, blocks, wide)
            blocks, targets = [], []
        elif step == 3:
            held[1][1], wide = lax.optimization_barrier(
                (held[1][1], placed(targets, blocks, wide))
            )
            blocks, targets = [], []
        if step < farthest:
            for s, way, sign in lanes:
                blocks.append(held[s][way])
                targets.append((s * half, (2 * step - 1 + way) * width))
    wide = placed(targets, blocks, wide)
    lasts = [held[0][0], held[1][1]]
    state = project_begin(wide, weights, ring)
    query, *parts = project_finish(head_scale, state, weights, lasts, 3, head_size)
    halves, pieces = parts[:2], parts[2:]

    far, straight, crossed = [], [], []
    for step in range(outer):
        source = 2 * ((chip + outer - step) % outer)
        straight.append((source + core) * rows)
        crossed.append((source + 1 - core) * rows)
        if step:
            shift = [(2 * a + b, 2 * ((a + step) % outer) + b) for a in range(outer) for b in (0, 1)]
            far.append([lax.ppermute(part, "seq", shift) for part in halves])
    first = [seq_at * rows]
    (acc,) = attend(numbers(straight[:1] + first), scale_ids, query, [halves], head_size)
    near = [[swapped(piece, seqs) for piece in pieces]]
    acc, near = lax.optimization_barrier((acc, near))
    (acc,) = attend(numbers(crossed[:1] + first), scale_ids, query, near, head_size, acc)
    acc, far = lax.optimization_barrier((acc, far))
    far_crossed = [[swapped(part, seqs) for part in block] for block in far]
    (acc,) = attend(numbers(straight[1:] + first), scale_ids, query, far, head_size, acc)

    goals = [[*range(up, 0, -1), *range(-down, 0), 0] for up, down in reach]
    info = numbers(crossed[1:] + first + [at[goal % ring] for goal in goals[0] + goals[1]])
    parts = attend(
        info, scale_ids, query, far_crossed, head_size, acc, w_out, len(streams)
    )
    parts = [dict(zip(goals[s], parts[s * ring : (s + 1) * ring])) for s in streams]
    sums = [[None, None] for s in streams]
    for step in range(farthest, 0, -1):
        for s, way, sign in lanes:
            if step <= reach[s][way]:
                part = parts[s][sign * step]
                if sums[s][way] is not None:
                    part = total_of(part, sums[s][way])
                sums[s][way] = along(part, sign, ring)
    ends = lax.optimization_barrier([sums[s][way] for s, way, sign in lanes[::-1]])
    for (s, way, sign), end in zip(lanes[::-1], ends):
        sums[s][way] = end
    return jnp.concatenate([total_of(parts[s][0], *sums[s]) for s in streams])


def solution(mesh):
    placed = (P("seq", "head"), P(), P(None, None, "head"), P("head"), P("head", None), P())
    return jax.shard_map(
        functools.partial(body, dict(mesh.shape)),
        mesh=mesh,
        in_specs=placed,
        out_specs=P("seq", "head"),
        check_vma=False,
    )
```

```python
import functools
import math

import jax
import jax.numpy as jnp
from jax import lax
from jax.experimental import pallas as pl
from jax.experimental.pallas import tpu as pltpu
from jax.sharding import PartitionSpec as P

LOG2E = math.log2(math.e)
VMEM = pl.BlockSpec(memory_space=pltpu.VMEM)
SMEM = pl.BlockSpec(memory_space=pltpu.SMEM)
F32 = jnp.float32
BF16 = jnp.bfloat16


def ring_order(count):
    line = count // 2
    return [2 * z for z in range(line)] + [2 * z + 1 for z in reversed(range(line))]


def ring_place(index, count):
    return jnp.where(index % 2 == 0, index // 2, count - 1 - index // 2)


def ring_index(place, count):
    return jnp.where(place < count // 2, 2 * place, 2 * (count - 1 - place) + 1)


def along(value, step, count):
    order = ring_order(count)
    return lax.ppermute(
        value, "head", [(order[p], order[(p + step) % count]) for p in range(count)]
    )


def swapped(value, seq_count):
    return lax.ppermute(value, "seq", [(seq, seq + 1 - 2 * (seq % 2)) for seq in range(seq_count)])


def in_hbm(value):
    return pltpu.with_memory_space_constraint(value, pltpu.HBM)


def in_vmem(value):
    return pltpu.with_memory_space_constraint(value, pltpu.VMEM)


def load_kernel(order, at, w_hbm, tokens, out_ref, wide, sems):
    size = w_hbm.shape[1] // len(order)
    copies = [pltpu.make_async_copy(tokens, wide.at[:, : tokens.shape[1]], sems.at[len(order)])]
    for n in range(len(order)):
        start = pl.multiple_of(at[order[n]] * size, size)
        copies.append(
            pltpu.make_async_copy(
                w_hbm.at[:, pl.ds(start, size), :],
                out_ref.at[:, n * size : (n + 1) * size, :],
                sems.at[n],
            )
        )
    for copy in copies:
        copy.start()
    for copy in copies:
        copy.wait()


def loaded(order, at, weights, tokens):
    hbm = pl.BlockSpec(memory_space=pltpu.HBM)
    return pl.pallas_call(
        functools.partial(load_kernel, order),
        out_shape=(
            pltpu.VMEM(weights.shape, BF16),
            pltpu.VMEM((tokens.shape[0], weights.shape[1]), BF16),
        ),
        in_specs=[SMEM, hbm, hbm],
        out_specs=(pl.BlockSpec(memory_space=pl.ANY),) * 2,
        scratch_shapes=[pltpu.SemaphoreType.DMA((len(order) + 1,))],
        compiler_params=pltpu.CompilerParams(vmem_limit_bytes=1 << 20),
        cost_estimate=pl.CostEstimate(
            flops=weights.size, bytes_accessed=4 * weights.size, transcendentals=0
        ),
        name="load",
    )(at, in_hbm(weights), in_hbm(tokens))


def gain_of(gain_ref, offset, ring, part, parts):
    place = ring_place(lax.axis_index("head"), ring)
    index = ring_index((place + offset) % ring, ring)
    return gain_ref[pl.ds(index * parts + part, 1), :]


def place_kernel(targets, *refs):
    blocks, wide, sems = refs[: len(targets)], refs[-2], refs[-1]
    copies = []
    for n, (block, (row, lane)) in enumerate(zip(blocks, targets)):
        rows, width = block.shape
        here = wide.at[row : row + rows, lane : lane + width]
        copies.append(pltpu.make_async_copy(block, here, sems.at[n]))
    for copy in copies:
        copy.start()
    for copy in copies:
        copy.wait()


def placed(targets, blocks, wide):
    operands = [*map(in_vmem, blocks), in_vmem(wide)]
    return pl.pallas_call(
        functools.partial(place_kernel, targets),
        out_shape=pltpu.VMEM(wide.shape, BF16),
        in_specs=[pl.BlockSpec(memory_space=pl.ANY)] * len(operands),
        out_specs=pl.BlockSpec(memory_space=pl.ANY),
        scratch_shapes=[pltpu.SemaphoreType.DMA((len(targets),))],
        input_output_aliases={len(blocks): 0},
        compiler_params=pltpu.CompilerParams(vmem_limit_bytes=1 << 20),
        cost_estimate=pl.CostEstimate(flops=0, bytes_accessed=1 << 20, transcendentals=0),
        name="place",
    )(*operands)


def begin_kernel(order, gain_ref, wide, w_ref, state, scaled):
    rows, depth = wide.shape
    ring = len(order)
    out_width, parts = w_ref.shape[2], depth // ring // 128
    tile, done = scaled.shape
    for first in range(0, rows, tile):
        here = slice(first, first + tile)
        power = None
        for lane in range(0, done, 128):
            n, part = lane // 128 // parts, lane // 128 % parts
            values = wide[here, lane : lane + 128].astype(F32)
            power = values * values if power is None else power + values * values
            row = gain_of(gain_ref, order[n], ring, part, parts)
            scaled[:, lane : lane + 128] = (values * row).astype(BF16)
        state[here, 3 * out_width :] = power
        for group in range(3):
            state[here, group * out_width : (group + 1) * out_width] = jnp.dot(
                scaled[...], w_ref[group, :done, :], preferred_element_type=F32
            )


def finish_kernel(head_size, order, factor, gain_ref, state, w_ref, *refs):
    count = 2
    lasts, q_ref = refs[:count], refs[count]
    halves, pieces = refs[count + 1 : 2 * count + 1], refs[2 * count + 1 :]
    rows, width = lasts[0].shape
    depth, out_width = w_ref.shape[1:]
    for stream, last in enumerate(lasts):
        here = slice(stream * rows, (stream + 1) * rows)
        kv_ref = halves[stream]
        power = state[here, 3 * out_width :]
        scaled = []
        for part in range(width // 128):
            values = last[:, part * 128 : (part + 1) * 128].astype(F32)
            power += values * values
            row = gain_of(gain_ref, order[-1], len(order), part, width // 128)
            scaled.append((values * row).astype(BF16))
        scaled = jnp.concatenate(scaled, axis=1)
        q, k, v = (
            state[here, group * out_width : (group + 1) * out_width]
            + jnp.dot(scaled, w_ref[group, depth - width :, :], preferred_element_type=F32)
            for group in range(3)
        )
        scale = lax.rsqrt(jnp.sum(power, axis=-1, keepdims=True) * (1.0 / depth) + 1e-06)
        q, k, v = q * scale, k * scale, v * scale
        for head in range(out_width // head_size):
            lanes = slice(head * head_size, (head + 1) * head_size)
            qh, kh = q[:, lanes], k[:, lanes]
            q_size = lax.rsqrt(jnp.sum(qh * qh, axis=-1, keepdims=True) + 1e-06)
            k_size = lax.rsqrt(jnp.sum(kh * kh, axis=-1, keepdims=True) + 1e-06)
            q_ref[here, lanes] = (qh * (q_size * (factor[head] * LOG2E))).astype(BF16)
            kv_ref[:, lanes] = (kh * k_size).astype(BF16)
        kv_ref[:, out_width:] = v.astype(BF16)
    start = 0
    for piece in pieces:
        end = start + piece.shape[0]
        for stream, half in enumerate(halves):
            base = stream * rows
            low, high = max(start, base), min(end, base + rows)
            if low < high:
                piece[low - start : high - start, :] = half[low - base : high - base, :]
        start = end


def project_begin(gain, wide, weights, order):
    rows, depth = wide.shape
    done = depth - depth // len(order)
    groups, _, out_width = weights.shape
    return pl.pallas_call(
        functools.partial(begin_kernel, order),
        out_shape=pltpu.VMEM((rows, groups * out_width + 128), F32),
        in_specs=[VMEM] * 3,
        out_specs=VMEM,
        scratch_shapes=[pltpu.VMEM((math.gcd(rows, 256), done), BF16)],
        compiler_params=pltpu.CompilerParams(vmem_limit_bytes=16 << 20),
        cost_estimate=pl.CostEstimate(
            flops=2 * rows * depth * groups * out_width,
            bytes_accessed=2 * depth * (rows + groups * out_width),
            transcendentals=0,
        ),
        name="project_begin",
    )(in_hbm(gain), in_vmem(wide), in_vmem(weights))


def project_finish(factor, gain, state, weights, lasts, count_pieces, order, head_size):
    rows, width = lasts[0].shape
    out_width = weights.shape[2]
    total = rows * len(lasts)
    units = total // 16
    sizes = [rows] * len(lasts)
    sizes += [16 * ((units + n) // count_pieces) for n in range(count_pieces)]
    return pl.pallas_call(
        functools.partial(finish_kernel, head_size, order),
        out_shape=(
            pltpu.VMEM((total, out_width), BF16),
            *[pltpu.VMEM((size, 2 * out_width), BF16) for size in sizes],
        ),
        in_specs=[SMEM] + [VMEM] * (3 + len(lasts)),
        out_specs=(VMEM,) * (1 + len(sizes)),
        compiler_params=pltpu.CompilerParams(vmem_limit_bytes=16 << 20),
        cost_estimate=pl.CostEstimate(
            flops=6 * total * width * out_width, bytes_accessed=8 * total * out_width, transcendentals=0
        ),
        name="project_finish",
    )(in_hbm(factor), in_hbm(gain), in_vmem(state), in_vmem(weights), *map(in_vmem, lasts))


def attend_kernel(
    head_size, counts, has_acc, count_out, count_streams, info, ids, id_row, q_ref, *refs
):
    count_blocks, count_parts = counts
    kv_refs, rest = refs[: count_blocks * count_parts], refs[count_blocks * count_parts :]
    if has_acc:
        acc_in, rest = rest[0], rest[1:]
    if count_out:
        w_hbm, outs, (k_all, v_ones, acc, attended, w_ref, sem) = rest[0], rest[1:-6], rest[-6:]
        fetch_w = pltpu.make_async_copy(w_hbm, w_ref, sem)
        fetch_w.start()
    else:
        acc_out, k_all, v_ones, acc = rest
    acc[...] = acc_in[...] if has_acc else jnp.zeros_like(acc)
    rows, width = q_ref.shape
    heads = width // head_size
    keys = k_all.shape[0]
    tile = id_row.shape[2]
    q_first = info[count_blocks]
    v_ones[:, :, head_size:] = jnp.ones((heads, keys, head_size), BF16)
    for number in range(count_blocks):
        begin = 0
        for kv_ref in kv_refs[number * count_parts : (number + 1) * count_parts]:
            here = slice(begin, begin + kv_ref.shape[0])
            begin += kv_ref.shape[0]
            k_all[here, :] = kv_ref[:, :width]
            for head in range(heads):
                start = width + head * head_size
                v_ones[head, here, :head_size] = kv_ref[:, start : start + head_size]
        first = info[number]
        key_low, key_high = ids[first], ids[first + keys - 1]

        @pl.loop(0, rows // tile)
        def _(index):
            base = pl.multiple_of(index * tile, tile)
            here = pl.ds(base, tile)
            q_low, q_high = ids[q_first + base], ids[q_first + base + tile - 1]

            def add(masked):
                if masked:
                    own = jnp.broadcast_to(id_row[q_first // tile + index], (8, tile))
                    own = jnp.transpose(own)[:, :1]
                    allowed = [id_row[first // tile + n] <= own for n in range(keys // tile)]
                for head in range(heads):
                    lanes = slice(head * head_size, (head + 1) * head_size)
                    spread = slice(2 * head * head_size, 2 * (head + 1) * head_size)
                    total = acc[here, spread]
                    for low in range(0, keys, tile):
                        score = lax.dot_general(
                            q_ref[here, lanes],
                            k_all[low : low + tile, lanes],
                            (((1,), (1,)), ((), ())),
                            preferred_element_type=F32,
                        )
                        weight = jnp.exp2(score)
                        if masked:
                            weight = jnp.where(allowed[low // tile], weight, 0.0)
                        total += jnp.dot(
                            weight.astype(BF16),
                            v_ones[head, low : low + tile, :],
                            preferred_element_type=F32,
                        )
                    acc[here, spread] = total

            @pl.when(key_high <= q_low)
            def _():
                add(False)

            @pl.when((key_high > q_low) & (key_low <= q_high))
            def _():
                add(True)

    if not count_out:
        acc_out[...] = acc[...]
        return
    for head in range(heads):
        start = 2 * head * head_size
        attended[:, head * head_size : (head + 1) * head_size] = (
            acc[:, start : start + head_size]
            / acc[:, start + head_size : start + 2 * head_size]
        ).astype(BF16)
    out_rows, out_width = outs[0].shape
    fetch_w.wait()
    for number, out in enumerate(outs):
        lane = info[count_blocks + 1 + number] * out_width
        first = number * count_streams // count_out * out_rows
        out[...] = jnp.dot(
            attended[first : first + out_rows, :],
            w_ref[:, pl.ds(pl.multiple_of(lane, out_width), out_width)],
            preferred_element_type=F32,
        ).astype(BF16)


def attend(info, ids, query, blocks, head_size, acc=None, w_out=None, streams=0):
    total, width = query.shape
    parts = [part for block in blocks for part in block]
    keys = sum(part.shape[0] for part in blocks[0])
    heads = width // head_size
    count_out = streams * w_out.shape[1] // width if streams else 0
    scratch = [
        pltpu.VMEM((keys, width), BF16),
        pltpu.VMEM((heads, keys, 2 * head_size), BF16),
        pltpu.VMEM((total, 2 * width), F32),
    ]
    id_rows = ids.reshape(-1, 1, math.gcd(total, 256))
    operands = [in_vmem(query), *map(in_vmem, parts)]
    if acc is not None:
        operands.append(in_vmem(acc))
    if count_out:
        operands.append(in_hbm(w_out))
        scratch += [
            pltpu.VMEM((total, width), BF16),
            pltpu.VMEM(w_out.shape, BF16),
            pltpu.SemaphoreType.DMA(()),
        ]
        shape = pltpu.VMEM((total // streams, w_out.shape[1] * streams // count_out), BF16)
    else:
        shape = pltpu.VMEM((total, 2 * width), F32)
    outs = count_out or 1
    in_specs = [SMEM, SMEM, VMEM] + [VMEM] * len(operands)
    if count_out:
        in_specs[-1] = pl.BlockSpec(memory_space=pltpu.HBM)
    return pl.pallas_call(
        functools.partial(
            attend_kernel, head_size, (len(blocks), len(blocks[0])), acc is not None, count_out, streams
        ),
        out_shape=(shape,) * outs,
        in_specs=in_specs,
        out_specs=(VMEM,) * outs,
        scratch_shapes=scratch,
        compiler_params=pltpu.CompilerParams(
            vmem_limit_bytes=(16 << 20) + 4 * sum(part.size for part in parts)
        ),
        cost_estimate=pl.CostEstimate(flops=1 << 20, bytes_accessed=1 << 10, transcendentals=0),
        name="attend_last" if count_out else "attend",
    )(info, in_hbm(ids), in_hbm(id_rows), *operands)


def total_of(*parts):
    return sum(part.astype(F32) for part in parts).astype(BF16)


def body(mesh_shape, tokens, norm_gain, w_qkv, head_scale, w_out, scale_ids):
    ring, seqs = mesh_shape["head"], mesh_shape["seq"]
    outer = seqs // 2
    rows, width = tokens.shape
    half = rows // 2
    head_size = w_qkv.shape[2] // head_scale.shape[0]
    head_at, seq_at = lax.axis_index("head"), lax.axis_index("seq")
    place = ring_place(head_at, ring)
    chip, core = seq_at // 2, seq_at % 2
    index_at = lambda offset: ring_index((place + offset + ring) % ring, ring)
    numbers = lambda values: jnp.stack(values).astype(jnp.int32)
    at = [index_at(offset) for offset in range(ring)]

    streams = (0, 1)
    lanes = ((0, 0, 1), (1, 1, -1), (0, 1, -1), (1, 0, 1))
    farthest = ring // 2
    reach = [(farthest, farthest - 1), (farthest - 1, farthest)]

    order = [0] + [sign * step % ring for step in range(1, farthest) for sign in (-1, 1)] + [farthest]
    held = [[tokens[s * half : (s + 1) * half]] * 2 for s in streams]
    blocks, targets = [], []
    for step in range(1, farthest + 1):
        for s, way, sign in lanes:
            if step <= reach[s][way]:
                held[s][way] = along(held[s][way], sign, ring)
        if step == 1:
            held[0][0], (weights, wide) = lax.optimization_barrier(
                (held[0][0], loaded(order, numbers(at), w_qkv, tokens))
            )
        elif step == 2:
            wide = placed(targets, blocks, wide)
            blocks, targets = [], []
        elif step == 3:
            held[1][1], wide = lax.optimization_barrier(
                (held[1][1], placed(targets, blocks, wide))
            )
            blocks, targets = [], []
        if step < farthest:
            for s, way, sign in lanes:
                blocks.append(held[s][way])
                targets.append((s * half, (2 * step - 1 + way) * width))
    wide = placed(targets, blocks, wide)
    lasts = [held[0][0], held[1][1]]
    gain = norm_gain.reshape(-1, 128)
    state = project_begin(gain, wide, weights, order)
    query, *parts = project_finish(head_scale, gain, state, weights, lasts, 3, order, head_size)
    halves, pieces = parts[:2], parts[2:]

    far, straight, crossed = [], [], []
    for step in range(outer):
        source = 2 * ((chip + outer - step) % outer)
        straight.append((source + core) * rows)
        crossed.append((source + 1 - core) * rows)
        if step:
            shift = [(2 * a + b, 2 * ((a + step) % outer) + b) for a in range(outer) for b in (0, 1)]
            far.append([lax.ppermute(part, "seq", shift) for part in halves])
    first = [seq_at * rows]
    (acc,) = attend(numbers(straight[:1] + first), scale_ids, query, [halves], head_size)
    near = [[swapped(piece, seqs) for piece in pieces]]
    acc, near = lax.optimization_barrier((acc, near))
    (acc,) = attend(numbers(crossed[:1] + first), scale_ids, query, near, head_size, acc)
    acc, far = lax.optimization_barrier((acc, far))
    far_crossed = [[swapped(part, seqs) for part in block] for block in far]
    (acc,) = attend(numbers(straight[1:] + first), scale_ids, query, far, head_size, acc)

    goals = [[*range(up, 0, -1), *range(-down, 0), 0] for up, down in reach]
    info = numbers(crossed[1:] + first + [at[goal % ring] for goal in goals[0] + goals[1]])
    parts = attend(
        info, scale_ids, query, far_crossed, head_size, acc, w_out, len(streams)
    )
    parts = [dict(zip(goals[s], parts[s * ring : (s + 1) * ring])) for s in streams]
    sums = [[None, None] for s in streams]
    for step in range(farthest, 0, -1):
        for s, way, sign in lanes:
            if step <= reach[s][way]:
                part = parts[s][sign * step]
                if sums[s][way] is not None:
                    part = total_of(part, sums[s][way])
                sums[s][way] = along(part, sign, ring)
    ends = lax.optimization_barrier([sums[s][way] for s, way, sign in lanes[::-1]])
    for (s, way, sign), end in zip(lanes[::-1], ends):
        sums[s][way] = end
    return jnp.concatenate([total_of(parts[s][0], *sums[s]) for s in streams])


def solution(mesh):
    placed = (P("seq", "head"), P(), P(None, None, "head"), P("head"), P("head", None), P())
    return jax.shard_map(
        functools.partial(body, dict(mesh.shape)),
        mesh=mesh,
        in_specs=placed,
        out_specs=P("seq", "head"),
        check_vma=False,
    )
```

```python
import functools
import math

import jax
import jax.numpy as jnp
from jax import lax
from jax.experimental import pallas as pl
from jax.experimental.pallas import tpu as pltpu
from jax.sharding import PartitionSpec as P

LOG2E = math.log2(math.e)
VMEM = pl.BlockSpec(memory_space=pltpu.VMEM)
SMEM = pl.BlockSpec(memory_space=pltpu.SMEM)
F32 = jnp.float32
BF16 = jnp.bfloat16


def ring_order(count):
    line = count // 2
    return [2 * z for z in range(line)] + [2 * z + 1 for z in reversed(range(line))]


def ring_place(index, count):
    return jnp.where(index % 2 == 0, index // 2, count - 1 - index // 2)


def ring_index(place, count):
    return jnp.where(place < count // 2, 2 * place, 2 * (count - 1 - place) + 1)


def along(value, step, count):
    order = ring_order(count)
    return lax.ppermute(
        value, "head", [(order[p], order[(p + step) % count]) for p in range(count)]
    )


def swapped(value, seq_count):
    return lax.ppermute(value, "seq", [(seq, seq + 1 - 2 * (seq % 2)) for seq in range(seq_count)])


def in_hbm(value):
    return pltpu.with_memory_space_constraint(value, pltpu.HBM)


def in_vmem(value):
    return pltpu.with_memory_space_constraint(value, pltpu.VMEM)


def load_kernel(order, groups, at, w_hbm, *refs):
    size = w_hbm.shape[1] // len(order)
    sems, copies, out_ref = refs[-1], [], refs[len(refs) // 2 - 1]
    if len(refs) > 2:
        tokens, wide = refs[0], refs[2]
        place = wide.at[:, : tokens.shape[1]]
        copies.append(pltpu.make_async_copy(tokens, place, sems.at[len(order)]))
    for n in range(len(order)):
        start = pl.multiple_of(at[order[n]] * size, size)
        copies.append(
            pltpu.make_async_copy(
                w_hbm.at[groups[0] : groups[-1] + 1, pl.ds(start, size), :],
                out_ref.at[:, n * size : (n + 1) * size, :],
                sems.at[n],
            )
        )
    for copy in copies:
        copy.start()
    for copy in copies:
        copy.wait()


def loaded(order, groups, at, weights, tokens=None):
    hbm, spot = pl.BlockSpec(memory_space=pltpu.HBM), pl.BlockSpec(memory_space=pl.ANY)
    depth, width = weights.shape[1:]
    operands = [at, in_hbm(weights)]
    shapes = [pltpu.VMEM((len(groups), depth, width), BF16)]
    if tokens is not None:
        operands.append(in_hbm(tokens))
        shapes.append(pltpu.VMEM((tokens.shape[0], depth), BF16))
    size = len(groups) * depth * width
    return pl.pallas_call(
        functools.partial(load_kernel, order, groups),
        out_shape=tuple(shapes),
        in_specs=[SMEM] + [hbm] * (len(operands) - 1),
        out_specs=(spot,) * len(shapes),
        scratch_shapes=[pltpu.SemaphoreType.DMA((len(order) + 1,))],
        compiler_params=pltpu.CompilerParams(vmem_limit_bytes=1 << 20),
        cost_estimate=pl.CostEstimate(flops=size, bytes_accessed=4 * size, transcendentals=0),
        name="load",
    )(*operands)


def gain_of(gain_ref, offset, ring, part, parts):
    place = ring_place(lax.axis_index("head"), ring)
    index = ring_index((place + offset) % ring, ring)
    return gain_ref[pl.ds(index * parts + part, 1), :]


def place_kernel(targets, *refs):
    blocks, wide, sems = refs[: len(targets)], refs[-2], refs[-1]
    copies = []
    for n, (block, (row, lane)) in enumerate(zip(blocks, targets)):
        rows, width = block.shape
        here = wide.at[row : row + rows, lane : lane + width]
        copies.append(pltpu.make_async_copy(block, here, sems.at[n]))
    for copy in copies:
        copy.start()
    for copy in copies:
        copy.wait()


def placed(targets, blocks, wide):
    operands = [*map(in_vmem, blocks), in_vmem(wide)]
    return pl.pallas_call(
        functools.partial(place_kernel, targets),
        out_shape=pltpu.VMEM(wide.shape, BF16),
        in_specs=[pl.BlockSpec(memory_space=pl.ANY)] * len(operands),
        out_specs=pl.BlockSpec(memory_space=pl.ANY),
        scratch_shapes=[pltpu.SemaphoreType.DMA((len(targets),))],
        input_output_aliases={len(blocks): 0},
        compiler_params=pltpu.CompilerParams(vmem_limit_bytes=1 << 20),
        cost_estimate=pl.CostEstimate(flops=0, bytes_accessed=1 << 20, transcendentals=0),
        name="place",
    )(*operands)


def begin_kernel(order, gain_ref, wide, wq_ref, wkv_ref, state, scaled):
    rows, depth = wide.shape
    ring = len(order)
    out_width, parts = wq_ref.shape[2], depth // ring // 128
    weights = [wq_ref.at[0], wkv_ref.at[0], wkv_ref.at[1]]
    tile, done = scaled.shape
    for first in range(0, rows, tile):
        here = slice(first, first + tile)
        power = None
        for lane in range(0, done, 128):
            n, part = lane // 128 // parts, lane // 128 % parts
            values = wide[here, lane : lane + 128].astype(F32)
            power = values * values if power is None else power + values * values
            row = gain_of(gain_ref, order[n], ring, part, parts)
            scaled[:, lane : lane + 128] = (values * row).astype(BF16)
        state[here, 3 * out_width :] = power
        for group in range(3):
            state[here, group * out_width : (group + 1) * out_width] = jnp.dot(
                scaled[...], weights[group][:done, :], preferred_element_type=F32
            )


def finish_kernel(head_size, order, factor, gain_ref, state, wq_ref, wkv_ref, *refs):
    count = 2
    lasts, q_ref = refs[:count], refs[count]
    halves, pieces = refs[count + 1 : 2 * count + 1], refs[2 * count + 1 :]
    rows, width = lasts[0].shape
    depth, out_width = wq_ref.shape[1:]
    weights = [wq_ref.at[0], wkv_ref.at[0], wkv_ref.at[1]]
    for stream, last in enumerate(lasts):
        here = slice(stream * rows, (stream + 1) * rows)
        kv_ref = halves[stream]
        power = state[here, 3 * out_width :]
        scaled = []
        for part in range(width // 128):
            values = last[:, part * 128 : (part + 1) * 128].astype(F32)
            power += values * values
            row = gain_of(gain_ref, order[-1], len(order), part, width // 128)
            scaled.append((values * row).astype(BF16))
        scaled = jnp.concatenate(scaled, axis=1)
        q, k, v = (
            state[here, group * out_width : (group + 1) * out_width]
            + jnp.dot(scaled, weights[group][depth - width :, :], preferred_element_type=F32)
            for group in range(3)
        )
        scale = lax.rsqrt(jnp.sum(power, axis=-1, keepdims=True) * (1.0 / depth) + 1e-06)
        q, k, v = q * scale, k * scale, v * scale
        for head in range(out_width // head_size):
            lanes = slice(head * head_size, (head + 1) * head_size)
            qh, kh = q[:, lanes], k[:, lanes]
            q_size = lax.rsqrt(jnp.sum(qh * qh, axis=-1, keepdims=True) + 1e-06)
            k_size = lax.rsqrt(jnp.sum(kh * kh, axis=-1, keepdims=True) + 1e-06)
            q_ref[here, lanes] = (qh * (q_size * (factor[head] * LOG2E))).astype(BF16)
            kv_ref[:, lanes] = (kh * k_size).astype(BF16)
        kv_ref[:, out_width:] = v.astype(BF16)
    start = 0
    for piece in pieces:
        end = start + piece.shape[0]
        for stream, half in enumerate(halves):
            base = stream * rows
            low, high = max(start, base), min(end, base + rows)
            if low < high:
                piece[low - start : high - start, :] = half[low - base : high - base, :]
        start = end


def project_begin(gain, wide, w_q, w_kv, order):
    rows, depth = wide.shape
    done = depth - depth // len(order)
    groups, out_width = 3, w_q.shape[2]
    return pl.pallas_call(
        functools.partial(begin_kernel, order),
        out_shape=pltpu.VMEM((rows, groups * out_width + 128), F32),
        in_specs=[VMEM] * 4,
        out_specs=VMEM,
        scratch_shapes=[pltpu.VMEM((math.gcd(rows, 256), done), BF16)],
        compiler_params=pltpu.CompilerParams(vmem_limit_bytes=16 << 20),
        cost_estimate=pl.CostEstimate(
            flops=2 * rows * depth * groups * out_width,
            bytes_accessed=2 * depth * (rows + groups * out_width),
            transcendentals=0,
        ),
        name="project_begin",
    )(in_hbm(gain), in_vmem(wide), in_vmem(w_q), in_vmem(w_kv))


def project_finish(factor, gain, state, w_q, w_kv, lasts, count_pieces, order, head_size):
    rows, width = lasts[0].shape
    out_width = w_q.shape[2]
    total = rows * len(lasts)
    units = total // 16
    sizes = [rows] * len(lasts)
    sizes += [16 * ((units + n) // count_pieces) for n in range(count_pieces)]
    return pl.pallas_call(
        functools.partial(finish_kernel, head_size, order),
        out_shape=(
            pltpu.VMEM((total, out_width), BF16),
            *[pltpu.VMEM((size, 2 * out_width), BF16) for size in sizes],
        ),
        in_specs=[SMEM] + [VMEM] * (4 + len(lasts)),
        out_specs=(VMEM,) * (1 + len(sizes)),
        compiler_params=pltpu.CompilerParams(vmem_limit_bytes=16 << 20),
        cost_estimate=pl.CostEstimate(
            flops=6 * total * width * out_width, bytes_accessed=8 * total * out_width, transcendentals=0
        ),
        name="project_finish",
    )(in_hbm(factor), in_hbm(gain), *map(in_vmem, (state, w_q, w_kv)), *map(in_vmem, lasts))


def attend_kernel(
    head_size, counts, has_acc, goals, info, ids, id_row, q_ref, *refs
):
    count_blocks, count_parts = counts
    count_streams = len(goals)
    count_out = sum(map(len, goals))
    kv_refs, rest = refs[: count_blocks * count_parts], refs[count_blocks * count_parts :]
    if has_acc:
        acc_in, rest = rest[0], rest[1:]
    if count_out:
        w_hbm, outs, (k_all, v_ones, acc, attended, w_ref, sem) = rest[0], rest[1:-6], rest[-6:]
        fetch_w = pltpu.make_async_copy(w_hbm, w_ref, sem)
        fetch_w.start()
    else:
        acc_out, k_all, v_ones, acc = rest
    acc[...] = acc_in[...] if has_acc else jnp.zeros_like(acc)
    rows, width = q_ref.shape
    heads = width // head_size
    keys = k_all.shape[0]
    tile = id_row.shape[2]
    q_first = info[count_blocks]
    v_ones[:, :, head_size:] = jnp.ones((heads, keys, head_size), BF16)
    for number in range(count_blocks):
        begin = 0
        for kv_ref in kv_refs[number * count_parts : (number + 1) * count_parts]:
            here = slice(begin, begin + kv_ref.shape[0])
            begin += kv_ref.shape[0]
            k_all[here, :] = kv_ref[:, :width]
            for head in range(heads):
                start = width + head * head_size
                v_ones[head, here, :head_size] = kv_ref[:, start : start + head_size]
        first = info[number]
        key_low, key_high = ids[first], ids[first + keys - 1]

        @pl.loop(0, rows // tile)
        def _(index):
            base = pl.multiple_of(index * tile, tile)
            here = pl.ds(base, tile)
            q_low, q_high = ids[q_first + base], ids[q_first + base + tile - 1]

            def add(masked):
                if masked:
                    own = jnp.broadcast_to(id_row[q_first // tile + index], (8, tile))
                    own = jnp.transpose(own)[:, :1]
                    allowed = [id_row[first // tile + n] <= own for n in range(keys // tile)]
                for head in range(heads):
                    lanes = slice(head * head_size, (head + 1) * head_size)
                    spread = slice(2 * head * head_size, 2 * (head + 1) * head_size)
                    total = acc[here, spread]
                    for low in range(0, keys, tile):
                        score = lax.dot_general(
                            q_ref[here, lanes],
                            k_all[low : low + tile, lanes],
                            (((1,), (1,)), ((), ())),
                            preferred_element_type=F32,
                        )
                        weight = jnp.exp2(score)
                        if masked:
                            weight = jnp.where(allowed[low // tile], weight, 0.0)
                        total += jnp.dot(
                            weight.astype(BF16),
                            v_ones[head, low : low + tile, :],
                            preferred_element_type=F32,
                        )
                    acc[here, spread] = total

            @pl.when(key_high <= q_low)
            def _():
                add(False)

            @pl.when((key_high > q_low) & (key_low <= q_high))
            def _():
                add(True)

    if not count_out:
        acc_out[...] = acc[...]
        return
    for head in range(heads):
        start = 2 * head * head_size
        attended[:, head * head_size : (head + 1) * head_size] = (
            acc[:, start : start + head_size]
            / acc[:, start + head_size : start + 2 * head_size]
        ).astype(BF16)
    out_rows, out_width = outs[0].shape
    fetch_w.wait()
    per = count_out // count_streams
    for offset in range(per):
        picks = [own.index(offset) for own in goals]
        lane = info[count_blocks + 1 + picks[0]] * out_width
        product = jnp.dot(
            attended[...],
            w_ref[:, pl.ds(pl.multiple_of(lane, out_width), out_width)],
            preferred_element_type=F32,
        )
        for stream, pick in enumerate(picks):
            rows_of = slice(stream * out_rows, (stream + 1) * out_rows)
            outs[stream * per + pick][...] = product[rows_of, :].astype(BF16)


def attend(info, ids, query, blocks, head_size, acc=None, w_out=None, goals=()):
    total, width = query.shape
    parts = [part for block in blocks for part in block]
    keys = sum(part.shape[0] for part in blocks[0])
    heads = width // head_size
    streams, count_out = len(goals), sum(map(len, goals))
    scratch = [
        pltpu.VMEM((keys, width), BF16),
        pltpu.VMEM((heads, keys, 2 * head_size), BF16),
        pltpu.VMEM((total, 2 * width), F32),
    ]
    id_rows = ids.reshape(-1, 1, math.gcd(total, 256))
    operands = [in_vmem(query), *map(in_vmem, parts)]
    if acc is not None:
        operands.append(in_vmem(acc))
    if count_out:
        operands.append(in_hbm(w_out))
        scratch += [
            pltpu.VMEM((total, width), BF16),
            pltpu.VMEM(w_out.shape, BF16),
            pltpu.SemaphoreType.DMA(()),
        ]
        shape = pltpu.VMEM((total // streams, w_out.shape[1] * streams // count_out), BF16)
    else:
        shape = pltpu.VMEM((total, 2 * width), F32)
    outs = count_out or 1
    in_specs = [SMEM, SMEM, VMEM] + [VMEM] * len(operands)
    if count_out:
        in_specs[-1] = pl.BlockSpec(memory_space=pltpu.HBM)
    return pl.pallas_call(
        functools.partial(
            attend_kernel, head_size, (len(blocks), len(blocks[0])), acc is not None, goals
        ),
        out_shape=(shape,) * outs,
        in_specs=in_specs,
        out_specs=(VMEM,) * outs,
        scratch_shapes=scratch,
        compiler_params=pltpu.CompilerParams(
            vmem_limit_bytes=(16 << 20) + 4 * sum(part.size for part in parts)
        ),
        cost_estimate=pl.CostEstimate(flops=1 << 20, bytes_accessed=1 << 10, transcendentals=0),
        name="attend_last" if count_out else "attend",
    )(info, in_hbm(ids), in_hbm(id_rows), *operands)


def total_of(*parts):
    return sum(part.astype(F32) for part in parts).astype(BF16)


def body(mesh_shape, tokens, norm_gain, w_qkv, head_scale, w_out, scale_ids):
    ring, seqs = mesh_shape["head"], mesh_shape["seq"]
    outer = seqs // 2
    rows, width = tokens.shape
    half = rows // 2
    head_size = w_qkv.shape[2] // head_scale.shape[0]
    head_at, seq_at = lax.axis_index("head"), lax.axis_index("seq")
    place = ring_place(head_at, ring)
    chip, core = seq_at // 2, seq_at % 2
    index_at = lambda offset: ring_index((place + offset + ring) % ring, ring)
    numbers = lambda values: jnp.stack(values).astype(jnp.int32)
    at = [index_at(offset) for offset in range(ring)]

    streams = (0, 1)
    lanes = ((0, 0, 1), (1, 1, -1), (0, 1, -1), (1, 0, 1))
    farthest = ring // 2
    reach = [(farthest, farthest - 1), (farthest - 1, farthest)]

    order = [0] + [sign * step % ring for step in range(1, farthest) for sign in (-1, 1)] + [farthest]
    held = [[tokens[s * half : (s + 1) * half]] * 2 for s in streams]
    blocks, targets = [], []
    for step in range(1, farthest + 1):
        for s, way, sign in lanes:
            if step <= reach[s][way]:
                held[s][way] = along(held[s][way], sign, ring)
        if step == 1:
            held[0][0], (w_q, wide) = lax.optimization_barrier(
                (held[0][0], loaded(order, (0,), numbers(at), w_qkv, tokens))
            )
        elif step == 2:
            held[1][1], (w_kv,) = lax.optimization_barrier(
                (held[1][1], loaded(order, (1, 2), numbers(at), w_qkv))
            )
            wide = placed(targets, blocks, wide)
            blocks, targets = [], []
        elif step == 3:
            held[1][1], wide = lax.optimization_barrier(
                (held[1][1], placed(targets, blocks, wide))
            )
            blocks, targets = [], []
        if step < farthest:
            for s, way, sign in lanes:
                blocks.append(held[s][way])
                targets.append((s * half, (2 * step - 1 + way) * width))
    wide = placed(targets, blocks, wide)
    lasts = [held[0][0], held[1][1]]
    gain = norm_gain.reshape(-1, 128)
    state = project_begin(gain, wide, w_q, w_kv, order)
    query, *parts = project_finish(head_scale, gain, state, w_q, w_kv, lasts, 3, order, head_size)
    halves, pieces = parts[:2], parts[2:]

    far, straight, crossed = [], [], []
    for step in range(outer):
        source = 2 * ((chip + outer - step) % outer)
        straight.append((source + core) * rows)
        crossed.append((source + 1 - core) * rows)
        if step:
            shift = [(2 * a + b, 2 * ((a + step) % outer) + b) for a in range(outer) for b in (0, 1)]
            far.append([lax.ppermute(part, "seq", shift) for part in halves])
    first = [seq_at * rows]
    (acc,) = attend(numbers(straight[:1] + first), scale_ids, query, [halves], head_size)
    near = [[swapped(piece, seqs) for piece in pieces]]
    acc, near = lax.optimization_barrier((acc, near))
    (acc,) = attend(numbers(crossed[:1] + first), scale_ids, query, near, head_size, acc)
    acc, far = lax.optimization_barrier((acc, far))
    far_crossed = [[swapped(part, seqs) for part in block] for block in far]
    (acc,) = attend(numbers(straight[1:] + first), scale_ids, query, far, head_size, acc)

    goals = [[*range(up, 0, -1), *range(-down, 0), 0] for up, down in reach]
    info = numbers(crossed[1:] + first + [at[goal % ring] for goal in goals[0] + goals[1]])
    parts = attend(
        info, scale_ids, query, far_crossed, head_size, acc, w_out,
        [[goal % ring for goal in goals[s]] for s in streams],
    )
    parts = [dict(zip(goals[s], parts[s * ring : (s + 1) * ring])) for s in streams]
    sums = [[None, None] for s in streams]
    for step in range(farthest, 0, -1):
        for s, way, sign in lanes:
            if step <= reach[s][way]:
                part = parts[s][sign * step]
                if sums[s][way] is not None:
                    part = total_of(part, sums[s][way])
                sums[s][way] = along(part, sign, ring)
    ends = lax.optimization_barrier([sums[s][way] for s, way, sign in lanes[::-1]])
    for (s, way, sign), end in zip(lanes[::-1], ends):
        sums[s][way] = end
    return jnp.concatenate([total_of(parts[s][0], *sums[s]) for s in streams])


def solution(mesh):
    placed = (P("seq", "head"), P(), P(None, None, "head"), P("head"), P("head", None), P())
    return jax.shard_map(
        functools.partial(body, dict(mesh.shape)),
        mesh=mesh,
        in_specs=placed,
        out_specs=P("seq", "head"),
        check_vma=False,
    )
```

```python
import functools
import math

import jax
import jax.numpy as jnp
from jax import lax
from jax.experimental import pallas as pl
from jax.experimental.pallas import tpu as pltpu
from jax.sharding import PartitionSpec as P

LOG2E = math.log2(math.e)
VMEM = pl.BlockSpec(memory_space=pltpu.VMEM)
SMEM = pl.BlockSpec(memory_space=pltpu.SMEM)
F32 = jnp.float32
BF16 = jnp.bfloat16


def ring_order(count):
    line = count // 2
    return [2 * z for z in range(line)] + [2 * z + 1 for z in reversed(range(line))]


def ring_place(index, count):
    return jnp.where(index % 2 == 0, index // 2, count - 1 - index // 2)


def ring_index(place, count):
    return jnp.where(place < count // 2, 2 * place, 2 * (count - 1 - place) + 1)


def along(value, step, count):
    order = ring_order(count)
    return lax.ppermute(
        value, "head", [(order[p], order[(p + step) % count]) for p in range(count)]
    )


def swapped(value, seq_count):
    return lax.ppermute(value, "seq", [(seq, seq + 1 - 2 * (seq % 2)) for seq in range(seq_count)])


def in_hbm(value):
    return pltpu.with_memory_space_constraint(value, pltpu.HBM)


def in_vmem(value):
    return pltpu.with_memory_space_constraint(value, pltpu.VMEM)


def fold_kernel(order, at, gain_hbm, w_hbm, tokens, out_ref, wide, gain_ref, sems):
    lanes = gain_ref.shape[1]
    size = w_hbm.shape[1] // len(order)
    per = size // lanes

    def fetch(n):
        start = pl.multiple_of(at[order[n]] * size, size)
        return pltpu.make_async_copy(
            w_hbm.at[:, pl.ds(start, size), :],
            out_ref.at[:, n * size : (n + 1) * size, :],
            sems.at[n],
        )

    gains = pltpu.make_async_copy(gain_hbm, gain_ref, sems.at[len(order) + 1])
    gains.start()
    for n in range(len(order)):
        fetch(n).start()
    own = pltpu.make_async_copy(tokens, wide.at[:, : tokens.shape[1]], sems.at[len(order)])
    own.start()
    gains.wait()
    for n in range(len(order)):
        columns = jnp.transpose(gain_ref[pl.ds(at[order[n]] * per, per), :])
        fetch(n).wait()
        for piece in range(per):
            first = n * size + piece * lanes
            for group in range(w_hbm.shape[0]):
                here = (group, slice(first, first + lanes), slice(None))
                scaled = out_ref[here].astype(F32) * columns[:, piece : piece + 1]
                out_ref[here] = scaled.astype(BF16)
    own.wait()


def fold_gain(order, at, gain, weights, tokens):
    depth = weights.shape[1]
    lanes = math.gcd(depth // len(order), 128)
    hbm = pl.BlockSpec(memory_space=pltpu.HBM)
    return pl.pallas_call(
        functools.partial(fold_kernel, order),
        out_shape=(pltpu.VMEM(weights.shape, BF16), pltpu.VMEM((tokens.shape[0], depth), BF16)),
        in_specs=[SMEM, hbm, hbm, hbm],
        out_specs=(VMEM, pl.BlockSpec(memory_space=pl.ANY)),
        scratch_shapes=[
            pltpu.VMEM((depth // lanes, lanes), F32),
            pltpu.SemaphoreType.DMA((len(order) + 2,)),
        ],
        compiler_params=pltpu.CompilerParams(vmem_limit_bytes=16 << 20),
        cost_estimate=pl.CostEstimate(
            flops=weights.size, bytes_accessed=4 * weights.size, transcendentals=0
        ),
        name="fold_gain",
    )(at, in_hbm(gain.reshape(depth // lanes, lanes)), in_hbm(weights), in_hbm(tokens))


def place_kernel(targets, *refs):
    blocks, wide, sems = refs[: len(targets)], refs[-2], refs[-1]
    copies = []
    for n, (block, (row, lane)) in enumerate(zip(blocks, targets)):
        rows, width = block.shape
        here = wide.at[row : row + rows, lane : lane + width]
        copies.append(pltpu.make_async_copy(block, here, sems.at[n]))
    for copy in copies:
        copy.start()
    for copy in copies:
        copy.wait()


def placed(targets, blocks, wide):
    operands = [*map(in_vmem, blocks), in_vmem(wide)]
    return pl.pallas_call(
        functools.partial(place_kernel, targets),
        out_shape=pltpu.VMEM(wide.shape, BF16),
        in_specs=[pl.BlockSpec(memory_space=pl.ANY)] * len(operands),
        out_specs=pl.BlockSpec(memory_space=pl.ANY),
        scratch_shapes=[pltpu.SemaphoreType.DMA((len(targets),))],
        input_output_aliases={len(blocks): 0},
        compiler_params=pltpu.CompilerParams(vmem_limit_bytes=1 << 20),
        cost_estimate=pl.CostEstimate(flops=0, bytes_accessed=1 << 20, transcendentals=0),
        name="place",
    )(*operands)


def begin_kernel(blocks, wide, w_ref, state):
    rows, depth = wide.shape
    out_width = w_ref.shape[2]
    done = depth - depth // blocks
    tile = math.gcd(rows, 256)
    for first in range(0, rows, tile):
        here = slice(first, first + tile)
        for group in range(3):
            state[here, group * out_width : (group + 1) * out_width] = jnp.dot(
                wide[here, :done], w_ref[group, :done, :], preferred_element_type=F32
            )
        power = None
        for lane in range(0, done, 128):
            values = wide[here, lane : lane + 128].astype(F32)
            power = values * values if power is None else power + values * values
        state[here, 3 * out_width :] = power


def finish_kernel(head_size, factor, state, w_ref, *refs):
    count = 2
    lasts, q_ref = refs[:count], refs[count]
    halves, pieces = refs[count + 1 : 2 * count + 1], refs[2 * count + 1 :]
    rows, width = lasts[0].shape
    depth, out_width = w_ref.shape[1:]
    for stream, last in enumerate(lasts):
        here = slice(stream * rows, (stream + 1) * rows)
        kv_ref = halves[stream]
        q, k, v = (
            state[here, group * out_width : (group + 1) * out_width]
            + jnp.dot(last[...], w_ref[group, depth - width :, :], preferred_element_type=F32)
            for group in range(3)
        )
        power = state[here, 3 * out_width :]
        for lane in range(0, width, 128):
            values = last[:, lane : lane + 128].astype(F32)
            power += values * values
        scale = lax.rsqrt(jnp.sum(power, axis=-1, keepdims=True) * (1.0 / depth) + 1e-06)
        q, k, v = q * scale, k * scale, v * scale
        for head in range(out_width // head_size):
            lanes = slice(head * head_size, (head + 1) * head_size)
            qh, kh = q[:, lanes], k[:, lanes]
            q_size = lax.rsqrt(jnp.sum(qh * qh, axis=-1, keepdims=True) + 1e-06)
            k_size = lax.rsqrt(jnp.sum(kh * kh, axis=-1, keepdims=True) + 1e-06)
            q_ref[here, lanes] = (qh * (q_size * (factor[head] * LOG2E))).astype(BF16)
            kv_ref[:, lanes] = (kh * k_size).astype(BF16)
        kv_ref[:, out_width:] = v.astype(BF16)
    start = 0
    for piece in pieces:
        end = start + piece.shape[0]
        for stream, half in enumerate(halves):
            base = stream * rows
            low, high = max(start, base), min(end, base + rows)
            if low < high:
                piece[low - start : high - start, :] = half[low - base : high - base, :]
        start = end


def project_begin(wide, weights, blocks):
    rows, depth = wide.shape
    groups, _, out_width = weights.shape
    return pl.pallas_call(
        functools.partial(begin_kernel, blocks),
        out_shape=pltpu.VMEM((rows, groups * out_width + 128), F32),
        in_specs=[VMEM] * 2,
        out_specs=VMEM,
        compiler_params=pltpu.CompilerParams(vmem_limit_bytes=16 << 20),
        cost_estimate=pl.CostEstimate(
            flops=2 * rows * depth * groups * out_width,
            bytes_accessed=2 * depth * (rows + groups * out_width),
            transcendentals=0,
        ),
        name="project_begin",
    )(in_vmem(wide), in_vmem(weights))


def project_finish(factor, state, weights, lasts, count_pieces, head_size):
    rows, width = lasts[0].shape
    out_width = weights.shape[2]
    total = rows * len(lasts)
    units = total // 16
    sizes = [rows] * len(lasts)
    sizes += [16 * ((units + n) // count_pieces) for n in range(count_pieces)]
    return pl.pallas_call(
        functools.partial(finish_kernel, head_size),
        out_shape=(
            pltpu.VMEM((total, out_width), BF16),
            *[pltpu.VMEM((size, 2 * out_width), BF16) for size in sizes],
        ),
        in_specs=[SMEM] + [VMEM] * (2 + len(lasts)),
        out_specs=(VMEM,) * (1 + len(sizes)),
        compiler_params=pltpu.CompilerParams(vmem_limit_bytes=16 << 20),
        cost_estimate=pl.CostEstimate(
            flops=6 * total * width * out_width, bytes_accessed=8 * total * out_width, transcendentals=0
        ),
        name="project_finish",
    )(in_hbm(factor), in_vmem(state), in_vmem(weights), *map(in_vmem, lasts))


def attend_kernel(
    head_size, counts, has_acc, count_out, count_streams, info, ids, id_row, q_ref, *refs
):
    count_blocks, count_parts = counts
    kv_refs, rest = refs[: count_blocks * count_parts], refs[count_blocks * count_parts :]
    if has_acc:
        acc_in, rest = rest[0], rest[1:]
    if count_out:
        w_hbm, outs, (k_all, v_ones, acc, attended, w_ref, sem) = rest[0], rest[1:-6], rest[-6:]
        fetch_w = pltpu.make_async_copy(w_hbm, w_ref, sem)
        fetch_w.start()
    else:
        acc_out, k_all, v_ones, acc = rest
    acc[...] = acc_in[...] if has_acc else jnp.zeros_like(acc)
    rows, width = q_ref.shape
    heads = width // head_size
    keys = k_all.shape[0]
    tile = id_row.shape[2]
    q_first = info[count_blocks]
    v_ones[:, :, head_size:] = jnp.ones((heads, keys, head_size), BF16)
    for number in range(count_blocks):
        begin = 0
        for kv_ref in kv_refs[number * count_parts : (number + 1) * count_parts]:
            here = slice(begin, begin + kv_ref.shape[0])
            begin += kv_ref.shape[0]
            k_all[here, :] = kv_ref[:, :width]
            for head in range(heads):
                start = width + head * head_size
                v_ones[head, here, :head_size] = kv_ref[:, start : start + head_size]
        first = info[number]
        key_low, key_high = ids[first], ids[first + keys - 1]

        @pl.loop(0, rows // tile)
        def _(index):
            base = pl.multiple_of(index * tile, tile)
            here = pl.ds(base, tile)
            q_low, q_high = ids[q_first + base], ids[q_first + base + tile - 1]

            def add(masked):
                if masked:
                    own = jnp.broadcast_to(id_row[q_first // tile + index], (8, tile))
                    own = jnp.transpose(own)[:, :1]
                    allowed = [id_row[first // tile + n] <= own for n in range(keys // tile)]
                for head in range(heads):
                    lanes = slice(head * head_size, (head + 1) * head_size)
                    spread = slice(2 * head * head_size, 2 * (head + 1) * head_size)
                    total = acc[here, spread]
                    for low in range(0, keys, tile):
                        score = lax.dot_general(
                            q_ref[here, lanes],
                            k_all[low : low + tile, lanes],
                            (((1,), (1,)), ((), ())),
                            preferred_element_type=F32,
                        )
                        weight = jnp.exp2(score)
                        if masked:
                            weight = jnp.where(allowed[low // tile], weight, 0.0)
                        total += jnp.dot(
                            weight.astype(BF16),
                            v_ones[head, low : low + tile, :],
                            preferred_element_type=F32,
                        )
                    acc[here, spread] = total

            @pl.when(key_high <= q_low)
            def _():
                add(False)

            @pl.when((key_high > q_low) & (key_low <= q_high))
            def _():
                add(True)

    if not count_out:
        acc_out[...] = acc[...]
        return
    for head in range(heads):
        start = 2 * head * head_size
        attended[:, head * head_size : (head + 1) * head_size] = (
            acc[:, start : start + head_size]
            / acc[:, start + head_size : start + 2 * head_size]
        ).astype(BF16)
    out_rows, out_width = outs[0].shape
    fetch_w.wait()
    for number, out in enumerate(outs):
        lane = info[count_blocks + 1 + number] * out_width
        first = number * count_streams // count_out * out_rows
        out[...] = jnp.dot(
            attended[first : first + out_rows, :],
            w_ref[:, pl.ds(pl.multiple_of(lane, out_width), out_width)],
            preferred_element_type=F32,
        ).astype(BF16)


def attend(info, ids, query, blocks, head_size, acc=None, w_out=None, streams=0):
    total, width = query.shape
    parts = [part for block in blocks for part in block]
    keys = sum(part.shape[0] for part in blocks[0])
    heads = width // head_size
    count_out = streams * w_out.shape[1] // width if streams else 0
    scratch = [
        pltpu.VMEM((keys, width), BF16),
        pltpu.VMEM((heads, keys, 2 * head_size), BF16),
        pltpu.VMEM((total, 2 * width), F32),
    ]
    id_rows = ids.reshape(-1, 1, math.gcd(total, 512))
    operands = [in_vmem(query), *map(in_vmem, parts)]
    if acc is not None:
        operands.append(in_vmem(acc))
    if count_out:
        operands.append(in_hbm(w_out))
        scratch += [
            pltpu.VMEM((total, width), BF16),
            pltpu.VMEM(w_out.shape, BF16),
            pltpu.SemaphoreType.DMA(()),
        ]
        shape = pltpu.VMEM((total // streams, w_out.shape[1] * streams // count_out), BF16)
    else:
        shape = pltpu.VMEM((total, 2 * width), F32)
    outs = count_out or 1
    in_specs = [SMEM, SMEM, VMEM] + [VMEM] * len(operands)
    if count_out:
        in_specs[-1] = pl.BlockSpec(memory_space=pltpu.HBM)
    return pl.pallas_call(
        functools.partial(
            attend_kernel, head_size, (len(blocks), len(blocks[0])), acc is not None, count_out, streams
        ),
        out_shape=(shape,) * outs,
        in_specs=in_specs,
        out_specs=(VMEM,) * outs,
        scratch_shapes=scratch,
        compiler_params=pltpu.CompilerParams(
            vmem_limit_bytes=(16 << 20) + 4 * sum(part.size for part in parts)
        ),
        cost_estimate=pl.CostEstimate(flops=1 << 20, bytes_accessed=1 << 10, transcendentals=0),
        name="attend_last" if count_out else "attend",
    )(info, in_hbm(ids), in_hbm(id_rows), *operands)


def total_of(*parts):
    return sum(part.astype(F32) for part in parts).astype(BF16)


def body(mesh_shape, tokens, norm_gain, w_qkv, head_scale, w_out, scale_ids):
    ring, seqs = mesh_shape["head"], mesh_shape["seq"]
    outer = seqs // 2
    rows, width = tokens.shape
    half = rows // 2
    head_size = w_qkv.shape[2] // head_scale.shape[0]
    head_at, seq_at = lax.axis_index("head"), lax.axis_index("seq")
    place = ring_place(head_at, ring)
    chip, core = seq_at // 2, seq_at % 2
    index_at = lambda offset: ring_index((place + offset + ring) % ring, ring)
    numbers = lambda values: jnp.stack(values).astype(jnp.int32)
    at = [index_at(offset) for offset in range(ring)]

    streams = (0, 1)
    lanes = ((0, 0, 1), (1, 1, -1), (0, 1, -1), (1, 0, 1))
    farthest = ring // 2
    reach = [(farthest, farthest - 1), (farthest - 1, farthest)]

    order = [0] + [sign * step % ring for step in range(1, farthest) for sign in (-1, 1)] + [farthest]
    held = [[tokens[s * half : (s + 1) * half]] * 2 for s in streams]
    blocks, targets = [], []
    for step in range(1, farthest + 1):
        for s, way, sign in lanes:
            if step <= reach[s][way]:
                held[s][way] = along(held[s][way], sign, ring)
        if step == 1:
            held[0][0], (weights, wide) = lax.optimization_barrier(
                (held[0][0], fold_gain(order, numbers(at), norm_gain, w_qkv, tokens))
            )
        elif step == 2:
            wide = placed(targets, blocks, wide)
            blocks, targets = [], []
        elif step == 3:
            held[1][1], wide = lax.optimization_barrier(
                (held[1][1], placed(targets, blocks, wide))
            )
            blocks, targets = [], []
        if step < farthest:
            for s, way, sign in lanes:
                blocks.append(held[s][way])
                targets.append((s * half, (2 * step - 1 + way) * width))
    wide = placed(targets, blocks, wide)
    lasts = [held[0][0], held[1][1]]
    state = project_begin(wide, weights, ring)
    query, *parts = project_finish(head_scale, state, weights, lasts, 3, head_size)
    halves, pieces = parts[:2], parts[2:]

    far, straight, crossed = [], [], []
    for step in range(outer):
        source = 2 * ((chip + outer - step) % outer)
        straight.append((source + core) * rows)
        crossed.append((source + 1 - core) * rows)
        if step:
            shift = [(2 * a + b, 2 * ((a + step) % outer) + b) for a in range(outer) for b in (0, 1)]
            far.append([lax.ppermute(part, "seq", shift) for part in halves])
    first = [seq_at * rows]
    (acc,) = attend(numbers(straight[:1] + first), scale_ids, query, [halves], head_size)
    near = [[swapped(piece, seqs) for piece in pieces]]
    acc, near = lax.optimization_barrier((acc, near))
    (acc,) = attend(numbers(crossed[:1] + first), scale_ids, query, near, head_size, acc)
    acc, far = lax.optimization_barrier((acc, far))
    far_crossed = [[swapped(part, seqs) for part in block] for block in far]
    (acc,) = attend(numbers(straight[1:] + first), scale_ids, query, far, head_size, acc)

    goals = [[*range(up, 0, -1), *range(-down, 0), 0] for up, down in reach]
    info = numbers(crossed[1:] + first + [at[goal % ring] for goal in goals[0] + goals[1]])
    parts = attend(
        info, scale_ids, query, far_crossed, head_size, acc, w_out, len(streams)
    )
    parts = [dict(zip(goals[s], parts[s * ring : (s + 1) * ring])) for s in streams]
    sums = [[None, None] for s in streams]
    for step in range(farthest, 0, -1):
        for s, way, sign in lanes:
            if step <= reach[s][way]:
                part = parts[s][sign * step]
                if sums[s][way] is not None:
                    part = total_of(part, sums[s][way])
                sums[s][way] = along(part, sign, ring)
    ends = lax.optimization_barrier([sums[s][way] for s, way, sign in lanes[::-1]])
    for (s, way, sign), end in zip(lanes[::-1], ends):
        sums[s][way] = end
    return jnp.concatenate([total_of(parts[s][0], *sums[s]) for s in streams])


def solution(mesh):
    placed = (P("seq", "head"), P(), P(None, None, "head"), P("head"), P("head", None), P())
    return jax.shard_map(
        functools.partial(body, dict(mesh.shape)),
        mesh=mesh,
        in_specs=placed,
        out_specs=P("seq", "head"),
        check_vma=False,
    )
```

```python
import functools
import math

import jax
import jax.numpy as jnp
from jax import lax
from jax.experimental import pallas as pl
from jax.experimental.pallas import tpu as pltpu
from jax.sharding import PartitionSpec as P

LOG2E = math.log2(math.e)
VMEM = pl.BlockSpec(memory_space=pltpu.VMEM)
SMEM = pl.BlockSpec(memory_space=pltpu.SMEM)
F32 = jnp.float32
BF16 = jnp.bfloat16


def ring_order(count):
    line = count // 2
    return [2 * z for z in range(line)] + [2 * z + 1 for z in reversed(range(line))]


def ring_place(index, count):
    return jnp.where(index % 2 == 0, index // 2, count - 1 - index // 2)


def ring_index(place, count):
    return jnp.where(place < count // 2, 2 * place, 2 * (count - 1 - place) + 1)


def along(value, step, count):
    order = ring_order(count)
    return lax.ppermute(
        value, "head", [(order[p], order[(p + step) % count]) for p in range(count)]
    )


def swapped(value, seq_count):
    return lax.ppermute(value, "seq", [(seq, seq + 1 - 2 * (seq % 2)) for seq in range(seq_count)])


def in_hbm(value):
    return pltpu.with_memory_space_constraint(value, pltpu.HBM)


def in_vmem(value):
    return pltpu.with_memory_space_constraint(value, pltpu.VMEM)


def fold_kernel(order, at, gain_hbm, w_hbm, tokens, out_ref, wide, gain_ref, sems):
    lanes = gain_ref.shape[1]
    size = w_hbm.shape[1] // len(order)
    per = size // lanes

    def fetch(n):
        start = pl.multiple_of(at[order[n]] * size, size)
        return pltpu.make_async_copy(
            w_hbm.at[:, pl.ds(start, size), :],
            out_ref.at[:, n * size : (n + 1) * size, :],
            sems.at[n],
        )

    gains = pltpu.make_async_copy(gain_hbm, gain_ref, sems.at[len(order) + 1])
    gains.start()
    for n in range(len(order)):
        fetch(n).start()
    own = pltpu.make_async_copy(tokens, wide.at[:, : tokens.shape[1]], sems.at[len(order)])
    own.start()
    gains.wait()
    for n in range(len(order)):
        columns = jnp.transpose(gain_ref[pl.ds(at[order[n]] * per, per), :])
        fetch(n).wait()
        for piece in range(per):
            first = n * size + piece * lanes
            for group in range(w_hbm.shape[0]):
                here = (group, slice(first, first + lanes), slice(None))
                scaled = out_ref[here].astype(F32) * columns[:, piece : piece + 1]
                out_ref[here] = scaled.astype(BF16)
    own.wait()


def fold_gain(order, at, gain, weights, tokens):
    depth = weights.shape[1]
    lanes = math.gcd(depth // len(order), 128)
    hbm = pl.BlockSpec(memory_space=pltpu.HBM)
    return pl.pallas_call(
        functools.partial(fold_kernel, order),
        out_shape=(pltpu.VMEM(weights.shape, BF16), pltpu.VMEM((tokens.shape[0], depth), BF16)),
        in_specs=[SMEM, hbm, hbm, hbm],
        out_specs=(VMEM, pl.BlockSpec(memory_space=pl.ANY)),
        scratch_shapes=[
            pltpu.VMEM((depth // lanes, lanes), F32),
            pltpu.SemaphoreType.DMA((len(order) + 2,)),
        ],
        compiler_params=pltpu.CompilerParams(vmem_limit_bytes=16 << 20),
        cost_estimate=pl.CostEstimate(
            flops=weights.size, bytes_accessed=4 * weights.size, transcendentals=0
        ),
        name="fold_gain",
    )(at, in_hbm(gain.reshape(depth // lanes, lanes)), in_hbm(weights), in_hbm(tokens))


def place_kernel(targets, *refs):
    blocks, wide, sems = refs[: len(targets)], refs[-2], refs[-1]
    copies = []
    for n, (block, (row, lane)) in enumerate(zip(blocks, targets)):
        rows, width = block.shape
        here = wide.at[row : row + rows, lane : lane + width]
        copies.append(pltpu.make_async_copy(block, here, sems.at[n]))
    for copy in copies:
        copy.start()
    for copy in copies:
        copy.wait()


def placed(targets, blocks, wide):
    operands = [*map(in_vmem, blocks), in_vmem(wide)]
    return pl.pallas_call(
        functools.partial(place_kernel, targets),
        out_shape=pltpu.VMEM(wide.shape, BF16),
        in_specs=[pl.BlockSpec(memory_space=pl.ANY)] * len(operands),
        out_specs=pl.BlockSpec(memory_space=pl.ANY),
        scratch_shapes=[pltpu.SemaphoreType.DMA((len(targets),))],
        input_output_aliases={len(blocks): 0},
        compiler_params=pltpu.CompilerParams(vmem_limit_bytes=1 << 20),
        cost_estimate=pl.CostEstimate(flops=0, bytes_accessed=1 << 20, transcendentals=0),
        name="place",
    )(*operands)


def begin_kernel(blocks, wide, w_ref, state):
    rows, depth = wide.shape
    out_width = w_ref.shape[2]
    done = depth - depth // blocks
    tile = math.gcd(rows, 256)
    for first in range(0, rows, tile):
        here = slice(first, first + tile)
        for group in range(3):
            state[here, group * out_width : (group + 1) * out_width] = jnp.dot(
                wide[here, :done], w_ref[group, :done, :], preferred_element_type=F32
            )
        power = None
        for lane in range(0, done, 128):
            values = wide[here, lane : lane + 128].astype(F32)
            power = values * values if power is None else power + values * values
        state[here, 3 * out_width :] = power


def finish_kernel(head_size, factor, state, w_ref, *refs):
    count = 2
    lasts, q_ref = refs[:count], refs[count]
    halves, pieces = refs[count + 1 : 2 * count + 1], refs[2 * count + 1 :]
    rows, width = lasts[0].shape
    depth, out_width = w_ref.shape[1:]
    for stream, last in enumerate(lasts):
        here = slice(stream * rows, (stream + 1) * rows)
        kv_ref = halves[stream]
        q, k, v = (
            state[here, group * out_width : (group + 1) * out_width]
            + jnp.dot(last[...], w_ref[group, depth - width :, :], preferred_element_type=F32)
            for group in range(3)
        )
        power = state[here, 3 * out_width :]
        for lane in range(0, width, 128):
            values = last[:, lane : lane + 128].astype(F32)
            power += values * values
        scale = lax.rsqrt(jnp.sum(power, axis=-1, keepdims=True) * (1.0 / depth) + 1e-06)
        q, k, v = q * scale, k * scale, v * scale
        for head in range(out_width // head_size):
            lanes = slice(head * head_size, (head + 1) * head_size)
            qh, kh = q[:, lanes], k[:, lanes]
            q_size = lax.rsqrt(jnp.sum(qh * qh, axis=-1, keepdims=True) + 1e-06)
            k_size = lax.rsqrt(jnp.sum(kh * kh, axis=-1, keepdims=True) + 1e-06)
            q_ref[here, lanes] = (qh * (q_size * (factor[head] * LOG2E))).astype(BF16)
            kv_ref[:, lanes] = (kh * k_size).astype(BF16)
        kv_ref[:, out_width:] = v.astype(BF16)
    start = 0
    for piece in pieces:
        end = start + piece.shape[0]
        for stream, half in enumerate(halves):
            base = stream * rows
            low, high = max(start, base), min(end, base + rows)
            if low < high:
                piece[low - start : high - start, :] = half[low - base : high - base, :]
        start = end


def project_begin(wide, weights, blocks):
    rows, depth = wide.shape
    groups, _, out_width = weights.shape
    return pl.pallas_call(
        functools.partial(begin_kernel, blocks),
        out_shape=pltpu.VMEM((rows, groups * out_width + 128), F32),
        in_specs=[VMEM] * 2,
        out_specs=VMEM,
        compiler_params=pltpu.CompilerParams(vmem_limit_bytes=16 << 20),
        cost_estimate=pl.CostEstimate(
            flops=2 * rows * depth * groups * out_width,
            bytes_accessed=2 * depth * (rows + groups * out_width),
            transcendentals=0,
        ),
        name="project_begin",
    )(in_vmem(wide), in_vmem(weights))


def project_finish(factor, state, weights, lasts, count_pieces, head_size):
    rows, width = lasts[0].shape
    out_width = weights.shape[2]
    total = rows * len(lasts)
    units = total // 16
    sizes = [rows] * len(lasts)
    sizes += [16 * ((units + n) // count_pieces) for n in range(count_pieces)]
    return pl.pallas_call(
        functools.partial(finish_kernel, head_size),
        out_shape=(
            pltpu.VMEM((total, out_width), BF16),
            *[pltpu.VMEM((size, 2 * out_width), BF16) for size in sizes],
        ),
        in_specs=[SMEM] + [VMEM] * (2 + len(lasts)),
        out_specs=(VMEM,) * (1 + len(sizes)),
        compiler_params=pltpu.CompilerParams(vmem_limit_bytes=16 << 20),
        cost_estimate=pl.CostEstimate(
            flops=6 * total * width * out_width, bytes_accessed=8 * total * out_width, transcendentals=0
        ),
        name="project_finish",
    )(in_hbm(factor), in_vmem(state), in_vmem(weights), *map(in_vmem, lasts))


def attend_kernel(
    head_size, counts, has_acc, count_out, count_streams, info, ids, id_row, q_ref, *refs
):
    count_blocks, count_parts = counts
    kv_refs, rest = refs[: count_blocks * count_parts], refs[count_blocks * count_parts :]
    if has_acc:
        acc_in, rest = rest[0], rest[1:]
    if count_out:
        w_hbm, outs, (k_all, v_ones, acc, attended, w_ref, sem) = rest[0], rest[1:-6], rest[-6:]
        fetch_w = pltpu.make_async_copy(w_hbm, w_ref, sem)
        fetch_w.start()
    else:
        acc_out, k_all, v_ones, acc = rest
    acc[...] = acc_in[...] if has_acc else jnp.zeros_like(acc)
    rows, width = q_ref.shape
    heads = width // head_size
    keys = k_all.shape[0]
    tile = id_row.shape[2]
    q_first = info[count_blocks]
    v_ones[:, :, head_size:] = jnp.ones((heads, keys, head_size), BF16)
    for number in range(count_blocks):
        begin = 0
        for kv_ref in kv_refs[number * count_parts : (number + 1) * count_parts]:
            here = slice(begin, begin + kv_ref.shape[0])
            begin += kv_ref.shape[0]
            k_all[here, :] = kv_ref[:, :width]
            for head in range(heads):
                start = width + head * head_size
                v_ones[head, here, :head_size] = kv_ref[:, start : start + head_size]
        first = info[number]
        key_low, key_high = ids[first], ids[first + keys - 1]

        @pl.loop(0, rows // tile)
        def _(index):
            base = pl.multiple_of(index * tile, tile)
            here = pl.ds(base, tile)
            q_low, q_high = ids[q_first + base], ids[q_first + base + tile - 1]

            def add(masked):
                if masked:
                    own = jnp.broadcast_to(id_row[q_first // tile + index], (8, tile))
                    own = jnp.transpose(own)[:, :1]
                    allowed = [id_row[first // tile + n] <= own for n in range(keys // tile)]
                for head in range(heads):
                    lanes = slice(head * head_size, (head + 1) * head_size)
                    spread = slice(2 * head * head_size, 2 * (head + 1) * head_size)
                    total = acc[here, spread]
                    for low in range(0, keys, tile):
                        score = lax.dot_general(
                            q_ref[here, lanes],
                            k_all[low : low + tile, lanes],
                            (((1,), (1,)), ((), ())),
                            preferred_element_type=F32,
                        )
                        weight = jnp.exp2(score)
                        if masked:
                            weight = jnp.where(allowed[low // tile], weight, 0.0)
                        total += jnp.dot(
                            weight.astype(BF16),
                            v_ones[head, low : low + tile, :],
                            preferred_element_type=F32,
                        )
                    acc[here, spread] = total

            @pl.when(key_high <= q_low)
            def _():
                add(False)

            @pl.when((key_high > q_low) & (key_low <= q_high))
            def _():
                add(True)

    if not count_out:
        acc_out[...] = acc[...]
        return
    for head in range(heads):
        start = 2 * head * head_size
        attended[:, head * head_size : (head + 1) * head_size] = (
            acc[:, start : start + head_size]
            / acc[:, start + head_size : start + 2 * head_size]
        ).astype(BF16)
    out_rows, out_width = outs[0].shape
    fetch_w.wait()
    for number, out in enumerate(outs):
        lane = info[count_blocks + 1 + number] * out_width
        first = number * count_streams // count_out * out_rows
        out[...] = jnp.dot(
            attended[first : first + out_rows, :],
            w_ref[:, pl.ds(pl.multiple_of(lane, out_width), out_width)],
            preferred_element_type=F32,
        ).astype(BF16)


def attend(info, ids, query, blocks, head_size, acc=None, w_out=None, streams=0, tile=512):
    total, width = query.shape
    parts = [part for block in blocks for part in block]
    keys = sum(part.shape[0] for part in blocks[0])
    heads = width // head_size
    count_out = streams * w_out.shape[1] // width if streams else 0
    scratch = [
        pltpu.VMEM((keys, width), BF16),
        pltpu.VMEM((heads, keys, 2 * head_size), BF16),
        pltpu.VMEM((total, 2 * width), F32),
    ]
    id_rows = ids.reshape(-1, 1, math.gcd(total, tile))
    operands = [in_vmem(query), *map(in_vmem, parts)]
    if acc is not None:
        operands.append(in_vmem(acc))
    if count_out:
        operands.append(in_hbm(w_out))
        scratch += [
            pltpu.VMEM((total, width), BF16),
            pltpu.VMEM(w_out.shape, BF16),
            pltpu.SemaphoreType.DMA(()),
        ]
        shape = pltpu.VMEM((total // streams, w_out.shape[1] * streams // count_out), BF16)
    else:
        shape = pltpu.VMEM((total, 2 * width), F32)
    outs = count_out or 1
    in_specs = [SMEM, SMEM, VMEM] + [VMEM] * len(operands)
    if count_out:
        in_specs[-1] = pl.BlockSpec(memory_space=pltpu.HBM)
    return pl.pallas_call(
        functools.partial(
            attend_kernel, head_size, (len(blocks), len(blocks[0])), acc is not None, count_out, streams
        ),
        out_shape=(shape,) * outs,
        in_specs=in_specs,
        out_specs=(VMEM,) * outs,
        scratch_shapes=scratch,
        compiler_params=pltpu.CompilerParams(
            vmem_limit_bytes=(16 << 20) + 4 * sum(part.size for part in parts)
        ),
        cost_estimate=pl.CostEstimate(flops=1 << 20, bytes_accessed=1 << 10, transcendentals=0),
        name="attend_last" if count_out else "attend",
    )(info, in_hbm(ids), in_hbm(id_rows), *operands)


def total_of(*parts):
    return sum(part.astype(F32) for part in parts).astype(BF16)


def body(mesh_shape, tokens, norm_gain, w_qkv, head_scale, w_out, scale_ids):
    ring, seqs = mesh_shape["head"], mesh_shape["seq"]
    outer = seqs // 2
    rows, width = tokens.shape
    half = rows // 2
    head_size = w_qkv.shape[2] // head_scale.shape[0]
    head_at, seq_at = lax.axis_index("head"), lax.axis_index("seq")
    place = ring_place(head_at, ring)
    chip, core = seq_at // 2, seq_at % 2
    index_at = lambda offset: ring_index((place + offset + ring) % ring, ring)
    numbers = lambda values: jnp.stack(values).astype(jnp.int32)
    at = [index_at(offset) for offset in range(ring)]

    streams = (0, 1)
    lanes = ((0, 0, 1), (1, 1, -1), (0, 1, -1), (1, 0, 1))
    farthest = ring // 2
    reach = [(farthest, farthest - 1), (farthest - 1, farthest)]

    order = [0] + [sign * step % ring for step in range(1, farthest) for sign in (-1, 1)] + [farthest]
    held = [[tokens[s * half : (s + 1) * half]] * 2 for s in streams]
    blocks, targets = [], []
    for step in range(1, farthest + 1):
        for s, way, sign in lanes:
            if step <= reach[s][way]:
                held[s][way] = along(held[s][way], sign, ring)
        if step == 1:
            held[0][0], (weights, wide) = lax.optimization_barrier(
                (held[0][0], fold_gain(order, numbers(at), norm_gain, w_qkv, tokens))
            )
        elif step == 2:
            wide = placed(targets, blocks, wide)
            blocks, targets = [], []
        elif step == 3:
            held[1][1], wide = lax.optimization_barrier(
                (held[1][1], placed(targets, blocks, wide))
            )
            blocks, targets = [], []
        if step < farthest:
            for s, way, sign in lanes:
                blocks.append(held[s][way])
                targets.append((s * half, (2 * step - 1 + way) * width))
    wide = placed(targets, blocks, wide)
    lasts = [held[0][0], held[1][1]]
    state = project_begin(wide, weights, ring)
    query, *parts = project_finish(head_scale, state, weights, lasts, 3, head_size)
    halves, pieces = parts[:2], parts[2:]

    far, straight, crossed = [], [], []
    for step in range(outer):
        source = 2 * ((chip + outer - step) % outer)
        straight.append((source + core) * rows)
        crossed.append((source + 1 - core) * rows)
        if step:
            shift = [(2 * a + b, 2 * ((a + step) % outer) + b) for a in range(outer) for b in (0, 1)]
            far.append([lax.ppermute(part, "seq", shift) for part in halves])
    first = [seq_at * rows]
    (acc,) = attend(numbers(straight[:1] + first), scale_ids, query, [halves], head_size, tile=256)
    near = [[swapped(piece, seqs) for piece in pieces]]
    acc, near = lax.optimization_barrier((acc, near))
    (acc,) = attend(numbers(crossed[:1] + first), scale_ids, query, near, head_size, acc, tile=256)
    acc, far = lax.optimization_barrier((acc, far))
    far_crossed = [[swapped(part, seqs) for part in block] for block in far]
    (acc,) = attend(numbers(straight[1:] + first), scale_ids, query, far, head_size, acc)

    goals = [[*range(up, 0, -1), *range(-down, 0), 0] for up, down in reach]
    info = numbers(crossed[1:] + first + [at[goal % ring] for goal in goals[0] + goals[1]])
    parts = attend(
        info, scale_ids, query, far_crossed, head_size, acc, w_out, len(streams)
    )
    parts = [dict(zip(goals[s], parts[s * ring : (s + 1) * ring])) for s in streams]
    sums = [[None, None] for s in streams]
    for step in range(farthest, 0, -1):
        for s, way, sign in lanes:
            if step <= reach[s][way]:
                part = parts[s][sign * step]
                if sums[s][way] is not None:
                    part = total_of(part, sums[s][way])
                sums[s][way] = along(part, sign, ring)
    ends = lax.optimization_barrier([sums[s][way] for s, way, sign in lanes[::-1]])
    for (s, way, sign), end in zip(lanes[::-1], ends):
        sums[s][way] = end
    return jnp.concatenate([total_of(parts[s][0], *sums[s]) for s in streams])


def solution(mesh):
    placed = (P("seq", "head"), P(), P(None, None, "head"), P("head"), P("head", None), P())
    return jax.shard_map(
        functools.partial(body, dict(mesh.shape)),
        mesh=mesh,
        in_specs=placed,
        out_specs=P("seq", "head"),
        check_vma=False,
    )
```
